32 devices in a mesh: groups: 2 (over y), chaos: 4 (over z), space: 4 (over x, core).
Axes of the slice: x: 2, y: 2, z: 4, core: 2. Of those that a mesh axis runs over, the one named last changes fastest.
Arguments:
- source_chaos_terms: float32 [176, 8, 4096], P(('groups', 'chaos'), 'space'), parts along dimension 0, may hold values from -6 to 6
- mean_conductivity: float32 [8, 4096], P('space'), may hold values from 0.1 to 0.4
- mode_shapes: float32 [6, 8, 4096], P(None, 'space'), may hold values from -0.07 to 0.07
- coupling: int32 [6, 28, 3], replicated, may hold values from 0 to 83, as said below
- slot_term: int32 [88], replicated, may hold values from -1 to 83, as said below
- bounds: float32 [4], P('groups'), parts along dimension 0, may hold values from 0.05 to 14, as said below
Outputs:
- solution_field: float32 [176, 8, 4096], P(('groups', 'chaos'), 'space'), parts along dimension 0
- residual: float32 [176, 8, 4096], P(('groups', 'chaos'), 'space'), parts along dimension 0
The draws below stay inside these ranges and needn't reach their ends.
There are 2 independent parts, one for each index of `groups`. The reference program is written for one: setup_inputs(seed, part) draws one part's arguments, and reference() takes and returns one part's arrays. A program takes and returns all parts, laid end to end along the dimension named above; an argument that names none is the same for every part. Nothing has to cross between parts.
Inputs may be any that keep to these rules, and one draw needn't show every extreme that they name: The basis is the 84 products of normalized Hermite polynomials of total degree at most 3 in 6 variables, numbered in some order. coupling[k] lists, once each, every pair of terms whose multi-indices differ only by one in mode k: the raised term, the lowered term, and the raised term's degree in mode k. `slot_term`: every term 0 to 83 stands in exactly one slot; the other slots hold -1. Slots s * 22 to s * 22 + 21 belong to index s of chaos; some index holds 22 terms. bounds[0] < bounds[1].
All inputs are finite; a program needn't handle non-finite values.
Results may differ from the reference program's by a relative error of at most 0.00011.
Values sent between devices are 32-bit elements; how exact they have to be, the bound alone decides.
No kernel may reach another device: no remote copies, remote signals or barrier semaphores. Data moves between devices by JAX's collectives and lax.ppermute only.
A program may use at most 128 MiB of HBM per device.

```python
import math
import jax
import jax.numpy as jnp
import numpy as np
from jax import lax

KL = 6
ORDER = 3
P_SIZE = 84
NY = 64
ITERS = 3
SLOTS_PER_INDEX = 22
TOTAL_SLOTS = 88
VERTICAL_CELLS = 8
LAYER_CELLS = 4096
N_CHAOS = 4


def multi_indices():
    combos = [()]
    for mode_index in range(KL):
        combos = [combo + (degree,) for combo in combos for degree in range(ORDER + 1)]
    return [combo for combo in combos if sum(combo) <= ORDER]


def chaos_pairs():
    multis = multi_indices()
    position = {combo: place for place, combo in enumerate(multis)}
    raised_list, lowered_list, level_list = ([], [], [])
    for mode_index in range(KL):
        raised_row, lowered_row, level_row = ([], [], [])
        for combo in multis:
            if sum(combo) < ORDER:
                upper = list(combo)
                upper[mode_index] += 1
                raised_row.append(position[tuple(upper)])
                lowered_row.append(position[combo])
                level_row.append(upper[mode_index])
        raised_list.append(raised_row)
        lowered_list.append(lowered_row)
        level_list.append(level_row)
    return (np.array(raised_list, np.int32), np.array(lowered_list, np.int32), np.array(level_list, np.int32))


def draw_coupling(key, part):
    key = jax.random.fold_in(key, 11)
    numbering = jax.random.permutation(key, P_SIZE).astype(jnp.int32)
    raised, lowered, levels = chaos_pairs()
    return jnp.stack([numbering[raised], numbering[lowered], jnp.asarray(levels)], axis=-1).astype(jnp.int32)


def draw_slot_term(key, part):
    key = jax.random.fold_in(key, 23)
    sorting_key, key_full = jax.random.split(key)
    ranking_values = jax.random.permutation(sorting_key, TOTAL_SLOTS).astype(jnp.int32)
    whole_device = jax.random.randint(key_full, (), 0, N_CHAOS)
    slot_entries = jnp.arange(TOTAL_SLOTS, dtype=jnp.int32)
    ranking_values = jnp.where(slot_entries // SLOTS_PER_INDEX == whole_device, slot_entries - TOTAL_SLOTS, ranking_values)
    ordering = jnp.argsort(ranking_values, stable=True)
    slot_keeper = jnp.full((TOTAL_SLOTS,), -1, jnp.int32)
    return slot_keeper.at[ordering[:P_SIZE]].set(jnp.arange(P_SIZE, dtype=jnp.int32))


def draw_bounds(key, part):
    key = jax.random.fold_in(key, 37)
    key_lower, key_upper = jax.random.split(key)
    lower_value = jax.random.uniform(key_lower, (), jnp.float32, 0.05, 0.3)
    upper_value = jax.random.uniform(key_upper, (), jnp.float32, 10.0, 14.0)
    return jnp.stack([lower_value, upper_value]).astype(jnp.float32)


def steps_of(key, shape, pieces, least, largest):
    level = 1.0
    for dim, parts in pieces:
        draws = jax.random.uniform(jax.random.fold_in(jax.random.fold_in(key, 6), dim), (parts,), jnp.float32, least / len(pieces), largest / len(pieces))
        level = level * jnp.repeat(jnp.exp(draws), shape[dim] // parts).reshape((-1,) + (1,) * (len(shape) - 1 - dim))
    return level


def centred(key, extent, spread, bound, cuts=(), held_as=jnp.bfloat16):
    result = spread * jax.random.normal(key, extent, jnp.float32)
    if cuts:
        result = result * steps_of(key, extent, cuts, -0.22, 0.18)
    return jnp.clip(result, -bound, bound).astype(held_as)


def setup_inputs(seed: int = 0, part: int = 0) -> dict:
    arg_keys = jax.random.split(jax.random.key(seed), 7)
    own_keys = jax.random.split(jax.random.fold_in(arg_keys[6], part), 7)
    source_chaos_terms = centred(own_keys[0], (TOTAL_SLOTS, VERTICAL_CELLS, LAYER_CELLS), 1.0, 6.0, ((0, 4), (1, 4)), jnp.float32)
    mean_conductivity = jnp.clip(jnp.exp(math.log(0.4) - 1.3862944 * jax.random.uniform(arg_keys[1], (VERTICAL_CELLS, LAYER_CELLS), jnp.float32) ** steps_of(arg_keys[1], (VERTICAL_CELLS, LAYER_CELLS), ((0, 4),), -0.2, 0.2)), 0.1, 0.4)
    mode_shapes = jnp.clip(jax.random.uniform(arg_keys[2], (KL, VERTICAL_CELLS, LAYER_CELLS), jnp.float32, -0.07, 0.07) * steps_of(arg_keys[2], (KL, VERTICAL_CELLS, LAYER_CELLS), ((1, 4),), -0.4, 0.0), -0.07, 0.07)
    coupling = draw_coupling(jax.random.fold_in(arg_keys[6], 71), part)
    slot_term = draw_slot_term(jax.random.fold_in(arg_keys[6], 71), part)
    bounds = draw_bounds(jax.random.fold_in(jax.random.fold_in(arg_keys[6], part), 71), part)
    return dict(source_chaos_terms=source_chaos_terms, mean_conductivity=mean_conductivity, mode_shapes=mode_shapes, coupling=coupling, slot_term=slot_term, bounds=bounds)


full_precision = lax.Precision.HIGHEST

def mixing_matrices(coupling, slot_term):
    occupied = (slot_term >= 0).astype(jnp.float32)
    raising = (slot_term[None, None, :] == coupling[:, :, 0:1]).astype(jnp.float32)
    lowering = (slot_term[None, None, :] == coupling[:, :, 1:2]).astype(jnp.float32)
    weight = jnp.sqrt(coupling[:, :, 2].astype(jnp.float32))
    raised = jnp.einsum('kps,kp,kpr->ksr', raising, weight, lowering, precision=full_precision)
    mode_mats = raised + jnp.transpose(raised, (0, 2, 1))
    return jnp.concatenate([jnp.diag(occupied)[None], mode_mats], axis=0)

def shift_cells(values, offset, edge_mask):
    fill = jnp.zeros(values.shape[:-1] + (abs(offset),), values.dtype)
    if offset > 0:
        shifted = jnp.concatenate([values[..., offset:], fill], axis=-1)
    else:
        shifted = jnp.concatenate([fill, values[..., :offset]], axis=-1)
    return shifted * edge_mask

def diffuse(field_padded, conduct_padded):
    centre = field_padded[..., 1:-1, :]
    conduct = conduct_padded[..., 1:-1, :]
    accumulated = 0.5 * (conduct + conduct_padded[..., :-2, :]) * (centre - field_padded[..., :-2, :])
    accumulated = accumulated + 0.5 * (conduct + conduct_padded[..., 2:, :]) * (centre - field_padded[..., 2:, :])
    cells = centre.shape[-1]
    column_in_row = lax.iota(jnp.int32, cells) % NY
    upper_mask = (column_in_row < NY - 1).astype(centre.dtype)
    lower_mask = (column_in_row > 0).astype(centre.dtype)
    all_mask = jnp.ones((cells,), centre.dtype)
    for offset, edge_mask in ((1, upper_mask), (-1, lower_mask), (NY, all_mask), (-NY, all_mask)):
        neighbour = shift_cells(centre, offset, edge_mask)
        neighbour_conduct = shift_cells(conduct, offset, edge_mask)
        accumulated = accumulated + 0.5 * (conduct + neighbour_conduct) * (centre - neighbour)
    return accumulated

def reference(source_chaos_terms, mean_conductivity, mode_shapes, coupling, slot_term, bounds):
    conductivity = jnp.concatenate([mean_conductivity[None], mean_conductivity[None] * mode_shapes], axis=0)
    matrices = mixing_matrices(coupling, slot_term)
    occupied = (slot_term >= 0).astype(jnp.float32)[:, None, None]

    def operator(direction):
        accumulated = jnp.zeros_like(direction)
        for mode_index in range(KL + 1):
            mixed_terms = jnp.einsum('sr,rzc->szc', matrices[mode_index], direction, precision=full_precision)
            field_padded = jnp.pad(mixed_terms, ((0, 0), (1, 1), (0, 0)))
            conduct_padded = jnp.pad(conductivity[mode_index], ((1, 1), (0, 0)))
            accumulated = accumulated + diffuse(field_padded, conduct_padded)
        return accumulated
    lower_bound = bounds[0]
    upper_bound = bounds[1]
    midpoint = 0.5 * (upper_bound + lower_bound)
    half_span = 0.5 * (upper_bound - lower_bound)
    sigma_one = midpoint / half_span
    rho_now = 1.0 / sigma_one
    residual = source_chaos_terms * occupied
    solution_field = jnp.zeros_like(residual)
    direction = residual / midpoint
    for iteration in range(ITERS):
        solution_field = solution_field + direction
        residual = residual - operator(direction)
        if iteration + 1 < ITERS:
            rho_next = 1.0 / (2.0 * sigma_one - rho_now)
            direction = rho_next * rho_now * direction + 2.0 * rho_next / half_span * residual
            rho_now = rho_next
    return (solution_field, residual)
```

```python
import functools

import jax
import jax.numpy as jnp
from jax import lax
from jax.experimental import pallas as pl
from jax.experimental.pallas import tpu as pltpu
from jax.sharding import PartitionSpec as P

NY = 64
ITERS = 3
LANES = 128
LAYERS = 8
BOTH = ("chaos", "space")


full_precision = lax.Precision.HIGHEST


def with_halo(cells, sides, width):
    for axis, dim in sides:
        count = lax.axis_size(axis)
        ends = count - 1
        head = lax.slice_in_dim(cells, 0, width, axis=dim)
        tail = lax.slice_in_dim(cells, cells.shape[dim] - width, cells.shape[dim], axis=dim)
        cells = jnp.concatenate(
            [
                lax.ppermute(tail, axis, [(i, (i + 1) % count) for i in range(ends)]),
                cells,
                lax.ppermute(head, axis, [((i + 1) % count, i) for i in range(ends)]),
            ],
            axis=dim,
        )
    return cells


def mixing_matrices(coupling, slot_term):
    occupied = (slot_term >= 0).astype(jnp.float32)
    raising = (slot_term[None, None, :] == coupling[:, :, 0:1]).astype(jnp.float32)
    lowering = (slot_term[None, None, :] == coupling[:, :, 1:2]).astype(jnp.float32)
    weight = jnp.sqrt(coupling[:, :, 2].astype(jnp.float32))
    raised = jnp.einsum("kps,kp,kpr->ksr", raising, weight, lowering, precision=full_precision)
    mode_mats = raised + jnp.transpose(raised, (0, 2, 1))
    return jnp.concatenate([jnp.diag(occupied)[None], mode_mats], axis=0)


def shift_cells(values, offset, edge_mask):
    fill = jnp.zeros(values.shape[:-1] + (abs(offset),), values.dtype)
    if offset > 0:
        shifted = jnp.concatenate([values[..., offset:], fill], axis=-1)
    else:
        shifted = jnp.concatenate([fill, values[..., :offset]], axis=-1)
    return shifted * edge_mask


def diffuse(field_padded, conduct_padded):
    centre = field_padded[..., 1:-1, :]
    conduct = conduct_padded[..., 1:-1, :]
    accumulated = (
        0.5 * (conduct + conduct_padded[..., :-2, :]) * (centre - field_padded[..., :-2, :])
    )
    accumulated = accumulated + 0.5 * (conduct + conduct_padded[..., 2:, :]) * (
        centre - field_padded[..., 2:, :]
    )
    cells = centre.shape[-1]
    column_in_row = lax.iota(jnp.int32, cells) % NY
    upper_mask = (column_in_row < NY - 1).astype(centre.dtype)
    lower_mask = (column_in_row > 0).astype(centre.dtype)
    all_mask = jnp.ones((cells,), centre.dtype)
    for offset, edge_mask in ((1, upper_mask), (-1, lower_mask), (NY, all_mask), (-NY, all_mask)):
        neighbour = shift_cells(centre, offset, edge_mask)
        neighbour_conduct = shift_cells(conduct, offset, edge_mask)
        accumulated = accumulated + 0.5 * (conduct + neighbour_conduct) * (centre - neighbour)
    return accumulated


def local_by_slots(source_chaos_terms, mean_conductivity, mode_shapes, coupling, slot_term, bounds):
    slot_count = source_chaos_terms.shape[0]
    conductivity = jnp.concatenate(
        [mean_conductivity[None], mean_conductivity[None] * mode_shapes], axis=0
    )
    conduct_padded = with_halo(conductivity, (("space", 1),), 1)
    matrices = mixing_matrices(coupling, slot_term)
    first_own = lax.axis_index("chaos") * slot_count
    own_rows = lax.dynamic_slice_in_dim(matrices, first_own, slot_count, 1)
    own_terms = lax.dynamic_slice_in_dim(slot_term, first_own, slot_count, 0)
    occupied = (own_terms >= 0).astype(jnp.float32)[:, None, None]
    lower_bound = bounds[0]
    upper_bound = bounds[1]
    midpoint = 0.5 * (upper_bound + lower_bound)
    half_span = 0.5 * (upper_bound - lower_bound)
    sigma_one = midpoint / half_span
    rho_now = 1.0 / sigma_one
    residual = source_chaos_terms * occupied
    solution_field = jnp.zeros_like(residual)
    direction = residual / midpoint
    for iteration in range(ITERS):
        solution_field = solution_field + direction
        fields = jnp.einsum(
            "ksr,rzc->kszc",
            own_rows,
            lax.all_gather(direction, "chaos", axis=0, tiled=True),
            precision=full_precision,
        )
        field_padded = with_halo(fields, (("space", 2),), 1)
        diffused = diffuse(field_padded, conduct_padded[:, None])
        residual = residual - jnp.sum(diffused, axis=0)
        if iteration + 1 < ITERS:
            rho_next = 1.0 / (2.0 * sigma_one - rho_now)
            direction = rho_next * rho_now * direction + 2.0 * rho_next / half_span * residual
            rho_now = rho_next
    return (solution_field, residual)


def block_of(device, spaces):
    chaos, space = divmod(device, spaces)
    return chaos * spaces + (space if chaos % 2 == 0 else spaces - 1 - space)


def iotas():
    lane = lax.broadcasted_iota(jnp.int32, (LAYERS, LANES), 1)
    layer = lax.broadcasted_iota(jnp.int32, (LAYERS, LANES), 0)
    return lane, layer


def half_masks():
    lane, layer = iotas()
    return lane < NY, lane % NY > 0, lane % NY < NY - 1, layer > 0, layer < LAYERS - 1


def neighbour_sum(tiles, masks, halo=None):
    low_half, has_left, has_right, has_below, has_above = masks
    zero = jnp.zeros((LAYERS, LANES), jnp.float32)
    edge = zero if halo is None else halo
    swapped = [pltpu.roll(tile, NY, 1) for tile in tiles]
    between = [
        jnp.where(low_half, swapped[t], swapped[t + 1]) for t in range(len(tiles) - 1)
    ]
    sums = []
    for t, tile in enumerate(tiles):
        upward = between[t] if t + 1 < len(tiles) else jnp.where(low_half, swapped[t], edge)
        downward = between[t - 1] if t > 0 else jnp.where(low_half, edge, swapped[t])
        left = jnp.where(has_left, pltpu.roll(tile, 1, 1), zero)
        right = jnp.where(has_right, pltpu.roll(tile, LANES - 1, 1), zero)
        below = jnp.where(has_below, pltpu.roll(tile, 1, 0), zero)
        above = jnp.where(has_above, pltpu.roll(tile, LAYERS - 1, 0), zero)
        sums.append((upward + downward) + (left + right) + (below + above))
    return sums


def tiles_of(ref, index, count):
    return [ref[index, :, pl.ds(t * LANES, LANES)] for t in range(count)]


def put_tiles(ref, index, tiles):
    for t, tile in enumerate(tiles):
        ref[index, :, pl.ds(t * LANES, LANES)] = tile


def scatter_kernel(blocks, source_ref, out_ref):
    width = out_ref.shape[-1]
    for device, block in enumerate(blocks):
        out_ref[device] = source_ref[:, :, block * width : (block + 1) * width]


def collect_kernel(blocks, in_ref, out_ref):
    width = in_ref.shape[-1]
    for device, block in enumerate(blocks):
        out_ref[:, :, block * width : (block + 1) * width] = in_ref[device]


def messages(low, high, up_ref, down_ref, pair, low_half):
    up_ref[pair] = jnp.where(low_half, pltpu.roll(high[-1], NY, 1), low[-1])
    down_ref[pair] = jnp.where(low_half, low[0], pltpu.roll(high[0], NY, 1))


def start_kernel(
    chaos, spaces, occupied, scales, in_ref, residual_ref, direction_ref, up_ref, down_ref
):
    own = in_ref.shape[1]
    thick = in_ref.shape[2]
    count = in_ref.shape[3] // LANES
    for c in range(chaos):
        for s in range(spaces):
            residual_ref[c * own : (c + 1) * own, s * thick : (s + 1) * thick, :] = in_ref[
                c * spaces + s
            ]
    half = chaos * own // 2
    low_half = iotas()[0] < NY
    scale = scales[0]

    def step(pair, carry):
        kept = []
        for slot in (pair, pair + half):
            weight = occupied[slot]
            tiles = [tile * weight for tile in tiles_of(residual_ref, slot, count)]
            put_tiles(residual_ref, slot, tiles)
            direction = [tile * scale for tile in tiles]
            put_tiles(direction_ref, slot, direction)
            kept.append(direction)
        messages(kept[0], kept[1], up_ref, down_ref, pair, low_half)
        return carry

    lax.fori_loop(0, half, step, 0, unroll=2)


def coefficient_kernel(field_ref, halo_ref, a_ref, b_ref, face_ref):
    modes = field_ref.shape[0]
    count = field_ref.shape[2] // LANES
    masks = half_masks()
    low_half = masks[0]
    mean = None
    for k in range(modes):
        tiles = tiles_of(field_ref, k, count)
        halo = halo_ref[k]
        if k == 0:
            mean, mean_halo = tiles, halo
        else:
            tiles = [tile * m for tile, m in zip(tiles, mean)]
            halo = halo * mean_halo
        sums = neighbour_sum(tiles, masks, halo)
        put_tiles(a_ref, k, tiles)
        put_tiles(b_ref, k, [6.0 * tile + total for tile, total in zip(tiles, sums)])
        face_ref[k] = 0.5 * (jnp.where(low_half, tiles[0], tiles[-1]) + halo)


def own_kernel(raised, lowered, up_weight, down_weight, a_ref, b_ref, d_ref, out_ref, sum_ref):
    slots = d_ref.shape[0]
    count = d_ref.shape[2] // LANES
    modes = a_ref.shape[0]
    masks = half_masks()

    def sums(slot, carry):
        put_tiles(sum_ref, slot, neighbour_sum(tiles_of(d_ref, slot, count), masks))
        return carry

    lax.fori_loop(0, slots, sums, 0, unroll=4)

    def mix(slot, carry):
        total, edge = [], []
        a, b = tiles_of(a_ref, 0, count), tiles_of(b_ref, 0, count)
        d, s = tiles_of(d_ref, slot, count), tiles_of(sum_ref, slot, count)
        for t in range(count):
            total.append(b[t] * d[t] - a[t] * s[t])
            edge.append(a[t] * d[t])
        for k in range(1, modes):
            place = (k - 1) * slots + slot
            high, low = raised[place], lowered[place]
            up, down = up_weight[place], down_weight[place]
            a, b = tiles_of(a_ref, k, count), tiles_of(b_ref, k, count)
            d_high, d_low = tiles_of(d_ref, high, count), tiles_of(d_ref, low, count)
            s_high, s_low = tiles_of(sum_ref, high, count), tiles_of(sum_ref, low, count)
            for t in range(count):
                mixed = up * d_high[t] + down * d_low[t]
                around = up * s_high[t] + down * s_low[t]
                total[t] = total[t] + (b[t] * mixed - a[t] * around)
                edge[t] = edge[t] + a[t] * mixed
        spread = neighbour_sum(edge, masks)
        put_tiles(out_ref, slot, [0.5 * (total[t] - spread[t]) for t in range(count)])
        return carry

    lax.fori_loop(0, slots, mix, 0, unroll=2)


def step_kernel(
    step_index,
    chaos,
    spaces,
    raised,
    lowered,
    up_weight,
    down_weight,
    scales,
    face_ref,
    diffused_ref,
    from_below_ref,
    from_above_ref,
    *rest,
):
    last = step_index == ITERS - 1
    before_last = step_index == ITERS - 2
    rest = list(rest)
    residual_ref = rest.pop(0)
    if not last:
        direction_ref = rest.pop(0)
    if step_index > 0 and not last:
        solution_ref = rest.pop(0)
    if last:
        residual_out, halo_ref, held_ref = rest
    elif before_last:
        new_residual_ref, new_direction_ref, solution_out, up_ref, down_ref, halo_ref, held_ref = rest
    else:
        new_residual_ref, new_direction_ref, new_solution_ref, up_ref, down_ref, halo_ref = rest
    slots = diffused_ref.shape[0]
    count = diffused_ref.shape[2] // LANES
    modes = face_ref.shape[0]
    half = slots // 2
    low_half = iotas()[0] < NY
    zero = jnp.zeros((LAYERS, LANES), jnp.float32)

    def unpack(pair, carry):
        below, above = from_below_ref[pair], from_above_ref[pair]
        halo_ref[pair] = pltpu.roll(jnp.where(low_half, above, below), NY, 1)
        halo_ref[pair + half] = jnp.where(low_half, below, above)
        return carry

    lax.fori_loop(0, half, unpack, 0, unroll=4)

    def update(pair, carry):
        kept = []
        for slot in (pair, pair + half):
            part = face_ref[0] * halo_ref[slot]
            for k in range(1, modes):
                place = (k - 1) * slots + slot
                mixed = (
                    up_weight[place] * halo_ref[raised[place]]
                    + down_weight[place] * halo_ref[lowered[place]]
                )
                part = part + face_ref[k] * mixed
            diffused = tiles_of(diffused_ref, slot, count)
            diffused[0] = diffused[0] - jnp.where(low_half, part, zero)
            diffused[-1] = diffused[-1] - jnp.where(low_half, zero, part)
            residual = [
                r - x for r, x in zip(tiles_of(residual_ref, slot, count), diffused)
            ]
            if last:
                put_tiles(held_ref, slot, residual)
                continue
            put_tiles(new_residual_ref, slot, residual)
            old = tiles_of(direction_ref, slot, count)
            keep, add = scales[1 + 2 * step_index], scales[2 + 2 * step_index]
            direction = [keep * d + add * r for d, r in zip(old, residual)]
            put_tiles(new_direction_ref, slot, direction)
            start = old if step_index == 0 else tiles_of(solution_ref, slot, count)
            solution = [x + d for x, d in zip(start, direction)]
            put_tiles(held_ref if before_last else new_solution_ref, slot, solution)
            kept.append(direction)
        if not last:
            messages(kept[0], kept[1], up_ref, down_ref, pair, low_half)
        return carry

    lax.fori_loop(0, half, update, 0)
    if last or before_last:
        out_ref = residual_out if last else solution_out
        own = out_ref.shape[1]
        thick = out_ref.shape[2]
        for c in range(chaos):
            for s in range(spaces):
                out_ref[c * spaces + s] = held_ref[
                    c * own : (c + 1) * own, s * thick : (s + 1) * thick, :
                ]


def call(kernel, outs, scalars, arrays, scratch=(), flops=0):
    in_specs = [pl.BlockSpec(memory_space=pltpu.SMEM)] * len(scalars) + [
        pl.BlockSpec(memory_space=pltpu.VMEM)
    ] * len(arrays)
    moved = sum(4 * x.size for x in arrays) + sum(4 * x.size for x in outs)
    return pl.pallas_call(
        kernel,
        out_shape=outs,
        in_specs=in_specs,
        out_specs=[pl.BlockSpec(memory_space=pltpu.VMEM)] * len(outs),
        scratch_shapes=[pltpu.VMEM(shape, jnp.float32) for shape in scratch],
        compiler_params=pltpu.CompilerParams(vmem_limit_bytes=32 * 1024 * 1024),
        cost_estimate=pl.CostEstimate(flops=flops, bytes_accessed=moved, transcendentals=0),
    )(*scalars, *arrays)


def coupling_tables(coupling, slot_term):
    slots = slot_term.shape[0]
    number = lax.iota(jnp.int32, slots)
    raising = (slot_term[None, None, :] == coupling[:, :, 0:1]).astype(jnp.int32)
    lowering = (slot_term[None, None, :] == coupling[:, :, 1:2]).astype(jnp.int32)
    raising_slot = jnp.sum(raising * number, axis=2)
    lowering_slot = jnp.sum(lowering * number, axis=2)
    weight = jnp.sqrt(coupling[:, :, 2].astype(jnp.float32))
    raised = jnp.sum(lowering * raising_slot[:, :, None], axis=1)
    lowered = jnp.sum(raising * lowering_slot[:, :, None], axis=1)
    up_weight = jnp.sum(lowering.astype(jnp.float32) * weight[:, :, None], axis=1)
    down_weight = jnp.sum(raising.astype(jnp.float32) * weight[:, :, None], axis=1)
    return [table.reshape(-1) for table in (raised, lowered, up_weight, down_weight)]


def local_by_cells(source_chaos_terms, mean_conductivity, mode_shapes, coupling, slot_term, bounds):
    own, thick, cells = source_chaos_terms.shape
    chaos, spaces = lax.axis_size("chaos"), lax.axis_size("space")
    devices = chaos * spaces
    width = cells // devices
    slots = own * chaos
    blocks = [block_of(device, spaces) for device in range(devices)]
    f32 = jnp.float32

    def shape(*sizes):
        return jax.ShapeDtypeStruct(sizes, f32)

    scattered = call(
        functools.partial(scatter_kernel, blocks),
        [shape(devices, own, thick, width)],
        [],
        [source_chaos_terms],
    )[0]
    gathered = lax.all_to_all(scattered, BOTH, 0, 0, tiled=True)

    modes = mode_shapes.shape[0] + 1
    raw = jnp.concatenate([mean_conductivity[None], mode_shapes], axis=0)
    padded = jnp.pad(raw, ((0, 0), (0, 0), (NY, NY)))
    row = lax.axis_index("chaos")
    run = lax.dynamic_slice_in_dim(padded, row * spaces * width, spaces * width + 2 * NY, 2)
    pieces = jnp.stack(
        [run[:, :, s * width : (s + 1) * width + 2 * NY] for s in range(spaces)], axis=0
    )
    pieces = jnp.where(row % 2 == 0, pieces, pieces[::-1])
    pieces = lax.all_to_all(pieces, "space", 0, 0, tiled=True)
    wide = jnp.transpose(pieces, (1, 0, 2, 3)).reshape(modes, LAYERS, width + 2 * NY)
    field = wide[:, :, NY : NY + width]
    edges = jnp.concatenate([wide[:, :, :NY], wide[:, :, NY + width :]], axis=2)
    a, b, face = call(
        coefficient_kernel,
        [shape(modes, LAYERS, width), shape(modes, LAYERS, width), shape(modes, LAYERS, LANES)],
        [],
        [field, edges],
    )

    tables = coupling_tables(coupling, slot_term)
    occupied = (slot_term >= 0).astype(f32)
    midpoint = 0.5 * (bounds[1] + bounds[0])
    half_span = 0.5 * (bounds[1] - bounds[0])
    sigma_one = midpoint / half_span
    rho_now = 1.0 / sigma_one
    scales = [1.0 / midpoint]
    for _ in range(ITERS - 1):
        rho_next = 1.0 / (2.0 * sigma_one - rho_now)
        scales += [rho_next * rho_now, 2.0 * rho_next / half_span]
        rho_now = rho_next
    scales = jnp.stack(scales)

    full = shape(slots, LAYERS, width)
    packed = shape(slots // 2, LAYERS, LANES)
    sent = shape(devices, own, thick, width)
    residual, direction, up, down = call(
        functools.partial(start_kernel, chaos, spaces),
        [full, full, packed, packed],
        [occupied, scales],
        [gathered],
    )
    place = {block: device for device, block in enumerate(blocks)}
    upward = [(place[n], place[n + 1]) for n in range(devices - 1)]
    downward = [(place[n + 1], place[n]) for n in range(devices - 1)]
    solution_field = None
    for step_index in range(ITERS):
        from_below = lax.ppermute(up, BOTH, upward)
        from_above = lax.ppermute(down, BOTH, downward)
        diffused = call(
            own_kernel, [full], tables, [a, b, direction], [full.shape], flops=40000000
        )[0]
        last = step_index == ITERS - 1
        before_last = step_index == ITERS - 2
        arrays = [face, diffused, from_below, from_above, residual]
        if not last:
            arrays.append(direction)
        if step_index > 0 and not last:
            arrays.append(solution_field)
        halo = (slots, LAYERS, LANES)
        if last:
            outs, scratch = [sent], [halo, full.shape]
        elif before_last:
            outs, scratch = [full, full, sent, packed, packed], [halo, full.shape]
        else:
            outs, scratch = [full, full, full, packed, packed], [halo]
        results = call(
            functools.partial(step_kernel, step_index, chaos, spaces),
            outs,
            tables + [scales],
            arrays,
            scratch,
            flops=10000000,
        )
        if last:
            residual = results[0]
        else:
            residual, direction, solution_field, up, down = results

    def back(field_sent):
        received = lax.all_to_all(field_sent, BOTH, 0, 0, tiled=True)
        return call(
            functools.partial(collect_kernel, blocks), [shape(own, thick, cells)], [], [received]
        )[0]

    return (back(solution_field), back(residual))


def local(source_chaos_terms, mean_conductivity, mode_shapes, coupling, slot_term, bounds):
    own, thick, cells = source_chaos_terms.shape
    chaos, spaces = lax.axis_size("chaos"), lax.axis_size("space")
    fits = (
        thick * spaces == LAYERS
        and cells % (chaos * spaces * LANES) == 0
        and (own * chaos) % 2 == 0
    )
    plan = local_by_cells if fits else local_by_slots
    return plan(
        source_chaos_terms, mean_conductivity, mode_shapes, coupling, slot_term, bounds
    )


def solution(mesh):
    in_specs = (
        P(("groups", "chaos"), "space", None),
        P("space", None),
        P(None, "space", None),
        P(),
        P(),
        P("groups"),
    )
    out_specs = (P(("groups", "chaos"), "space", None), P(("groups", "chaos"), "space", None))
    return jax.shard_map(local, mesh=mesh, in_specs=in_specs, out_specs=out_specs, check_vma=False)
```

```python
import functools

import jax
import jax.numpy as jnp
from jax import lax
from jax.experimental import pallas as pl
from jax.experimental.pallas import tpu as pltpu
from jax.sharding import PartitionSpec as P

NY = 64
ITERS = 3
LANES = 128
BOTH = ("chaos", "space")


full_precision = lax.Precision.HIGHEST


def with_halo(cells, sides, width):
    for axis, dim in sides:
        count = lax.axis_size(axis)
        ends = count - 1
        head = lax.slice_in_dim(cells, 0, width, axis=dim)
        tail = lax.slice_in_dim(cells, cells.shape[dim] - width, cells.shape[dim], axis=dim)
        cells = jnp.concatenate(
            [
                lax.ppermute(tail, axis, [(i, (i + 1) % count) for i in range(ends)]),
                cells,
                lax.ppermute(head, axis, [((i + 1) % count, i) for i in range(ends)]),
            ],
            axis=dim,
        )
    return cells


def mixing_matrices(coupling, slot_term):
    occupied = (slot_term >= 0).astype(jnp.float32)
    raising = (slot_term[None, None, :] == coupling[:, :, 0:1]).astype(jnp.float32)
    lowering = (slot_term[None, None, :] == coupling[:, :, 1:2]).astype(jnp.float32)
    weight = jnp.sqrt(coupling[:, :, 2].astype(jnp.float32))
    raised = jnp.einsum("kps,kp,kpr->ksr", raising, weight, lowering, precision=full_precision)
    mode_mats = raised + jnp.transpose(raised, (0, 2, 1))
    return jnp.concatenate([jnp.diag(occupied)[None], mode_mats], axis=0)


def shift_cells(values, offset, edge_mask):
    fill = jnp.zeros(values.shape[:-1] + (abs(offset),), values.dtype)
    if offset > 0:
        shifted = jnp.concatenate([values[..., offset:], fill], axis=-1)
    else:
        shifted = jnp.concatenate([fill, values[..., :offset]], axis=-1)
    return shifted * edge_mask


def diffuse(field_padded, conduct_padded):
    centre = field_padded[..., 1:-1, :]
    conduct = conduct_padded[..., 1:-1, :]
    accumulated = (
        0.5 * (conduct + conduct_padded[..., :-2, :]) * (centre - field_padded[..., :-2, :])
    )
    accumulated = accumulated + 0.5 * (conduct + conduct_padded[..., 2:, :]) * (
        centre - field_padded[..., 2:, :]
    )
    cells = centre.shape[-1]
    column_in_row = lax.iota(jnp.int32, cells) % NY
    upper_mask = (column_in_row < NY - 1).astype(centre.dtype)
    lower_mask = (column_in_row > 0).astype(centre.dtype)
    all_mask = jnp.ones((cells,), centre.dtype)
    for offset, edge_mask in ((1, upper_mask), (-1, lower_mask), (NY, all_mask), (-NY, all_mask)):
        neighbour = shift_cells(centre, offset, edge_mask)
        neighbour_conduct = shift_cells(conduct, offset, edge_mask)
        accumulated = accumulated + 0.5 * (conduct + neighbour_conduct) * (centre - neighbour)
    return accumulated


def local_by_slots(source_chaos_terms, mean_conductivity, mode_shapes, coupling, slot_term, bounds):
    slot_count = source_chaos_terms.shape[0]
    conductivity = jnp.concatenate(
        [mean_conductivity[None], mean_conductivity[None] * mode_shapes], axis=0
    )
    conduct_padded = with_halo(conductivity, (("space", 1),), 1)
    matrices = mixing_matrices(coupling, slot_term)
    first_own = lax.axis_index("chaos") * slot_count
    own_rows = lax.dynamic_slice_in_dim(matrices, first_own, slot_count, 1)
    own_terms = lax.dynamic_slice_in_dim(slot_term, first_own, slot_count, 0)
    occupied = (own_terms >= 0).astype(jnp.float32)[:, None, None]
    lower_bound = bounds[0]
    upper_bound = bounds[1]
    midpoint = 0.5 * (upper_bound + lower_bound)
    half_span = 0.5 * (upper_bound - lower_bound)
    sigma_one = midpoint / half_span
    rho_now = 1.0 / sigma_one
    residual = source_chaos_terms * occupied
    solution_field = jnp.zeros_like(residual)
    direction = residual / midpoint
    for iteration in range(ITERS):
        solution_field = solution_field + direction
        fields = jnp.einsum(
            "ksr,rzc->kszc",
            own_rows,
            lax.all_gather(direction, "chaos", axis=0, tiled=True),
            precision=full_precision,
        )
        field_padded = with_halo(fields, (("space", 2),), 1)
        diffused = diffuse(field_padded, conduct_padded[:, None])
        residual = residual - jnp.sum(diffused, axis=0)
        if iteration + 1 < ITERS:
            rho_next = 1.0 / (2.0 * sigma_one - rho_now)
            direction = rho_next * rho_now * direction + 2.0 * rho_next / half_span * residual
            rho_now = rho_next
    return (solution_field, residual)


def block_of(device, spaces):
    chaos, space = divmod(device, spaces)
    return chaos * spaces + (space if chaos % 2 == 0 else spaces - 1 - space)


def lane_masks(rows):
    lane = lax.broadcasted_iota(jnp.int32, (rows, LANES), 1)
    return lane < NY, lane % NY > 0, lane % NY < NY - 1


def plane_sum(tiles, masks, halo=None):
    low_half, has_left, has_right = masks
    zero = jnp.zeros(tiles[0].shape, jnp.float32)
    edge = zero if halo is None else halo
    count = len(tiles)
    swapped = [pltpu.roll(tile, NY, 1) for tile in tiles]
    between = [jnp.where(low_half, swapped[t], swapped[t + 1]) for t in range(count - 1)]
    sums = []
    for t, tile in enumerate(tiles):
        upward = between[t] if t + 1 < count else jnp.where(low_half, swapped[t], edge)
        downward = between[t - 1] if t > 0 else jnp.where(low_half, edge, swapped[t])
        left = jnp.where(has_left, pltpu.roll(tile, 1, 1), zero)
        right = jnp.where(has_right, pltpu.roll(tile, LANES - 1, 1), zero)
        sums.append((upward + downward) + (left + right))
    return sums


def neighbour_sums(read, layer, layers, masks):
    sums = plane_sum(read(layer), masks)
    for other in (layer - 1, layer + 1):
        if 0 <= other < layers:
            sums = [total + tile for total, tile in zip(sums, read(other))]
    return sums


def split_stack(tiles, depth):
    wide = jnp.concatenate(tiles, axis=1)
    spare = depth // 2 - wide.shape[0]
    if spare:
        wide = jnp.concatenate([wide, jnp.zeros((spare, wide.shape[1]), wide.dtype)], axis=0)
    high = wide.astype(jnp.bfloat16)
    low = (wide - high.astype(jnp.float32)).astype(jnp.bfloat16)
    return jnp.concatenate([high, low], axis=0)


def lanes(t):
    return pl.ds(t * LANES, LANES)


def scatter_kernel(blocks, own, thick, tiles, in_ref, out_ref):
    stride = in_ref.shape[0] // own
    for device, block in enumerate(blocks):
        for t in range(tiles):
            for z in range(thick):
                out_ref[device, pl.ds((t * thick + z) * own, own), :] = in_ref[
                    pl.ds((block * tiles + t) * thick + z, own, stride=stride), :
                ]


def collect_kernel(blocks, own, thick, tiles, in_ref, out_ref):
    stride = out_ref.shape[0] // own
    for device, block in enumerate(blocks):
        for t in range(tiles):
            for z in range(thick):
                out_ref[pl.ds((block * tiles + t) * thick + z, own, stride=stride), :] = in_ref[
                    device, pl.ds((t * thick + z) * own, own), :
                ]


def put_messages(read, up_ref, down_ref, low_half):
    half = up_ref.shape[0]
    for l in range(half):
        first, second = read(l), read(l + half)
        up_ref[l] = jnp.where(low_half, pltpu.roll(second[-1], NY, 1), first[-1])
        down_ref[l] = jnp.where(low_half, first[0], pltpu.roll(second[0], NY, 1))


def start_kernel(
    chaos, spaces, scales, weight_ref, in_ref, residual_ref, direction_ref, up_ref, down_ref
):
    layers, tiles, slots, _ = residual_ref.shape
    own = slots // chaos
    thick = layers // spaces
    low_half = lane_masks(slots)[0]
    weight = weight_ref[...]
    scale = scales[0]
    for l in range(layers):
        i, z = divmod(l, thick)
        for t in range(tiles):
            rows = pl.ds((t * thick + z) * own, own)
            residual = weight * jnp.concatenate(
                [in_ref[c * spaces + i, rows, :] for c in range(chaos)], axis=0
            )
            residual_ref[l, t] = residual
            direction_ref[l, t] = residual * scale
    put_messages(
        lambda l: [direction_ref[l, t] for t in range(tiles)], up_ref, down_ref, low_half
    )


def coefficient_kernel(field_ref, halo_ref, a_ref, b_ref, face_ref):
    modes, layers, width = field_ref.shape
    tiles = width // LANES
    masks = lane_masks(layers)
    layer = lax.broadcasted_iota(jnp.int32, (layers, LANES), 0)
    zero = jnp.zeros((layers, LANES), jnp.float32)
    mean = mean_halo = None
    for k in range(modes):
        values = [field_ref[k, :, lanes(t)] for t in range(tiles)]
        halo = halo_ref[k]
        if k == 0:
            mean, mean_halo = values, halo
        else:
            values = [value * m for value, m in zip(values, mean)]
            halo = halo * mean_halo
        sums = plane_sum(values, masks, halo)
        for t in range(tiles):
            below = jnp.where(layer > 0, pltpu.roll(values[t], 1, 0), zero)
            above = jnp.where(layer < layers - 1, pltpu.roll(values[t], layers - 1, 0), zero)
            a_ref[k, :, lanes(t)] = values[t]
            b_ref[k, :, lanes(t)] = 6.0 * values[t] + (sums[t] + (below + above))
        face_ref[k] = 0.5 * (jnp.where(masks[0], values[0], values[-1]) + halo)


def own_kernel(mix_ref, a_ref, b_ref, d_ref, out_ref, edge_ref):
    layers, tiles, slots, _ = d_ref.shape
    modes = a_ref.shape[0]
    masks = lane_masks(slots)
    mix = mix_ref[...]
    depth = mix.shape[1]

    def read(l):
        return [d_ref[l, t] for t in range(tiles)]

    def read_edge(l):
        return [edge_ref[l, t] for t in range(tiles)]

    for l in range(layers):
        direct = read(l)
        around = neighbour_sums(read, l, layers, masks)
        mixed = jnp.dot(mix, split_stack(direct, depth), preferred_element_type=jnp.float32)
        mixed_around = jnp.dot(
            mix, split_stack(around, depth), preferred_element_type=jnp.float32
        )
        for t in range(tiles):
            a, b = a_ref[0, l : l + 1, lanes(t)], b_ref[0, l : l + 1, lanes(t)]
            total = b * direct[t] - a * around[t]
            edge = a * direct[t]
            for k in range(1, modes):
                a, b = a_ref[k, l : l + 1, lanes(t)], b_ref[k, l : l + 1, lanes(t)]
                rows = slice((k - 1) * slots, k * slots)
                columns = slice(t * LANES, (t + 1) * LANES)
                total = total + (b * mixed[rows, columns] - a * mixed_around[rows, columns])
                edge = edge + a * mixed[rows, columns]
            out_ref[l, t] = total
            edge_ref[l, t] = edge
    for l in range(layers):
        spread = neighbour_sums(read_edge, l, layers, masks)
        for t in range(tiles):
            out_ref[l, t] = 0.5 * (out_ref[l, t] - spread[t])


def step_kernel(
    step_index,
    chaos,
    spaces,
    scales,
    mix_ref,
    face_ref,
    weight_ref,
    diffused_ref,
    from_below_ref,
    from_above_ref,
    *rest,
):
    last = step_index == ITERS - 1
    before_last = step_index == ITERS - 2
    rest = list(rest)
    residual_ref = rest.pop(0)
    if not last:
        direction_ref = rest.pop(0)
    if step_index > 0 and not last:
        solution_ref = rest.pop(0)
    if last:
        sent_ref, held_ref = rest
    elif before_last:
        new_residual_ref, new_direction_ref, sent_ref, up_ref, down_ref, held_ref = rest
    else:
        new_residual_ref, new_direction_ref, new_solution_ref, up_ref, down_ref = rest
    layers, tiles, slots, _ = diffused_ref.shape
    modes = face_ref.shape[0]
    half = layers // 2
    low_half = lane_masks(slots)[0]
    zero = jnp.zeros((slots, LANES), jnp.float32)
    mix = mix_ref[...]
    for pair in range(half):
        below, above = from_below_ref[pair], from_above_ref[pair]
        halos = [
            pltpu.roll(jnp.where(low_half, above, below), NY, 1),
            jnp.where(low_half, below, above),
        ]
        mixed = jnp.dot(
            mix, split_stack(halos, mix.shape[1]), preferred_element_type=jnp.float32
        )
        for n, l in enumerate((pair, pair + half)):
            part = face_ref[0, l : l + 1, :] * halos[n]
            for k in range(1, modes):
                part = part + face_ref[k, l : l + 1, :] * (
                    mixed[(k - 1) * slots : k * slots, n * LANES : (n + 1) * LANES]
                )
            for t in range(tiles):
                residual = residual_ref[l, t] - diffused_ref[l, t]
                if t == 0:
                    residual = residual + jnp.where(low_half, part, zero)
                if t == tiles - 1:
                    residual = residual + jnp.where(low_half, zero, part)
                if last:
                    held_ref[l, t] = residual * weight_ref[...]
                    continue
                new_residual_ref[l, t] = residual
                old = direction_ref[l, t]
                keep, add = scales[1 + 2 * step_index], scales[2 + 2 * step_index]
                direction = keep * old + add * residual
                new_direction_ref[l, t] = direction
                start = old if step_index == 0 else solution_ref[l, t]
                if before_last:
                    held_ref[l, t] = (start + direction) * weight_ref[...]
                else:
                    new_solution_ref[l, t] = start + direction
    if not last:
        put_messages(
            lambda l: [new_direction_ref[l, t] for t in range(tiles)],
            up_ref,
            down_ref,
            low_half,
        )
    if last or before_last:
        own = slots // chaos
        thick = layers // spaces
        for c in range(chaos):
            for l in range(layers):
                i, z = divmod(l, thick)
                for t in range(tiles):
                    sent_ref[c * spaces + i, pl.ds((t * thick + z) * own, own), :] = held_ref[
                        l, t, pl.ds(c * own, own), :
                    ]


def call(kernel, outs, scalars, arrays, scratch=(), flops=0):
    in_specs = [pl.BlockSpec(memory_space=pltpu.SMEM)] * len(scalars) + [
        pl.BlockSpec(memory_space=pltpu.VMEM)
    ] * len(arrays)
    moved = sum(4 * x.size for x in arrays) + sum(4 * x.size for x in outs)
    return pl.pallas_call(
        kernel,
        out_shape=outs,
        in_specs=in_specs,
        out_specs=[pl.BlockSpec(memory_space=pltpu.VMEM)] * len(outs),
        scratch_shapes=[pltpu.VMEM(shape, jnp.float32) for shape in scratch],
        compiler_params=pltpu.CompilerParams(vmem_limit_bytes=32 * 1024 * 1024),
        cost_estimate=pl.CostEstimate(flops=flops, bytes_accessed=moved, transcendentals=0),
    )(*scalars, *arrays)


def coupling_tables(coupling, slot_term):
    bf16 = jnp.bfloat16
    slots = slot_term.shape[0]
    raising = (slot_term[None, None, :] == coupling[:, :, 0:1]).astype(bf16)
    lowering = (slot_term[None, None, :] == coupling[:, :, 1:2]).astype(bf16)
    weighted = raising * coupling[:, :, 2:3].astype(bf16)
    matrices = jnp.einsum(
        "kps,kpr->ksr", weighted, lowering, preferred_element_type=jnp.float32
    ) + jnp.einsum("kps,kpr->ksr", lowering, raising, preferred_element_type=jnp.float32)
    spare = -slots % 16
    matrices = jnp.pad(matrices.astype(bf16), ((0, 0), (0, 0), (0, spare)))
    matrices = matrices.reshape(-1, slots + spare)
    degree = jnp.sum(weighted.astype(jnp.float32), axis=1)
    factorial = jnp.where(degree > 2.5, 6.0, jnp.where(degree > 1.5, 2.0, 1.0))
    scale = jnp.sqrt(jnp.prod(factorial, axis=0))
    occupied = (slot_term >= 0).astype(jnp.float32)
    spread = jnp.ones((1, LANES), jnp.float32)
    return (
        jnp.concatenate([matrices, matrices], axis=1),
        (occupied * scale)[:, None] * spread,
        (occupied / scale)[:, None] * spread,
    )


def local_by_cells(source_chaos_terms, mean_conductivity, mode_shapes, coupling, slot_term, bounds):
    own, thick, cells = source_chaos_terms.shape
    chaos, spaces = lax.axis_size("chaos"), lax.axis_size("space")
    devices = chaos * spaces
    width = cells // devices
    slots = own * chaos
    layers = thick * spaces
    tiles = width // LANES
    columns = cells // LANES
    blocks = [block_of(device, spaces) for device in range(devices)]
    f32 = jnp.float32

    def shape(*sizes):
        return jax.ShapeDtypeStruct(sizes, f32)

    rows = source_chaos_terms.reshape(own, thick, columns, LANES)
    rows = jnp.transpose(rows, (0, 2, 1, 3)).reshape(-1, LANES)
    sent = shape(devices, tiles * thick * own, LANES)
    scattered = call(
        functools.partial(scatter_kernel, blocks, own, thick, tiles), [sent], [], [rows]
    )[0]
    scattered, mean_conductivity, mode_shapes = lax.optimization_barrier(
        (scattered, mean_conductivity, mode_shapes)
    )
    gathered = lax.all_to_all(scattered, BOTH, 0, 0, tiled=True)

    modes = mode_shapes.shape[0] + 1
    raw = jnp.concatenate([mean_conductivity[None], mode_shapes], axis=0)
    padded = jnp.pad(raw, ((0, 0), (0, 0), (NY, NY)))
    row = lax.axis_index("chaos")
    run = lax.dynamic_slice_in_dim(padded, row * spaces * width, spaces * width + 2 * NY, 2)
    pieces = jnp.stack(
        [run[:, :, s * width : (s + 1) * width + 2 * NY] for s in range(spaces)], axis=0
    )
    pieces = jnp.where(row % 2 == 0, pieces, pieces[::-1])
    pieces = lax.all_to_all(pieces, "space", 0, 0, tiled=True)
    wide = jnp.transpose(pieces, (1, 0, 2, 3)).reshape(modes, layers, width + 2 * NY)
    field = wide[:, :, NY : NY + width]
    edges = jnp.concatenate([wide[:, :, :NY], wide[:, :, NY + width :]], axis=2)
    a, b, face = call(
        coefficient_kernel,
        [shape(modes, layers, width), shape(modes, layers, width), shape(modes, layers, LANES)],
        [],
        [field, edges],
    )

    mix, weight, unweight = coupling_tables(coupling, slot_term)
    midpoint = 0.5 * (bounds[1] + bounds[0])
    half_span = 0.5 * (bounds[1] - bounds[0])
    sigma_one = midpoint / half_span
    rho_now = 1.0 / sigma_one
    scales = [1.0 / midpoint]
    for _ in range(ITERS - 1):
        rho_next = 1.0 / (2.0 * sigma_one - rho_now)
        scales += [rho_next * rho_now, 2.0 * rho_next / half_span]
        rho_now = rho_next
    scales = jnp.stack(scales)

    full = shape(layers, tiles, slots, LANES)
    packed = shape(layers // 2, slots, LANES)
    residual, direction, up, down = call(
        functools.partial(start_kernel, chaos, spaces),
        [full, full, packed, packed],
        [scales],
        [weight, gathered],
    )
    place = {block: device for device, block in enumerate(blocks)}
    upward = [(place[n], place[n + 1]) for n in range(devices - 1)]
    downward = [(place[n + 1], place[n]) for n in range(devices - 1)]
    solution_field = None
    for step_index in range(ITERS):
        from_below = lax.ppermute(up, BOTH, upward)
        from_above = lax.ppermute(down, BOTH, downward)
        diffused = call(
            own_kernel, [full], [], [mix, a, b, direction], [full.shape], flops=3000000000
        )[0]
        last = step_index == ITERS - 1
        before_last = step_index == ITERS - 2
        arrays = [mix, face, unweight, diffused, from_below, from_above, residual]
        if not last:
            arrays.append(direction)
        if step_index > 0 and not last:
            arrays.append(solution_field)
        if last:
            outs, scratch = [sent], [full.shape]
        elif before_last:
            outs, scratch = [full, full, sent, packed, packed], [full.shape]
        else:
            outs, scratch = [full, full, full, packed, packed], []
        results = call(
            functools.partial(step_kernel, step_index, chaos, spaces),
            outs,
            [scales],
            arrays,
            scratch,
            flops=1000000000,
        )
        if last:
            residual = results[0]
        else:
            residual, direction, solution_field, up, down = results

    def back(field_sent):
        received = lax.all_to_all(field_sent, BOTH, 0, 0, tiled=True)
        out = call(
            functools.partial(collect_kernel, blocks, own, thick, tiles),
            [shape(own * columns * thick, LANES)],
            [],
            [received],
        )[0]
        out = jnp.transpose(out.reshape(own, columns, thick, LANES), (0, 2, 1, 3))
        return out.reshape(own, thick, cells)

    return (back(solution_field), back(residual))


def local(source_chaos_terms, mean_conductivity, mode_shapes, coupling, slot_term, bounds):
    own, thick, cells = source_chaos_terms.shape
    chaos, spaces = lax.axis_size("chaos"), lax.axis_size("space")
    fits = (
        thick * spaces == 8
        and cells % (chaos * spaces * LANES) == 0
        and (own * chaos) % 8 == 0
    )
    plan = local_by_cells if fits else local_by_slots
    return plan(
        source_chaos_terms, mean_conductivity, mode_shapes, coupling, slot_term, bounds
    )


def solution(mesh):
    in_specs = (
        P(("groups", "chaos"), "space", None),
        P("space", None),
        P(None, "space", None),
        P(),
        P(),
        P("groups"),
    )
    out_specs = (P(("groups", "chaos"), "space", None), P(("groups", "chaos"), "space", None))
    return jax.shard_map(local, mesh=mesh, in_specs=in_specs, out_specs=out_specs, check_vma=False)
```

```python
import functools

import jax
import jax.numpy as jnp
from jax import lax
from jax.experimental import pallas as pl
from jax.experimental.pallas import tpu as pltpu
from jax.sharding import PartitionSpec as P

NY = 64
ITERS = 3
LANES = 128
BOTH = ("chaos", "space")


full_precision = lax.Precision.HIGHEST


def with_halo(cells, sides, width):
    for axis, dim in sides:
        count = lax.axis_size(axis)
        ends = count - 1
        head = lax.slice_in_dim(cells, 0, width, axis=dim)
        tail = lax.slice_in_dim(cells, cells.shape[dim] - width, cells.shape[dim], axis=dim)
        cells = jnp.concatenate(
            [
                lax.ppermute(tail, axis, [(i, (i + 1) % count) for i in range(ends)]),
                cells,
                lax.ppermute(head, axis, [((i + 1) % count, i) for i in range(ends)]),
            ],
            axis=dim,
        )
    return cells


def mixing_matrices(coupling, slot_term):
    occupied = (slot_term >= 0).astype(jnp.float32)
    raising = (slot_term[None, None, :] == coupling[:, :, 0:1]).astype(jnp.float32)
    lowering = (slot_term[None, None, :] == coupling[:, :, 1:2]).astype(jnp.float32)
    weight = jnp.sqrt(coupling[:, :, 2].astype(jnp.float32))
    raised = jnp.einsum("kps,kp,kpr->ksr", raising, weight, lowering, precision=full_precision)
    mode_mats = raised + jnp.transpose(raised, (0, 2, 1))
    return jnp.concatenate([jnp.diag(occupied)[None], mode_mats], axis=0)


def shift_cells(values, offset, edge_mask):
    fill = jnp.zeros(values.shape[:-1] + (abs(offset),), values.dtype)
    if offset > 0:
        shifted = jnp.concatenate([values[..., offset:], fill], axis=-1)
    else:
        shifted = jnp.concatenate([fill, values[..., :offset]], axis=-1)
    return shifted * edge_mask


def diffuse(field_padded, conduct_padded):
    centre = field_padded[..., 1:-1, :]
    conduct = conduct_padded[..., 1:-1, :]
    accumulated = (
        0.5 * (conduct + conduct_padded[..., :-2, :]) * (centre - field_padded[..., :-2, :])
    )
    accumulated = accumulated + 0.5 * (conduct + conduct_padded[..., 2:, :]) * (
        centre - field_padded[..., 2:, :]
    )
    cells = centre.shape[-1]
    column_in_row = lax.iota(jnp.int32, cells) % NY
    upper_mask = (column_in_row < NY - 1).astype(centre.dtype)
    lower_mask = (column_in_row > 0).astype(centre.dtype)
    all_mask = jnp.ones((cells,), centre.dtype)
    for offset, edge_mask in ((1, upper_mask), (-1, lower_mask), (NY, all_mask), (-NY, all_mask)):
        neighbour = shift_cells(centre, offset, edge_mask)
        neighbour_conduct = shift_cells(conduct, offset, edge_mask)
        accumulated = accumulated + 0.5 * (conduct + neighbour_conduct) * (centre - neighbour)
    return accumulated


def local_by_slots(source_chaos_terms, mean_conductivity, mode_shapes, coupling, slot_term, bounds):
    slot_count = source_chaos_terms.shape[0]
    conductivity = jnp.concatenate(
        [mean_conductivity[None], mean_conductivity[None] * mode_shapes], axis=0
    )
    conduct_padded = with_halo(conductivity, (("space", 1),), 1)
    matrices = mixing_matrices(coupling, slot_term)
    first_own = lax.axis_index("chaos") * slot_count
    own_rows = lax.dynamic_slice_in_dim(matrices, first_own, slot_count, 1)
    own_terms = lax.dynamic_slice_in_dim(slot_term, first_own, slot_count, 0)
    occupied = (own_terms >= 0).astype(jnp.float32)[:, None, None]
    lower_bound = bounds[0]
    upper_bound = bounds[1]
    midpoint = 0.5 * (upper_bound + lower_bound)
    half_span = 0.5 * (upper_bound - lower_bound)
    sigma_one = midpoint / half_span
    rho_now = 1.0 / sigma_one
    residual = source_chaos_terms * occupied
    solution_field = jnp.zeros_like(residual)
    direction = residual / midpoint
    for iteration in range(ITERS):
        solution_field = solution_field + direction
        fields = jnp.einsum(
            "ksr,rzc->kszc",
            own_rows,
            lax.all_gather(direction, "chaos", axis=0, tiled=True),
            precision=full_precision,
        )
        field_padded = with_halo(fields, (("space", 2),), 1)
        diffused = diffuse(field_padded, conduct_padded[:, None])
        residual = residual - jnp.sum(diffused, axis=0)
        if iteration + 1 < ITERS:
            rho_next = 1.0 / (2.0 * sigma_one - rho_now)
            direction = rho_next * rho_now * direction + 2.0 * rho_next / half_span * residual
            rho_now = rho_next
    return (solution_field, residual)


OWN_TILES = 2
FOLDED = OWN_TILES + ITERS


def block_of(device, spaces):
    chaos, space = divmod(device, spaces)
    return chaos * spaces + (space if chaos % 2 == 0 else spaces - 1 - space)


def lane_masks(rows):
    lane = lax.broadcasted_iota(jnp.int32, (rows, LANES), 1)
    return lane < NY, lane % NY > 0, lane % NY < NY - 1


def plane_sums(tiles, masks):
    low_half, has_left, has_right = masks
    zero = jnp.zeros(tiles[0].shape, jnp.float32)
    swapped = [pltpu.roll(tile, NY, 1) for tile in tiles]
    sums = []
    for t, tile in enumerate(tiles[:-1]):
        if t == 0:
            across = swapped[0] + jnp.where(low_half, swapped[2], swapped[1])
        elif t == 1:
            across = swapped[1] + jnp.where(low_half, swapped[0], swapped[2])
        elif t == 2:
            across = swapped[3] + jnp.where(low_half, swapped[1], swapped[0])
        else:
            across = swapped[t - 1] + swapped[t + 1]
        left = jnp.where(has_left, pltpu.roll(tile, 1, 1), zero)
        right = jnp.where(has_right, pltpu.roll(tile, LANES - 1, 1), zero)
        sums.append(across + (left + right))
    return sums


def neighbour_sums(ref, layer, count, masks):
    sums = plane_sums([ref[layer, t] for t in range(count)], masks)
    for other in (layer - 1, layer + 1):
        if 0 <= other < ref.shape[0]:
            sums = [total + ref[other, t] for t, total in enumerate(sums)]
    return sums


def split_stack(tiles, depth):
    wide = jnp.concatenate(tiles, axis=1)
    spare = depth // 2 - wide.shape[0]
    if spare:
        wide = jnp.concatenate([wide, jnp.zeros((spare, wide.shape[1]), wide.dtype)], axis=0)
    high = wide.astype(jnp.bfloat16)
    low = (wide - high.astype(jnp.float32)).astype(jnp.bfloat16)
    return jnp.concatenate([high, low], axis=0)


def lanes(t):
    return pl.ds(t * LANES, LANES)


def run_copies(copies):
    for copy in copies:
        copy.start()
    for copy in copies:
        copy.wait()


def scatter_kernel(blocks, in_ref, out_ref, sems):
    run_copies(
        [
            pltpu.make_async_copy(in_ref.at[:, block], out_ref.at[device], sems.at[device])
            for device, block in enumerate(blocks)
        ]
    )


def collect_kernel(blocks, in_ref, *rest):
    *outs, sems = rest
    run_copies(
        [
            pltpu.make_async_copy(
                in_ref.at[device, n], out_ref.at[:, block], sems.at[n, device]
            )
            for n, out_ref in enumerate(outs)
            for device, block in enumerate(blocks)
        ]
    )


def start_kernel(chaos, spaces, weight_ref, in_ref, residual_ref, up_ref, down_ref):
    layers, tiles, slots, _ = residual_ref.shape
    own = slots // chaos
    thick = layers // spaces
    pieces = tiles * thick
    half = layers // 2
    low_half = lane_masks(slots)[0]
    weight = weight_ref[...]
    for l in range(layers):
        i, z = divmod(l, thick)
        for t in range(tiles):
            first = t * thick + z
            residual_ref[l, t] = weight * jnp.concatenate(
                [
                    in_ref[pl.ds((c * spaces + i) * own * pieces + first, own, stride=pieces), :]
                    for c in range(chaos)
                ],
                axis=0,
            )
        up_ref[l] = residual_ref[l, 1]
        down_ref[l] = residual_ref[l, 0]
    for l in range(half):
        later = l + half
        up_ref[layers + l] = jnp.where(
            low_half, pltpu.roll(residual_ref[later, 0], NY, 1), residual_ref[l, 0]
        )
        down_ref[layers + l] = jnp.where(
            low_half, residual_ref[l, 1], pltpu.roll(residual_ref[later, 1], NY, 1)
        )


def coefficient_kernel(place, inside, mean_ref, modes_ref, a_ref, b_ref):
    modes, layers, _ = a_ref.shape
    columns = mean_ref.shape[-1] // LANES
    masks = lane_masks(layers)
    low_half = masks[0]
    layer = lax.broadcasted_iota(jnp.int32, (layers, LANES), 0)
    zero = jnp.zeros((layers, LANES), jnp.float32)
    weights = [inside[0], inside[0], None, None, inside[1], inside[1]]
    starts = []
    for u in range(6):
        column = jnp.clip(place[0] * OWN_TILES + (u - 2), 0, columns - 1)
        starts.append(pl.multiple_of(column * LANES, LANES))

    def folded(read):
        runs = []
        for start, weight in zip(starts, weights):
            run = read(pl.ds(start, LANES))
            runs.append(run if weight is None else run * weight)
        return [
            runs[2],
            runs[3],
            jnp.where(low_half, runs[4], runs[1]),
            jnp.where(low_half, runs[1], runs[4]),
            jnp.where(low_half, runs[5], runs[0]),
        ]

    spaces = mean_ref.shape[0]
    mean = folded(
        lambda part: jnp.concatenate([mean_ref[i, :, part] for i in range(spaces)], axis=0)
    )
    for k in range(modes):
        values = mean
        if k > 0:
            mode = folded(
                lambda part: jnp.concatenate(
                    [modes_ref[i, k - 1, :, part] for i in range(spaces)], axis=0
                )
            )
            values = [m * value for m, value in zip(mean, mode)]
        sums = plane_sums(values, masks)
        for t in range(FOLDED):
            a_ref[k, :, lanes(t)] = 0.5 * values[t]
        for t in range(FOLDED - 1):
            below = jnp.where(layer > 0, pltpu.roll(values[t], 1, 0), zero)
            above = jnp.where(layer < layers - 1, pltpu.roll(values[t], layers - 1, 0), zero)
            b_ref[k, :, lanes(t)] = 3.0 * values[t] + 0.5 * (sums[t] + (below + above))


def iterate_kernel(
    chaos,
    spaces,
    scales,
    inside,
    mix_ref,
    a_ref,
    b_ref,
    unweight_ref,
    start_ref,
    up_ref,
    down_ref,
    sent_ref,
    r_ref,
    d_ref,
    total_ref,
    edge_ref,
    x_ref,
):
    layers, _, slots, _ = start_ref.shape
    modes = a_ref.shape[0]
    own = slots // chaos
    thick = layers // spaces
    pieces = OWN_TILES * thick
    half = layers // 2
    masks = lane_masks(slots)
    low_half = masks[0]
    mix = mix_ref[...]
    depth = mix.shape[1]

    def send(field, l, t, value):
        i, z = divmod(l, thick)
        value = value * unweight_ref[...]
        for c in range(chaos):
            first = ((c * spaces + i) * 2 + field) * own * pieces + t * thick + z
            sent_ref[pl.ds(first, own, stride=pieces), :] = value[c * own : (c + 1) * own]

    for l in range(layers):
        below, above = up_ref[l], down_ref[l]
        far_below, far_above = up_ref[layers + l % half], down_ref[layers + l % half]
        if l < half:
            far = jnp.where(low_half, far_above, far_below)
        else:
            far = pltpu.roll(jnp.where(low_half, far_below, far_above), NY, 1)
        tiles = [
            start_ref[l, 0],
            start_ref[l, 1],
            jnp.where(low_half, above, below),
            jnp.where(low_half, below, above),
            far,
        ]
        for t, tile in enumerate(tiles):
            if t < FOLDED - 1:
                r_ref[l, t] = tile
            d_ref[l, t] = tile * scales[0]

    for step in range(ITERS):
        count = FOLDED - step
        full = count - 1
        for l in range(layers):
            direct = [d_ref[l, t] for t in range(count)]
            around = neighbour_sums(d_ref, l, count, masks)
            mixed = jnp.dot(
                mix, split_stack(direct + around, depth), preferred_element_type=jnp.float32
            )

            def part(k, n):
                return mixed[(k - 1) * slots : k * slots, n * LANES : (n + 1) * LANES]

            for t in range(count):
                a = a_ref[0, l : l + 1, lanes(t)]
                edge = a * direct[t]
                if t < full:
                    total = b_ref[0, l : l + 1, lanes(t)] * direct[t] - a * around[t]
                for k in range(1, modes):
                    a = a_ref[k, l : l + 1, lanes(t)]
                    edge = edge + a * part(k, t)
                    if t < full:
                        b = b_ref[k, l : l + 1, lanes(t)]
                        total = total + (b * part(k, t) - a * part(k, count + t))
                edge_ref[l, t] = edge
                if t < full:
                    total_ref[l, t] = total
        for l in range(layers):
            spread = neighbour_sums(edge_ref, l, count, masks)
            for t in range(full):
                diffused = total_ref[l, t] - spread[t]
                if t >= OWN_TILES:
                    first, second = inside[(t + 1) % 2], inside[t % 2]
                    diffused = diffused * jnp.where(low_half, first, second)
                residual = r_ref[l, t] - diffused
                if step == ITERS - 1:
                    send(1, l, t, residual)
                    continue
                r_ref[l, t] = residual
                old = d_ref[l, t]
                direction = scales[1 + 2 * step] * old + scales[2 + 2 * step] * residual
                d_ref[l, t] = direction
                if t < OWN_TILES:
                    value = (old if step == 0 else x_ref[l, t]) + direction
                    if step == ITERS - 2:
                        send(0, l, t, value)
                    else:
                        x_ref[l, t] = value


def call(kernel, outs, scalars, arrays, scratch=(), flops=0, copies=False):
    kind = pl.ANY if copies else pltpu.VMEM
    in_specs = [pl.BlockSpec(memory_space=pltpu.SMEM)] * len(scalars) + [
        pl.BlockSpec(memory_space=kind)
    ] * len(arrays)
    moved = sum(4 * x.size for x in arrays) + sum(4 * x.size for x in outs)
    return pl.pallas_call(
        kernel,
        out_shape=outs,
        in_specs=in_specs,
        out_specs=[pl.BlockSpec(memory_space=kind)] * len(outs),
        scratch_shapes=scratch,
        compiler_params=pltpu.CompilerParams(vmem_limit_bytes=40 * 1024 * 1024),
        cost_estimate=pl.CostEstimate(flops=flops, bytes_accessed=moved, transcendentals=0),
    )(*scalars, *arrays)


def coupling_tables(coupling, slot_term):
    bf16 = jnp.bfloat16
    slots = slot_term.shape[0]
    raising = (slot_term[None, None, :] == coupling[:, :, 0:1]).astype(bf16)
    lowering = (slot_term[None, None, :] == coupling[:, :, 1:2]).astype(bf16)
    weighted = raising * coupling[:, :, 2:3].astype(bf16)
    matrices = jnp.einsum(
        "kps,kpr->ksr", weighted, lowering, preferred_element_type=jnp.float32
    ) + jnp.einsum("kps,kpr->ksr", lowering, raising, preferred_element_type=jnp.float32)
    spare = -slots % 16
    matrices = jnp.pad(matrices.astype(bf16), ((0, 0), (0, 0), (0, spare)))
    matrices = matrices.reshape(-1, slots + spare)
    degree = jnp.sum(weighted.astype(jnp.float32), axis=1)
    factorial = jnp.where(degree > 2.5, 6.0, jnp.where(degree > 1.5, 2.0, 1.0))
    scale = jnp.sqrt(jnp.prod(factorial, axis=0))
    occupied = (slot_term >= 0).astype(jnp.float32)
    spread = jnp.ones((1, LANES), jnp.float32)
    return (
        jnp.concatenate([matrices, matrices], axis=1),
        (occupied * scale)[:, None] * spread,
        (occupied / scale)[:, None] * spread,
    )


def local_by_cells(source_chaos_terms, mean_conductivity, mode_shapes, coupling, slot_term, bounds):
    own, thick, cells = source_chaos_terms.shape
    chaos, spaces = lax.axis_size("chaos"), lax.axis_size("space")
    devices = chaos * spaces
    slots = own * chaos
    layers = thick * spaces
    columns = cells // LANES
    pieces = OWN_TILES * thick
    blocks = [block_of(device, spaces) for device in range(devices)]
    f32 = jnp.float32

    def shape(*sizes):
        return jax.ShapeDtypeStruct(sizes, f32)

    rows = source_chaos_terms.reshape(own, thick, columns, LANES)
    rows = jnp.transpose(rows, (0, 2, 1, 3)).reshape(own, devices, pieces, LANES)
    scattered = call(
        functools.partial(scatter_kernel, blocks),
        [shape(devices, own, pieces, LANES)],
        [],
        [rows],
        [pltpu.SemaphoreType.DMA((devices,))],
        copies=True,
    )[0]
    gathered = lax.all_to_all(scattered, BOTH, 0, 0, tiled=True).reshape(-1, LANES)

    mean = lax.all_gather(mean_conductivity, "space")
    modes = lax.all_gather(mode_shapes, "space")
    row, column = lax.axis_index("chaos"), lax.axis_index("space")
    block = row * spaces + jnp.where(row % 2 == 0, column, spaces - 1 - column)
    inside = jnp.stack([block > 0, block < devices - 1]).astype(f32)
    count = mode_shapes.shape[0] + 1
    a, b = call(
        coefficient_kernel,
        [shape(count, layers, FOLDED * LANES), shape(count, layers, (FOLDED - 1) * LANES)],
        [block[None], inside],
        [mean, modes],
    )

    mix, weight, unweight = coupling_tables(coupling, slot_term)
    midpoint = 0.5 * (bounds[1] + bounds[0])
    half_span = 0.5 * (bounds[1] - bounds[0])
    sigma_one = midpoint / half_span
    rho_now = 1.0 / sigma_one
    scales = [1.0 / midpoint]
    for _ in range(ITERS - 1):
        rho_next = 1.0 / (2.0 * sigma_one - rho_now)
        scales += [rho_next * rho_now, 2.0 * rho_next / half_span]
        rho_now = rho_next
    scales = jnp.stack(scales)

    message = shape(layers + layers // 2, slots, LANES)
    start, up, down = call(
        functools.partial(start_kernel, chaos, spaces),
        [shape(layers, OWN_TILES, slots, LANES), message, message],
        [],
        [weight, gathered],
    )
    place = {n: device for device, n in enumerate(blocks)}
    upward = [(place[n], place[n + 1]) for n in range(devices - 1)]
    downward = [(place[n + 1], place[n]) for n in range(devices - 1)]
    from_below = lax.ppermute(up, BOTH, upward)
    from_above = lax.ppermute(down, BOTH, downward)

    def held(tiles):
        return pltpu.VMEM((layers, tiles, slots, LANES), f32)

    sent = call(
        functools.partial(iterate_kernel, chaos, spaces),
        [shape(devices * 2 * own * pieces, LANES)],
        [scales, inside],
        [mix, a, b, unweight, start, from_below, from_above],
        [held(FOLDED - 1), held(FOLDED), held(FOLDED - 1), held(FOLDED), held(OWN_TILES)],
        flops=10000000000,
    )[0]
    sent = sent.reshape(devices, 2, own, pieces, LANES)
    received = lax.all_to_all(sent, BOTH, 0, 0, tiled=True)
    outs = call(
        functools.partial(collect_kernel, blocks),
        [shape(own, devices, pieces, LANES)] * 2,
        [],
        [received],
        [pltpu.SemaphoreType.DMA((2, devices))],
        copies=True,
    )
    return tuple(
        jnp.transpose(out.reshape(own, columns, thick, LANES), (0, 2, 1, 3)).reshape(
            own, thick, cells
        )
        for out in outs
    )


def local(source_chaos_terms, mean_conductivity, mode_shapes, coupling, slot_term, bounds):
    own, thick, cells = source_chaos_terms.shape
    chaos, spaces = lax.axis_size("chaos"), lax.axis_size("space")
    fits = (
        thick * spaces == 8
        and cells == chaos * spaces * OWN_TILES * LANES
        and (own * chaos) % 8 == 0
    )
    plan = local_by_cells if fits else local_by_slots
    return plan(
        source_chaos_terms, mean_conductivity, mode_shapes, coupling, slot_term, bounds
    )


def solution(mesh):
    in_specs = (
        P(("groups", "chaos"), "space", None),
        P("space", None),
        P(None, "space", None),
        P(),
        P(),
        P("groups"),
    )
    out_specs = (P(("groups", "chaos"), "space", None), P(("groups", "chaos"), "space", None))
    return jax.shard_map(local, mesh=mesh, in_specs=in_specs, out_specs=out_specs, check_vma=False)
```

```python
import functools

import jax
import jax.numpy as jnp
from jax import lax
from jax.experimental import pallas as pl
from jax.experimental.pallas import tpu as pltpu
from jax.sharding import PartitionSpec as P

NY = 64
ITERS = 3
LANES = 128
BOTH = ("chaos", "space")


full_precision = lax.Precision.HIGHEST


def with_halo(cells, sides, width):
    for axis, dim in sides:
        count = lax.axis_size(axis)
        ends = count - 1
        head = lax.slice_in_dim(cells, 0, width, axis=dim)
        tail = lax.slice_in_dim(cells, cells.shape[dim] - width, cells.shape[dim], axis=dim)
        cells = jnp.concatenate(
            [
                lax.ppermute(tail, axis, [(i, (i + 1) % count) for i in range(ends)]),
                cells,
                lax.ppermute(head, axis, [((i + 1) % count, i) for i in range(ends)]),
            ],
            axis=dim,
        )
    return cells


def mixing_matrices(coupling, slot_term):
    occupied = (slot_term >= 0).astype(jnp.float32)
    raising = (slot_term[None, None, :] == coupling[:, :, 0:1]).astype(jnp.float32)
    lowering = (slot_term[None, None, :] == coupling[:, :, 1:2]).astype(jnp.float32)
    weight = jnp.sqrt(coupling[:, :, 2].astype(jnp.float32))
    raised = jnp.einsum("kps,kp,kpr->ksr", raising, weight, lowering, precision=full_precision)
    mode_mats = raised + jnp.transpose(raised, (0, 2, 1))
    return jnp.concatenate([jnp.diag(occupied)[None], mode_mats], axis=0)


def shift_cells(values, offset, edge_mask):
    fill = jnp.zeros(values.shape[:-1] + (abs(offset),), values.dtype)
    if offset > 0:
        shifted = jnp.concatenate([values[..., offset:], fill], axis=-1)
    else:
        shifted = jnp.concatenate([fill, values[..., :offset]], axis=-1)
    return shifted * edge_mask


def diffuse(field_padded, conduct_padded):
    centre = field_padded[..., 1:-1, :]
    conduct = conduct_padded[..., 1:-1, :]
    accumulated = (
        0.5 * (conduct + conduct_padded[..., :-2, :]) * (centre - field_padded[..., :-2, :])
    )
    accumulated = accumulated + 0.5 * (conduct + conduct_padded[..., 2:, :]) * (
        centre - field_padded[..., 2:, :]
    )
    cells = centre.shape[-1]
    column_in_row = lax.iota(jnp.int32, cells) % NY
    upper_mask = (column_in_row < NY - 1).astype(centre.dtype)
    lower_mask = (column_in_row > 0).astype(centre.dtype)
    all_mask = jnp.ones((cells,), centre.dtype)
    for offset, edge_mask in ((1, upper_mask), (-1, lower_mask), (NY, all_mask), (-NY, all_mask)):
        neighbour = shift_cells(centre, offset, edge_mask)
        neighbour_conduct = shift_cells(conduct, offset, edge_mask)
        accumulated = accumulated + 0.5 * (conduct + neighbour_conduct) * (centre - neighbour)
    return accumulated


def local_by_slots(source_chaos_terms, mean_conductivity, mode_shapes, coupling, slot_term, bounds):
    slot_count = source_chaos_terms.shape[0]
    conductivity = jnp.concatenate(
        [mean_conductivity[None], mean_conductivity[None] * mode_shapes], axis=0
    )
    conduct_padded = with_halo(conductivity, (("space", 1),), 1)
    matrices = mixing_matrices(coupling, slot_term)
    first_own = lax.axis_index("chaos") * slot_count
    own_rows = lax.dynamic_slice_in_dim(matrices, first_own, slot_count, 1)
    own_terms = lax.dynamic_slice_in_dim(slot_term, first_own, slot_count, 0)
    occupied = (own_terms >= 0).astype(jnp.float32)[:, None, None]
    lower_bound = bounds[0]
    upper_bound = bounds[1]
    midpoint = 0.5 * (upper_bound + lower_bound)
    half_span = 0.5 * (upper_bound - lower_bound)
    sigma_one = midpoint / half_span
    rho_now = 1.0 / sigma_one
    residual = source_chaos_terms * occupied
    solution_field = jnp.zeros_like(residual)
    direction = residual / midpoint
    for iteration in range(ITERS):
        solution_field = solution_field + direction
        fields = jnp.einsum(
            "ksr,rzc->kszc",
            own_rows,
            lax.all_gather(direction, "chaos", axis=0, tiled=True),
            precision=full_precision,
        )
        field_padded = with_halo(fields, (("space", 2),), 1)
        diffused = diffuse(field_padded, conduct_padded[:, None])
        residual = residual - jnp.sum(diffused, axis=0)
        if iteration + 1 < ITERS:
            rho_next = 1.0 / (2.0 * sigma_one - rho_now)
            direction = rho_next * rho_now * direction + 2.0 * rho_next / half_span * residual
            rho_now = rho_next
    return (solution_field, residual)


OWN_TILES = 2
FOLDED = OWN_TILES + ITERS


def block_of(device, spaces):
    chaos, space = divmod(device, spaces)
    return chaos * spaces + (space if chaos % 2 == 0 else spaces - 1 - space)


def lane_masks(rows):
    lane = lax.broadcasted_iota(jnp.int32, (rows, LANES), 1)
    return lane < NY, lane % NY > 0, lane % NY < NY - 1


def plane_sums(tiles, masks):
    low_half, has_left, has_right = masks
    zero = jnp.zeros(tiles[0].shape, jnp.float32)
    swapped = [pltpu.roll(tile, NY, 1) for tile in tiles]
    sums = []
    for t, tile in enumerate(tiles[:-1]):
        if t == 0:
            across = swapped[0] + jnp.where(low_half, swapped[2], swapped[1])
        elif t == 1:
            across = swapped[1] + jnp.where(low_half, swapped[0], swapped[2])
        elif t == 2:
            across = swapped[3] + jnp.where(low_half, swapped[1], swapped[0])
        else:
            across = swapped[t - 1] + swapped[t + 1]
        left = jnp.where(has_left, pltpu.roll(tile, 1, 1), zero)
        right = jnp.where(has_right, pltpu.roll(tile, LANES - 1, 1), zero)
        sums.append(across + (left + right))
    return sums


def neighbour_sums(ref, layer, count, masks):
    sums = plane_sums([ref[layer, t] for t in range(count)], masks)
    for other in (layer - 1, layer + 1):
        if 0 <= other < ref.shape[0]:
            sums = [total + ref[other, t] for t, total in enumerate(sums)]
    return sums


def split_stack(tiles, depth):
    wide = jnp.concatenate(tiles, axis=1)
    spare = depth // 2 - wide.shape[0]
    if spare:
        wide = jnp.concatenate([wide, jnp.zeros((spare, wide.shape[1]), wide.dtype)], axis=0)
    high = wide.astype(jnp.bfloat16)
    low = (wide - high.astype(jnp.float32)).astype(jnp.bfloat16)
    return jnp.concatenate([high, low], axis=0)


def lanes(t):
    return pl.ds(t * LANES, LANES)


def run_copies(copies):
    for copy in copies:
        copy.start()
    for copy in copies:
        copy.wait()


def scatter_kernel(blocks, chaos_index, in_ref, mean_ref, modes_ref, out_ref, sems):
    own, devices, pieces, _ = in_ref.shape
    modes = modes_ref.shape[0] // (devices * pieces)
    copies = [
        pltpu.make_async_copy(
            in_ref.at[:, block], out_ref.at[device, pl.ds(0, own)], sems.at[device]
        )
        for device, block in enumerate(blocks)
    ]
    for copy in copies:
        copy.start()
    for device, block in enumerate(blocks):
        row = block * pieces + chaos_index[0]
        values = modes_ref[pl.ds(row, modes, stride=devices * pieces), :]
        out_ref[device, own] = values[:pieces]
        out_ref[device, own + 1] = jnp.concatenate(
            [
                values[pieces:],
                mean_ref[pl.ds(row, 1), :],
                jnp.zeros((2 * pieces - modes - 1, LANES), jnp.float32),
            ],
            axis=0,
        )
    for copy in copies:
        copy.wait()


def collect_kernel(blocks, in_ref, *rest):
    *outs, sems = rest
    run_copies(
        [
            pltpu.make_async_copy(
                in_ref.at[device, n], out_ref.at[:, block], sems.at[n, device]
            )
            for n, out_ref in enumerate(outs)
            for device, block in enumerate(blocks)
        ]
    )


def start_kernel(chaos, spaces, modes, weight_ref, in_ref, residual_ref, a_ref, up_ref, down_ref):
    layers, tiles, slots, _ = residual_ref.shape
    own = slots // chaos
    thick = layers // spaces
    pieces = tiles * thick
    block = (own + 2) * pieces
    half = layers // 2
    low_half = lane_masks(slots)[0]
    weight = weight_ref[...]

    def put(ref, place, value):
        ref[pl.ds(place * slots, slots), :] = value

    for l in range(layers):
        i, z = divmod(l, thick)
        for t in range(tiles):
            first = t * thick + z
            residual_ref[l, t] = weight * jnp.concatenate(
                [
                    in_ref[pl.ds((c * spaces + i) * block + first, own, stride=pieces), :]
                    for c in range(chaos)
                ],
                axis=0,
            )
        put(up_ref, l, residual_ref[l, 1])
        put(down_ref, l, residual_ref[l, 0])
    for l in range(half):
        later = l + half
        put(
            up_ref,
            layers + l,
            jnp.where(low_half, pltpu.roll(residual_ref[later, 0], NY, 1), residual_ref[l, 0]),
        )
        put(
            down_ref,
            layers + l,
            jnp.where(low_half, residual_ref[l, 1], pltpu.roll(residual_ref[later, 1], NY, 1)),
        )

    for t in range(tiles):
        for z in range(thick):
            for k in range(modes):
                first = (t * thick + z) * spaces * block + own * pieces
                first += k - 1 if k > 0 else modes - 1
                a_ref[k, t, pl.ds(z, spaces, stride=thick), :] = in_ref[
                    pl.ds(first, spaces, stride=block), :
                ]
        mean = 0.5 * a_ref[0, t]
        for k in range(modes):
            value = mean if k == 0 else mean * a_ref[k, t]
            a_ref[k, t] = value
            rows = pl.ds((layers + half) * slots + (k * tiles + t) * layers, layers)
            up_ref[rows, :] = value
            down_ref[rows, :] = value


def iterate_kernel(
    chaos,
    spaces,
    scales,
    inside,
    mix_ref,
    own_a_ref,
    unweight_ref,
    start_ref,
    up_ref,
    down_ref,
    sent_ref,
    a_ref,
    b_ref,
    r_ref,
    d_ref,
    total_ref,
    edge_ref,
    x_ref,
):
    layers, _, slots, _ = start_ref.shape
    modes = own_a_ref.shape[0]
    own = slots // chaos
    thick = layers // spaces
    pieces = OWN_TILES * thick
    half = layers // 2
    masks = lane_masks(slots)
    low_half = masks[0]
    mix = mix_ref[...]
    depth = mix.shape[1]

    def send(field, l, t, value):
        i, z = divmod(l, thick)
        value = value * unweight_ref[...]
        for c in range(chaos):
            first = ((c * spaces + i) * 2 + field) * own * pieces + t * thick + z
            sent_ref[pl.ds(first, own, stride=pieces), :] = value[c * own : (c + 1) * own]

    layer = lax.broadcasted_iota(jnp.int32, (layers, LANES), 0)
    zero = jnp.zeros((layers, LANES), jnp.float32)
    narrow_masks = lane_masks(layers)
    low = narrow_masks[0]
    for k in range(modes):
        below, above = [
            [
                ref[pl.ds((layers + half) * slots + (k * OWN_TILES + t) * layers, layers), :]
                for t in range(OWN_TILES)
            ]
            for ref in (up_ref, down_ref)
        ]
        values = [
            own_a_ref[k, 0],
            own_a_ref[k, 1],
            jnp.where(low, above[0], below[1]),
            jnp.where(low, below[1], above[0]),
            jnp.where(low, above[1], below[0]),
        ]
        sums = plane_sums(values, narrow_masks)
        for t in range(FOLDED):
            a_ref[k, :, lanes(t)] = values[t]
        for t in range(FOLDED - 1):
            under = jnp.where(layer > 0, pltpu.roll(values[t], 1, 0), zero)
            over = jnp.where(layer < layers - 1, pltpu.roll(values[t], layers - 1, 0), zero)
            b_ref[k, :, lanes(t)] = 6.0 * values[t] + (sums[t] + (under + over))

    def message(ref, place):
        return ref[pl.ds(place * slots, slots), :]

    for l in range(layers):
        below, above = message(up_ref, l), message(down_ref, l)
        far_below = message(up_ref, layers + l % half)
        far_above = message(down_ref, layers + l % half)
        if l < half:
            far = jnp.where(low_half, far_above, far_below)
        else:
            far = pltpu.roll(jnp.where(low_half, far_below, far_above), NY, 1)
        tiles = [
            start_ref[l, 0],
            start_ref[l, 1],
            jnp.where(low_half, above, below),
            jnp.where(low_half, below, above),
            far,
        ]
        for t, tile in enumerate(tiles):
            if t < FOLDED - 1:
                r_ref[l, t] = tile
            d_ref[l, t] = tile * scales[0]

    for step in range(ITERS):
        count = FOLDED - step
        full = count - 1
        for l in range(layers):
            direct = [d_ref[l, t] for t in range(count)]
            around = neighbour_sums(d_ref, l, count, masks)
            mixed = jnp.dot(
                mix, split_stack(direct + around, depth), preferred_element_type=jnp.float32
            )

            def part(k, n):
                return jnp.concatenate(
                    [
                        mixed[row : row + 8, n * LANES : (n + 1) * LANES]
                        for row in range((k - 1) * 8, (modes - 1) * slots, (modes - 1) * 8)
                    ],
                    axis=0,
                )

            for t in range(count):
                a = a_ref[0, l : l + 1, lanes(t)]
                edge = a * direct[t]
                if t < full:
                    total = b_ref[0, l : l + 1, lanes(t)] * direct[t] - a * around[t]
                for k in range(1, modes):
                    a = a_ref[k, l : l + 1, lanes(t)]
                    edge = edge + a * part(k, t)
                    if t < full:
                        b = b_ref[k, l : l + 1, lanes(t)]
                        total = total + (b * part(k, t) - a * part(k, count + t))
                edge_ref[l, t] = edge
                if t < full:
                    total_ref[l, t] = total
        for l in range(layers):
            spread = neighbour_sums(edge_ref, l, count, masks)
            for t in range(full):
                diffused = total_ref[l, t] - spread[t]
                if t >= OWN_TILES:
                    first, second = inside[(t + 1) % 2], inside[t % 2]
                    diffused = diffused * jnp.where(low_half, first, second)
                residual = r_ref[l, t] - diffused
                if step == ITERS - 1:
                    send(1, l, t, residual)
                    continue
                r_ref[l, t] = residual
                old = d_ref[l, t]
                direction = scales[1 + 2 * step] * old + scales[2 + 2 * step] * residual
                d_ref[l, t] = direction
                if t < OWN_TILES:
                    value = (old if step == 0 else x_ref[l, t]) + direction
                    if step == ITERS - 2:
                        send(0, l, t, value)
                    else:
                        x_ref[l, t] = value


def call(kernel, outs, scalars, arrays, scratch=(), flops=0, in_kinds=None, out_kind=pltpu.VMEM):
    kinds = in_kinds or [pltpu.VMEM] * len(arrays)
    in_specs = [pl.BlockSpec(memory_space=pltpu.SMEM)] * len(scalars) + [
        pl.BlockSpec(memory_space=kind) for kind in kinds
    ]
    moved = sum(4 * x.size for x in arrays) + sum(4 * x.size for x in outs)
    return pl.pallas_call(
        kernel,
        out_shape=outs,
        in_specs=in_specs,
        out_specs=[pl.BlockSpec(memory_space=out_kind)] * len(outs),
        scratch_shapes=scratch,
        compiler_params=pltpu.CompilerParams(vmem_limit_bytes=40 * 1024 * 1024),
        cost_estimate=pl.CostEstimate(flops=flops, bytes_accessed=moved, transcendentals=0),
    )(*scalars, *arrays)


def coupling_tables(coupling, slot_term):
    bf16 = jnp.bfloat16
    slots = slot_term.shape[0]
    raising = (slot_term[None, None, :] == coupling[:, :, 0:1]).astype(bf16)
    lowering = (slot_term[None, None, :] == coupling[:, :, 1:2]).astype(bf16)
    weighted = raising * coupling[:, :, 2:3].astype(bf16)
    matrices = jnp.einsum(
        "kps,kpr->ksr", weighted, lowering, preferred_element_type=jnp.float32
    ) + jnp.einsum("kps,kpr->ksr", lowering, raising, preferred_element_type=jnp.float32)
    spare = -slots % 16
    matrices = jnp.pad(matrices.astype(bf16), ((0, 0), (0, 0), (0, spare)))
    matrices = matrices.reshape(-1, slots // 8, 8, slots + spare).transpose(1, 0, 2, 3)
    matrices = matrices.reshape(-1, slots + spare)
    degree = jnp.sum(weighted.astype(jnp.float32), axis=1)
    factorial = jnp.where(degree > 2.5, 6.0, jnp.where(degree > 1.5, 2.0, 1.0))
    scale = jnp.sqrt(jnp.prod(factorial, axis=0))
    occupied = (slot_term >= 0).astype(jnp.float32)
    spread = jnp.ones((1, LANES), jnp.float32)
    return (
        jnp.concatenate([matrices, matrices], axis=1),
        (occupied * scale)[:, None] * spread,
        (occupied / scale)[:, None] * spread,
    )


def local_by_cells(source_chaos_terms, mean_conductivity, mode_shapes, coupling, slot_term, bounds):
    own, thick, cells = source_chaos_terms.shape
    chaos, spaces = lax.axis_size("chaos"), lax.axis_size("space")
    devices = chaos * spaces
    slots = own * chaos
    layers = thick * spaces
    columns = cells // LANES
    pieces = OWN_TILES * thick
    blocks = [block_of(device, spaces) for device in range(devices)]
    f32 = jnp.float32

    def shape(*sizes):
        return jax.ShapeDtypeStruct(sizes, f32)

    def by_blocks(field):
        lead = field.shape[:-2]
        tiled = field.reshape(*lead, thick, columns, LANES)
        return jnp.swapaxes(tiled, -3, -2)

    row, column = lax.axis_index("chaos"), lax.axis_index("space")
    block = row * spaces + jnp.where(row % 2 == 0, column, spaces - 1 - column)
    inside = jnp.stack([block > 0, block < devices - 1]).astype(f32)
    modes = mode_shapes.shape[0] + 1
    scattered = call(
        functools.partial(scatter_kernel, blocks),
        [shape(devices, own + 2, pieces, LANES)],
        [row[None]],
        [
            by_blocks(source_chaos_terms).reshape(own, devices, pieces, LANES),
            by_blocks(mean_conductivity).reshape(-1, LANES),
            by_blocks(mode_shapes).reshape(-1, LANES),
        ],
        [pltpu.SemaphoreType.DMA((devices,))],
        in_kinds=[pltpu.HBM, pltpu.VMEM, pltpu.VMEM],
    )[0]
    gathered = lax.all_to_all(scattered, BOTH, 0, 0, tiled=True).reshape(-1, LANES)

    mix, weight, unweight = coupling_tables(coupling, slot_term)
    midpoint = 0.5 * (bounds[1] + bounds[0])
    half_span = 0.5 * (bounds[1] - bounds[0])
    sigma_one = midpoint / half_span
    rho_now = 1.0 / sigma_one
    scales = [1.0 / midpoint]
    for _ in range(ITERS - 1):
        rho_next = 1.0 / (2.0 * sigma_one - rho_now)
        scales += [rho_next * rho_now, 2.0 * rho_next / half_span]
        rho_now = rho_next
    scales = jnp.stack(scales)

    message = shape((layers + layers // 2) * slots + modes * OWN_TILES * layers, LANES)
    start, own_a, up, down = call(
        functools.partial(start_kernel, chaos, spaces, modes),
        [
            shape(layers, OWN_TILES, slots, LANES),
            shape(modes, OWN_TILES, layers, LANES),
            message,
            message,
        ],
        [],
        [weight, gathered],
    )
    place = {n: device for device, n in enumerate(blocks)}
    upward = [(place[n], place[n + 1]) for n in range(devices - 1)]
    downward = [(place[n + 1], place[n]) for n in range(devices - 1)]
    from_below = lax.ppermute(up, BOTH, upward)
    from_above = lax.ppermute(down, BOTH, downward)

    def held(tiles):
        return pltpu.VMEM((layers, tiles, slots, LANES), f32)

    sent = call(
        functools.partial(iterate_kernel, chaos, spaces),
        [shape(devices * 2 * own * pieces, LANES)],
        [scales, inside],
        [mix, own_a, unweight, start, from_below, from_above],
        [
            pltpu.VMEM((modes, layers, FOLDED * LANES), f32),
            pltpu.VMEM((modes, layers, (FOLDED - 1) * LANES), f32),
            held(FOLDED - 1),
            held(FOLDED),
            held(FOLDED - 1),
            held(FOLDED),
            held(OWN_TILES),
        ],
        flops=10000000000,
    )[0]
    sent = sent.reshape(devices, 2, own, pieces, LANES)
    received = lax.all_to_all(sent, BOTH, 0, 0, tiled=True)
    outs = call(
        functools.partial(collect_kernel, blocks),
        [shape(own, devices, pieces, LANES)] * 2,
        [],
        [received],
        [pltpu.SemaphoreType.DMA((2, devices))],
        in_kinds=[pl.ANY],
        out_kind=pltpu.HBM,
    )
    return tuple(
        jnp.transpose(out.reshape(own, columns, thick, LANES), (0, 2, 1, 3)).reshape(
            own, thick, cells
        )
        for out in outs
    )


def local(source_chaos_terms, mean_conductivity, mode_shapes, coupling, slot_term, bounds):
    own, thick, cells = source_chaos_terms.shape
    chaos, spaces = lax.axis_size("chaos"), lax.axis_size("space")
    fits = (
        thick * spaces == 8
        and cells == chaos * spaces * OWN_TILES * LANES
        and (own * chaos) % 8 == 0
        and chaos == OWN_TILES * thick
        and chaos <= mode_shapes.shape[0] < 2 * chaos
    )
    plan = local_by_cells if fits else local_by_slots
    return plan(
        source_chaos_terms, mean_conductivity, mode_shapes, coupling, slot_term, bounds
    )


def solution(mesh):
    in_specs = (
        P(("groups", "chaos"), "space", None),
        P("space", None),
        P(None, "space", None),
        P(),
        P(),
        P("groups"),
    )
    out_specs = (P(("groups", "chaos"), "space", None), P(("groups", "chaos"), "space", None))
    return jax.shard_map(local, mesh=mesh, in_specs=in_specs, out_specs=out_specs, check_vma=False)
```

```python
import functools

import jax
import jax.numpy as jnp
from jax import lax
from jax.experimental import pallas as pl
from jax.experimental.pallas import tpu as pltpu
from jax.sharding import PartitionSpec as P

NY = 64
ITERS = 3
LANES = 128
BOTH = ("chaos", "space")


full_precision = lax.Precision.HIGHEST


def with_halo(cells, sides, width):
    for axis, dim in sides:
        count = lax.axis_size(axis)
        ends = count - 1
        head = lax.slice_in_dim(cells, 0, width, axis=dim)
        tail = lax.slice_in_dim(cells, cells.shape[dim] - width, cells.shape[dim], axis=dim)
        cells = jnp.concatenate(
            [
                lax.ppermute(tail, axis, [(i, (i + 1) % count) for i in range(ends)]),
                cells,
                lax.ppermute(head, axis, [((i + 1) % count, i) for i in range(ends)]),
            ],
            axis=dim,
        )
    return cells


def mixing_matrices(coupling, slot_term):
    occupied = (slot_term >= 0).astype(jnp.float32)
    raising = (slot_term[None, None, :] == coupling[:, :, 0:1]).astype(jnp.float32)
    lowering = (slot_term[None, None, :] == coupling[:, :, 1:2]).astype(jnp.float32)
    weight = jnp.sqrt(coupling[:, :, 2].astype(jnp.float32))
    raised = jnp.einsum("kps,kp,kpr->ksr", raising, weight, lowering, precision=full_precision)
    mode_mats = raised + jnp.transpose(raised, (0, 2, 1))
    return jnp.concatenate([jnp.diag(occupied)[None], mode_mats], axis=0)


def shift_cells(values, offset, edge_mask):
    fill = jnp.zeros(values.shape[:-1] + (abs(offset),), values.dtype)
    if offset > 0:
        shifted = jnp.concatenate([values[..., offset:], fill], axis=-1)
    else:
        shifted = jnp.concatenate([fill, values[..., :offset]], axis=-1)
    return shifted * edge_mask


def diffuse(field_padded, conduct_padded):
    centre = field_padded[..., 1:-1, :]
    conduct = conduct_padded[..., 1:-1, :]
    accumulated = (
        0.5 * (conduct + conduct_padded[..., :-2, :]) * (centre - field_padded[..., :-2, :])
    )
    accumulated = accumulated + 0.5 * (conduct + conduct_padded[..., 2:, :]) * (
        centre - field_padded[..., 2:, :]
    )
    cells = centre.shape[-1]
    column_in_row = lax.iota(jnp.int32, cells) % NY
    upper_mask = (column_in_row < NY - 1).astype(centre.dtype)
    lower_mask = (column_in_row > 0).astype(centre.dtype)
    all_mask = jnp.ones((cells,), centre.dtype)
    for offset, edge_mask in ((1, upper_mask), (-1, lower_mask), (NY, all_mask), (-NY, all_mask)):
        neighbour = shift_cells(centre, offset, edge_mask)
        neighbour_conduct = shift_cells(conduct, offset, edge_mask)
        accumulated = accumulated + 0.5 * (conduct + neighbour_conduct) * (centre - neighbour)
    return accumulated


def local_by_slots(source_chaos_terms, mean_conductivity, mode_shapes, coupling, slot_term, bounds):
    slot_count = source_chaos_terms.shape[0]
    conductivity = jnp.concatenate(
        [mean_conductivity[None], mean_conductivity[None] * mode_shapes], axis=0
    )
    conduct_padded = with_halo(conductivity, (("space", 1),), 1)
    matrices = mixing_matrices(coupling, slot_term)
    first_own = lax.axis_index("chaos") * slot_count
    own_rows = lax.dynamic_slice_in_dim(matrices, first_own, slot_count, 1)
    own_terms = lax.dynamic_slice_in_dim(slot_term, first_own, slot_count, 0)
    occupied = (own_terms >= 0).astype(jnp.float32)[:, None, None]
    lower_bound = bounds[0]
    upper_bound = bounds[1]
    midpoint = 0.5 * (upper_bound + lower_bound)
    half_span = 0.5 * (upper_bound - lower_bound)
    sigma_one = midpoint / half_span
    rho_now = 1.0 / sigma_one
    residual = source_chaos_terms * occupied
    solution_field = jnp.zeros_like(residual)
    direction = residual / midpoint
    for iteration in range(ITERS):
        solution_field = solution_field + direction
        fields = jnp.einsum(
            "ksr,rzc->kszc",
            own_rows,
            lax.all_gather(direction, "chaos", axis=0, tiled=True),
            precision=full_precision,
        )
        field_padded = with_halo(fields, (("space", 2),), 1)
        diffused = diffuse(field_padded, conduct_padded[:, None])
        residual = residual - jnp.sum(diffused, axis=0)
        if iteration + 1 < ITERS:
            rho_next = 1.0 / (2.0 * sigma_one - rho_now)
            direction = rho_next * rho_now * direction + 2.0 * rho_next / half_span * residual
            rho_now = rho_next
    return (solution_field, residual)


OWN_TILES = 2
FOLDED = OWN_TILES + ITERS


def block_of(device, spaces):
    chaos, space = divmod(device, spaces)
    return chaos * spaces + (space if chaos % 2 == 0 else spaces - 1 - space)


def lane_masks(rows):
    lane = lax.broadcasted_iota(jnp.int32, (rows, LANES), 1)
    return lane < NY, lane % NY > 0, lane % NY < NY - 1


def plane_sums(tiles, masks):
    low_half, has_left, has_right = masks
    zero = jnp.zeros(tiles[0].shape, jnp.float32)
    swapped = [pltpu.roll(tile, NY, 1) for tile in tiles]
    sums = []
    for t, tile in enumerate(tiles[:-1]):
        if t == 0:
            across = swapped[0] + jnp.where(low_half, swapped[2], swapped[1])
        elif t == 1:
            across = swapped[1] + jnp.where(low_half, swapped[0], swapped[2])
        elif t == 2:
            across = swapped[3] + jnp.where(low_half, swapped[1], swapped[0])
        else:
            across = swapped[t - 1] + swapped[t + 1]
        left = jnp.where(has_left, pltpu.roll(tile, 1, 1), zero)
        right = jnp.where(has_right, pltpu.roll(tile, LANES - 1, 1), zero)
        sums.append(across + (left + right))
    return sums


def neighbour_sums(ref, layer, count, masks):
    sums = plane_sums([ref[layer, t] for t in range(count)], masks)
    for other in (layer - 1, layer + 1):
        if 0 <= other < ref.shape[0]:
            sums = [total + ref[other, t] for t, total in enumerate(sums)]
    return sums


def split_stack(tiles, depth):
    wide = jnp.concatenate(tiles, axis=1)
    spare = depth // 2 - wide.shape[0]
    if spare:
        wide = jnp.concatenate([wide, jnp.zeros((spare, wide.shape[1]), wide.dtype)], axis=0)
    high = wide.astype(jnp.bfloat16)
    low = (wide - high.astype(jnp.float32)).astype(jnp.bfloat16)
    return jnp.concatenate([high, low], axis=0)


def lanes(t):
    return pl.ds(t * LANES, LANES)


def scatter_kernel(
    blocks, chaos_index, in_ref, mean_ref, modes_ref, out_ref, mean_held, modes_held, sems
):
    own, devices, pieces, _ = in_ref.shape
    modes = modes_ref.shape[0] // (devices * pieces)
    small = [
        pltpu.make_async_copy(mean_ref, mean_held, sems.at[devices]),
        pltpu.make_async_copy(modes_ref, modes_held, sems.at[devices + 1]),
    ]
    copies = [
        pltpu.make_async_copy(
            in_ref.at[:, block], out_ref.at[device, pl.ds(0, own)], sems.at[device]
        )
        for device, block in enumerate(blocks)
    ]
    for copy in small + copies:
        copy.start()
    for copy in small:
        copy.wait()
    for device, block in enumerate(blocks):
        row = block * pieces + chaos_index[0]
        values = modes_held[pl.ds(row, modes, stride=devices * pieces), :]
        out_ref[device, own] = values[:pieces]
        out_ref[device, own + 1] = jnp.concatenate(
            [
                values[pieces:],
                mean_held[pl.ds(row, 1), :],
                jnp.zeros((2 * pieces - modes - 1, LANES), jnp.float32),
            ],
            axis=0,
        )
    for copy in copies:
        copy.wait()


def collect_kernel(blocks, *refs):
    *arrays, sems = refs
    fields = len(arrays) // 2
    copies = [
        pltpu.make_async_copy(in_ref.at[device], out_ref.at[:, block], sems.at[n, device])
        for n, (in_ref, out_ref) in enumerate(zip(arrays[:fields], arrays[fields:]))
        for device, block in enumerate(blocks)
    ]
    for copy in copies:
        copy.start()
    for copy in copies:
        copy.wait()


def start_kernel(chaos, spaces, modes, weight_ref, in_ref, residual_ref, a_ref, up_ref, down_ref):
    layers, tiles, slots, _ = residual_ref.shape
    own = slots // chaos
    thick = layers // spaces
    pieces = tiles * thick
    block = (own + 2) * pieces
    half = layers // 2
    low_half = lane_masks(slots)[0]
    weight = weight_ref[...]

    def put(ref, place, value):
        ref[pl.ds(place * slots, slots), :] = value

    for l in range(layers):
        i, z = divmod(l, thick)
        for t in range(tiles):
            first = t * thick + z
            residual_ref[l, t] = weight * jnp.concatenate(
                [
                    in_ref[pl.ds((c * spaces + i) * block + first, own, stride=pieces), :]
                    for c in range(chaos)
                ],
                axis=0,
            )
        put(up_ref, l, residual_ref[l, 1])
        put(down_ref, l, residual_ref[l, 0])
    for l in range(half):
        later = l + half
        put(
            up_ref,
            layers + l,
            jnp.where(low_half, pltpu.roll(residual_ref[later, 0], NY, 1), residual_ref[l, 0]),
        )
        put(
            down_ref,
            layers + l,
            jnp.where(low_half, residual_ref[l, 1], pltpu.roll(residual_ref[later, 1], NY, 1)),
        )

    for t in range(tiles):
        for z in range(thick):
            for k in range(modes):
                first = (t * thick + z) * spaces * block + own * pieces
                first += k - 1 if k > 0 else modes - 1
                a_ref[k, t, pl.ds(z, spaces, stride=thick), :] = in_ref[
                    pl.ds(first, spaces, stride=block), :
                ]
        mean = 0.5 * a_ref[0, t]
        for k in range(modes):
            value = mean if k == 0 else mean * a_ref[k, t]
            a_ref[k, t] = value
            rows = pl.ds((layers + half) * slots + (k * tiles + t) * layers, layers)
            up_ref[rows, :] = value
            down_ref[rows, :] = value


def iterate(step, scales, inside, mix_ref, a_ref, b_ref, r_ref, d_ref, total_ref, edge_ref, x_ref, send):
    layers, _, slots, _ = r_ref.shape
    modes = a_ref.shape[0]
    masks = lane_masks(slots)
    low_half = masks[0]
    mix = mix_ref[...]
    depth = mix.shape[1]
    count = FOLDED - step
    full = count - 1
    for l in range(layers):
        direct = [d_ref[l, t] for t in range(count)]
        around = neighbour_sums(d_ref, l, count, masks)
        mixed = jnp.dot(
            mix, split_stack(direct + around, depth), preferred_element_type=jnp.float32
        )

        def part(k, n):
            return jnp.concatenate(
                [
                    mixed[row : row + 8, n * LANES : (n + 1) * LANES]
                    for row in range((k - 1) * 8, (modes - 1) * slots, (modes - 1) * 8)
                ],
                axis=0,
            )

        for t in range(count):
            a = a_ref[0, l : l + 1, lanes(t)]
            edge = a * direct[t]
            if t < full:
                total = b_ref[0, l : l + 1, lanes(t)] * direct[t] - a * around[t]
            for k in range(1, modes):
                a = a_ref[k, l : l + 1, lanes(t)]
                edge = edge + a * part(k, t)
                if t < full:
                    b = b_ref[k, l : l + 1, lanes(t)]
                    total = total + (b * part(k, t) - a * part(k, count + t))
            edge_ref[l, t] = edge
            if t < full:
                total_ref[l, t] = total
    for l in range(layers):
        spread = neighbour_sums(edge_ref, l, count, masks)
        for t in range(full):
            diffused = total_ref[l, t] - spread[t]
            if t >= OWN_TILES:
                first, second = inside[(t + 1) % 2], inside[t % 2]
                diffused = diffused * jnp.where(low_half, first, second)
            residual = r_ref[l, t] - diffused
            if step == ITERS - 1:
                send(l, t, residual)
                continue
            r_ref[l, t] = residual
            old = d_ref[l, t]
            direction = scales[1 + 2 * step] * old + scales[2 + 2 * step] * residual
            d_ref[l, t] = direction
            if t < OWN_TILES:
                value = (old if step == 0 else x_ref[l, t]) + direction
                if step == ITERS - 2:
                    send(l, t, value)
                else:
                    x_ref[l, t] = value


def sender(chaos, spaces, shape, unweight_ref, sent_ref):
    layers, _, slots, _ = shape
    own = slots // chaos
    thick = layers // spaces
    pieces = OWN_TILES * thick

    def send(l, t, value):
        i, z = divmod(l, thick)
        value = value * unweight_ref[...]
        for c in range(chaos):
            first = (c * spaces + i) * own * pieces + t * thick + z
            sent_ref[pl.ds(first, own, stride=pieces), :] = value[c * own : (c + 1) * own]

    return send


def first_kernel(
    chaos,
    spaces,
    scales,
    inside,
    mix_ref,
    own_a_ref,
    unweight_ref,
    start_ref,
    up_ref,
    down_ref,
    sent_ref,
    a_ref,
    b_ref,
    r_ref,
    d_ref,
    total_ref,
    edge_ref,
    x_ref,
):
    layers, _, slots, _ = start_ref.shape
    modes = own_a_ref.shape[0]
    half = layers // 2
    low_half = lane_masks(slots)[0]
    send = sender(chaos, spaces, start_ref.shape, unweight_ref, sent_ref)

    layer = lax.broadcasted_iota(jnp.int32, (layers, LANES), 0)
    zero = jnp.zeros((layers, LANES), jnp.float32)
    narrow_masks = lane_masks(layers)
    low = narrow_masks[0]
    for k in range(modes):
        below, above = [
            [
                ref[pl.ds((layers + half) * slots + (k * OWN_TILES + t) * layers, layers), :]
                for t in range(OWN_TILES)
            ]
            for ref in (up_ref, down_ref)
        ]
        values = [
            own_a_ref[k, 0],
            own_a_ref[k, 1],
            jnp.where(low, above[0], below[1]),
            jnp.where(low, below[1], above[0]),
            jnp.where(low, above[1], below[0]),
        ]
        sums = plane_sums(values, narrow_masks)
        for t in range(FOLDED):
            a_ref[k, :, lanes(t)] = values[t]
        for t in range(FOLDED - 1):
            under = jnp.where(layer > 0, pltpu.roll(values[t], 1, 0), zero)
            over = jnp.where(layer < layers - 1, pltpu.roll(values[t], layers - 1, 0), zero)
            b_ref[k, :, lanes(t)] = 6.0 * values[t] + (sums[t] + (under + over))

    def message(ref, place):
        return ref[pl.ds(place * slots, slots), :]

    for l in range(layers):
        below, above = message(up_ref, l), message(down_ref, l)
        far_below = message(up_ref, layers + l % half)
        far_above = message(down_ref, layers + l % half)
        if l < half:
            far = jnp.where(low_half, far_above, far_below)
        else:
            far = pltpu.roll(jnp.where(low_half, far_below, far_above), NY, 1)
        tiles = [
            start_ref[l, 0],
            start_ref[l, 1],
            jnp.where(low_half, above, below),
            jnp.where(low_half, below, above),
            far,
        ]
        for t, tile in enumerate(tiles):
            if t < FOLDED - 1:
                r_ref[l, t] = tile
            d_ref[l, t] = tile * scales[0]

    for step in range(ITERS - 1):
        iterate(
            step, scales, inside, mix_ref, a_ref, b_ref, r_ref, d_ref, total_ref, edge_ref, x_ref, send
        )


def last_kernel(
    chaos,
    spaces,
    scales,
    inside,
    mix_ref,
    unweight_ref,
    a_ref,
    b_ref,
    r_ref,
    d_ref,
    sent_ref,
    total_ref,
    edge_ref,
):
    send = sender(chaos, spaces, r_ref.shape, unweight_ref, sent_ref)
    iterate(
        ITERS - 1, scales, inside, mix_ref, a_ref, b_ref, r_ref, d_ref, total_ref, edge_ref, None, send
    )


def call(kernel, outs, scalars, arrays, scratch=(), flops=0, in_kinds=None, out_kind=pltpu.VMEM):
    kinds = in_kinds or [pltpu.VMEM] * len(arrays)
    in_specs = [pl.BlockSpec(memory_space=pltpu.SMEM)] * len(scalars) + [
        pl.BlockSpec(memory_space=kind) for kind in kinds
    ]
    arrays = [
        pltpu.with_memory_space_constraint(x, kind) if kind == pltpu.HBM else x
        for x, kind in zip(arrays, kinds)
    ]
    moved = sum(4 * x.size for x in arrays) + sum(4 * x.size for x in outs)
    return pl.pallas_call(
        kernel,
        out_shape=outs,
        in_specs=in_specs,
        out_specs=[pl.BlockSpec(memory_space=out_kind)] * len(outs),
        scratch_shapes=scratch,
        compiler_params=pltpu.CompilerParams(vmem_limit_bytes=40 * 1024 * 1024),
        cost_estimate=pl.CostEstimate(flops=flops, bytes_accessed=moved, transcendentals=0),
    )(*scalars, *arrays)


def coupling_tables(coupling, slot_term):
    bf16 = jnp.bfloat16
    slots = slot_term.shape[0]
    raising = (slot_term[None, None, :] == coupling[:, :, 0:1]).astype(bf16)
    lowering = (slot_term[None, None, :] == coupling[:, :, 1:2]).astype(bf16)
    weighted = raising * coupling[:, :, 2:3].astype(bf16)
    matrices = jnp.einsum(
        "kps,kpr->ksr", weighted, lowering, preferred_element_type=jnp.float32
    ) + jnp.einsum("kps,kpr->ksr", lowering, raising, preferred_element_type=jnp.float32)
    spare = -slots % 16
    matrices = jnp.pad(matrices.astype(bf16), ((0, 0), (0, 0), (0, spare)))
    matrices = matrices.reshape(-1, slots // 8, 8, slots + spare).transpose(1, 0, 2, 3)
    matrices = matrices.reshape(-1, slots + spare)
    degree = jnp.sum(weighted.astype(jnp.float32), axis=1)
    factorial = jnp.where(degree > 2.5, 6.0, jnp.where(degree > 1.5, 2.0, 1.0))
    scale = jnp.sqrt(jnp.prod(factorial, axis=0))
    occupied = (slot_term >= 0).astype(jnp.float32)
    spread = jnp.ones((1, LANES), jnp.float32)
    return (
        jnp.concatenate([matrices, matrices], axis=1),
        (occupied * scale)[:, None] * spread,
        (occupied / scale)[:, None] * spread,
    )


def local_by_cells(source_chaos_terms, mean_conductivity, mode_shapes, coupling, slot_term, bounds):
    own, thick, cells = source_chaos_terms.shape
    chaos, spaces = lax.axis_size("chaos"), lax.axis_size("space")
    devices = chaos * spaces
    slots = own * chaos
    layers = thick * spaces
    columns = cells // LANES
    pieces = OWN_TILES * thick
    blocks = [block_of(device, spaces) for device in range(devices)]
    f32 = jnp.float32

    def shape(*sizes):
        return jax.ShapeDtypeStruct(sizes, f32)

    def by_blocks(field):
        lead = field.shape[:-2]
        tiled = field.reshape(*lead, thick, columns, LANES)
        return jnp.swapaxes(tiled, -3, -2)

    row, column = lax.axis_index("chaos"), lax.axis_index("space")
    block = row * spaces + jnp.where(row % 2 == 0, column, spaces - 1 - column)
    inside = jnp.stack([block > 0, block < devices - 1]).astype(f32)
    modes = mode_shapes.shape[0] + 1
    scattered = call(
        functools.partial(scatter_kernel, blocks),
        [shape(devices, own + 2, pieces, LANES)],
        [row[None]],
        [
            by_blocks(source_chaos_terms).reshape(own, devices, pieces, LANES),
            by_blocks(mean_conductivity).reshape(-1, LANES),
            by_blocks(mode_shapes).reshape(-1, LANES),
        ],
        [
            pltpu.VMEM((devices * pieces, LANES), f32),
            pltpu.VMEM(((modes - 1) * devices * pieces, LANES), f32),
            pltpu.SemaphoreType.DMA((devices + 2,)),
        ],
        in_kinds=[pltpu.HBM] * 3,
    )[0]
    gathered = lax.all_to_all(scattered, BOTH, 0, 0, tiled=True).reshape(-1, LANES)

    mix, weight, unweight = coupling_tables(coupling, slot_term)
    midpoint = 0.5 * (bounds[1] + bounds[0])
    half_span = 0.5 * (bounds[1] - bounds[0])
    sigma_one = midpoint / half_span
    rho_now = 1.0 / sigma_one
    scales = [1.0 / midpoint]
    for _ in range(ITERS - 1):
        rho_next = 1.0 / (2.0 * sigma_one - rho_now)
        scales += [rho_next * rho_now, 2.0 * rho_next / half_span]
        rho_now = rho_next
    scales = jnp.stack(scales)

    message = shape((layers + layers // 2) * slots + modes * OWN_TILES * layers, LANES)
    start, own_a, up, down = call(
        functools.partial(start_kernel, chaos, spaces, modes),
        [
            shape(layers, OWN_TILES, slots, LANES),
            shape(modes, OWN_TILES, layers, LANES),
            message,
            message,
        ],
        [],
        [weight, gathered],
    )
    place = {n: device for device, n in enumerate(blocks)}
    upward = [(place[n], place[n + 1]) for n in range(devices - 1)]
    downward = [(place[n + 1], place[n]) for n in range(devices - 1)]
    from_below = lax.ppermute(up, BOTH, upward)
    from_above = lax.ppermute(down, BOTH, downward)

    def held(tiles):
        return pltpu.VMEM((layers, tiles, slots, LANES), f32)

    sent, a, b, residual, direction = call(
        functools.partial(first_kernel, chaos, spaces),
        [
            shape(devices * own * pieces, LANES),
            shape(modes, layers, FOLDED * LANES),
            shape(modes, layers, (FOLDED - 1) * LANES),
            shape(layers, FOLDED - 1, slots, LANES),
            shape(layers, FOLDED, slots, LANES),
        ],
        [scales, inside],
        [mix, own_a, unweight, start, from_below, from_above],
        [held(FOLDED - 1), held(FOLDED), held(OWN_TILES)],
        flops=8000000000,
    )
    received = [lax.all_to_all(sent.reshape(devices, own, pieces, LANES), BOTH, 0, 0, tiled=True)]
    sent = call(
        functools.partial(last_kernel, chaos, spaces),
        [shape(devices * own * pieces, LANES)],
        [scales, inside],
        [mix, unweight, a, b, residual, direction],
        [held(OWN_TILES), held(OWN_TILES + 1)],
        flops=3000000000,
    )[0]
    received.append(
        lax.all_to_all(sent.reshape(devices, own, pieces, LANES), BOTH, 0, 0, tiled=True)
    )
    outs = call(
        functools.partial(collect_kernel, blocks),
        [shape(own, devices, pieces, LANES)] * 2,
        [],
        received,
        [pltpu.SemaphoreType.DMA((2, devices))],
        in_kinds=[pl.ANY] * 2,
        out_kind=pltpu.HBM,
    )
    return tuple(
        jnp.transpose(out.reshape(own, columns, thick, LANES), (0, 2, 1, 3)).reshape(
            own, thick, cells
        )
        for out in outs
    )


def local(source_chaos_terms, mean_conductivity, mode_shapes, coupling, slot_term, bounds):
    own, thick, cells = source_chaos_terms.shape
    chaos, spaces = lax.axis_size("chaos"), lax.axis_size("space")
    fits = (
        thick * spaces == 8
        and cells == chaos * spaces * OWN_TILES * LANES
        and (own * chaos) % 8 == 0
        and chaos == OWN_TILES * thick
        and chaos <= mode_shapes.shape[0] < 2 * chaos
    )
    plan = local_by_cells if fits else local_by_slots
    return plan(
        source_chaos_terms, mean_conductivity, mode_shapes, coupling, slot_term, bounds
    )


def solution(mesh):
    in_specs = (
        P(("groups", "chaos"), "space", None),
        P("space", None),
        P(None, "space", None),
        P(),
        P(),
        P("groups"),
    )
    out_specs = (P(("groups", "chaos"), "space", None), P(("groups", "chaos"), "space", None))
    return jax.shard_map(local, mesh=mesh, in_specs=in_specs, out_specs=out_specs, check_vma=False)
```

```python
import functools

import jax
import jax.numpy as jnp
from jax import lax
from jax.experimental import pallas as pl
from jax.experimental.pallas import tpu as pltpu
from jax.sharding import PartitionSpec as P

NY = 64
ITERS = 3
LANES = 128
BOTH = ("chaos", "space")


full_precision = lax.Precision.HIGHEST


def with_halo(cells, sides, width):
    for axis, dim in sides:
        count = lax.axis_size(axis)
        ends = count - 1
        head = lax.slice_in_dim(cells, 0, width, axis=dim)
        tail = lax.slice_in_dim(cells, cells.shape[dim] - width, cells.shape[dim], axis=dim)
        cells = jnp.concatenate(
            [
                lax.ppermute(tail, axis, [(i, (i + 1) % count) for i in range(ends)]),
                cells,
                lax.ppermute(head, axis, [((i + 1) % count, i) for i in range(ends)]),
            ],
            axis=dim,
        )
    return cells


def mixing_matrices(coupling, slot_term):
    occupied = (slot_term >= 0).astype(jnp.float32)
    raising = (slot_term[None, None, :] == coupling[:, :, 0:1]).astype(jnp.float32)
    lowering = (slot_term[None, None, :] == coupling[:, :, 1:2]).astype(jnp.float32)
    weight = jnp.sqrt(coupling[:, :, 2].astype(jnp.float32))
    raised = jnp.einsum("kps,kp,kpr->ksr", raising, weight, lowering, precision=full_precision)
    mode_mats = raised + jnp.transpose(raised, (0, 2, 1))
    return jnp.concatenate([jnp.diag(occupied)[None], mode_mats], axis=0)


def shift_cells(values, offset, edge_mask):
    fill = jnp.zeros(values.shape[:-1] + (abs(offset),), values.dtype)
    if offset > 0:
        shifted = jnp.concatenate([values[..., offset:], fill], axis=-1)
    else:
        shifted = jnp.concatenate([fill, values[..., :offset]], axis=-1)
    return shifted * edge_mask


def diffuse(field_padded, conduct_padded):
    centre = field_padded[..., 1:-1, :]
    conduct = conduct_padded[..., 1:-1, :]
    accumulated = (
        0.5 * (conduct + conduct_padded[..., :-2, :]) * (centre - field_padded[..., :-2, :])
    )
    accumulated = accumulated + 0.5 * (conduct + conduct_padded[..., 2:, :]) * (
        centre - field_padded[..., 2:, :]
    )
    cells = centre.shape[-1]
    column_in_row = lax.iota(jnp.int32, cells) % NY
    upper_mask = (column_in_row < NY - 1).astype(centre.dtype)
    lower_mask = (column_in_row > 0).astype(centre.dtype)
    all_mask = jnp.ones((cells,), centre.dtype)
    for offset, edge_mask in ((1, upper_mask), (-1, lower_mask), (NY, all_mask), (-NY, all_mask)):
        neighbour = shift_cells(centre, offset, edge_mask)
        neighbour_conduct = shift_cells(conduct, offset, edge_mask)
        accumulated = accumulated + 0.5 * (conduct + neighbour_conduct) * (centre - neighbour)
    return accumulated


def local_by_slots(source_chaos_terms, mean_conductivity, mode_shapes, coupling, slot_term, bounds):
    slot_count = source_chaos_terms.shape[0]
    conductivity = jnp.concatenate(
        [mean_conductivity[None], mean_conductivity[None] * mode_shapes], axis=0
    )
    conduct_padded = with_halo(conductivity, (("space", 1),), 1)
    matrices = mixing_matrices(coupling, slot_term)
    first_own = lax.axis_index("chaos") * slot_count
    own_rows = lax.dynamic_slice_in_dim(matrices, first_own, slot_count, 1)
    own_terms = lax.dynamic_slice_in_dim(slot_term, first_own, slot_count, 0)
    occupied = (own_terms >= 0).astype(jnp.float32)[:, None, None]
    lower_bound = bounds[0]
    upper_bound = bounds[1]
    midpoint = 0.5 * (upper_bound + lower_bound)
    half_span = 0.5 * (upper_bound - lower_bound)
    sigma_one = midpoint / half_span
    rho_now = 1.0 / sigma_one
    residual = source_chaos_terms * occupied
    solution_field = jnp.zeros_like(residual)
    direction = residual / midpoint
    for iteration in range(ITERS):
        solution_field = solution_field + direction
        fields = jnp.einsum(
            "ksr,rzc->kszc",
            own_rows,
            lax.all_gather(direction, "chaos", axis=0, tiled=True),
            precision=full_precision,
        )
        field_padded = with_halo(fields, (("space", 2),), 1)
        diffused = diffuse(field_padded, conduct_padded[:, None])
        residual = residual - jnp.sum(diffused, axis=0)
        if iteration + 1 < ITERS:
            rho_next = 1.0 / (2.0 * sigma_one - rho_now)
            direction = rho_next * rho_now * direction + 2.0 * rho_next / half_span * residual
            rho_now = rho_next
    return (solution_field, residual)


OWN_TILES = 2
FOLDED = OWN_TILES + ITERS


def block_of(device, spaces):
    chaos, space = divmod(device, spaces)
    return chaos * spaces + (space if chaos % 2 == 0 else spaces - 1 - space)


def lane_masks(rows):
    lane = lax.broadcasted_iota(jnp.int32, (rows, LANES), 1)
    return lane < NY, lane % NY > 0, lane % NY < NY - 1


def plane_sums(tiles, masks, first=0):
    low_half, has_left, has_right = masks
    zero = jnp.zeros(tiles[0].shape, jnp.float32)
    swapped = [pltpu.roll(tile, NY, 1) for tile in tiles]
    sums = []
    for t in range(first, len(tiles) - 1):
        if t == 0:
            across = swapped[0] + jnp.where(low_half, swapped[2], swapped[1])
        elif t == 1:
            across = swapped[1] + jnp.where(low_half, swapped[0], swapped[2])
        elif t == 2:
            across = swapped[3] + jnp.where(low_half, swapped[1], swapped[0])
        else:
            across = swapped[t - 1] + swapped[t + 1]
        left = jnp.where(has_left, pltpu.roll(tiles[t], 1, 1), zero)
        right = jnp.where(has_right, pltpu.roll(tiles[t], LANES - 1, 1), zero)
        sums.append(across + (left + right))
    return sums


def neighbour_sums(read, layer, layers, count, masks, first=0):
    sums = plane_sums([read(layer, t) for t in range(count)], masks, first)
    for other in (layer - 1, layer + 1):
        if 0 <= other < layers:
            sums = [total + read(other, first + n) for n, total in enumerate(sums)]
    return sums


def split_stack(tiles, depth):
    wide = jnp.concatenate(tiles, axis=1)
    spare = depth // 2 - wide.shape[0]
    if spare:
        wide = jnp.concatenate([wide, jnp.zeros((spare, wide.shape[1]), wide.dtype)], axis=0)
    high = wide.astype(jnp.bfloat16)
    low = (wide - high.astype(jnp.float32)).astype(jnp.bfloat16)
    return jnp.concatenate([high, low], axis=0)


def lanes(t):
    return pl.ds(t * LANES, LANES)


def run_copies(copies):
    for copy in copies:
        copy.start()
    for copy in copies:
        copy.wait()


def scatter_kernel(
    blocks, chaos_index, in_ref, mean_ref, modes_ref, out_ref, mean_held, modes_held, sems
):
    own, devices, pieces, _ = in_ref.shape
    modes = modes_ref.shape[0] // (devices * pieces)
    small = [
        pltpu.make_async_copy(mean_ref, mean_held, sems.at[devices]),
        pltpu.make_async_copy(modes_ref, modes_held, sems.at[devices + 1]),
    ]
    copies = [
        pltpu.make_async_copy(
            in_ref.at[:, block], out_ref.at[device, pl.ds(0, own)], sems.at[device]
        )
        for device, block in enumerate(blocks)
    ]
    for copy in small + copies:
        copy.start()
    for copy in small:
        copy.wait()
    for device, block in enumerate(blocks):
        row = block * pieces + chaos_index[0]
        values = modes_held[pl.ds(row, modes, stride=devices * pieces), :]
        out_ref[device, own] = values[:pieces]
        out_ref[device, own + 1] = jnp.concatenate(
            [
                values[pieces:],
                mean_held[pl.ds(row, 1), :],
                jnp.zeros((2 * pieces - modes - 1, LANES), jnp.float32),
            ],
            axis=0,
        )
    for copy in copies:
        copy.wait()


def collect_kernel(blocks, in_ref, *rest):
    *outs, sems = rest
    run_copies(
        [
            pltpu.make_async_copy(
                in_ref.at[device, n], out_ref.at[:, block], sems.at[n, device]
            )
            for n, out_ref in enumerate(outs)
            for device, block in enumerate(blocks)
        ]
    )


def start_kernel(
    chaos,
    spaces,
    modes,
    odd,
    scales,
    mix_ref,
    weight_ref,
    in_ref,
    residual_ref,
    a_ref,
    chip_ref,
    core_ref,
):
    upward = odd[0] > 0
    layers, tiles, slots, _ = residual_ref.shape
    own = slots // chaos
    thick = layers // spaces
    pieces = tiles * thick
    block = (own + 2) * pieces
    half = layers // 2
    low_half = lane_masks(slots)[0]
    weight = weight_ref[...]

    def put(rows, up, down):
        chip_ref[rows, :] = jnp.where(upward, up, down)
        core_ref[rows, :] = jnp.where(upward, down, up)

    for l in range(layers):
        i, z = divmod(l, thick)
        for t in range(tiles):
            first = t * thick + z
            residual_ref[l, t] = weight * jnp.concatenate(
                [
                    in_ref[pl.ds((c * spaces + i) * block + first, own, stride=pieces), :]
                    for c in range(chaos)
                ],
                axis=0,
            )
        put(pl.ds(l * slots, slots), residual_ref[l, 1], residual_ref[l, 0])
    for l in range(half):
        later = l + half
        put(
            pl.ds((layers + l) * slots, slots),
            jnp.where(low_half, pltpu.roll(residual_ref[later, 0], NY, 1), residual_ref[l, 0]),
            jnp.where(low_half, residual_ref[l, 1], pltpu.roll(residual_ref[later, 1], NY, 1)),
        )

    for t in range(tiles):
        for z in range(thick):
            for k in range(modes):
                first = (t * thick + z) * spaces * block + own * pieces
                first += k - 1 if k > 0 else modes - 1
                a_ref[k, t, pl.ds(z, spaces, stride=thick), :] = in_ref[
                    pl.ds(first, spaces, stride=block), :
                ]
        mean = 0.5 * a_ref[0, t]
        for k in range(modes):
            value = mean if k == 0 else mean * a_ref[k, t]
            a_ref[k, t] = value
            rows = pl.ds((layers + half) * slots + (k * tiles + t) * layers, layers)
            put(rows, value, value)


def mode_part(mixed, modes, k, n):
    group = 8 * (modes - 1)
    return jnp.concatenate(
        [
            mixed[row : row + 8, n * LANES : (n + 1) * LANES]
            for row in range((k - 1) * 8, mixed.shape[0], group)
        ],
        axis=0,
    )


def layer_sum(values, layer):
    layers = values.shape[0]
    zero = jnp.zeros(values.shape, jnp.float32)
    under = jnp.where(layer > 0, pltpu.roll(values, 1, 0), zero)
    over = jnp.where(layer < layers - 1, pltpu.roll(values, layers - 1, 0), zero)
    return under + over


def weighted_tiles(mixed, modes, count, full, direct, around, a_of, b_of):
    results = []
    for t in range(count):
        a = a_of(0, t)
        edge = a * direct[t]
        total = b_of(0, t) * direct[t] - a * around[t] if t < full else None
        for k in range(1, modes):
            a = a_of(k, t)
            part = mode_part(mixed, modes, k, t)
            edge = edge + a * part
            if t < full:
                beside = mode_part(mixed, modes, k, mixed.shape[1] // LANES - full + t)
                total = total + (b_of(k, t) * part - a * beside)
        results.append((total, edge))
    return results


def own_kernel(scales, mix_ref, own_a_ref, start_ref, total_ref, edge_ref, b_ref):
    layers, tiles, slots, _ = start_ref.shape
    modes = own_a_ref.shape[0]
    masks = lane_masks(slots)
    mix = mix_ref[...]
    layer = lax.broadcasted_iota(jnp.int32, (layers, LANES), 0)
    outside = jnp.zeros((layers, LANES), jnp.float32)
    for k in range(modes):
        values = [own_a_ref[k, t] for t in range(tiles)]
        sums = plane_sums(values + [outside], lane_masks(layers))
        for t in range(tiles):
            b_ref[k, :, lanes(t)] = 6.0 * values[t] + (sums[t] + layer_sum(values[t], layer))
    nothing = jnp.zeros((slots, LANES), jnp.float32)

    def read(l, t):
        return start_ref[l, t] * scales[0] if t < tiles else nothing

    for l in range(layers):
        direct = [read(l, t) for t in range(tiles)]
        around = neighbour_sums(read, l, layers, tiles + 1, masks)
        mixed = jnp.dot(
            mix, split_stack(direct + around, mix.shape[1]), preferred_element_type=jnp.float32
        )
        results = weighted_tiles(
            mixed,
            modes,
            tiles,
            tiles,
            direct,
            around,
            lambda k, t: own_a_ref[k, t, l : l + 1, :],
            lambda k, t: b_ref[k, l : l + 1, lanes(t)],
        )
        for t, (total, edge) in enumerate(results):
            total_ref[l, t] = total
            edge_ref[l, t] = edge


def iterate_kernel(
    chaos,
    spaces,
    scales,
    inside,
    odd,
    mix_ref,
    own_a_ref,
    unweight_ref,
    start_ref,
    own_total_ref,
    own_edge_ref,
    chip_ref,
    core_ref,
    sent_ref,
    a_ref,
    b_ref,
    face_ref,
    r_ref,
    d_ref,
    total_ref,
    edge_ref,
    x_ref,
):
    layers, _, slots, _ = start_ref.shape
    modes = own_a_ref.shape[0]
    own = slots // chaos
    thick = layers // spaces
    pieces = OWN_TILES * thick
    half = layers // 2
    masks = lane_masks(slots)
    low_half = masks[0]
    mix = mix_ref[...]
    depth = mix.shape[1]
    upward = odd[0] > 0

    def message(start, size):
        chip, core = chip_ref[pl.ds(start, size), :], core_ref[pl.ds(start, size), :]
        return jnp.where(upward, core, chip), jnp.where(upward, chip, core)

    def send(field, l, t, value):
        i, z = divmod(l, thick)
        value = value * unweight_ref[...]
        for c in range(chaos):
            first = ((c * spaces + i) * 2 + field) * own * pieces + t * thick + z
            sent_ref[pl.ds(first, own, stride=pieces), :] = value[c * own : (c + 1) * own]

    layer = lax.broadcasted_iota(jnp.int32, (layers, LANES), 0)
    narrow_masks = lane_masks(layers)
    low = narrow_masks[0]
    for k in range(modes):
        places = [(layers + half) * slots + (k * OWN_TILES + t) * layers for t in range(OWN_TILES)]
        below, above = zip(*[message(place, layers) for place in places])
        values = [
            own_a_ref[k, 0],
            own_a_ref[k, 1],
            jnp.where(low, above[0], below[1]),
            jnp.where(low, below[1], above[0]),
            jnp.where(low, above[1], below[0]),
        ]
        sums = plane_sums(values, narrow_masks)
        for t in range(FOLDED):
            a_ref[k, :, lanes(t)] = values[t]
        for t in range(FOLDED - 1):
            b_ref[k, :, lanes(t)] = 6.0 * values[t] + (sums[t] + layer_sum(values[t], layer))
        face_ref[k, :, lanes(0)] = jnp.where(low, values[0], values[1])
        face_ref[k, :, lanes(1)] = pltpu.roll(values[2], NY, 1)

    for l in range(layers):
        below, above = message(l * slots, slots)
        far_below, far_above = message((layers + l % half) * slots, slots)
        if l < half:
            far = jnp.where(low_half, far_above, far_below)
        else:
            far = pltpu.roll(jnp.where(low_half, far_below, far_above), NY, 1)
        tiles = [
            start_ref[l, 0],
            start_ref[l, 1],
            jnp.where(low_half, above, below),
            jnp.where(low_half, below, above),
            far,
        ]
        for t, tile in enumerate(tiles):
            if t < FOLDED - 1:
                r_ref[l, t] = tile
            d_ref[l, t] = tile * scales[0]

    def read(l, t):
        return d_ref[l, t]

    zero = jnp.zeros((slots, LANES), jnp.float32)
    for step in range(ITERS):
        count = FOLDED - step
        full = count - 1
        first = OWN_TILES if step == 0 else 0
        for l in range(layers):
            direct = [d_ref[l, t] for t in range(first, count)]
            around = neighbour_sums(read, l, layers, count, masks, first)
            extra = []
            if step == 0:
                extra = [jnp.where(low_half, d_ref[l, 0], d_ref[l, 1])]
            mixed = jnp.dot(
                mix, split_stack(direct + extra + around, depth), preferred_element_type=jnp.float32
            )
            results = weighted_tiles(
                mixed,
                modes,
                count - first,
                full - first,
                direct,
                around,
                lambda k, t: a_ref[k, l : l + 1, lanes(first + t)],
                lambda k, t: b_ref[k, l : l + 1, lanes(first + t)],
            )
            for t, (total, edge) in enumerate(results):
                edge_ref[l, first + t] = edge
                if first + t < full:
                    total_ref[l, first + t] = total
            if step == 0:
                own_face = face_ref[0, l : l + 1, lanes(0)]
                other_face = face_ref[0, l : l + 1, lanes(1)]
                part = other_face * extra[0] - own_face * pltpu.roll(direct[0], NY, 1)
                for k in range(1, modes):
                    own_face = face_ref[k, l : l + 1, lanes(0)]
                    other_face = face_ref[k, l : l + 1, lanes(1)]
                    own_mixed = mode_part(mixed, modes, k, len(direct))
                    other_mixed = pltpu.roll(mode_part(mixed, modes, k, 0), NY, 1)
                    part = part + (other_face * own_mixed - own_face * other_mixed)
                total_ref[l, 0] = own_total_ref[l, 0] + jnp.where(low_half, part, zero)
                total_ref[l, 1] = own_total_ref[l, 1] + jnp.where(low_half, zero, part)

        def read_edge(l, t):
            return own_edge_ref[l, t] if t < first else edge_ref[l, t]

        for l in range(layers):
            spread = neighbour_sums(read_edge, l, layers, count, masks)
            for t in range(full):
                diffused = total_ref[l, t] - spread[t]
                if t >= OWN_TILES:
                    lower, upper = inside[(t + 1) % 2], inside[t % 2]
                    diffused = diffused * jnp.where(low_half, lower, upper)
                residual = r_ref[l, t] - diffused
                if step == ITERS - 1:
                    send(1, l, t, residual)
                    continue
                r_ref[l, t] = residual
                old = d_ref[l, t]
                direction = scales[1 + 2 * step] * old + scales[2 + 2 * step] * residual
                d_ref[l, t] = direction
                if t < OWN_TILES:
                    value = (old if step == 0 else x_ref[l, t]) + direction
                    if step == ITERS - 2:
                        send(0, l, t, value)
                    else:
                        x_ref[l, t] = value


def call(kernel, outs, scalars, arrays, scratch=(), flops=0, in_kinds=None, out_kind=pltpu.VMEM):
    kinds = in_kinds or [pltpu.VMEM] * len(arrays)
    in_specs = [pl.BlockSpec(memory_space=pltpu.SMEM)] * len(scalars) + [
        pl.BlockSpec(memory_space=kind) for kind in kinds
    ]
    arrays = [
        pltpu.with_memory_space_constraint(x, kind) if kind == pltpu.HBM else x
        for x, kind in zip(arrays, kinds)
    ]
    moved = sum(4 * x.size for x in arrays) + sum(4 * x.size for x in outs)
    return pl.pallas_call(
        kernel,
        out_shape=outs,
        in_specs=in_specs,
        out_specs=[pl.BlockSpec(memory_space=out_kind)] * len(outs),
        scratch_shapes=scratch,
        compiler_params=pltpu.CompilerParams(vmem_limit_bytes=40 * 1024 * 1024),
        cost_estimate=pl.CostEstimate(flops=flops, bytes_accessed=moved, transcendentals=0),
    )(*scalars, *arrays)


def coupling_tables(coupling, slot_term):
    bf16 = jnp.bfloat16
    slots = slot_term.shape[0]
    raising = (slot_term[None, None, :] == coupling[:, :, 0:1]).astype(bf16)
    lowering = (slot_term[None, None, :] == coupling[:, :, 1:2]).astype(bf16)
    weighted = raising * coupling[:, :, 2:3].astype(bf16)
    matrices = jnp.einsum(
        "kps,kpr->ksr", weighted, lowering, preferred_element_type=jnp.float32
    ) + jnp.einsum("kps,kpr->ksr", lowering, raising, preferred_element_type=jnp.float32)
    spare = -slots % 16
    matrices = jnp.pad(matrices.astype(bf16), ((0, 0), (0, 0), (0, spare)))
    matrices = matrices.reshape(-1, slots // 8, 8, slots + spare).transpose(1, 0, 2, 3)
    matrices = matrices.reshape(-1, slots + spare)
    degree = jnp.sum(weighted.astype(jnp.float32), axis=1)
    factorial = jnp.where(degree > 2.5, 6.0, jnp.where(degree > 1.5, 2.0, 1.0))
    scale = jnp.sqrt(jnp.prod(factorial, axis=0))
    occupied = (slot_term >= 0).astype(jnp.float32)
    spread = jnp.ones((1, LANES), jnp.float32)
    return (
        jnp.concatenate([matrices, matrices], axis=1),
        (occupied * scale)[:, None] * spread,
        (occupied / scale)[:, None] * spread,
    )


def local_by_cells(source_chaos_terms, mean_conductivity, mode_shapes, coupling, slot_term, bounds):
    own, thick, cells = source_chaos_terms.shape
    chaos, spaces = lax.axis_size("chaos"), lax.axis_size("space")
    devices = chaos * spaces
    slots = own * chaos
    layers = thick * spaces
    columns = cells // LANES
    pieces = OWN_TILES * thick
    blocks = [block_of(device, spaces) for device in range(devices)]
    f32 = jnp.float32

    def shape(*sizes):
        return jax.ShapeDtypeStruct(sizes, f32)

    def by_blocks(field):
        lead = field.shape[:-2]
        tiled = field.reshape(*lead, thick, columns, LANES)
        return jnp.swapaxes(tiled, -3, -2)

    row, column = lax.axis_index("chaos"), lax.axis_index("space")
    block = row * spaces + jnp.where(row % 2 == 0, column, spaces - 1 - column)
    inside = jnp.stack([block > 0, block < devices - 1]).astype(f32)
    modes = mode_shapes.shape[0] + 1
    scattered = call(
        functools.partial(scatter_kernel, blocks),
        [shape(devices, own + 2, pieces, LANES)],
        [row[None]],
        [
            by_blocks(source_chaos_terms).reshape(own, devices, pieces, LANES),
            by_blocks(mean_conductivity).reshape(-1, LANES),
            by_blocks(mode_shapes).reshape(-1, LANES),
        ],
        [
            pltpu.VMEM((devices * pieces, LANES), f32),
            pltpu.VMEM(((modes - 1) * devices * pieces, LANES), f32),
            pltpu.SemaphoreType.DMA((devices + 2,)),
        ],
        in_kinds=[pltpu.HBM] * 3,
    )[0]
    gathered = lax.all_to_all(scattered, BOTH, 0, 0, tiled=True).reshape(-1, LANES)

    mix, weight, unweight = coupling_tables(coupling, slot_term)
    midpoint = 0.5 * (bounds[1] + bounds[0])
    half_span = 0.5 * (bounds[1] - bounds[0])
    sigma_one = midpoint / half_span
    rho_now = 1.0 / sigma_one
    scales = [1.0 / midpoint]
    for _ in range(ITERS - 1):
        rho_next = 1.0 / (2.0 * sigma_one - rho_now)
        scales += [rho_next * rho_now, 2.0 * rho_next / half_span]
        rho_now = rho_next
    scales = jnp.stack(scales)

    message = shape((layers + layers // 2) * slots + modes * OWN_TILES * layers, LANES)
    odd = (block % 2)[None]
    start, own_a, to_chip, to_core = call(
        functools.partial(start_kernel, chaos, spaces, modes),
        [
            shape(layers, OWN_TILES, slots, LANES),
            shape(modes, OWN_TILES, layers, LANES),
            message,
            message,
        ],
        [odd, scales],
        [mix, weight, gathered],
    )
    place = {n: device for device, n in enumerate(blocks)}

    def swap(field, lowest):
        pairs = [(place[n], place[n + 1]) for n in range(lowest, devices - 1, 2)]
        return lax.ppermute(field, BOTH, pairs + [(b, a) for a, b in pairs])

    from_chip = swap(to_chip, 1)
    from_core = swap(to_core, 0)
    own_field = shape(layers, OWN_TILES, slots, LANES)
    own_total, own_edge = call(
        own_kernel,
        [own_field, own_field],
        [scales],
        [mix, own_a, start],
        [pltpu.VMEM((modes, layers, OWN_TILES * LANES), f32)],
        flops=3000000000,
    )

    def held(tiles):
        return pltpu.VMEM((layers, tiles, slots, LANES), f32)

    sent = call(
        functools.partial(iterate_kernel, chaos, spaces),
        [shape(devices * 2 * own * pieces, LANES)],
        [scales, inside, odd],
        [mix, own_a, unweight, start, own_total, own_edge, from_chip, from_core],
        [
            pltpu.VMEM((modes, layers, FOLDED * LANES), f32),
            pltpu.VMEM((modes, layers, (FOLDED - 1) * LANES), f32),
            pltpu.VMEM((modes, layers, 2 * LANES), f32),
            held(FOLDED - 1),
            held(FOLDED),
            held(FOLDED - 1),
            held(FOLDED),
            held(OWN_TILES),
        ],
        flops=10000000000,
    )[0]
    sent = sent.reshape(devices, 2, own, pieces, LANES)
    received = lax.all_to_all(sent, BOTH, 0, 0, tiled=True)
    outs = call(
        functools.partial(collect_kernel, blocks),
        [shape(own, devices, pieces, LANES)] * 2,
        [],
        [received],
        [pltpu.SemaphoreType.DMA((2, devices))],
        in_kinds=[pl.ANY],
        out_kind=pltpu.HBM,
    )
    return tuple(
        jnp.transpose(out.reshape(own, columns, thick, LANES), (0, 2, 1, 3)).reshape(
            own, thick, cells
        )
        for out in outs
    )


def local(source_chaos_terms, mean_conductivity, mode_shapes, coupling, slot_term, bounds):
    own, thick, cells = source_chaos_terms.shape
    chaos, spaces = lax.axis_size("chaos"), lax.axis_size("space")
    fits = (
        thick * spaces == 8
        and cells == chaos * spaces * OWN_TILES * LANES
        and (own * chaos) % 8 == 0
        and spaces % 2 == 0
        and chaos == OWN_TILES * thick
        and chaos <= mode_shapes.shape[0] < 2 * chaos
    )
    plan = local_by_cells if fits else local_by_slots
    return plan(
        source_chaos_terms, mean_conductivity, mode_shapes, coupling, slot_term, bounds
    )


def solution(mesh):
    in_specs = (
        P(("groups", "chaos"), "space", None),
        P("space", None),
        P(None, "space", None),
        P(),
        P(),
        P("groups"),
    )
    out_specs = (P(("groups", "chaos"), "space", None), P(("groups", "chaos"), "space", None))
    return jax.shard_map(local, mesh=mesh, in_specs=in_specs, out_specs=out_specs, check_vma=False)
```

```python
import functools

import jax
import jax.numpy as jnp
from jax import lax
from jax.experimental import pallas as pl
from jax.experimental.pallas import tpu as pltpu
from jax.sharding import PartitionSpec as P

NY = 64
ITERS = 3
LANES = 128
BOTH = ("chaos", "space")


full_precision = lax.Precision.HIGHEST


def with_halo(cells, sides, width):
    for axis, dim in sides:
        count = lax.axis_size(axis)
        ends = count - 1
        head = lax.slice_in_dim(cells, 0, width, axis=dim)
        tail = lax.slice_in_dim(cells, cells.shape[dim] - width, cells.shape[dim], axis=dim)
        cells = jnp.concatenate(
            [
                lax.ppermute(tail, axis, [(i, (i + 1) % count) for i in range(ends)]),
                cells,
                lax.ppermute(head, axis, [((i + 1) % count, i) for i in range(ends)]),
            ],
            axis=dim,
        )
    return cells


def mixing_matrices(coupling, slot_term):
    occupied = (slot_term >= 0).astype(jnp.float32)
    raising = (slot_term[None, None, :] == coupling[:, :, 0:1]).astype(jnp.float32)
    lowering = (slot_term[None, None, :] == coupling[:, :, 1:2]).astype(jnp.float32)
    weight = jnp.sqrt(coupling[:, :, 2].astype(jnp.float32))
    raised = jnp.einsum("kps,kp,kpr->ksr", raising, weight, lowering, precision=full_precision)
    mode_mats = raised + jnp.transpose(raised, (0, 2, 1))
    return jnp.concatenate([jnp.diag(occupied)[None], mode_mats], axis=0)


def shift_cells(values, offset, edge_mask):
    fill = jnp.zeros(values.shape[:-1] + (abs(offset),), values.dtype)
    if offset > 0:
        shifted = jnp.concatenate([values[..., offset:], fill], axis=-1)
    else:
        shifted = jnp.concatenate([fill, values[..., :offset]], axis=-1)
    return shifted * edge_mask


def diffuse(field_padded, conduct_padded):
    centre = field_padded[..., 1:-1, :]
    conduct = conduct_padded[..., 1:-1, :]
    accumulated = (
        0.5 * (conduct + conduct_padded[..., :-2, :]) * (centre - field_padded[..., :-2, :])
    )
    accumulated = accumulated + 0.5 * (conduct + conduct_padded[..., 2:, :]) * (
        centre - field_padded[..., 2:, :]
    )
    cells = centre.shape[-1]
    column_in_row = lax.iota(jnp.int32, cells) % NY
    upper_mask = (column_in_row < NY - 1).astype(centre.dtype)
    lower_mask = (column_in_row > 0).astype(centre.dtype)
    all_mask = jnp.ones((cells,), centre.dtype)
    for offset, edge_mask in ((1, upper_mask), (-1, lower_mask), (NY, all_mask), (-NY, all_mask)):
        neighbour = shift_cells(centre, offset, edge_mask)
        neighbour_conduct = shift_cells(conduct, offset, edge_mask)
        accumulated = accumulated + 0.5 * (conduct + neighbour_conduct) * (centre - neighbour)
    return accumulated


def local_by_slots(source_chaos_terms, mean_conductivity, mode_shapes, coupling, slot_term, bounds):
    slot_count = source_chaos_terms.shape[0]
    conductivity = jnp.concatenate(
        [mean_conductivity[None], mean_conductivity[None] * mode_shapes], axis=0
    )
    conduct_padded = with_halo(conductivity, (("space", 1),), 1)
    matrices = mixing_matrices(coupling, slot_term)
    first_own = lax.axis_index("chaos") * slot_count
    own_rows = lax.dynamic_slice_in_dim(matrices, first_own, slot_count, 1)
    own_terms = lax.dynamic_slice_in_dim(slot_term, first_own, slot_count, 0)
    occupied = (own_terms >= 0).astype(jnp.float32)[:, None, None]
    lower_bound = bounds[0]
    upper_bound = bounds[1]
    midpoint = 0.5 * (upper_bound + lower_bound)
    half_span = 0.5 * (upper_bound - lower_bound)
    sigma_one = midpoint / half_span
    rho_now = 1.0 / sigma_one
    residual = source_chaos_terms * occupied
    solution_field = jnp.zeros_like(residual)
    direction = residual / midpoint
    for iteration in range(ITERS):
        solution_field = solution_field + direction
        fields = jnp.einsum(
            "ksr,rzc->kszc",
            own_rows,
            lax.all_gather(direction, "chaos", axis=0, tiled=True),
            precision=full_precision,
        )
        field_padded = with_halo(fields, (("space", 2),), 1)
        diffused = diffuse(field_padded, conduct_padded[:, None])
        residual = residual - jnp.sum(diffused, axis=0)
        if iteration + 1 < ITERS:
            rho_next = 1.0 / (2.0 * sigma_one - rho_now)
            direction = rho_next * rho_now * direction + 2.0 * rho_next / half_span * residual
            rho_now = rho_next
    return (solution_field, residual)


OWN_TILES = 2
FOLDED = OWN_TILES + ITERS


def block_of(device, spaces):
    chaos, space = divmod(device, spaces)
    return chaos * spaces + (space if chaos % 2 == 0 else spaces - 1 - space)


def lane_masks(rows):
    lane = lax.broadcasted_iota(jnp.int32, (rows, LANES), 1)
    return lane < NY, lane % NY > 0, lane % NY < NY - 1


def plane_sums(tiles, masks, first=0):
    low_half, has_left, has_right = masks
    zero = jnp.zeros(tiles[0].shape, jnp.float32)
    swapped = [pltpu.roll(tile, NY, 1) for tile in tiles]
    sums = []
    for t in range(first, len(tiles) - 1):
        if t == 0:
            across = swapped[0] + jnp.where(low_half, swapped[2], swapped[1])
        elif t == 1:
            across = swapped[1] + jnp.where(low_half, swapped[0], swapped[2])
        elif t == 2:
            across = swapped[3] + jnp.where(low_half, swapped[1], swapped[0])
        else:
            across = swapped[t - 1] + swapped[t + 1]
        left = jnp.where(has_left, pltpu.roll(tiles[t], 1, 1), zero)
        right = jnp.where(has_right, pltpu.roll(tiles[t], LANES - 1, 1), zero)
        sums.append(across + (left + right))
    return sums


def neighbour_sums(read, layer, layers, count, masks, first=0):
    sums = plane_sums([read(layer, t) for t in range(count)], masks, first)
    for other in (layer - 1, layer + 1):
        if 0 <= other < layers:
            sums = [total + read(other, first + n) for n, total in enumerate(sums)]
    return sums


def split_stack(tiles, depth):
    wide = jnp.concatenate(tiles, axis=1)
    spare = depth // 2 - wide.shape[0]
    if spare:
        wide = jnp.concatenate([wide, jnp.zeros((spare, wide.shape[1]), wide.dtype)], axis=0)
    high = wide.astype(jnp.bfloat16)
    low = (wide - high.astype(jnp.float32)).astype(jnp.bfloat16)
    return jnp.concatenate([high, low], axis=0)


def lanes(t):
    return pl.ds(t * LANES, LANES)


def run_copies(copies):
    for copy in copies:
        copy.start()
    for copy in copies:
        copy.wait()


def scatter_kernel(blocks, in_ref, out_ref, held_ref, sems):
    own = in_ref.shape[0]
    parts = sems.shape[0]
    bounds = [own * n // parts for n in range(parts + 1)]
    spans = [pl.ds(a, b - a) for a, b in zip(bounds[:-1], bounds[1:])]
    copies = [
        pltpu.make_async_copy(in_ref.at[span], held_ref.at[span], sems.at[n])
        for n, span in enumerate(spans)
    ]
    for copy in copies:
        copy.start()
    for copy, span in zip(copies, spans):
        copy.wait()
        for device, block in enumerate(blocks):
            out_ref[device, span] = held_ref[span, block]


def pick_kernel(targets, scales, mix_ref, mean_ref, modes_ref, *outs):
    count, per_mode = mean_ref.shape[0], outs[0].shape[0] // (1 + modes_ref.shape[0] // mean_ref.shape[0])
    side = per_mode // 3
    last = count // side - 1
    for n, out_ref in enumerate(outs):
        block = targets[n]
        lower = jnp.where(block > 0, 1.0, 0.0)
        upper = jnp.where(block < last, 1.0, 0.0)
        before = jnp.maximum(block - 1, 0) * side
        after = jnp.minimum(block + 1, last) * side
        for k in range(out_ref.shape[0] // per_mode):
            ref, base = (mean_ref, 0) if k == 0 else (modes_ref, (k - 1) * count)
            first = k * per_mode
            out_ref[pl.ds(first, side), :] = ref[pl.ds(base + before, side), :] * lower
            out_ref[pl.ds(first + side, side), :] = ref[pl.ds(base + block * side, side), :]
            out_ref[pl.ds(first + 2 * side, side), :] = ref[pl.ds(base + after, side), :] * upper


def layer_sum(values, layer):
    layers = values.shape[0]
    zero = jnp.zeros(values.shape, jnp.float32)
    under = jnp.where(layer > 0, pltpu.roll(values, 1, 0), zero)
    over = jnp.where(layer < layers - 1, pltpu.roll(values, layers - 1, 0), zero)
    return under + over


def coefficient_kernel(thick, sources, *refs):
    *ins, a_ref, b_ref, own_b_ref, face_ref, held_ref = refs
    modes, layers, _ = a_ref.shape
    tiles = held_ref.shape[1]
    layer = lax.broadcasted_iota(jnp.int32, (layers, LANES), 0)
    masks = lane_masks(layers)
    low_half = masks[0]
    for n, in_ref in enumerate(ins):
        for k in range(modes):
            for u in range(tiles):
                held_ref[k, u, pl.ds(sources[n] * thick, thick), :] = in_ref[
                    pl.ds((k * tiles + u) * thick, thick), :
                ]
    mean = None
    for k in range(modes):
        runs = [held_ref[k, u] for u in range(tiles)]
        values = [
            runs[2],
            runs[3],
            jnp.where(low_half, runs[4], runs[1]),
            jnp.where(low_half, runs[1], runs[4]),
            jnp.where(low_half, runs[5], runs[0]),
        ]
        if k == 0:
            values = mean = [0.5 * value for value in values]
        else:
            values = [m * value for m, value in zip(mean, values)]
        sums = plane_sums(values, masks)
        for t in range(FOLDED):
            a_ref[k, :, lanes(t)] = values[t]
        for t in range(FOLDED - 1):
            b_ref[k, :, lanes(t)] = 6.0 * values[t] + (sums[t] + layer_sum(values[t], layer))
        outside = jnp.zeros((layers, LANES), jnp.float32)
        sums = plane_sums(values[:OWN_TILES] + [outside], masks)
        for t in range(OWN_TILES):
            own_b_ref[k, :, lanes(t)] = 6.0 * values[t] + (sums[t] + layer_sum(values[t], layer))
        face_ref[k, :, lanes(0)] = jnp.where(low_half, values[0], values[1])
        face_ref[k, :, lanes(1)] = pltpu.roll(values[2], NY, 1)


def collect_kernel(blocks, in_ref, *rest):
    *outs, sems = rest
    run_copies(
        [
            pltpu.make_async_copy(
                in_ref.at[device, n], out_ref.at[:, block], sems.at[n, device]
            )
            for n, out_ref in enumerate(outs)
            for device, block in enumerate(blocks)
        ]
    )


def slot_parts(own, chaos):
    whole = own // 8 * 8
    parts = [(c, 0, whole, c * whole) for c in range(chaos)]
    return parts + [
        (c, whole, own - whole, chaos * whole + c * (own - whole)) for c in range(chaos)
    ]


def start_kernel(chaos, spaces, odd, a_ref, weight_ref, in_ref, residual_ref, chip_ref, core_ref):
    upward = odd[0] > 0
    layers, tiles, slots, _ = residual_ref.shape
    own = slots // chaos
    thick = layers // spaces
    pieces = tiles * thick
    half = layers // 2
    low_half = lane_masks(slots)[0]
    weight = weight_ref[...]

    def put(place, up, down):
        rows = pl.ds(place * slots, slots)
        chip_ref[rows, :] = jnp.where(upward, up, down)
        core_ref[rows, :] = jnp.where(upward, down, up)

    for l in range(layers):
        i, z = divmod(l, thick)
        for t in range(tiles):
            rows = [
                in_ref[
                    pl.ds(
                        ((c * spaces + i) * own + slot) * pieces + t * thick + z,
                        number,
                        stride=pieces,
                    ),
                    :,
                ]
                for c, slot, number, _ in slot_parts(own, chaos)
            ]
            residual_ref[l, t] = weight * jnp.concatenate(rows, axis=0)
        put(l, residual_ref[l, 1], residual_ref[l, 0])
    for l in range(half):
        later = l + half
        put(
            layers + l,
            jnp.where(low_half, pltpu.roll(residual_ref[later, 0], NY, 1), residual_ref[l, 0]),
            jnp.where(low_half, residual_ref[l, 1], pltpu.roll(residual_ref[later, 1], NY, 1)),
        )


def mode_part(mixed, modes, k, n):
    group = 8 * (modes - 1)
    return jnp.concatenate(
        [
            mixed[row : row + 8, n * LANES : (n + 1) * LANES]
            for row in range((k - 1) * 8, mixed.shape[0], group)
        ],
        axis=0,
    )


def weighted_tiles(mixed, modes, place, beside, direct, around, a_of, b_of):
    results = []
    for t, tile in enumerate(direct):
        full = t < len(around)
        a = a_of(0, t)
        edge = a * tile
        total = b_of(0, t) * tile - a * around[t] if full else None
        for k in range(1, modes):
            a = a_of(k, t)
            part = mode_part(mixed, modes, k, place + t)
            edge = edge + a * part
            if full:
                total = total + (b_of(k, t) * part - a * mode_part(mixed, modes, k, beside + t))
        results.append((total, edge))
    return results


def own_kernel(scales, mix_ref, a_ref, b_ref, start_ref, total_ref, edge_ref):
    layers, tiles, slots, _ = start_ref.shape
    modes = a_ref.shape[0]
    masks = lane_masks(slots)
    mix = mix_ref[...]
    nothing = jnp.zeros((slots, LANES), jnp.float32)

    def read(l, t):
        return start_ref[l, t] * scales[0] if t < tiles else nothing

    for l in range(layers):
        direct = [read(l, t) for t in range(tiles)]
        around = neighbour_sums(read, l, layers, tiles + 1, masks)
        mixed = jnp.dot(
            mix, split_stack(direct + around, mix.shape[1]), preferred_element_type=jnp.float32
        )
        results = weighted_tiles(
            mixed,
            modes,
            0,
            tiles,
            direct,
            around,
            lambda k, t: a_ref[k, l : l + 1, lanes(t)],
            lambda k, t: b_ref[k, l : l + 1, lanes(t)],
        )
        for t, (total, edge) in enumerate(results):
            total_ref[l, t] = total
            edge_ref[l, t] = edge


def iterate_kernel(
    chaos,
    spaces,
    scales,
    inside,
    odd,
    mix_ref,
    a_ref,
    b_ref,
    face_ref,
    unweight_ref,
    start_ref,
    own_total_ref,
    own_edge_ref,
    chip_ref,
    core_ref,
    sent_ref,
    r_ref,
    d_ref,
    total_ref,
    edge_ref,
    x_ref,
):
    layers, _, slots, _ = start_ref.shape
    modes = a_ref.shape[0]
    own = slots // chaos
    thick = layers // spaces
    pieces = OWN_TILES * thick
    half = layers // 2
    masks = lane_masks(slots)
    low_half = masks[0]
    mix = mix_ref[...]
    depth = mix.shape[1]
    upward = odd[0] > 0

    def message(start, size):
        chip, core = chip_ref[pl.ds(start, size), :], core_ref[pl.ds(start, size), :]
        return jnp.where(upward, core, chip), jnp.where(upward, chip, core)

    def send(field, l, t, value):
        i, z = divmod(l, thick)
        value = value * unweight_ref[...]
        for c, slot, number, row in slot_parts(own, chaos):
            first = (((c * spaces + i) * 2 + field) * own + slot) * pieces + t * thick + z
            sent_ref[pl.ds(first, number, stride=pieces), :] = value[row : row + number]

    for l in range(layers):
        below, above = message(l * slots, slots)
        far_below, far_above = message((layers + l % half) * slots, slots)
        if l < half:
            far = jnp.where(low_half, far_above, far_below)
        else:
            far = pltpu.roll(jnp.where(low_half, far_below, far_above), NY, 1)
        tiles = [
            start_ref[l, 0],
            start_ref[l, 1],
            jnp.where(low_half, above, below),
            jnp.where(low_half, below, above),
            far,
        ]
        for t, tile in enumerate(tiles):
            if t < FOLDED - 1:
                r_ref[l, t] = tile
            d_ref[l, t] = tile * scales[0]

    def read(l, t):
        return d_ref[l, t]

    zero = jnp.zeros((slots, LANES), jnp.float32)
    for step in range(ITERS):
        count = FOLDED - step
        full = count - 1
        first = OWN_TILES if step == 0 else 0
        group = 1 if step == 0 else 2
        for lowest in range(0, layers, group):
            gathered, stacked = [], []
            for l in range(lowest, lowest + group):
                direct = [d_ref[l, t] for t in range(first, count)]
                around = neighbour_sums(read, l, layers, count, masks, first)
                extra = []
                if step == 0:
                    extra = [jnp.where(low_half, d_ref[l, 0], d_ref[l, 1])]
                gathered.append((l, len(stacked), direct, extra, around))
                stacked += direct + extra + around
            mixed = jnp.dot(
                mix, split_stack(stacked, depth), preferred_element_type=jnp.float32
            )
            for l, place, direct, extra, around in gathered:
                results = weighted_tiles(
                    mixed,
                    modes,
                    place,
                    place + len(direct) + len(extra),
                    direct,
                    around,
                    lambda k, t: a_ref[k, l : l + 1, lanes(first + t)],
                    lambda k, t: b_ref[k, l : l + 1, lanes(first + t)],
                )
                for t, (total, edge) in enumerate(results):
                    edge_ref[l, first + t] = edge
                    if first + t < full:
                        total_ref[l, first + t] = total
                if not extra:
                    continue
                own_face = face_ref[0, l : l + 1, lanes(0)]
                other_face = face_ref[0, l : l + 1, lanes(1)]
                part = other_face * extra[0] - own_face * pltpu.roll(direct[0], NY, 1)
                for k in range(1, modes):
                    own_face = face_ref[k, l : l + 1, lanes(0)]
                    other_face = face_ref[k, l : l + 1, lanes(1)]
                    own_mixed = mode_part(mixed, modes, k, place + len(direct))
                    other_mixed = pltpu.roll(mode_part(mixed, modes, k, place), NY, 1)
                    part = part + (other_face * own_mixed - own_face * other_mixed)
                total_ref[l, 0] = own_total_ref[l, 0] + jnp.where(low_half, part, zero)
                total_ref[l, 1] = own_total_ref[l, 1] + jnp.where(low_half, zero, part)

        def read_edge(l, t):
            return own_edge_ref[l, t] if t < first else edge_ref[l, t]

        for l in range(layers):
            spread = neighbour_sums(read_edge, l, layers, count, masks)
            for t in range(full):
                diffused = total_ref[l, t] - spread[t]
                if t >= OWN_TILES:
                    lower, upper = inside[(t + 1) % 2], inside[t % 2]
                    diffused = diffused * jnp.where(low_half, lower, upper)
                residual = r_ref[l, t] - diffused
                if step == ITERS - 1:
                    send(1, l, t, residual)
                    continue
                r_ref[l, t] = residual
                old = d_ref[l, t]
                direction = scales[1 + 2 * step] * old + scales[2 + 2 * step] * residual
                d_ref[l, t] = direction
                if t < OWN_TILES:
                    value = (old if step == 0 else x_ref[l, t]) + direction
                    if step == ITERS - 2:
                        send(0, l, t, value)
                    else:
                        x_ref[l, t] = value


def call(kernel, outs, scalars, arrays, scratch=(), flops=0, in_kinds=None, out_kind=pltpu.VMEM):
    kinds = in_kinds or [pltpu.VMEM] * len(arrays)
    in_specs = [pl.BlockSpec(memory_space=pltpu.SMEM)] * len(scalars) + [
        pl.BlockSpec(memory_space=kind) for kind in kinds
    ]
    arrays = [
        pltpu.with_memory_space_constraint(x, kind) if kind == pltpu.HBM else x
        for x, kind in zip(arrays, kinds)
    ]
    moved = sum(4 * x.size for x in arrays) + sum(4 * x.size for x in outs)
    return pl.pallas_call(
        kernel,
        out_shape=outs,
        in_specs=in_specs,
        out_specs=[pl.BlockSpec(memory_space=out_kind)] * len(outs),
        scratch_shapes=scratch,
        compiler_params=pltpu.CompilerParams(vmem_limit_bytes=40 * 1024 * 1024),
        cost_estimate=pl.CostEstimate(flops=flops, bytes_accessed=moved, transcendentals=0),
    )(*scalars, *arrays)


def coupling_tables(coupling, slot_term, chaos):
    bf16 = jnp.bfloat16
    slots = slot_term.shape[0]
    by_source = slot_term.reshape(chaos, -1)
    slot_term = jnp.concatenate(
        [
            by_source[c, slot : slot + number]
            for c, slot, number, _ in slot_parts(slots // chaos, chaos)
        ]
    )
    raising = (slot_term[None, None, :] == coupling[:, :, 0:1]).astype(bf16)
    lowering = (slot_term[None, None, :] == coupling[:, :, 1:2]).astype(bf16)
    weighted = raising * coupling[:, :, 2:3].astype(bf16)
    matrices = jnp.einsum(
        "kps,kpr->ksr", weighted, lowering, preferred_element_type=jnp.float32
    ) + jnp.einsum("kps,kpr->ksr", lowering, raising, preferred_element_type=jnp.float32)
    spare = -slots % 16
    matrices = jnp.pad(matrices.astype(bf16), ((0, 0), (0, 0), (0, spare)))
    matrices = matrices.reshape(-1, slots // 8, 8, slots + spare).transpose(1, 0, 2, 3)
    matrices = matrices.reshape(-1, slots + spare)
    degree = jnp.sum(weighted.astype(jnp.float32), axis=1)
    factorial = jnp.where(degree > 2.5, 6.0, jnp.where(degree > 1.5, 2.0, 1.0))
    scale = jnp.sqrt(jnp.prod(factorial, axis=0))
    occupied = (slot_term >= 0).astype(jnp.float32)
    spread = jnp.ones((1, LANES), jnp.float32)
    return (
        jnp.concatenate([matrices, matrices], axis=1),
        (occupied * scale)[:, None] * spread,
        (occupied / scale)[:, None] * spread,
    )


def local_by_cells(source_chaos_terms, mean_conductivity, mode_shapes, coupling, slot_term, bounds):
    own, thick, cells = source_chaos_terms.shape
    chaos, spaces = lax.axis_size("chaos"), lax.axis_size("space")
    devices = chaos * spaces
    slots = own * chaos
    layers = thick * spaces
    columns = cells // LANES
    pieces = OWN_TILES * thick
    blocks = [block_of(device, spaces) for device in range(devices)]
    f32 = jnp.float32

    def shape(*sizes):
        return jax.ShapeDtypeStruct(sizes, f32)

    mix, weight, unweight = coupling_tables(coupling, slot_term, chaos)
    midpoint = 0.5 * (bounds[1] + bounds[0])
    half_span = 0.5 * (bounds[1] - bounds[0])
    sigma_one = midpoint / half_span
    rho_now = 1.0 / sigma_one
    scales = [1.0 / midpoint]
    for _ in range(ITERS - 1):
        rho_next = 1.0 / (2.0 * sigma_one - rho_now)
        scales += [rho_next * rho_now, 2.0 * rho_next / half_span]
        rho_now = rho_next
    scales = jnp.stack(scales)

    def by_columns(field):
        tiled = field.reshape(*field.shape[:-2], thick, columns, LANES)
        return jnp.swapaxes(tiled, -3, -2)

    scattered = call(
        functools.partial(scatter_kernel, blocks),
        [shape(devices, own, pieces, LANES)],
        [],
        [by_columns(source_chaos_terms).reshape(own, devices, pieces, LANES)],
        [pltpu.VMEM((own, devices, pieces, LANES), f32), pltpu.SemaphoreType.DMA((2,))],
        in_kinds=[pltpu.HBM],
    )[0]
    gathered = lax.all_to_all(scattered, BOTH, 0, 0, tiled=True).reshape(-1, LANES)

    row, column = lax.axis_index("chaos"), lax.axis_index("space")

    def block_at(space):
        return row * spaces + jnp.where(row % 2 == 0, space, spaces - 1 - space)

    block = block_at(column)
    inside = jnp.stack([block > 0, block < devices - 1]).astype(f32)
    odd = (block % 2)[None]
    modes = mode_shapes.shape[0] + 1
    steps = jnp.arange(spaces)
    picked = call(
        pick_kernel,
        [shape(modes * 3 * pieces, LANES)] * spaces,
        [block_at((column + steps) % spaces), scales],
        [
            mix,
            by_columns(mean_conductivity).reshape(-1, LANES),
            by_columns(mode_shapes).reshape(-1, LANES),
        ],
    )
    picked = [picked[0]] + [
        lax.ppermute(picked[n], "space", [(i, (i + n) % spaces) for i in range(spaces)])
        for n in range(1, spaces)
    ]
    a, b, own_b, face = call(
        functools.partial(coefficient_kernel, thick),
        [shape(modes, layers, tiles * LANES) for tiles in (FOLDED, FOLDED - 1, OWN_TILES, 2)],
        [(column - steps) % spaces],
        picked,
        [pltpu.VMEM((modes, 3 * OWN_TILES, layers, LANES), f32)],
    )

    message = shape((layers + layers // 2) * slots, LANES)
    start, to_chip, to_core = call(
        functools.partial(start_kernel, chaos, spaces),
        [shape(layers, OWN_TILES, slots, LANES), message, message],
        [odd],
        [a, weight, gathered],
    )
    place = {n: device for device, n in enumerate(blocks)}

    def swap(field, lowest):
        pairs = [(place[n], place[n + 1]) for n in range(lowest, devices - 1, 2)]
        return lax.ppermute(field, BOTH, pairs + [(b, a) for a, b in pairs])

    from_chip = swap(to_chip, 1)
    from_core = swap(to_core, 0)
    own_field = shape(layers, OWN_TILES, slots, LANES)
    own_total, own_edge = call(
        own_kernel,
        [own_field, own_field],
        [scales],
        [mix, a, own_b, start],
        flops=3000000000,
    )

    def held(tiles):
        return pltpu.VMEM((layers, tiles, slots, LANES), f32)

    sent = call(
        functools.partial(iterate_kernel, chaos, spaces),
        [shape(devices * 2 * own * pieces, LANES)],
        [scales, inside, odd],
        [mix, a, b, face, unweight, start, own_total, own_edge, from_chip, from_core],
        [
            held(FOLDED - 1),
            held(FOLDED),
            held(FOLDED - 1),
            held(FOLDED),
            held(OWN_TILES),
        ],
        flops=10000000000,
    )[0]
    sent = sent.reshape(devices, 2, own, pieces, LANES)
    received = lax.all_to_all(sent, BOTH, 0, 0, tiled=True)
    outs = call(
        functools.partial(collect_kernel, blocks),
        [shape(own, devices, pieces, LANES)] * 2,
        [],
        [received],
        [pltpu.SemaphoreType.DMA((2, devices))],
        in_kinds=[pl.ANY],
        out_kind=pltpu.HBM,
    )
    return tuple(
        jnp.transpose(out.reshape(own, columns, thick, LANES), (0, 2, 1, 3)).reshape(
            own, thick, cells
        )
        for out in outs
    )


def local(source_chaos_terms, mean_conductivity, mode_shapes, coupling, slot_term, bounds):
    own, thick, cells = source_chaos_terms.shape
    chaos, spaces = lax.axis_size("chaos"), lax.axis_size("space")
    fits = (
        thick * spaces == 8
        and cells == chaos * spaces * OWN_TILES * LANES
        and (own * chaos) % 8 == 0
        and spaces % 2 == 0
    )
    plan = local_by_cells if fits else local_by_slots
    return plan(
        source_chaos_terms, mean_conductivity, mode_shapes, coupling, slot_term, bounds
    )


def solution(mesh):
    in_specs = (
        P(("groups", "chaos"), "space", None),
        P("space", None),
        P(None, "space", None),
        P(),
        P(),
        P("groups"),
    )
    out_specs = (P(("groups", "chaos"), "space", None), P(("groups", "chaos"), "space", None))
    return jax.shard_map(local, mesh=mesh, in_specs=in_specs, out_specs=out_specs, check_vma=False)
```

```python
import functools

import jax
import jax.numpy as jnp
from jax import lax
from jax.experimental import pallas as pl
from jax.experimental.pallas import tpu as pltpu
from jax.sharding import PartitionSpec as P

NY = 64
ITERS = 3
LANES = 128
BOTH = ("chaos", "space")


full_precision = lax.Precision.HIGHEST


def with_halo(cells, sides, width):
    for axis, dim in sides:
        count = lax.axis_size(axis)
        ends = count - 1
        head = lax.slice_in_dim(cells, 0, width, axis=dim)
        tail = lax.slice_in_dim(cells, cells.shape[dim] - width, cells.shape[dim], axis=dim)
        cells = jnp.concatenate(
            [
                lax.ppermute(tail, axis, [(i, (i + 1) % count) for i in range(ends)]),
                cells,
                lax.ppermute(head, axis, [((i + 1) % count, i) for i in range(ends)]),
            ],
            axis=dim,
        )
    return cells


def mixing_matrices(coupling, slot_term):
    occupied = (slot_term >= 0).astype(jnp.float32)
    raising = (slot_term[None, None, :] == coupling[:, :, 0:1]).astype(jnp.float32)
    lowering = (slot_term[None, None, :] == coupling[:, :, 1:2]).astype(jnp.float32)
    weight = jnp.sqrt(coupling[:, :, 2].astype(jnp.float32))
    raised = jnp.einsum("kps,kp,kpr->ksr", raising, weight, lowering, precision=full_precision)
    mode_mats = raised + jnp.transpose(raised, (0, 2, 1))
    return jnp.concatenate([jnp.diag(occupied)[None], mode_mats], axis=0)


def shift_cells(values, offset, edge_mask):
    fill = jnp.zeros(values.shape[:-1] + (abs(offset),), values.dtype)
    if offset > 0:
        shifted = jnp.concatenate([values[..., offset:], fill], axis=-1)
    else:
        shifted = jnp.concatenate([fill, values[..., :offset]], axis=-1)
    return shifted * edge_mask


def diffuse(field_padded, conduct_padded):
    centre = field_padded[..., 1:-1, :]
    conduct = conduct_padded[..., 1:-1, :]
    accumulated = (
        0.5 * (conduct + conduct_padded[..., :-2, :]) * (centre - field_padded[..., :-2, :])
    )
    accumulated = accumulated + 0.5 * (conduct + conduct_padded[..., 2:, :]) * (
        centre - field_padded[..., 2:, :]
    )
    cells = centre.shape[-1]
    column_in_row = lax.iota(jnp.int32, cells) % NY
    upper_mask = (column_in_row < NY - 1).astype(centre.dtype)
    lower_mask = (column_in_row > 0).astype(centre.dtype)
    all_mask = jnp.ones((cells,), centre.dtype)
    for offset, edge_mask in ((1, upper_mask), (-1, lower_mask), (NY, all_mask), (-NY, all_mask)):
        neighbour = shift_cells(centre, offset, edge_mask)
        neighbour_conduct = shift_cells(conduct, offset, edge_mask)
        accumulated = accumulated + 0.5 * (conduct + neighbour_conduct) * (centre - neighbour)
    return accumulated


def local_by_slots(source_chaos_terms, mean_conductivity, mode_shapes, coupling, slot_term, bounds):
    slot_count = source_chaos_terms.shape[0]
    conductivity = jnp.concatenate(
        [mean_conductivity[None], mean_conductivity[None] * mode_shapes], axis=0
    )
    conduct_padded = with_halo(conductivity, (("space", 1),), 1)
    matrices = mixing_matrices(coupling, slot_term)
    first_own = lax.axis_index("chaos") * slot_count
    own_rows = lax.dynamic_slice_in_dim(matrices, first_own, slot_count, 1)
    own_terms = lax.dynamic_slice_in_dim(slot_term, first_own, slot_count, 0)
    occupied = (own_terms >= 0).astype(jnp.float32)[:, None, None]
    lower_bound = bounds[0]
    upper_bound = bounds[1]
    midpoint = 0.5 * (upper_bound + lower_bound)
    half_span = 0.5 * (upper_bound - lower_bound)
    sigma_one = midpoint / half_span
    rho_now = 1.0 / sigma_one
    residual = source_chaos_terms * occupied
    solution_field = jnp.zeros_like(residual)
    direction = residual / midpoint
    for iteration in range(ITERS):
        solution_field = solution_field + direction
        fields = jnp.einsum(
            "ksr,rzc->kszc",
            own_rows,
            lax.all_gather(direction, "chaos", axis=0, tiled=True),
            precision=full_precision,
        )
        field_padded = with_halo(fields, (("space", 2),), 1)
        diffused = diffuse(field_padded, conduct_padded[:, None])
        residual = residual - jnp.sum(diffused, axis=0)
        if iteration + 1 < ITERS:
            rho_next = 1.0 / (2.0 * sigma_one - rho_now)
            direction = rho_next * rho_now * direction + 2.0 * rho_next / half_span * residual
            rho_now = rho_next
    return (solution_field, residual)


OWN_TILES = 2
FOLDED = OWN_TILES + ITERS


def block_of(device, spaces):
    chaos, space = divmod(device, spaces)
    return chaos * spaces + (space if chaos % 2 == 0 else spaces - 1 - space)


def lane_masks(rows):
    lane = lax.broadcasted_iota(jnp.int32, (rows, LANES), 1)
    return lane < NY, lane % NY > 0, lane % NY < NY - 1


def plane_sums(tiles, masks, first=0):
    low_half, has_left, has_right = masks
    zero = jnp.zeros(tiles[0].shape, jnp.float32)
    swapped = [pltpu.roll(tile, NY, 1) for tile in tiles]
    sums = []
    for t in range(first, len(tiles) - 1):
        if t == 0:
            across = swapped[0] + jnp.where(low_half, swapped[2], swapped[1])
        elif t == 1:
            across = swapped[1] + jnp.where(low_half, swapped[0], swapped[2])
        elif t == 2:
            across = swapped[3] + jnp.where(low_half, swapped[1], swapped[0])
        else:
            across = swapped[t - 1] + swapped[t + 1]
        left = jnp.where(has_left, pltpu.roll(tiles[t], 1, 1), zero)
        right = jnp.where(has_right, pltpu.roll(tiles[t], LANES - 1, 1), zero)
        sums.append(across + (left + right))
    return sums


def neighbour_sums(read, layer, layers, count, masks, first=0):
    sums = plane_sums([read(layer, t) for t in range(count)], masks, first)
    for other in (layer - 1, layer + 1):
        if 0 <= other < layers:
            sums = [total + read(other, first + n) for n, total in enumerate(sums)]
    return sums


def split_stack(tiles, depth):
    wide = jnp.concatenate(tiles, axis=1)
    spare = depth // 2 - wide.shape[0]
    if spare:
        wide = jnp.concatenate([wide, jnp.zeros((spare, wide.shape[1]), wide.dtype)], axis=0)
    high = wide.astype(jnp.bfloat16)
    low = (wide - high.astype(jnp.float32)).astype(jnp.bfloat16)
    return jnp.concatenate([high, low], axis=0)


def lanes(t):
    return pl.ds(t * LANES, LANES)


def run_copies(copies):
    for copy in copies:
        copy.start()
    for copy in copies:
        copy.wait()


def scatter_kernel(targets, in_ref, terms_ref, *refs):
    *outs, terms_out_ref, held_ref, sems = refs
    own = in_ref.shape[0]
    parts = sems.shape[0] - 1
    terms_copy = pltpu.make_async_copy(terms_ref, terms_out_ref, sems.at[parts])
    terms_copy.start()
    bounds = [own * n // parts for n in range(parts + 1)]
    spans = [pl.ds(a, b - a) for a, b in zip(bounds[:-1], bounds[1:])]
    copies = [
        pltpu.make_async_copy(in_ref.at[span], held_ref.at[span], sems.at[n])
        for n, span in enumerate(spans)
    ]
    for copy in copies:
        copy.start()
    for copy, span in zip(copies, spans):
        copy.wait()
        for n, out_ref in enumerate(outs):
            out_ref[span] = held_ref[span, targets[n]]
    terms_copy.wait()


def pick_kernel(targets, scales, mix_ref, mean_ref, modes_ref, *outs):
    count, per_mode = mean_ref.shape[0], outs[0].shape[0] // (1 + modes_ref.shape[0] // mean_ref.shape[0])
    side = per_mode // 3
    last = count // side - 1
    for n, out_ref in enumerate(outs):
        block = targets[n]
        lower = jnp.where(block > 0, 1.0, 0.0)
        upper = jnp.where(block < last, 1.0, 0.0)
        before = jnp.maximum(block - 1, 0) * side
        after = jnp.minimum(block + 1, last) * side
        for k in range(out_ref.shape[0] // per_mode):
            ref, base = (mean_ref, 0) if k == 0 else (modes_ref, (k - 1) * count)
            first = k * per_mode
            out_ref[pl.ds(first, side), :] = ref[pl.ds(base + before, side), :] * lower
            out_ref[pl.ds(first + side, side), :] = ref[pl.ds(base + block * side, side), :]
            out_ref[pl.ds(first + 2 * side, side), :] = ref[pl.ds(base + after, side), :] * upper


def layer_sum(values, layer):
    layers = values.shape[0]
    zero = jnp.zeros(values.shape, jnp.float32)
    under = jnp.where(layer > 0, pltpu.roll(values, 1, 0), zero)
    over = jnp.where(layer < layers - 1, pltpu.roll(values, layers - 1, 0), zero)
    return under + over


def coefficient_kernel(thick, sources, *refs):
    *ins, a_ref, b_ref, own_b_ref, face_ref, held_ref = refs
    modes, layers, _ = a_ref.shape
    tiles = held_ref.shape[1]
    layer = lax.broadcasted_iota(jnp.int32, (layers, LANES), 0)
    masks = lane_masks(layers)
    low_half = masks[0]
    for n, in_ref in enumerate(ins):
        for k in range(modes):
            for u in range(tiles):
                held_ref[k, u, pl.ds(sources[n] * thick, thick), :] = in_ref[
                    pl.ds((k * tiles + u) * thick, thick), :
                ]
    mean = None
    for k in range(modes):
        runs = [held_ref[k, u] for u in range(tiles)]
        values = [
            runs[2],
            runs[3],
            jnp.where(low_half, runs[4], runs[1]),
            jnp.where(low_half, runs[1], runs[4]),
            jnp.where(low_half, runs[5], runs[0]),
        ]
        if k == 0:
            values = mean = [0.5 * value for value in values]
        else:
            values = [m * value for m, value in zip(mean, values)]
        sums = plane_sums(values, masks)
        for t in range(FOLDED):
            a_ref[k, :, lanes(t)] = values[t]
        for t in range(FOLDED - 1):
            b_ref[k, :, lanes(t)] = 6.0 * values[t] + (sums[t] + layer_sum(values[t], layer))
        outside = jnp.zeros((layers, LANES), jnp.float32)
        sums = plane_sums(values[:OWN_TILES] + [outside], masks)
        for t in range(OWN_TILES):
            own_b_ref[k, :, lanes(t)] = 6.0 * values[t] + (sums[t] + layer_sum(values[t], layer))
        face_ref[k, :, lanes(0)] = jnp.where(low_half, values[0], values[1])
        face_ref[k, :, lanes(1)] = pltpu.roll(values[2], NY, 1)


def collect_kernel(targets, *refs):
    *arrays, first_ref, second_ref, sems = refs
    half = len(arrays) // 2
    copies = [
        pltpu.make_async_copy(in_ref, out_ref.at[:, targets[n]], sems.at[f, n])
        for f, out_ref in enumerate((first_ref, second_ref))
        for n, in_ref in enumerate(arrays[f * half : (f + 1) * half])
    ]
    for copy in copies:
        copy.start()
    for copy in copies:
        copy.wait()


def slot_parts(own, chaos):
    whole = own // 8 * 8
    parts = [(c, 0, whole, c * whole) for c in range(chaos)]
    return parts + [
        (c, whole, own - whole, chaos * whole + c * (own - whole)) for c in range(chaos)
    ]


def partner_pieces(chaos_of, space_of, shape):
    layers, tiles, slots, _ = shape
    chaos, spaces = chaos_of.shape[0], space_of.shape[0]
    own = slots // chaos
    whole = own // 8 * 8
    rest = own - whole
    thick = layers // spaces
    pieces = tiles * thick
    for a in range(chaos):
        c = chaos_of[a]
        main = pl.ds(pl.multiple_of(c * whole, 8), whole)
        tail = pl.ds(chaos * whole + c * rest, rest)
        for b in range(spaces):
            first = space_of[b] * thick
            for t in range(tiles):
                for z in range(thick):
                    row = t * thick + z
                    there = pl.ds(row, whole, stride=pieces)
                    yield a * spaces + b, there, first + z, t, main
                    there = pl.ds(whole * pieces + row, rest, stride=pieces)
                    yield a * spaces + b, there, first + z, t, tail


def start_kernel(odd, chaos_of, space_of, a_ref, weight_ref, *refs):
    *ins, residual_ref, chip_ref, core_ref, raw_ref = refs
    upward = odd[0] > 0
    layers, tiles, slots, _ = residual_ref.shape
    half = layers // 2
    low_half = lane_masks(slots)[0]
    weight = weight_ref[...]

    def put(place, up, down):
        rows = pl.ds(place * slots, slots)
        chip_ref[rows, :] = jnp.where(upward, up, down)
        core_ref[rows, :] = jnp.where(upward, down, up)

    for n, there, l, t, here in partner_pieces(chaos_of, space_of, residual_ref.shape):
        raw_ref[l, t, here, :] = ins[n][there, :]
    for l in range(layers):
        for t in range(tiles):
            residual_ref[l, t] = weight * raw_ref[l, t]
        put(l, residual_ref[l, 1], residual_ref[l, 0])
    for l in range(half):
        later = l + half
        put(
            layers + l,
            jnp.where(low_half, pltpu.roll(residual_ref[later, 0], NY, 1), residual_ref[l, 0]),
            jnp.where(low_half, residual_ref[l, 1], pltpu.roll(residual_ref[later, 1], NY, 1)),
        )


def mode_part(mixed, modes, k, n):
    group = 8 * (modes - 1)
    return jnp.concatenate(
        [
            mixed[row : row + 8, n * LANES : (n + 1) * LANES]
            for row in range((k - 1) * 8, mixed.shape[0], group)
        ],
        axis=0,
    )


def weighted_tiles(mixed, modes, place, beside, direct, around, a_of, b_of):
    results = []
    for t, tile in enumerate(direct):
        full = t < len(around)
        a = a_of(0, t)
        edge = a * tile
        total = b_of(0, t) * tile - a * around[t] if full else None
        for k in range(1, modes):
            a = a_of(k, t)
            part = mode_part(mixed, modes, k, place + t)
            edge = edge + a * part
            if full:
                total = total + (b_of(k, t) * part - a * mode_part(mixed, modes, k, beside + t))
        results.append((total, edge))
    return results


def own_kernel(scales, mix_ref, a_ref, b_ref, start_ref, total_ref, edge_ref):
    layers, tiles, slots, _ = start_ref.shape
    modes = a_ref.shape[0]
    masks = lane_masks(slots)
    mix = mix_ref[...]
    nothing = jnp.zeros((slots, LANES), jnp.float32)

    def read(l, t):
        return start_ref[l, t] * scales[0] if t < tiles else nothing

    for l in range(layers):
        direct = [read(l, t) for t in range(tiles)]
        around = neighbour_sums(read, l, layers, tiles + 1, masks)
        mixed = jnp.dot(
            mix, split_stack(direct + around, mix.shape[1]), preferred_element_type=jnp.float32
        )
        results = weighted_tiles(
            mixed,
            modes,
            0,
            tiles,
            direct,
            around,
            lambda k, t: a_ref[k, l : l + 1, lanes(t)],
            lambda k, t: b_ref[k, l : l + 1, lanes(t)],
        )
        for t, (total, edge) in enumerate(results):
            total_ref[l, t] = total
            edge_ref[l, t] = edge


def run_step(
    step,
    scales,
    inside,
    mix_ref,
    a_ref,
    b_ref,
    r_ref,
    d_ref,
    total_ref,
    edge_ref,
    use,
    face_ref=None,
    own_total_ref=None,
    own_edge_ref=None,
):
    layers, _, slots, _ = r_ref.shape
    modes = a_ref.shape[0]
    masks = lane_masks(slots)
    low_half = masks[0]
    mix = mix_ref[...]
    depth = mix.shape[1]
    zero = jnp.zeros((slots, LANES), jnp.float32)
    count = FOLDED - step
    full = count - 1
    first = OWN_TILES if step == 0 else 0

    def read(l, t):
        return d_ref[l, t]

    group = 1
    for lowest in range(0, layers, group):
        gathered, stacked = [], []
        for l in range(lowest, lowest + group):
            direct = [d_ref[l, t] for t in range(first, count)]
            around = neighbour_sums(read, l, layers, count, masks, first)
            extra = []
            if step == 0:
                extra = [jnp.where(low_half, d_ref[l, 0], d_ref[l, 1])]
            gathered.append((l, len(stacked), direct, extra, around))
            stacked += direct + extra + around
        mixed = jnp.dot(
            mix, split_stack(stacked, depth), preferred_element_type=jnp.float32
        )
        for l, place, direct, extra, around in gathered:
            results = weighted_tiles(
                mixed,
                modes,
                place,
                place + len(direct) + len(extra),
                direct,
                around,
                lambda k, t: a_ref[k, l : l + 1, lanes(first + t)],
                lambda k, t: b_ref[k, l : l + 1, lanes(first + t)],
            )
            for t, (total, edge) in enumerate(results):
                edge_ref[l, first + t] = edge
                if first + t < full:
                    total_ref[l, first + t] = total
            if not extra:
                continue
            own_face = face_ref[0, l : l + 1, lanes(0)]
            other_face = face_ref[0, l : l + 1, lanes(1)]
            part = other_face * extra[0] - own_face * pltpu.roll(direct[0], NY, 1)
            for k in range(1, modes):
                own_face = face_ref[k, l : l + 1, lanes(0)]
                other_face = face_ref[k, l : l + 1, lanes(1)]
                own_mixed = mode_part(mixed, modes, k, place + len(direct))
                other_mixed = pltpu.roll(mode_part(mixed, modes, k, place), NY, 1)
                part = part + (other_face * own_mixed - own_face * other_mixed)
            total_ref[l, 0] = own_total_ref[l, 0] + jnp.where(low_half, part, zero)
            total_ref[l, 1] = own_total_ref[l, 1] + jnp.where(low_half, zero, part)

    def read_edge(l, t):
        return own_edge_ref[l, t] if t < first else edge_ref[l, t]

    for l in range(layers):
        spread = neighbour_sums(read_edge, l, layers, count, masks)
        for t in range(full):
            diffused = total_ref[l, t] - spread[t]
            if t >= OWN_TILES:
                lower, upper = inside[(t + 1) % 2], inside[t % 2]
                diffused = diffused * jnp.where(low_half, lower, upper)
            use(l, t, r_ref[l, t] - diffused)


def first_kernel(
    scales,
    inside,
    odd,
    chaos_of,
    space_of,
    mix_ref,
    a_ref,
    b_ref,
    face_ref,
    unweight_ref,
    start_ref,
    own_total_ref,
    own_edge_ref,
    chip_ref,
    core_ref,
    *refs,
):
    *outs, left_r_ref, left_d_ref, r_ref, d_ref, total_ref, edge_ref, x_ref = refs
    layers, _, slots, _ = start_ref.shape
    half = layers // 2
    low_half = lane_masks(slots)[0]
    upward = odd[0] > 0

    def message(start, size):
        chip, core = chip_ref[pl.ds(start, size), :], core_ref[pl.ds(start, size), :]
        return jnp.where(upward, core, chip), jnp.where(upward, chip, core)

    for l in range(layers):
        below, above = message(l * slots, slots)
        far_below, far_above = message((layers + l % half) * slots, slots)
        if l < half:
            far = jnp.where(low_half, far_above, far_below)
        else:
            far = pltpu.roll(jnp.where(low_half, far_below, far_above), NY, 1)
        tiles = [
            start_ref[l, 0],
            start_ref[l, 1],
            jnp.where(low_half, above, below),
            jnp.where(low_half, below, above),
            far,
        ]
        for t, tile in enumerate(tiles):
            if t < FOLDED - 1:
                r_ref[l, t] = tile
            d_ref[l, t] = tile * scales[0]

    for step in range(ITERS - 1):
        ready = step == ITERS - 2

        def use(l, t, residual):
            if not ready:
                r_ref[l, t] = residual
            elif t < OWN_TILES:
                left_r_ref[l, t] = residual
            old = d_ref[l, t]
            direction = scales[1 + 2 * step] * old + scales[2 + 2 * step] * residual
            (left_d_ref if ready else d_ref)[l, t] = direction
            if t < OWN_TILES:
                value = (old if step == 0 else x_ref[l, t]) + direction
                x_ref[l, t] = value * unweight_ref[...] if ready else value

        run_step(
            step,
            scales,
            inside,
            mix_ref,
            a_ref,
            b_ref,
            r_ref,
            d_ref,
            total_ref,
            edge_ref,
            use,
            face_ref,
            own_total_ref,
            own_edge_ref,
        )
    for n, there, l, t, here in partner_pieces(chaos_of, space_of, start_ref.shape):
        outs[n][there, :] = x_ref[l, t, here, :]


def last_kernel(
    scales, inside, chaos_of, space_of, mix_ref, a_ref, b_ref, unweight_ref, r_ref, d_ref, *refs
):
    *outs, total_ref, edge_ref, left_ref = refs

    def use(l, t, residual):
        left_ref[l, t] = residual * unweight_ref[...]

    run_step(
        ITERS - 1, scales, inside, mix_ref, a_ref, b_ref, r_ref, d_ref, total_ref, edge_ref, use
    )
    for n, there, l, t, here in partner_pieces(chaos_of, space_of, r_ref.shape):
        outs[n][there, :] = left_ref[l, t, here, :]


def call(kernel, outs, scalars, arrays, scratch=(), flops=0, in_kinds=None, out_kind=pltpu.VMEM):
    kinds = in_kinds or [pltpu.VMEM] * len(arrays)
    out_kinds = out_kind if isinstance(out_kind, list) else [out_kind] * len(outs)
    in_specs = [pl.BlockSpec(memory_space=pltpu.SMEM)] * len(scalars) + [
        pl.BlockSpec(memory_space=kind) for kind in kinds
    ]
    arrays = [
        pltpu.with_memory_space_constraint(x, kind) if kind == pltpu.HBM else x
        for x, kind in zip(arrays, kinds)
    ]
    moved = sum(4 * x.size for x in arrays) + sum(4 * x.size for x in outs)
    return pl.pallas_call(
        kernel,
        out_shape=outs,
        in_specs=in_specs,
        out_specs=[pl.BlockSpec(memory_space=kind) for kind in out_kinds],
        scratch_shapes=scratch,
        compiler_params=pltpu.CompilerParams(vmem_limit_bytes=24 * 1024 * 1024),
        cost_estimate=pl.CostEstimate(flops=flops, bytes_accessed=moved, transcendentals=0),
    )(*scalars, *arrays)


def coupling_tables(coupling, slot_term, chaos):
    bf16 = jnp.bfloat16
    slots = slot_term.shape[0]
    by_source = slot_term.reshape(chaos, -1)
    slot_term = jnp.concatenate(
        [
            by_source[c, slot : slot + number]
            for c, slot, number, _ in slot_parts(slots // chaos, chaos)
        ]
    )
    raising = (slot_term[None, None, :] == coupling[:, :, 0:1]).astype(bf16)
    lowering = (slot_term[None, None, :] == coupling[:, :, 1:2]).astype(bf16)
    weighted = raising * coupling[:, :, 2:3].astype(bf16)
    matrices = jnp.einsum(
        "kps,kpr->ksr", weighted, lowering, preferred_element_type=jnp.float32
    ) + jnp.einsum("kps,kpr->ksr", lowering, raising, preferred_element_type=jnp.float32)
    spare = -slots % 16
    matrices = jnp.pad(matrices.astype(bf16), ((0, 0), (0, 0), (0, spare)))
    matrices = matrices.reshape(-1, slots // 8, 8, slots + spare).transpose(1, 0, 2, 3)
    matrices = matrices.reshape(-1, slots + spare)
    degree = jnp.sum(weighted.astype(jnp.float32), axis=1)
    factorial = jnp.where(degree > 2.5, 6.0, jnp.where(degree > 1.5, 2.0, 1.0))
    scale = jnp.sqrt(jnp.prod(factorial, axis=0))
    occupied = (slot_term >= 0).astype(jnp.float32)
    spread = jnp.ones((1, LANES), jnp.float32)
    return (
        jnp.concatenate([matrices, matrices], axis=1),
        (occupied * scale)[:, None] * spread,
        (occupied / scale)[:, None] * spread,
    )


def local_by_cells(source_chaos_terms, mean_conductivity, mode_shapes, coupling, slot_term, bounds):
    own, thick, cells = source_chaos_terms.shape
    chaos, spaces = lax.axis_size("chaos"), lax.axis_size("space")
    devices = chaos * spaces
    slots = own * chaos
    layers = thick * spaces
    columns = cells // LANES
    pieces = OWN_TILES * thick
    blocks = [block_of(device, spaces) for device in range(devices)]
    f32 = jnp.float32

    def shape(*sizes):
        return jax.ShapeDtypeStruct(sizes, f32)

    midpoint = 0.5 * (bounds[1] + bounds[0])
    half_span = 0.5 * (bounds[1] - bounds[0])
    sigma_one = midpoint / half_span
    rho_now = 1.0 / sigma_one
    scales = [1.0 / midpoint]
    for _ in range(ITERS - 1):
        rho_next = 1.0 / (2.0 * sigma_one - rho_now)
        scales += [rho_next * rho_now, 2.0 * rho_next / half_span]
        rho_now = rho_next
    scales = jnp.stack(scales)

    def by_columns(field):
        tiled = field.reshape(*field.shape[:-2], thick, columns, LANES)
        return jnp.swapaxes(tiled, -3, -2)

    row, column = lax.axis_index("chaos"), lax.axis_index("space")

    def block_at(chaos_index, space):
        return chaos_index * spaces + jnp.where(chaos_index % 2 == 0, space, spaces - 1 - space)

    chaos_of = jnp.bitwise_xor(row, jnp.arange(chaos, dtype=jnp.int32))
    space_of = jnp.bitwise_xor(column, jnp.arange(spaces, dtype=jnp.int32))
    targets = block_at(chaos_of[:, None], space_of[None, :]).reshape(-1)

    far = [(a, b) for b in range(spaces) for a in range(chaos // 2, chaos)]
    near = [(a, b) for b in range(spaces) for a in range(chaos // 2) if a + b > 0]
    order = []
    while far or near:
        order += far[:2] + near[:2 if len(near) > len(far) else 1]
        far, near = far[2:], near[2 if len(near) > len(far) else 1 :]

    def swap_all(fields):
        received = list(fields)
        for a, b in order:
            pairs = [
                (c * spaces + i, (c ^ a) * spaces + (i ^ b))
                for c in range(chaos)
                for i in range(spaces)
            ]
            received[a * spaces + b] = lax.ppermute(fields[a * spaces + b], BOTH, pairs)
        return received

    piece = shape(own, pieces, LANES)
    *scattered, slot_term = call(
        scatter_kernel,
        [piece] * devices + [jax.ShapeDtypeStruct(slot_term.shape, slot_term.dtype)],
        [targets],
        [by_columns(source_chaos_terms).reshape(own, devices, pieces, LANES), slot_term],
        [pltpu.VMEM((own, devices, pieces, LANES), f32), pltpu.SemaphoreType.DMA((3,))],
        in_kinds=[pltpu.HBM] * 2,
        out_kind=[pltpu.VMEM] * devices + [pltpu.HBM],
    )
    gathered = [field.reshape(-1, LANES) for field in swap_all(scattered)]
    mix, weight, unweight = coupling_tables(coupling, slot_term, chaos)

    block = block_at(row, column)
    inside = jnp.stack([block > 0, block < devices - 1]).astype(f32)
    odd = (block % 2)[None]
    modes = mode_shapes.shape[0] + 1
    steps = jnp.arange(spaces)
    picked = call(
        pick_kernel,
        [shape(modes * 3 * pieces, LANES)] * spaces,
        [block_at(row, (column + steps) % spaces), scales],
        [
            mix,
            by_columns(mean_conductivity).reshape(-1, LANES),
            by_columns(mode_shapes).reshape(-1, LANES),
        ],
    )
    picked = [picked[0]] + [
        lax.ppermute(picked[n], "space", [(i, (i + n) % spaces) for i in range(spaces)])
        for n in range(1, spaces)
    ]
    a, b, own_b, face = call(
        functools.partial(coefficient_kernel, thick),
        [shape(modes, layers, tiles * LANES) for tiles in (FOLDED, FOLDED - 1, OWN_TILES, 2)],
        [(column - steps) % spaces],
        picked,
        [pltpu.VMEM((modes, 3 * OWN_TILES, layers, LANES), f32)],
    )

    message = shape((layers + layers // 2) * slots, LANES)
    start, to_chip, to_core = call(
        start_kernel,
        [shape(layers, OWN_TILES, slots, LANES), message, message],
        [odd, chaos_of, space_of],
        [a, weight, *gathered],
        [pltpu.VMEM((layers, OWN_TILES, slots, LANES), f32)],
    )
    place = {n: device for device, n in enumerate(blocks)}

    def swap(field, lowest):
        pairs = [(place[n], place[n + 1]) for n in range(lowest, devices - 1, 2)]
        return lax.ppermute(field, BOTH, pairs + [(b, a) for a, b in pairs])

    from_chip = swap(to_chip, 1)
    from_core = swap(to_core, 0)
    own_field = shape(layers, OWN_TILES, slots, LANES)
    own_total, own_edge = call(
        own_kernel,
        [own_field, own_field],
        [scales],
        [mix, a, own_b, start],
        flops=3000000000,
    )

    def held(tiles):
        return pltpu.VMEM((layers, tiles, slots, LANES), f32)

    flat = shape(own * pieces, LANES)
    *sent, residual, direction = call(
        first_kernel,
        [flat] * devices
        + [shape(layers, OWN_TILES, slots, LANES), shape(layers, OWN_TILES + 1, slots, LANES)],
        [scales, inside, odd, chaos_of, space_of],
        [mix, a, b, face, unweight, start, own_total, own_edge, from_chip, from_core],
        [held(FOLDED - 1), held(FOLDED), held(FOLDED - 1), held(FOLDED), held(OWN_TILES)],
        flops=8000000000,
    )
    received = swap_all([field.reshape(own, pieces, LANES) for field in sent])
    sent = call(
        last_kernel,
        [flat] * devices,
        [scales, inside, chaos_of, space_of],
        [mix, a, b, unweight, residual, direction],
        [held(OWN_TILES), held(OWN_TILES + 1), held(OWN_TILES)],
        flops=3000000000,
    )
    received += swap_all([field.reshape(own, pieces, LANES) for field in sent])
    outs = call(
        collect_kernel,
        [shape(own, devices, pieces, LANES)] * 2,
        [targets],
        received,
        [pltpu.SemaphoreType.DMA((2, devices))],
        in_kinds=[pl.ANY] * len(received),
        out_kind=pltpu.HBM,
    )
    return tuple(
        jnp.transpose(out.reshape(own, columns, thick, LANES), (0, 2, 1, 3)).reshape(
            own, thick, cells
        )
        for out in outs
    )


def local(source_chaos_terms, mean_conductivity, mode_shapes, coupling, slot_term, bounds):
    own, thick, cells = source_chaos_terms.shape
    chaos, spaces = lax.axis_size("chaos"), lax.axis_size("space")
    fits = (
        thick * spaces == 8
        and cells == chaos * spaces * OWN_TILES * LANES
        and (own * chaos) % 8 == 0
        and chaos & (chaos - 1) == 0
        and spaces & (spaces - 1) == 0
    )
    plan = local_by_cells if fits else local_by_slots
    return plan(
        source_chaos_terms, mean_conductivity, mode_shapes, coupling, slot_term, bounds
    )


def solution(mesh):
    in_specs = (
        P(("groups", "chaos"), "space", None),
        P("space", None),
        P(None, "space", None),
        P(),
        P(),
        P("groups"),
    )
    out_specs = (P(("groups", "chaos"), "space", None), P(("groups", "chaos"), "space", None))
    return jax.shard_map(local, mesh=mesh, in_specs=in_specs, out_specs=out_specs, check_vma=False)
```

```python
import functools

import jax
import jax.numpy as jnp
from jax import lax
from jax.experimental import pallas as pl
from jax.experimental.pallas import tpu as pltpu
from jax.sharding import PartitionSpec as P

NY = 64
ITERS = 3
LANES = 128
BOTH = ("chaos", "space")


full_precision = lax.Precision.HIGHEST


def with_halo(cells, sides, width):
    for axis, dim in sides:
        count = lax.axis_size(axis)
        ends = count - 1
        head = lax.slice_in_dim(cells, 0, width, axis=dim)
        tail = lax.slice_in_dim(cells, cells.shape[dim] - width, cells.shape[dim], axis=dim)
        cells = jnp.concatenate(
            [
                lax.ppermute(tail, axis, [(i, (i + 1) % count) for i in range(ends)]),
                cells,
                lax.ppermute(head, axis, [((i + 1) % count, i) for i in range(ends)]),
            ],
            axis=dim,
        )
    return cells


def mixing_matrices(coupling, slot_term):
    occupied = (slot_term >= 0).astype(jnp.float32)
    raising = (slot_term[None, None, :] == coupling[:, :, 0:1]).astype(jnp.float32)
    lowering = (slot_term[None, None, :] == coupling[:, :, 1:2]).astype(jnp.float32)
    weight = jnp.sqrt(coupling[:, :, 2].astype(jnp.float32))
    raised = jnp.einsum("kps,kp,kpr->ksr", raising, weight, lowering, precision=full_precision)
    mode_mats = raised + jnp.transpose(raised, (0, 2, 1))
    return jnp.concatenate([jnp.diag(occupied)[None], mode_mats], axis=0)


def shift_cells(values, offset, edge_mask):
    fill = jnp.zeros(values.shape[:-1] + (abs(offset),), values.dtype)
    if offset > 0:
        shifted = jnp.concatenate([values[..., offset:], fill], axis=-1)
    else:
        shifted = jnp.concatenate([fill, values[..., :offset]], axis=-1)
    return shifted * edge_mask


def diffuse(field_padded, conduct_padded):
    centre = field_padded[..., 1:-1, :]
    conduct = conduct_padded[..., 1:-1, :]
    accumulated = (
        0.5 * (conduct + conduct_padded[..., :-2, :]) * (centre - field_padded[..., :-2, :])
    )
    accumulated = accumulated + 0.5 * (conduct + conduct_padded[..., 2:, :]) * (
        centre - field_padded[..., 2:, :]
    )
    cells = centre.shape[-1]
    column_in_row = lax.iota(jnp.int32, cells) % NY
    upper_mask = (column_in_row < NY - 1).astype(centre.dtype)
    lower_mask = (column_in_row > 0).astype(centre.dtype)
    all_mask = jnp.ones((cells,), centre.dtype)
    for offset, edge_mask in ((1, upper_mask), (-1, lower_mask), (NY, all_mask), (-NY, all_mask)):
        neighbour = shift_cells(centre, offset, edge_mask)
        neighbour_conduct = shift_cells(conduct, offset, edge_mask)
        accumulated = accumulated + 0.5 * (conduct + neighbour_conduct) * (centre - neighbour)
    return accumulated


def local_by_slots(source_chaos_terms, mean_conductivity, mode_shapes, coupling, slot_term, bounds):
    slot_count = source_chaos_terms.shape[0]
    conductivity = jnp.concatenate(
        [mean_conductivity[None], mean_conductivity[None] * mode_shapes], axis=0
    )
    conduct_padded = with_halo(conductivity, (("space", 1),), 1)
    matrices = mixing_matrices(coupling, slot_term)
    first_own = lax.axis_index("chaos") * slot_count
    own_rows = lax.dynamic_slice_in_dim(matrices, first_own, slot_count, 1)
    own_terms = lax.dynamic_slice_in_dim(slot_term, first_own, slot_count, 0)
    occupied = (own_terms >= 0).astype(jnp.float32)[:, None, None]
    lower_bound = bounds[0]
    upper_bound = bounds[1]
    midpoint = 0.5 * (upper_bound + lower_bound)
    half_span = 0.5 * (upper_bound - lower_bound)
    sigma_one = midpoint / half_span
    rho_now = 1.0 / sigma_one
    residual = source_chaos_terms * occupied
    solution_field = jnp.zeros_like(residual)
    direction = residual / midpoint
    for iteration in range(ITERS):
        solution_field = solution_field + direction
        fields = jnp.einsum(
            "ksr,rzc->kszc",
            own_rows,
            lax.all_gather(direction, "chaos", axis=0, tiled=True),
            precision=full_precision,
        )
        field_padded = with_halo(fields, (("space", 2),), 1)
        diffused = diffuse(field_padded, conduct_padded[:, None])
        residual = residual - jnp.sum(diffused, axis=0)
        if iteration + 1 < ITERS:
            rho_next = 1.0 / (2.0 * sigma_one - rho_now)
            direction = rho_next * rho_now * direction + 2.0 * rho_next / half_span * residual
            rho_now = rho_next
    return (solution_field, residual)


OWN_TILES = 2
FOLDED = OWN_TILES + ITERS


def block_of(device, spaces):
    chaos, space = divmod(device, spaces)
    return chaos * spaces + (space if chaos % 2 == 0 else spaces - 1 - space)


def lane_masks(rows):
    lane = lax.broadcasted_iota(jnp.int32, (rows, LANES), 1)
    return lane < NY, lane % NY > 0, lane % NY < NY - 1


def plane_sums(tiles, masks, first=0):
    low_half, has_left, has_right = masks
    zero = jnp.zeros(tiles[0].shape, jnp.float32)
    swapped = [pltpu.roll(tile, NY, 1) for tile in tiles]
    sums = []
    for t in range(first, len(tiles) - 1):
        if t == 0:
            across = swapped[0] + jnp.where(low_half, swapped[2], swapped[1])
        elif t == 1:
            across = swapped[1] + jnp.where(low_half, swapped[0], swapped[2])
        elif t == 2:
            across = swapped[3] + jnp.where(low_half, swapped[1], swapped[0])
        else:
            across = swapped[t - 1] + swapped[t + 1]
        left = jnp.where(has_left, pltpu.roll(tiles[t], 1, 1), zero)
        right = jnp.where(has_right, pltpu.roll(tiles[t], LANES - 1, 1), zero)
        sums.append(across + (left + right))
    return sums


def neighbour_sums(read, layer, layers, count, masks, first=0):
    sums = plane_sums([read(layer, t) for t in range(count)], masks, first)
    for other in (layer - 1, layer + 1):
        if 0 <= other < layers:
            sums = [total + read(other, first + n) for n, total in enumerate(sums)]
    return sums


def split_stack(tiles, depth):
    wide = jnp.concatenate(tiles, axis=1)
    spare = depth // 2 - wide.shape[0]
    if spare:
        wide = jnp.concatenate([wide, jnp.zeros((spare, wide.shape[1]), wide.dtype)], axis=0)
    high = wide.astype(jnp.bfloat16)
    low = (wide - high.astype(jnp.float32)).astype(jnp.bfloat16)
    return jnp.concatenate([high, low], axis=0)


def lanes(t):
    return pl.ds(t * LANES, LANES)


def run_copies(copies):
    for copy in copies:
        copy.start()
    for copy in copies:
        copy.wait()


def scatter_kernel(blocks, in_ref, out_ref, held_ref, sems):
    own = in_ref.shape[0]
    parts = sems.shape[0]
    bounds = [own * n // parts for n in range(parts + 1)]
    spans = [pl.ds(a, b - a) for a, b in zip(bounds[:-1], bounds[1:])]
    copies = [
        pltpu.make_async_copy(in_ref.at[span], held_ref.at[span], sems.at[n])
        for n, span in enumerate(spans)
    ]
    for copy in copies:
        copy.start()
    for copy, span in zip(copies, spans):
        copy.wait()
        for device, block in enumerate(blocks):
            out_ref[device, span] = held_ref[span, block]


def pick_kernel(targets, scales, mix_ref, mean_ref, modes_ref, *outs):
    count, per_mode = mean_ref.shape[0], outs[0].shape[0] // (1 + modes_ref.shape[0] // mean_ref.shape[0])
    side = per_mode // 3
    last = count // side - 1
    for n, out_ref in enumerate(outs):
        block = targets[n]
        lower = jnp.where(block > 0, 1.0, 0.0)
        upper = jnp.where(block < last, 1.0, 0.0)
        before = jnp.maximum(block - 1, 0) * side
        after = jnp.minimum(block + 1, last) * side
        for k in range(out_ref.shape[0] // per_mode):
            ref, base = (mean_ref, 0) if k == 0 else (modes_ref, (k - 1) * count)
            first = k * per_mode
            out_ref[pl.ds(first, side), :] = ref[pl.ds(base + before, side), :] * lower
            out_ref[pl.ds(first + side, side), :] = ref[pl.ds(base + block * side, side), :]
            out_ref[pl.ds(first + 2 * side, side), :] = ref[pl.ds(base + after, side), :] * upper


def layer_sum(values, layer):
    layers = values.shape[0]
    zero = jnp.zeros(values.shape, jnp.float32)
    under = jnp.where(layer > 0, pltpu.roll(values, 1, 0), zero)
    over = jnp.where(layer < layers - 1, pltpu.roll(values, layers - 1, 0), zero)
    return under + over


def coefficient_kernel(thick, sources, *refs):
    *ins, a_ref, b_ref, own_b_ref, face_ref, held_ref = refs
    modes, layers, _ = a_ref.shape
    tiles = held_ref.shape[1]
    layer = lax.broadcasted_iota(jnp.int32, (layers, LANES), 0)
    masks = lane_masks(layers)
    low_half = masks[0]
    for n, in_ref in enumerate(ins):
        for k in range(modes):
            for u in range(tiles):
                held_ref[k, u, pl.ds(sources[n] * thick, thick), :] = in_ref[
                    pl.ds((k * tiles + u) * thick, thick), :
                ]
    mean = None
    for k in range(modes):
        runs = [held_ref[k, u] for u in range(tiles)]
        values = [
            runs[2],
            runs[3],
            jnp.where(low_half, runs[4], runs[1]),
            jnp.where(low_half, runs[1], runs[4]),
            jnp.where(low_half, runs[5], runs[0]),
        ]
        if k == 0:
            values = mean = [0.5 * value for value in values]
        else:
            values = [m * value for m, value in zip(mean, values)]
        sums = plane_sums(values, masks)
        for t in range(FOLDED):
            a_ref[k, :, lanes(t)] = values[t]
        for t in range(FOLDED - 1):
            b_ref[k, :, lanes(t)] = 6.0 * values[t] + (sums[t] + layer_sum(values[t], layer))
        outside = jnp.zeros((layers, LANES), jnp.float32)
        sums = plane_sums(values[:OWN_TILES] + [outside], masks)
        for t in range(OWN_TILES):
            own_b_ref[k, :, lanes(t)] = 6.0 * values[t] + (sums[t] + layer_sum(values[t], layer))
        face_ref[k, :, lanes(0)] = jnp.where(low_half, values[0], values[1])
        face_ref[k, :, lanes(1)] = pltpu.roll(values[2], NY, 1)


def collect_kernel(blocks, in_ref, *rest):
    *outs, sems = rest
    run_copies(
        [
            pltpu.make_async_copy(
                in_ref.at[device, n], out_ref.at[:, block], sems.at[n, device]
            )
            for n, out_ref in enumerate(outs)
            for device, block in enumerate(blocks)
        ]
    )


def slot_parts(own, chaos):
    whole = own // 8 * 8
    parts = [(c, 0, whole, c * whole) for c in range(chaos)]
    return parts + [
        (c, whole, own - whole, chaos * whole + c * (own - whole)) for c in range(chaos)
    ]


def start_kernel(chaos, spaces, odd, a_ref, weight_ref, in_ref, residual_ref, chip_ref, core_ref):
    upward = odd[0] > 0
    layers, tiles, slots, _ = residual_ref.shape
    own = slots // chaos
    thick = layers // spaces
    pieces = tiles * thick
    half = layers // 2
    low_half = lane_masks(slots)[0]
    weight = weight_ref[...]

    def put(place, up, down):
        rows = pl.ds(place * slots, slots)
        chip_ref[rows, :] = jnp.where(upward, up, down)
        core_ref[rows, :] = jnp.where(upward, down, up)

    for l in range(layers):
        i, z = divmod(l, thick)
        for t in range(tiles):
            rows = [
                in_ref[
                    pl.ds(
                        ((c * spaces + i) * own + slot) * pieces + t * thick + z,
                        number,
                        stride=pieces,
                    ),
                    :,
                ]
                for c, slot, number, _ in slot_parts(own, chaos)
            ]
            residual_ref[l, t] = weight * jnp.concatenate(rows, axis=0)
        put(l, residual_ref[l, 1], residual_ref[l, 0])
    for l in range(half):
        later = l + half
        put(
            layers + l,
            jnp.where(low_half, pltpu.roll(residual_ref[later, 0], NY, 1), residual_ref[l, 0]),
            jnp.where(low_half, residual_ref[l, 1], pltpu.roll(residual_ref[later, 1], NY, 1)),
        )


def mode_part(mixed, modes, k, n):
    group = 8 * (modes - 1)
    return jnp.concatenate(
        [
            mixed[row : row + 8, n * LANES : (n + 1) * LANES]
            for row in range((k - 1) * 8, mixed.shape[0], group)
        ],
        axis=0,
    )


def weighted_tiles(mixed, modes, place, beside, direct, around, a_of, b_of):
    results = []
    for t, tile in enumerate(direct):
        full = t < len(around)
        a = a_of(0, t)
        edge = a * tile
        total = b_of(0, t) * tile - a * around[t] if full else None
        for k in range(1, modes):
            a = a_of(k, t)
            part = mode_part(mixed, modes, k, place + t)
            edge = edge + a * part
            if full:
                total = total + (b_of(k, t) * part - a * mode_part(mixed, modes, k, beside + t))
        results.append((total, edge))
    return results


def own_kernel(scales, mix_ref, a_ref, b_ref, start_ref, total_ref, edge_ref):
    layers, tiles, slots, _ = start_ref.shape
    modes = a_ref.shape[0]
    masks = lane_masks(slots)
    mix = mix_ref[...]
    nothing = jnp.zeros((slots, LANES), jnp.float32)

    def read(l, t):
        return start_ref[l, t] * scales[0] if t < tiles else nothing

    for l in range(layers):
        direct = [read(l, t) for t in range(tiles)]
        around = neighbour_sums(read, l, layers, tiles + 1, masks)
        mixed = jnp.dot(
            mix, split_stack(direct + around, mix.shape[1]), preferred_element_type=jnp.float32
        )
        results = weighted_tiles(
            mixed,
            modes,
            0,
            tiles,
            direct,
            around,
            lambda k, t: a_ref[k, l : l + 1, lanes(t)],
            lambda k, t: b_ref[k, l : l + 1, lanes(t)],
        )
        for t, (total, edge) in enumerate(results):
            total_ref[l, t] = total
            edge_ref[l, t] = edge


def iterate_kernel(
    chaos,
    spaces,
    scales,
    inside,
    odd,
    mix_ref,
    a_ref,
    b_ref,
    face_ref,
    unweight_ref,
    start_ref,
    own_total_ref,
    own_edge_ref,
    chip_ref,
    core_ref,
    sent_ref,
    r_ref,
    d_ref,
    total_ref,
    edge_ref,
    x_ref,
):
    layers, _, slots, _ = start_ref.shape
    modes = a_ref.shape[0]
    own = slots // chaos
    thick = layers // spaces
    pieces = OWN_TILES * thick
    half = layers // 2
    masks = lane_masks(slots)
    low_half = masks[0]
    mix = mix_ref[...]
    depth = mix.shape[1]
    upward = odd[0] > 0

    def message(start, size):
        chip, core = chip_ref[pl.ds(start, size), :], core_ref[pl.ds(start, size), :]
        return jnp.where(upward, core, chip), jnp.where(upward, chip, core)

    def send(field, l, t, value):
        i, z = divmod(l, thick)
        value = value * unweight_ref[...]
        for c, slot, number, row in slot_parts(own, chaos):
            first = (((c * spaces + i) * 2 + field) * own + slot) * pieces + t * thick + z
            sent_ref[pl.ds(first, number, stride=pieces), :] = value[row : row + number]

    for l in range(layers):
        below, above = message(l * slots, slots)
        far_below, far_above = message((layers + l % half) * slots, slots)
        if l < half:
            far = jnp.where(low_half, far_above, far_below)
        else:
            far = pltpu.roll(jnp.where(low_half, far_below, far_above), NY, 1)
        tiles = [
            start_ref[l, 0],
            start_ref[l, 1],
            jnp.where(low_half, above, below),
            jnp.where(low_half, below, above),
            far,
        ]
        for t, tile in enumerate(tiles):
            if t < FOLDED - 1:
                r_ref[l, t] = tile
            d_ref[l, t] = tile * scales[0]

    def read(l, t):
        return d_ref[l, t]

    zero = jnp.zeros((slots, LANES), jnp.float32)
    for step in range(ITERS):
        count = FOLDED - step
        full = count - 1
        first = OWN_TILES if step == 0 else 0
        group = 1
        for lowest in range(0, layers, group):
            gathered, stacked = [], []
            for l in range(lowest, lowest + group):
                direct = [d_ref[l, t] for t in range(first, count)]
                around = neighbour_sums(read, l, layers, count, masks, first)
                extra = []
                if step == 0:
                    extra = [jnp.where(low_half, d_ref[l, 0], d_ref[l, 1])]
                gathered.append((l, len(stacked), direct, extra, around))
                stacked += direct + extra + around
            mixed = jnp.dot(
                mix, split_stack(stacked, depth), preferred_element_type=jnp.float32
            )
            for l, place, direct, extra, around in gathered:
                results = weighted_tiles(
                    mixed,
                    modes,
                    place,
                    place + len(direct) + len(extra),
                    direct,
                    around,
                    lambda k, t: a_ref[k, l : l + 1, lanes(first + t)],
                    lambda k, t: b_ref[k, l : l + 1, lanes(first + t)],
                )
                for t, (total, edge) in enumerate(results):
                    edge_ref[l, first + t] = edge
                    if first + t < full:
                        total_ref[l, first + t] = total
                if not extra:
                    continue
                own_face = face_ref[0, l : l + 1, lanes(0)]
                other_face = face_ref[0, l : l + 1, lanes(1)]
                part = other_face * extra[0] - own_face * pltpu.roll(direct[0], NY, 1)
                for k in range(1, modes):
                    own_face = face_ref[k, l : l + 1, lanes(0)]
                    other_face = face_ref[k, l : l + 1, lanes(1)]
                    own_mixed = mode_part(mixed, modes, k, place + len(direct))
                    other_mixed = pltpu.roll(mode_part(mixed, modes, k, place), NY, 1)
                    part = part + (other_face * own_mixed - own_face * other_mixed)
                total_ref[l, 0] = own_total_ref[l, 0] + jnp.where(low_half, part, zero)
                total_ref[l, 1] = own_total_ref[l, 1] + jnp.where(low_half, zero, part)

        def read_edge(l, t):
            return own_edge_ref[l, t] if t < first else edge_ref[l, t]

        for l in range(layers):
            spread = neighbour_sums(read_edge, l, layers, count, masks)
            for t in range(full):
                diffused = total_ref[l, t] - spread[t]
                if t >= OWN_TILES:
                    lower, upper = inside[(t + 1) % 2], inside[t % 2]
                    diffused = diffused * jnp.where(low_half, lower, upper)
                residual = r_ref[l, t] - diffused
                if step == ITERS - 1:
                    send(1, l, t, residual)
                    continue
                r_ref[l, t] = residual
                old = d_ref[l, t]
                direction = scales[1 + 2 * step] * old + scales[2 + 2 * step] * residual
                d_ref[l, t] = direction
                if t < OWN_TILES:
                    value = (old if step == 0 else x_ref[l, t]) + direction
                    if step == ITERS - 2:
                        send(0, l, t, value)
                    else:
                        x_ref[l, t] = value


def call(kernel, outs, scalars, arrays, scratch=(), flops=0, in_kinds=None, out_kind=pltpu.VMEM):
    kinds = in_kinds or [pltpu.VMEM] * len(arrays)
    in_specs = [pl.BlockSpec(memory_space=pltpu.SMEM)] * len(scalars) + [
        pl.BlockSpec(memory_space=kind) for kind in kinds
    ]
    arrays = [
        pltpu.with_memory_space_constraint(x, kind) if kind == pltpu.HBM else x
        for x, kind in zip(arrays, kinds)
    ]
    moved = sum(4 * x.size for x in arrays) + sum(4 * x.size for x in outs)
    return pl.pallas_call(
        kernel,
        out_shape=outs,
        in_specs=in_specs,
        out_specs=[pl.BlockSpec(memory_space=out_kind)] * len(outs),
        scratch_shapes=scratch,
        compiler_params=pltpu.CompilerParams(vmem_limit_bytes=40 * 1024 * 1024),
        cost_estimate=pl.CostEstimate(flops=flops, bytes_accessed=moved, transcendentals=0),
    )(*scalars, *arrays)


def coupling_tables(coupling, slot_term, chaos):
    bf16 = jnp.bfloat16
    slots = slot_term.shape[0]
    by_source = slot_term.reshape(chaos, -1)
    slot_term = jnp.concatenate(
        [
            by_source[c, slot : slot + number]
            for c, slot, number, _ in slot_parts(slots // chaos, chaos)
        ]
    )
    raising = (slot_term[None, None, :] == coupling[:, :, 0:1]).astype(bf16)
    lowering = (slot_term[None, None, :] == coupling[:, :, 1:2]).astype(bf16)
    weighted = raising * coupling[:, :, 2:3].astype(bf16)
    matrices = jnp.einsum(
        "kps,kpr->ksr", weighted, lowering, preferred_element_type=jnp.float32
    ) + jnp.einsum("kps,kpr->ksr", lowering, raising, preferred_element_type=jnp.float32)
    spare = -slots % 16
    matrices = jnp.pad(matrices.astype(bf16), ((0, 0), (0, 0), (0, spare)))
    matrices = matrices.reshape(-1, slots // 8, 8, slots + spare).transpose(1, 0, 2, 3)
    matrices = matrices.reshape(-1, slots + spare)
    degree = jnp.sum(weighted.astype(jnp.float32), axis=1)
    factorial = jnp.where(degree > 2.5, 6.0, jnp.where(degree > 1.5, 2.0, 1.0))
    scale = jnp.sqrt(jnp.prod(factorial, axis=0))
    occupied = (slot_term >= 0).astype(jnp.float32)
    spread = jnp.ones((1, LANES), jnp.float32)
    return (
        jnp.concatenate([matrices, matrices], axis=1),
        (occupied * scale)[:, None] * spread,
        (occupied / scale)[:, None] * spread,
    )


def local_by_cells(source_chaos_terms, mean_conductivity, mode_shapes, coupling, slot_term, bounds):
    own, thick, cells = source_chaos_terms.shape
    chaos, spaces = lax.axis_size("chaos"), lax.axis_size("space")
    devices = chaos * spaces
    slots = own * chaos
    layers = thick * spaces
    columns = cells // LANES
    pieces = OWN_TILES * thick
    blocks = [block_of(device, spaces) for device in range(devices)]
    f32 = jnp.float32

    def shape(*sizes):
        return jax.ShapeDtypeStruct(sizes, f32)

    mix, weight, unweight = coupling_tables(coupling, slot_term, chaos)
    midpoint = 0.5 * (bounds[1] + bounds[0])
    half_span = 0.5 * (bounds[1] - bounds[0])
    sigma_one = midpoint / half_span
    rho_now = 1.0 / sigma_one
    scales = [1.0 / midpoint]
    for _ in range(ITERS - 1):
        rho_next = 1.0 / (2.0 * sigma_one - rho_now)
        scales += [rho_next * rho_now, 2.0 * rho_next / half_span]
        rho_now = rho_next
    scales = jnp.stack(scales)

    def by_columns(field):
        tiled = field.reshape(*field.shape[:-2], thick, columns, LANES)
        return jnp.swapaxes(tiled, -3, -2)

    scattered = call(
        functools.partial(scatter_kernel, blocks),
        [shape(devices, own, pieces, LANES)],
        [],
        [by_columns(source_chaos_terms).reshape(own, devices, pieces, LANES)],
        [pltpu.VMEM((own, devices, pieces, LANES), f32), pltpu.SemaphoreType.DMA((4,))],
        in_kinds=[pltpu.HBM],
    )[0]
    gathered = lax.all_to_all(scattered, BOTH, 0, 0, tiled=True).reshape(-1, LANES)

    row, column = lax.axis_index("chaos"), lax.axis_index("space")

    def block_at(space):
        return row * spaces + jnp.where(row % 2 == 0, space, spaces - 1 - space)

    block = block_at(column)
    inside = jnp.stack([block > 0, block < devices - 1]).astype(f32)
    odd = (block % 2)[None]
    modes = mode_shapes.shape[0] + 1
    steps = jnp.arange(spaces)
    picked = call(
        pick_kernel,
        [shape(modes * 3 * pieces, LANES)] * spaces,
        [block_at((column + steps) % spaces), scales],
        [
            mix,
            by_columns(mean_conductivity).reshape(-1, LANES),
            by_columns(mode_shapes).reshape(-1, LANES),
        ],
    )
    picked = [picked[0]] + [
        lax.ppermute(picked[n], "space", [(i, (i + n) % spaces) for i in range(spaces)])
        for n in range(1, spaces)
    ]
    a, b, own_b, face = call(
        functools.partial(coefficient_kernel, thick),
        [shape(modes, layers, tiles * LANES) for tiles in (FOLDED, FOLDED - 1, OWN_TILES, 2)],
        [(column - steps) % spaces],
        picked,
        [pltpu.VMEM((modes, 3 * OWN_TILES, layers, LANES), f32)],
    )

    message = shape((layers + layers // 2) * slots, LANES)
    start, to_chip, to_core = call(
        functools.partial(start_kernel, chaos, spaces),
        [shape(layers, OWN_TILES, slots, LANES), message, message],
        [odd],
        [a, weight, gathered],
    )
    place = {n: device for device, n in enumerate(blocks)}

    def swap(field, lowest):
        pairs = [(place[n], place[n + 1]) for n in range(lowest, devices - 1, 2)]
        return lax.ppermute(field, BOTH, pairs + [(b, a) for a, b in pairs])

    from_chip = swap(to_chip, 1)
    from_core = swap(to_core, 0)
    own_field = shape(layers, OWN_TILES, slots, LANES)
    own_total, own_edge = call(
        own_kernel,
        [own_field, own_field],
        [scales],
        [mix, a, own_b, start],
        flops=3000000000,
    )

    def held(tiles):
        return pltpu.VMEM((layers, tiles, slots, LANES), f32)

    sent = call(
        functools.partial(iterate_kernel, chaos, spaces),
        [shape(devices * 2 * own * pieces, LANES)],
        [scales, inside, odd],
        [mix, a, b, face, unweight, start, own_total, own_edge, from_chip, from_core],
        [
            held(FOLDED - 1),
            held(FOLDED),
            held(FOLDED - 1),
            held(FOLDED),
            held(OWN_TILES),
        ],
        flops=10000000000,
    )[0]
    sent = sent.reshape(devices, 2, own, pieces, LANES)
    received = lax.all_to_all(sent, BOTH, 0, 0, tiled=True)
    outs = call(
        functools.partial(collect_kernel, blocks),
        [shape(own, devices, pieces, LANES)] * 2,
        [],
        [received],
        [pltpu.SemaphoreType.DMA((2, devices))],
        in_kinds=[pl.ANY],
        out_kind=pltpu.HBM,
    )
    return tuple(
        jnp.transpose(out.reshape(own, columns, thick, LANES), (0, 2, 1, 3)).reshape(
            own, thick, cells
        )
        for out in outs
    )


def local(source_chaos_terms, mean_conductivity, mode_shapes, coupling, slot_term, bounds):
    own, thick, cells = source_chaos_terms.shape
    chaos, spaces = lax.axis_size("chaos"), lax.axis_size("space")
    fits = (
        thick * spaces == 8
        and cells == chaos * spaces * OWN_TILES * LANES
        and (own * chaos) % 8 == 0
        and spaces % 2 == 0
    )
    plan = local_by_cells if fits else local_by_slots
    return plan(
        source_chaos_terms, mean_conductivity, mode_shapes, coupling, slot_term, bounds
    )


def solution(mesh):
    in_specs = (
        P(("groups", "chaos"), "space", None),
        P("space", None),
        P(None, "space", None),
        P(),
        P(),
        P("groups"),
    )
    out_specs = (P(("groups", "chaos"), "space", None), P(("groups", "chaos"), "space", None))
    return jax.shard_map(local, mesh=mesh, in_specs=in_specs, out_specs=out_specs, check_vma=False)
```

```python
import functools

import jax
import jax.numpy as jnp
from jax import lax
from jax.experimental import pallas as pl
from jax.experimental.pallas import tpu as pltpu
from jax.sharding import PartitionSpec as P

NY = 64
ITERS = 3
LANES = 128
BOTH = ("chaos", "space")


full_precision = lax.Precision.HIGHEST


def with_halo(cells, sides, width):
    for axis, dim in sides:
        count = lax.axis_size(axis)
        ends = count - 1
        head = lax.slice_in_dim(cells, 0, width, axis=dim)
        tail = lax.slice_in_dim(cells, cells.shape[dim] - width, cells.shape[dim], axis=dim)
        cells = jnp.concatenate(
            [
                lax.ppermute(tail, axis, [(i, (i + 1) % count) for i in range(ends)]),
                cells,
                lax.ppermute(head, axis, [((i + 1) % count, i) for i in range(ends)]),
            ],
            axis=dim,
        )
    return cells


def mixing_matrices(coupling, slot_term):
    occupied = (slot_term >= 0).astype(jnp.float32)
    raising = (slot_term[None, None, :] == coupling[:, :, 0:1]).astype(jnp.float32)
    lowering = (slot_term[None, None, :] == coupling[:, :, 1:2]).astype(jnp.float32)
    weight = jnp.sqrt(coupling[:, :, 2].astype(jnp.float32))
    raised = jnp.einsum("kps,kp,kpr->ksr", raising, weight, lowering, precision=full_precision)
    mode_mats = raised + jnp.transpose(raised, (0, 2, 1))
    return jnp.concatenate([jnp.diag(occupied)[None], mode_mats], axis=0)


def shift_cells(values, offset, edge_mask):
    fill = jnp.zeros(values.shape[:-1] + (abs(offset),), values.dtype)
    if offset > 0:
        shifted = jnp.concatenate([values[..., offset:], fill], axis=-1)
    else:
        shifted = jnp.concatenate([fill, values[..., :offset]], axis=-1)
    return shifted * edge_mask


def diffuse(field_padded, conduct_padded):
    centre = field_padded[..., 1:-1, :]
    conduct = conduct_padded[..., 1:-1, :]
    accumulated = (
        0.5 * (conduct + conduct_padded[..., :-2, :]) * (centre - field_padded[..., :-2, :])
    )
    accumulated = accumulated + 0.5 * (conduct + conduct_padded[..., 2:, :]) * (
        centre - field_padded[..., 2:, :]
    )
    cells = centre.shape[-1]
    column_in_row = lax.iota(jnp.int32, cells) % NY
    upper_mask = (column_in_row < NY - 1).astype(centre.dtype)
    lower_mask = (column_in_row > 0).astype(centre.dtype)
    all_mask = jnp.ones((cells,), centre.dtype)
    for offset, edge_mask in ((1, upper_mask), (-1, lower_mask), (NY, all_mask), (-NY, all_mask)):
        neighbour = shift_cells(centre, offset, edge_mask)
        neighbour_conduct = shift_cells(conduct, offset, edge_mask)
        accumulated = accumulated + 0.5 * (conduct + neighbour_conduct) * (centre - neighbour)
    return accumulated


def local_by_slots(source_chaos_terms, mean_conductivity, mode_shapes, coupling, slot_term, bounds):
    slot_count = source_chaos_terms.shape[0]
    conductivity = jnp.concatenate(
        [mean_conductivity[None], mean_conductivity[None] * mode_shapes], axis=0
    )
    conduct_padded = with_halo(conductivity, (("space", 1),), 1)
    matrices = mixing_matrices(coupling, slot_term)
    first_own = lax.axis_index("chaos") * slot_count
    own_rows = lax.dynamic_slice_in_dim(matrices, first_own, slot_count, 1)
    own_terms = lax.dynamic_slice_in_dim(slot_term, first_own, slot_count, 0)
    occupied = (own_terms >= 0).astype(jnp.float32)[:, None, None]
    lower_bound = bounds[0]
    upper_bound = bounds[1]
    midpoint = 0.5 * (upper_bound + lower_bound)
    half_span = 0.5 * (upper_bound - lower_bound)
    sigma_one = midpoint / half_span
    rho_now = 1.0 / sigma_one
    residual = source_chaos_terms * occupied
    solution_field = jnp.zeros_like(residual)
    direction = residual / midpoint
    for iteration in range(ITERS):
        solution_field = solution_field + direction
        fields = jnp.einsum(
            "ksr,rzc->kszc",
            own_rows,
            lax.all_gather(direction, "chaos", axis=0, tiled=True),
            precision=full_precision,
        )
        field_padded = with_halo(fields, (("space", 2),), 1)
        diffused = diffuse(field_padded, conduct_padded[:, None])
        residual = residual - jnp.sum(diffused, axis=0)
        if iteration + 1 < ITERS:
            rho_next = 1.0 / (2.0 * sigma_one - rho_now)
            direction = rho_next * rho_now * direction + 2.0 * rho_next / half_span * residual
            rho_now = rho_next
    return (solution_field, residual)


OWN_TILES = 2
FOLDED = OWN_TILES + ITERS


def block_of(device, spaces):
    chaos, space = divmod(device, spaces)
    return chaos * spaces + (space if chaos % 2 == 0 else spaces - 1 - space)


def lane_masks(rows):
    lane = lax.broadcasted_iota(jnp.int32, (rows, LANES), 1)
    return lane < NY, lane % NY > 0, lane % NY < NY - 1


def plane_sums(tiles, masks, first=0):
    low_half, has_left, has_right = masks
    zero = jnp.zeros(tiles[0].shape, jnp.float32)
    swapped = [pltpu.roll(tile, NY, 1) for tile in tiles]
    sums = []
    for t in range(first, len(tiles) - 1):
        if t == 0:
            across = swapped[0] + jnp.where(low_half, swapped[2], swapped[1])
        elif t == 1:
            across = swapped[1] + jnp.where(low_half, swapped[0], swapped[2])
        elif t == 2:
            across = swapped[3] + jnp.where(low_half, swapped[1], swapped[0])
        else:
            across = swapped[t - 1] + swapped[t + 1]
        left = jnp.where(has_left, pltpu.roll(tiles[t], 1, 1), zero)
        right = jnp.where(has_right, pltpu.roll(tiles[t], LANES - 1, 1), zero)
        sums.append(across + (left + right))
    return sums


def neighbour_sums(read, layer, count, masks, first=0):
    sums = plane_sums([read(layer, t) for t in range(count)], masks, first)
    return [
        total + (read(layer - 1, first + n) + read(layer + 1, first + n))
        for n, total in enumerate(sums)
    ]


def clear_ends(ref):
    for end in (0, ref.shape[0] - 1):
        ref[end] = jnp.zeros(ref.shape[1:], jnp.float32)


def split_stack(tiles, depth):
    wide = jnp.concatenate(tiles, axis=1)
    spare = depth // 2 - wide.shape[0]
    if spare:
        wide = jnp.concatenate([wide, jnp.zeros((spare, wide.shape[1]), wide.dtype)], axis=0)
    high = wide.astype(jnp.bfloat16)
    low = (wide - high.astype(jnp.float32)).astype(jnp.bfloat16)
    return jnp.concatenate([high, low], axis=0)


def lanes(t):
    return pl.ds(t * LANES, LANES)


def run_copies(copies):
    for copy in copies:
        copy.start()
    for copy in copies:
        copy.wait()


def scatter_kernel(blocks, in_ref, out_ref, held_ref, sems):
    own = in_ref.shape[0]
    parts = sems.shape[0]
    bounds = [own * n // parts for n in range(parts + 1)]
    spans = [pl.ds(a, b - a) for a, b in zip(bounds[:-1], bounds[1:])]
    copies = [
        pltpu.make_async_copy(in_ref.at[span], held_ref.at[span], sems.at[n])
        for n, span in enumerate(spans)
    ]
    for copy in copies:
        copy.start()
    for copy, span in zip(copies, spans):
        copy.wait()
        for device, block in enumerate(blocks):
            out_ref[device, span] = held_ref[span, block]


def pick_kernel(targets, scales, mix_ref, mean_ref, modes_ref, *outs):
    count, per_mode = mean_ref.shape[0], outs[0].shape[0] // (1 + modes_ref.shape[0] // mean_ref.shape[0])
    side = per_mode // 3
    last = count // side - 1
    for n, out_ref in enumerate(outs):
        block = targets[n]
        lower = jnp.where(block > 0, 1.0, 0.0)
        upper = jnp.where(block < last, 1.0, 0.0)
        before = jnp.maximum(block - 1, 0) * side
        after = jnp.minimum(block + 1, last) * side
        for k in range(out_ref.shape[0] // per_mode):
            ref, base = (mean_ref, 0) if k == 0 else (modes_ref, (k - 1) * count)
            first = k * per_mode
            out_ref[pl.ds(first, side), :] = ref[pl.ds(base + before, side), :] * lower
            out_ref[pl.ds(first + side, side), :] = ref[pl.ds(base + block * side, side), :]
            out_ref[pl.ds(first + 2 * side, side), :] = ref[pl.ds(base + after, side), :] * upper


def layer_sum(values, layer):
    layers = values.shape[0]
    zero = jnp.zeros(values.shape, jnp.float32)
    under = jnp.where(layer > 0, pltpu.roll(values, 1, 0), zero)
    over = jnp.where(layer < layers - 1, pltpu.roll(values, layers - 1, 0), zero)
    return under + over


def coefficient_kernel(thick, sources, *refs):
    *ins, a_ref, b_ref, own_b_ref, face_ref, held_ref = refs
    modes, tiles, layers, _ = held_ref.shape

    def put(ref, k, t, value):
        row = k * (ref.shape[1] // modes) + t
        for l in range(layers):
            ref[l, row : row + 1, :] = value[l : l + 1]

    layer = lax.broadcasted_iota(jnp.int32, (layers, LANES), 0)
    masks = lane_masks(layers)
    low_half = masks[0]
    for n, in_ref in enumerate(ins):
        for k in range(modes):
            for u in range(tiles):
                held_ref[k, u, pl.ds(sources[n] * thick, thick), :] = in_ref[
                    pl.ds((k * tiles + u) * thick, thick), :
                ]
    mean = None
    for k in range(modes):
        runs = [held_ref[k, u] for u in range(tiles)]
        values = [
            runs[2],
            runs[3],
            jnp.where(low_half, runs[4], runs[1]),
            jnp.where(low_half, runs[1], runs[4]),
            jnp.where(low_half, runs[5], runs[0]),
        ]
        if k == 0:
            values = mean = [0.5 * value for value in values]
        else:
            values = [m * value for m, value in zip(mean, values)]
        sums = plane_sums(values, masks)
        for t in range(FOLDED):
            put(a_ref, k, t, values[t])
        for t in range(FOLDED - 1):
            put(b_ref, k, t, 6.0 * values[t] + (sums[t] + layer_sum(values[t], layer)))
        outside = jnp.zeros((layers, LANES), jnp.float32)
        sums = plane_sums(values[:OWN_TILES] + [outside], masks)
        for t in range(OWN_TILES):
            put(own_b_ref, k, t, 6.0 * values[t] + (sums[t] + layer_sum(values[t], layer)))
        put(face_ref, k, 0, jnp.where(low_half, values[0], values[1]))
        put(face_ref, k, 1, pltpu.roll(values[2], NY, 1))


def collect_kernel(blocks, in_ref, *rest):
    *outs, sems = rest
    run_copies(
        [
            pltpu.make_async_copy(
                in_ref.at[device, n], out_ref.at[:, block], sems.at[n, device]
            )
            for n, out_ref in enumerate(outs)
            for device, block in enumerate(blocks)
        ]
    )


def slot_parts(own, chaos):
    whole = own // 8 * 8
    parts = [(c, 0, whole, c * whole) for c in range(chaos)]
    return parts + [
        (c, whole, own - whole, chaos * whole + c * (own - whole)) for c in range(chaos)
    ]


def start_kernel(chaos, spaces, odd, a_ref, weight_ref, in_ref, residual_ref, chip_ref, core_ref):
    upward = odd[0] > 0
    layers, tiles, slots, _ = residual_ref.shape
    layers -= 2
    own = slots // chaos
    thick = layers // spaces
    pieces = tiles * thick
    half = layers // 2
    low_half = lane_masks(slots)[0]
    weight = weight_ref[...]
    clear_ends(residual_ref)

    def put(place, up, down):
        rows = pl.ds(place * slots, slots)
        chip_ref[rows, :] = jnp.where(upward, up, down)
        core_ref[rows, :] = jnp.where(upward, down, up)

    for l in range(layers):
        i, z = divmod(l, thick)
        for t in range(tiles):
            rows = [
                in_ref[
                    pl.ds(
                        ((c * spaces + i) * own + slot) * pieces + t * thick + z,
                        number,
                        stride=pieces,
                    ),
                    :,
                ]
                for c, slot, number, _ in slot_parts(own, chaos)
            ]
            residual_ref[l + 1, t] = weight * jnp.concatenate(rows, axis=0)
        put(l, residual_ref[l + 1, 1], residual_ref[l + 1, 0])
    for l in range(half):
        first, later = residual_ref.at[l + 1], residual_ref.at[l + 1 + half]
        put(
            layers + l,
            jnp.where(low_half, pltpu.roll(later[0], NY, 1), first[0]),
            jnp.where(low_half, first[1], pltpu.roll(later[1], NY, 1)),
        )


def coefficient(ref, modes, l, k, t):
    row = k * (ref.shape[1] // modes) + t
    return ref[l, row : row + 1, :]


def mode_part(mixed, modes, k, n):
    group = 8 * (modes - 1)
    return jnp.concatenate(
        [
            mixed[row : row + 8, n * LANES : (n + 1) * LANES]
            for row in range((k - 1) * 8, mixed.shape[0], group)
        ],
        axis=0,
    )


def weighted_tiles(mixed, modes, place, beside, direct, around, a_of, b_of):
    results = []
    for t, tile in enumerate(direct):
        full = t < len(around)
        a = a_of(0, t)
        edge = a * tile
        total = b_of(0, t) * tile - a * around[t] if full else None
        for k in range(1, modes):
            a = a_of(k, t)
            part = mode_part(mixed, modes, k, place + t)
            edge = edge + a * part
            if full:
                total = total + (b_of(k, t) * part - a * mode_part(mixed, modes, k, beside + t))
        results.append((total, edge))
    return results


def own_kernel(scales, mix_ref, a_ref, b_ref, start_ref, total_ref, edge_ref):
    layers, tiles, slots, _ = total_ref.shape
    modes = b_ref.shape[1] // tiles
    masks = lane_masks(slots)
    nothing = jnp.zeros((slots, LANES), jnp.float32)
    clear_ends(edge_ref)

    def read(l, t):
        return start_ref[l + 1, t] * scales[0] if t < tiles else nothing

    def body(l, carry):
        direct = [read(l, t) for t in range(tiles)]
        around = neighbour_sums(read, l, tiles + 1, masks)
        mixed = jnp.dot(
            mix_ref[...],
            split_stack(direct + around, mix_ref.shape[1]),
            preferred_element_type=jnp.float32,
        )
        results = weighted_tiles(
            mixed,
            modes,
            0,
            tiles,
            direct,
            around,
            lambda k, t: coefficient(a_ref, modes, l, k, t),
            lambda k, t: coefficient(b_ref, modes, l, k, t),
        )
        for t, (total, edge) in enumerate(results):
            total_ref[l, t] = total
            edge_ref[l + 1, t] = edge
        return carry

    lax.fori_loop(0, layers, body, 0)


def iterate_kernel(
    chaos,
    spaces,
    scales,
    inside,
    odd,
    mix_ref,
    a_ref,
    b_ref,
    face_ref,
    unweight_ref,
    start_ref,
    own_total_ref,
    own_edge_ref,
    chip_ref,
    core_ref,
    sent_ref,
    r_ref,
    d_ref,
    total_ref,
    edge_ref,
    x_ref,
):
    layers, _, slots, _ = own_total_ref.shape
    modes = a_ref.shape[1] // FOLDED
    own = slots // chaos
    thick = layers // spaces
    pieces = OWN_TILES * thick
    half = layers // 2
    masks = lane_masks(slots)
    low_half = masks[0]
    upward = odd[0] > 0
    clear_ends(d_ref)
    clear_ends(edge_ref)

    def message(start, size):
        chip, core = chip_ref[pl.ds(start, size), :], core_ref[pl.ds(start, size), :]
        return jnp.where(upward, core, chip), jnp.where(upward, chip, core)

    def send(field, l, t, value):
        i, z = lax.div(l, thick), lax.rem(l, thick)
        value = value * unweight_ref[...]
        for c, slot, number, row in slot_parts(own, chaos):
            first = (((c * spaces + i) * 2 + field) * own + slot) * pieces + t * thick + z
            sent_ref[pl.ds(first, number, stride=pieces), :] = value[row : row + number]

    for l in range(layers):
        below, above = message(l * slots, slots)
        far_below, far_above = message((layers + l % half) * slots, slots)
        if l < half:
            far = jnp.where(low_half, far_above, far_below)
        else:
            far = pltpu.roll(jnp.where(low_half, far_below, far_above), NY, 1)
        tiles = [
            start_ref[l + 1, 0],
            start_ref[l + 1, 1],
            jnp.where(low_half, above, below),
            jnp.where(low_half, below, above),
            far,
        ]
        for t, tile in enumerate(tiles):
            if t < FOLDED - 1:
                r_ref[l, t] = tile
            d_ref[l + 1, t] = tile * scales[0]

    def read(l, t):
        return d_ref[l + 1, t]

    zero = jnp.zeros((slots, LANES), jnp.float32)
    for step in range(ITERS):
        count = FOLDED - step
        full = count - 1
        first = OWN_TILES if step == 0 else 0

        def sums(l, carry):
            direct = [read(l, t) for t in range(first, count)]
            around = neighbour_sums(read, l, count, masks, first)
            extra = [jnp.where(low_half, read(l, 0), read(l, 1))] if step == 0 else []
            mixed = jnp.dot(
                mix_ref[...],
                split_stack(direct + extra + around, mix_ref.shape[1]),
                preferred_element_type=jnp.float32,
            )
            results = weighted_tiles(
                mixed,
                modes,
                0,
                len(direct) + len(extra),
                direct,
                around,
                lambda k, t: coefficient(a_ref, modes, l, k, first + t),
                lambda k, t: coefficient(b_ref, modes, l, k, first + t),
            )
            for t, (total, edge) in enumerate(results):
                edge_ref[l + 1, first + t] = edge
                if first + t < full:
                    total_ref[l, first + t] = total
            if step == 0:
                own_face, other_face = [coefficient(face_ref, modes, l, 0, n) for n in range(2)]
                part = other_face * extra[0] - own_face * pltpu.roll(direct[0], NY, 1)
                for k in range(1, modes):
                    own_face, other_face = [coefficient(face_ref, modes, l, k, n) for n in range(2)]
                    own_mixed = mode_part(mixed, modes, k, len(direct))
                    other_mixed = pltpu.roll(mode_part(mixed, modes, k, 0), NY, 1)
                    part = part + (other_face * own_mixed - own_face * other_mixed)
                total_ref[l, 0] = own_total_ref[l, 0] + jnp.where(low_half, part, zero)
                total_ref[l, 1] = own_total_ref[l, 1] + jnp.where(low_half, zero, part)
            return carry

        def read_edge(l, t):
            return (own_edge_ref if t < first else edge_ref)[l + 1, t]

        def update(l, carry):
            spread = neighbour_sums(read_edge, l, count, masks)
            for t in range(full):
                diffused = total_ref[l, t] - spread[t]
                if t >= OWN_TILES:
                    lower, upper = inside[(t + 1) % 2], inside[t % 2]
                    diffused = diffused * jnp.where(low_half, lower, upper)
                residual = r_ref[l, t] - diffused
                if step == ITERS - 1:
                    send(1, l, t, residual)
                    continue
                r_ref[l, t] = residual
                old = read(l, t)
                direction = scales[1 + 2 * step] * old + scales[2 + 2 * step] * residual
                d_ref[l + 1, t] = direction
                if t < OWN_TILES:
                    value = (old if step == 0 else x_ref[l, t]) + direction
                    if step == ITERS - 2:
                        send(0, l, t, value)
                    else:
                        x_ref[l, t] = value
            return carry

        lax.fori_loop(0, layers, sums, 0)
        lax.fori_loop(0, layers, update, 0)


def call(kernel, outs, scalars, arrays, scratch=(), flops=0, in_kinds=None, out_kind=pltpu.VMEM):
    kinds = in_kinds or [pltpu.VMEM] * len(arrays)
    in_specs = [pl.BlockSpec(memory_space=pltpu.SMEM)] * len(scalars) + [
        pl.BlockSpec(memory_space=kind) for kind in kinds
    ]
    arrays = [
        pltpu.with_memory_space_constraint(x, kind) if kind == pltpu.HBM else x
        for x, kind in zip(arrays, kinds)
    ]
    moved = sum(4 * x.size for x in arrays) + sum(4 * x.size for x in outs)
    return pl.pallas_call(
        kernel,
        out_shape=outs,
        in_specs=in_specs,
        out_specs=[pl.BlockSpec(memory_space=out_kind)] * len(outs),
        scratch_shapes=scratch,
        compiler_params=pltpu.CompilerParams(vmem_limit_bytes=40 * 1024 * 1024),
        cost_estimate=pl.CostEstimate(flops=flops, bytes_accessed=moved, transcendentals=0),
    )(*scalars, *arrays)


def coupling_tables(coupling, slot_term, chaos):
    bf16 = jnp.bfloat16
    slots = slot_term.shape[0]
    by_source = slot_term.reshape(chaos, -1)
    slot_term = jnp.concatenate(
        [
            by_source[c, slot : slot + number]
            for c, slot, number, _ in slot_parts(slots // chaos, chaos)
        ]
    )
    raising = (slot_term[None, None, :] == coupling[:, :, 0:1]).astype(bf16)
    lowering = (slot_term[None, None, :] == coupling[:, :, 1:2]).astype(bf16)
    weighted = raising * coupling[:, :, 2:3].astype(bf16)
    matrices = jnp.einsum(
        "kps,kpr->ksr", weighted, lowering, preferred_element_type=jnp.float32
    ) + jnp.einsum("kps,kpr->ksr", lowering, raising, preferred_element_type=jnp.float32)
    spare = -slots % 16
    matrices = jnp.pad(matrices.astype(bf16), ((0, 0), (0, 0), (0, spare)))
    matrices = matrices.reshape(-1, slots // 8, 8, slots + spare).transpose(1, 0, 2, 3)
    matrices = matrices.reshape(-1, slots + spare)
    degree = jnp.sum(weighted.astype(jnp.float32), axis=1)
    factorial = jnp.where(degree > 2.5, 6.0, jnp.where(degree > 1.5, 2.0, 1.0))
    scale = jnp.sqrt(jnp.prod(factorial, axis=0))
    occupied = (slot_term >= 0).astype(jnp.float32)
    spread = jnp.ones((1, LANES), jnp.float32)
    return (
        jnp.concatenate([matrices, matrices], axis=1),
        (occupied * scale)[:, None] * spread,
        (occupied / scale)[:, None] * spread,
    )


def local_by_cells(source_chaos_terms, mean_conductivity, mode_shapes, coupling, slot_term, bounds):
    own, thick, cells = source_chaos_terms.shape
    chaos, spaces = lax.axis_size("chaos"), lax.axis_size("space")
    devices = chaos * spaces
    slots = own * chaos
    layers = thick * spaces
    columns = cells // LANES
    pieces = OWN_TILES * thick
    blocks = [block_of(device, spaces) for device in range(devices)]
    f32 = jnp.float32

    def shape(*sizes):
        return jax.ShapeDtypeStruct(sizes, f32)

    mix, weight, unweight = coupling_tables(coupling, slot_term, chaos)
    midpoint = 0.5 * (bounds[1] + bounds[0])
    half_span = 0.5 * (bounds[1] - bounds[0])
    sigma_one = midpoint / half_span
    rho_now = 1.0 / sigma_one
    scales = [1.0 / midpoint]
    for _ in range(ITERS - 1):
        rho_next = 1.0 / (2.0 * sigma_one - rho_now)
        scales += [rho_next * rho_now, 2.0 * rho_next / half_span]
        rho_now = rho_next
    scales = jnp.stack(scales)

    def by_columns(field):
        tiled = field.reshape(*field.shape[:-2], thick, columns, LANES)
        return jnp.swapaxes(tiled, -3, -2)

    scattered = call(
        functools.partial(scatter_kernel, blocks),
        [shape(devices, own, pieces, LANES)],
        [],
        [by_columns(source_chaos_terms).reshape(own, devices, pieces, LANES)],
        [pltpu.VMEM((own, devices, pieces, LANES), f32), pltpu.SemaphoreType.DMA((4,))],
        in_kinds=[pltpu.HBM],
    )[0]
    gathered = lax.all_to_all(scattered, BOTH, 0, 0, tiled=True).reshape(-1, LANES)

    row, column = lax.axis_index("chaos"), lax.axis_index("space")

    def block_at(space):
        return row * spaces + jnp.where(row % 2 == 0, space, spaces - 1 - space)

    block = block_at(column)
    inside = jnp.stack([block > 0, block < devices - 1]).astype(f32)
    odd = (block % 2)[None]
    modes = mode_shapes.shape[0] + 1
    steps = jnp.arange(spaces)
    picked = call(
        pick_kernel,
        [shape(modes * 3 * pieces, LANES)] * spaces,
        [block_at((column + steps) % spaces), scales],
        [
            mix,
            by_columns(mean_conductivity).reshape(-1, LANES),
            by_columns(mode_shapes).reshape(-1, LANES),
        ],
    )
    picked = [picked[0]] + [
        lax.ppermute(picked[n], "space", [(i, (i + n) % spaces) for i in range(spaces)])
        for n in range(1, spaces)
    ]
    a, b, own_b, face = call(
        functools.partial(coefficient_kernel, thick),
        [shape(layers, modes * tiles, LANES) for tiles in (FOLDED, FOLDED - 1, OWN_TILES, 2)],
        [(column - steps) % spaces],
        picked,
        [pltpu.VMEM((modes, 3 * OWN_TILES, layers, LANES), f32)],
    )

    message = shape((layers + layers // 2) * slots, LANES)
    start, to_chip, to_core = call(
        functools.partial(start_kernel, chaos, spaces),
        [shape(layers + 2, OWN_TILES, slots, LANES), message, message],
        [odd],
        [a, weight, gathered],
    )
    place = {n: device for device, n in enumerate(blocks)}

    def swap(field, lowest):
        pairs = [(place[n], place[n + 1]) for n in range(lowest, devices - 1, 2)]
        return lax.ppermute(field, BOTH, pairs + [(b, a) for a, b in pairs])

    from_chip = swap(to_chip, 1)
    from_core = swap(to_core, 0)
    own_total, own_edge = call(
        own_kernel,
        [shape(n, OWN_TILES, slots, LANES) for n in (layers, layers + 2)],
        [scales],
        [mix, a, own_b, start],
        flops=3000000000,
    )

    def held(tiles, depth=layers):
        return pltpu.VMEM((depth, tiles, slots, LANES), f32)

    sent = call(
        functools.partial(iterate_kernel, chaos, spaces),
        [shape(devices * 2 * own * pieces, LANES)],
        [scales, inside, odd],
        [mix, a, b, face, unweight, start, own_total, own_edge, from_chip, from_core],
        [
            held(FOLDED - 1),
            held(FOLDED, layers + 2),
            held(FOLDED - 1),
            held(FOLDED, layers + 2),
            held(OWN_TILES),
        ],
        flops=10000000000,
    )[0]
    sent = sent.reshape(devices, 2, own, pieces, LANES)
    received = lax.all_to_all(sent, BOTH, 0, 0, tiled=True)
    outs = call(
        functools.partial(collect_kernel, blocks),
        [shape(own, devices, pieces, LANES)] * 2,
        [],
        [received],
        [pltpu.SemaphoreType.DMA((2, devices))],
        in_kinds=[pl.ANY],
        out_kind=pltpu.HBM,
    )
    return tuple(
        jnp.transpose(out.reshape(own, columns, thick, LANES), (0, 2, 1, 3)).reshape(
            own, thick, cells
        )
        for out in outs
    )


def local(source_chaos_terms, mean_conductivity, mode_shapes, coupling, slot_term, bounds):
    own, thick, cells = source_chaos_terms.shape
    chaos, spaces = lax.axis_size("chaos"), lax.axis_size("space")
    fits = (
        thick * spaces == 8
        and cells == chaos * spaces * OWN_TILES * LANES
        and (own * chaos) % 8 == 0
        and spaces % 2 == 0
    )
    plan = local_by_cells if fits else local_by_slots
    return plan(
        source_chaos_terms, mean_conductivity, mode_shapes, coupling, slot_term, bounds
    )


def solution(mesh):
    in_specs = (
        P(("groups", "chaos"), "space", None),
        P("space", None),
        P(None, "space", None),
        P(),
        P(),
        P("groups"),
    )
    out_specs = (P(("groups", "chaos"), "space", None), P(("groups", "chaos"), "space", None))
    return jax.shard_map(local, mesh=mesh, in_specs=in_specs, out_specs=out_specs, check_vma=False)
```

```python
import functools

import jax
import jax.numpy as jnp
from jax import lax
from jax.experimental import pallas as pl
from jax.experimental.pallas import tpu as pltpu
from jax.sharding import PartitionSpec as P

NY = 64
ITERS = 3
LANES = 128
BOTH = ("chaos", "space")


full_precision = lax.Precision.HIGHEST


def with_halo(cells, sides, width):
    for axis, dim in sides:
        count = lax.axis_size(axis)
        ends = count - 1
        head = lax.slice_in_dim(cells, 0, width, axis=dim)
        tail = lax.slice_in_dim(cells, cells.shape[dim] - width, cells.shape[dim], axis=dim)
        cells = jnp.concatenate(
            [
                lax.ppermute(tail, axis, [(i, (i + 1) % count) for i in range(ends)]),
                cells,
                lax.ppermute(head, axis, [((i + 1) % count, i) for i in range(ends)]),
            ],
            axis=dim,
        )
    return cells


def mixing_matrices(coupling, slot_term):
    occupied = (slot_term >= 0).astype(jnp.float32)
    raising = (slot_term[None, None, :] == coupling[:, :, 0:1]).astype(jnp.float32)
    lowering = (slot_term[None, None, :] == coupling[:, :, 1:2]).astype(jnp.float32)
    weight = jnp.sqrt(coupling[:, :, 2].astype(jnp.float32))
    raised = jnp.einsum("kps,kp,kpr->ksr", raising, weight, lowering, precision=full_precision)
    mode_mats = raised + jnp.transpose(raised, (0, 2, 1))
    return jnp.concatenate([jnp.diag(occupied)[None], mode_mats], axis=0)


def shift_cells(values, offset, edge_mask):
    fill = jnp.zeros(values.shape[:-1] + (abs(offset),), values.dtype)
    if offset > 0:
        shifted = jnp.concatenate([values[..., offset:], fill], axis=-1)
    else:
        shifted = jnp.concatenate([fill, values[..., :offset]], axis=-1)
    return shifted * edge_mask


def diffuse(field_padded, conduct_padded):
    centre = field_padded[..., 1:-1, :]
    conduct = conduct_padded[..., 1:-1, :]
    accumulated = (
        0.5 * (conduct + conduct_padded[..., :-2, :]) * (centre - field_padded[..., :-2, :])
    )
    accumulated = accumulated + 0.5 * (conduct + conduct_padded[..., 2:, :]) * (
        centre - field_padded[..., 2:, :]
    )
    cells = centre.shape[-1]
    column_in_row = lax.iota(jnp.int32, cells) % NY
    upper_mask = (column_in_row < NY - 1).astype(centre.dtype)
    lower_mask = (column_in_row > 0).astype(centre.dtype)
    all_mask = jnp.ones((cells,), centre.dtype)
    for offset, edge_mask in ((1, upper_mask), (-1, lower_mask), (NY, all_mask), (-NY, all_mask)):
        neighbour = shift_cells(centre, offset, edge_mask)
        neighbour_conduct = shift_cells(conduct, offset, edge_mask)
        accumulated = accumulated + 0.5 * (conduct + neighbour_conduct) * (centre - neighbour)
    return accumulated


def local_by_slots(source_chaos_terms, mean_conductivity, mode_shapes, coupling, slot_term, bounds):
    slot_count = source_chaos_terms.shape[0]
    conductivity = jnp.concatenate(
        [mean_conductivity[None], mean_conductivity[None] * mode_shapes], axis=0
    )
    conduct_padded = with_halo(conductivity, (("space", 1),), 1)
    matrices = mixing_matrices(coupling, slot_term)
    first_own = lax.axis_index("chaos") * slot_count
    own_rows = lax.dynamic_slice_in_dim(matrices, first_own, slot_count, 1)
    own_terms = lax.dynamic_slice_in_dim(slot_term, first_own, slot_count, 0)
    occupied = (own_terms >= 0).astype(jnp.float32)[:, None, None]
    lower_bound = bounds[0]
    upper_bound = bounds[1]
    midpoint = 0.5 * (upper_bound + lower_bound)
    half_span = 0.5 * (upper_bound - lower_bound)
    sigma_one = midpoint / half_span
    rho_now = 1.0 / sigma_one
    residual = source_chaos_terms * occupied
    solution_field = jnp.zeros_like(residual)
    direction = residual / midpoint
    for iteration in range(ITERS):
        solution_field = solution_field + direction
        fields = jnp.einsum(
            "ksr,rzc->kszc",
            own_rows,
            lax.all_gather(direction, "chaos", axis=0, tiled=True),
            precision=full_precision,
        )
        field_padded = with_halo(fields, (("space", 2),), 1)
        diffused = diffuse(field_padded, conduct_padded[:, None])
        residual = residual - jnp.sum(diffused, axis=0)
        if iteration + 1 < ITERS:
            rho_next = 1.0 / (2.0 * sigma_one - rho_now)
            direction = rho_next * rho_now * direction + 2.0 * rho_next / half_span * residual
            rho_now = rho_next
    return (solution_field, residual)


OWN_TILES = 2
FOLDED = OWN_TILES + ITERS


def block_of(device, spaces):
    chaos, space = divmod(device, spaces)
    return chaos * spaces + (space if chaos % 2 == 0 else spaces - 1 - space)


def lane_masks(rows):
    lane = lax.broadcasted_iota(jnp.int32, (rows, LANES), 1)
    return lane < NY, lane % NY > 0, lane % NY < NY - 1


def plane_sums(tiles, masks, first=0):
    low_half, has_left, has_right = masks
    zero = jnp.zeros(tiles[0].shape, jnp.float32)
    swapped = [pltpu.roll(tile, NY, 1) for tile in tiles]
    sums = []
    for t in range(first, len(tiles) - 1):
        if t == 0:
            across = swapped[0] + jnp.where(low_half, swapped[2], swapped[1])
        elif t == 1:
            across = swapped[1] + jnp.where(low_half, swapped[0], swapped[2])
        elif t == 2:
            across = swapped[3] + jnp.where(low_half, swapped[1], swapped[0])
        else:
            across = swapped[t - 1] + swapped[t + 1]
        left = jnp.where(has_left, pltpu.roll(tiles[t], 1, 1), zero)
        right = jnp.where(has_right, pltpu.roll(tiles[t], LANES - 1, 1), zero)
        sums.append(across + (left + right))
    return sums


def neighbour_sums(read, layer, layers, count, masks, first=0):
    sums = plane_sums([read(layer, t) for t in range(count)], masks, first)
    for other in (layer - 1, layer + 1):
        if 0 <= other < layers:
            sums = [total + read(other, first + n) for n, total in enumerate(sums)]
    return sums


def split_stack(tiles, depth):
    wide = jnp.concatenate(tiles, axis=1)
    spare = depth // 2 - wide.shape[0]
    if spare:
        wide = jnp.concatenate([wide, jnp.zeros((spare, wide.shape[1]), wide.dtype)], axis=0)
    high = wide.astype(jnp.bfloat16)
    low = (wide - high.astype(jnp.float32)).astype(jnp.bfloat16)
    return jnp.concatenate([high, low], axis=0)


def lanes(t):
    return pl.ds(t * LANES, LANES)


def run_copies(copies):
    for copy in copies:
        copy.start()
    for copy in copies:
        copy.wait()


def scatter_kernel(blocks, in_ref, out_ref, held_ref, sems):
    own = in_ref.shape[0]
    parts = sems.shape[0]
    bounds = [own * n // parts for n in range(parts + 1)]
    spans = [pl.ds(a, b - a) for a, b in zip(bounds[:-1], bounds[1:])]
    copies = [
        pltpu.make_async_copy(in_ref.at[span], held_ref.at[span], sems.at[n])
        for n, span in enumerate(spans)
    ]
    for copy in copies:
        copy.start()
    for copy, span in zip(copies, spans):
        copy.wait()
        for device, block in enumerate(blocks):
            out_ref[device, span] = held_ref[span, block]


def pick_kernel(targets, scales, mix_ref, mean_ref, modes_ref, *outs):
    count, per_mode = mean_ref.shape[0], outs[0].shape[0] // (1 + modes_ref.shape[0] // mean_ref.shape[0])
    side = per_mode // 3
    last = count // side - 1
    for n, out_ref in enumerate(outs):
        block = targets[n]
        lower = jnp.where(block > 0, 1.0, 0.0)
        upper = jnp.where(block < last, 1.0, 0.0)
        before = jnp.maximum(block - 1, 0) * side
        after = jnp.minimum(block + 1, last) * side
        for k in range(out_ref.shape[0] // per_mode):
            ref, base = (mean_ref, 0) if k == 0 else (modes_ref, (k - 1) * count)
            first = k * per_mode
            out_ref[pl.ds(first, side), :] = ref[pl.ds(base + before, side), :] * lower
            out_ref[pl.ds(first + side, side), :] = ref[pl.ds(base + block * side, side), :]
            out_ref[pl.ds(first + 2 * side, side), :] = ref[pl.ds(base + after, side), :] * upper


def layer_sum(values, layer):
    layers = values.shape[0]
    zero = jnp.zeros(values.shape, jnp.float32)
    under = jnp.where(layer > 0, pltpu.roll(values, 1, 0), zero)
    over = jnp.where(layer < layers - 1, pltpu.roll(values, layers - 1, 0), zero)
    return under + over


def coefficient_kernel(thick, sources, *refs):
    *ins, a_ref, b_ref, own_b_ref, face_ref, held_ref = refs
    modes, layers, _ = a_ref.shape
    tiles = held_ref.shape[1]
    layer = lax.broadcasted_iota(jnp.int32, (layers, LANES), 0)
    masks = lane_masks(layers)
    low_half = masks[0]
    for n, in_ref in enumerate(ins):
        for k in range(modes):
            for u in range(tiles):
                held_ref[k, u, pl.ds(sources[n] * thick, thick), :] = in_ref[
                    pl.ds((k * tiles + u) * thick, thick), :
                ]
    mean = None
    for k in range(modes):
        runs = [held_ref[k, u] for u in range(tiles)]
        values = [
            runs[2],
            runs[3],
            jnp.where(low_half, runs[4], runs[1]),
            jnp.where(low_half, runs[1], runs[4]),
            jnp.where(low_half, runs[5], runs[0]),
        ]
        if k == 0:
            values = mean = [0.5 * value for value in values]
        else:
            values = [m * value for m, value in zip(mean, values)]
        sums = plane_sums(values, masks)
        for t in range(FOLDED):
            a_ref[k, :, lanes(t)] = values[t]
        for t in range(FOLDED - 1):
            b_ref[k, :, lanes(t)] = 6.0 * values[t] + (sums[t] + layer_sum(values[t], layer))
        outside = jnp.zeros((layers, LANES), jnp.float32)
        sums = plane_sums(values[:OWN_TILES] + [outside], masks)
        for t in range(OWN_TILES):
            own_b_ref[k, :, lanes(t)] = 6.0 * values[t] + (sums[t] + layer_sum(values[t], layer))
        face_ref[k, :, lanes(0)] = jnp.where(low_half, values[0], values[1])
        face_ref[k, :, lanes(1)] = pltpu.roll(values[2], NY, 1)


def collect_kernel(blocks, in_ref, *rest):
    *outs, sems = rest
    run_copies(
        [
            pltpu.make_async_copy(
                in_ref.at[device, n], out_ref.at[:, block], sems.at[n, device]
            )
            for n, out_ref in enumerate(outs)
            for device, block in enumerate(blocks)
        ]
    )


def slot_parts(own, chaos):
    whole = own // 8 * 8
    parts = [(c, 0, whole, c * whole) for c in range(chaos)]
    return parts + [
        (c, whole, own - whole, chaos * whole + c * (own - whole)) for c in range(chaos)
    ]


def start_kernel(chaos, spaces, odd, a_ref, weight_ref, in_ref, residual_ref, chip_ref, core_ref):
    upward = odd[0] > 0
    layers, tiles, slots, _ = residual_ref.shape
    own = slots // chaos
    thick = layers // spaces
    pieces = tiles * thick
    half = layers // 2
    low_half = lane_masks(slots)[0]
    weight = weight_ref[...]

    def put(place, up, down):
        rows = pl.ds(place * slots, slots)
        chip_ref[rows, :] = jnp.where(upward, up, down)
        core_ref[rows, :] = jnp.where(upward, down, up)

    for l in range(layers):
        i, z = divmod(l, thick)
        for t in range(tiles):
            rows = [
                in_ref[
                    pl.ds(
                        ((c * spaces + i) * own + slot) * pieces + t * thick + z,
                        number,
                        stride=pieces,
                    ),
                    :,
                ]
                for c, slot, number, _ in slot_parts(own, chaos)
            ]
            residual_ref[l, t] = weight * jnp.concatenate(rows, axis=0)
        put(l, residual_ref[l, 1], residual_ref[l, 0])
    for l in range(half):
        later = l + half
        put(
            layers + l,
            jnp.where(low_half, pltpu.roll(residual_ref[later, 0], NY, 1), residual_ref[l, 0]),
            jnp.where(low_half, residual_ref[l, 1], pltpu.roll(residual_ref[later, 1], NY, 1)),
        )


def mode_part(mixed, modes, k, n):
    group = 8 * (modes - 1)
    return jnp.concatenate(
        [
            mixed[row : row + 8, n * LANES : (n + 1) * LANES]
            for row in range((k - 1) * 8, mixed.shape[0], group)
        ],
        axis=0,
    )


def weighted_tiles(mixed, modes, place, beside, direct, around, a_of, b_of):
    results = []
    for t, tile in enumerate(direct):
        full = t < len(around)
        a = a_of(0, t)
        edge = a * tile
        total = b_of(0, t) * tile - a * around[t] if full else None
        for k in range(1, modes):
            a = a_of(k, t)
            part = mode_part(mixed, modes, k, place + t)
            edge = edge + a * part
            if full:
                total = total + (b_of(k, t) * part - a * mode_part(mixed, modes, k, beside + t))
        results.append((total, edge))
    return results


def own_kernel(scales, mix_ref, a_ref, b_ref, start_ref, total_ref, edge_ref):
    layers, tiles, slots, _ = start_ref.shape
    modes = a_ref.shape[0]
    masks = lane_masks(slots)
    mix = mix_ref[...]
    nothing = jnp.zeros((slots, LANES), jnp.float32)

    def read(l, t):
        return start_ref[l, t] * scales[0] if t < tiles else nothing

    def prepare(l):
        direct = [read(l, t) for t in range(tiles)]
        around = neighbour_sums(read, l, layers, tiles + 1, masks)
        mixed = jnp.dot(
            mix, split_stack(direct + around, mix.shape[1]), preferred_element_type=jnp.float32
        )
        return mixed, direct, around

    ahead = prepare(0)
    for l in range(layers):
        mixed, direct, around = ahead
        if l + 1 < layers:
            ahead = prepare(l + 1)
        results = weighted_tiles(
            mixed,
            modes,
            0,
            tiles,
            direct,
            around,
            lambda k, t: a_ref[k, l : l + 1, lanes(t)],
            lambda k, t: b_ref[k, l : l + 1, lanes(t)],
        )
        for t, (total, edge) in enumerate(results):
            total_ref[l, t] = total
            edge_ref[l, t] = edge


def iterate_kernel(
    chaos,
    spaces,
    scales,
    inside,
    odd,
    mix_ref,
    a_ref,
    b_ref,
    face_ref,
    unweight_ref,
    start_ref,
    own_total_ref,
    own_edge_ref,
    chip_ref,
    core_ref,
    sent_ref,
    r_ref,
    d_ref,
    total_ref,
    edge_ref,
    x_ref,
):
    layers, _, slots, _ = start_ref.shape
    modes = a_ref.shape[0]
    own = slots // chaos
    thick = layers // spaces
    pieces = OWN_TILES * thick
    half = layers // 2
    masks = lane_masks(slots)
    low_half = masks[0]
    mix = mix_ref[...]
    depth = mix.shape[1]
    upward = odd[0] > 0

    def message(start, size):
        chip, core = chip_ref[pl.ds(start, size), :], core_ref[pl.ds(start, size), :]
        return jnp.where(upward, core, chip), jnp.where(upward, chip, core)

    def send(field, l, t, value):
        i, z = divmod(l, thick)
        value = value * unweight_ref[...]
        for c, slot, number, row in slot_parts(own, chaos):
            first = (((c * spaces + i) * 2 + field) * own + slot) * pieces + t * thick + z
            sent_ref[pl.ds(first, number, stride=pieces), :] = value[row : row + number]

    def fold(l):
        below, above = message(l * slots, slots)
        far_below, far_above = message((layers + l % half) * slots, slots)
        if l < half:
            far = jnp.where(low_half, far_above, far_below)
        else:
            far = pltpu.roll(jnp.where(low_half, far_below, far_above), NY, 1)
        tiles = [
            start_ref[l, 0],
            start_ref[l, 1],
            jnp.where(low_half, above, below),
            jnp.where(low_half, below, above),
            far,
        ]
        for t, tile in enumerate(tiles):
            if t < FOLDED - 1:
                r_ref[l, t] = tile
            d_ref[l, t] = tile * scales[0]

    def read(l, t):
        return d_ref[l, t]

    zero = jnp.zeros((slots, LANES), jnp.float32)
    prepared = {}

    def prepare(step, l):
        count = FOLDED - step
        first = OWN_TILES if step == 0 else 0
        direct = [d_ref[l, t] for t in range(first, count)]
        around = neighbour_sums(read, l, layers, count, masks, first)
        extra = [jnp.where(low_half, d_ref[l, 0], d_ref[l, 1])] if step == 0 else []
        mixed = jnp.dot(
            mix, split_stack(direct + extra + around, depth), preferred_element_type=jnp.float32
        )
        prepared[step, l] = (mixed, direct, extra, around)

    def combine(step, l):
        first = OWN_TILES if step == 0 else 0
        mixed, direct, extra, around = prepared.pop((step, l))
        results = weighted_tiles(
            mixed,
            modes,
            0,
            len(direct) + len(extra),
            direct,
            around,
            lambda k, t: a_ref[k, l : l + 1, lanes(first + t)],
            lambda k, t: b_ref[k, l : l + 1, lanes(first + t)],
        )
        for t, (total, edge) in enumerate(results):
            edge_ref[l, first + t] = edge
            if total is not None:
                total_ref[l, first + t] = total
        if step > 0:
            return
        own_face = face_ref[0, l : l + 1, lanes(0)]
        other_face = face_ref[0, l : l + 1, lanes(1)]
        part = other_face * extra[0] - own_face * pltpu.roll(direct[0], NY, 1)
        for k in range(1, modes):
            own_face = face_ref[k, l : l + 1, lanes(0)]
            other_face = face_ref[k, l : l + 1, lanes(1)]
            own_mixed = mode_part(mixed, modes, k, len(direct))
            other_mixed = pltpu.roll(mode_part(mixed, modes, k, 0), NY, 1)
            part = part + (other_face * own_mixed - own_face * other_mixed)
        total_ref[l, 0] = own_total_ref[l, 0] + jnp.where(low_half, part, zero)
        total_ref[l, 1] = own_total_ref[l, 1] + jnp.where(low_half, zero, part)

    def update(step, l):
        count = FOLDED - step

        def read_edge(l, t):
            return own_edge_ref[l, t] if step == 0 and t < OWN_TILES else edge_ref[l, t]

        spread = neighbour_sums(read_edge, l, layers, count, masks)
        for t in range(count - 1):
            diffused = total_ref[l, t] - spread[t]
            if t >= OWN_TILES:
                lower, upper = inside[(t + 1) % 2], inside[t % 2]
                diffused = diffused * jnp.where(low_half, lower, upper)
            residual = r_ref[l, t] - diffused
            if step == ITERS - 1:
                send(1, l, t, residual)
                continue
            r_ref[l, t] = residual
            old = d_ref[l, t]
            direction = scales[1 + 2 * step] * old + scales[2 + 2 * step] * residual
            d_ref[l, t] = direction
            if t < OWN_TILES:
                value = (old if step == 0 else x_ref[l, t]) + direction
                if step == ITERS - 2:
                    send(0, l, t, value)
                else:
                    x_ref[l, t] = value

    tasks = []
    for l in range(layers):
        tasks.append((l - 1.5, lambda l=l: fold(l)))
        for step in range(ITERS):
            for wait, task in ((0, prepare), (1.25, combine), (2.5, update)):
                tasks.append((l + 4 * step + wait, functools.partial(task, step, l)))
    for _, task in sorted(tasks, key=lambda task: task[0]):
        task()


def call(kernel, outs, scalars, arrays, scratch=(), flops=0, in_kinds=None, out_kind=pltpu.VMEM):
    kinds = in_kinds or [pltpu.VMEM] * len(arrays)
    in_specs = [pl.BlockSpec(memory_space=pltpu.SMEM)] * len(scalars) + [
        pl.BlockSpec(memory_space=kind) for kind in kinds
    ]
    arrays = [
        pltpu.with_memory_space_constraint(x, kind) if kind == pltpu.HBM else x
        for x, kind in zip(arrays, kinds)
    ]
    moved = sum(4 * x.size for x in arrays) + sum(4 * x.size for x in outs)
    return pl.pallas_call(
        kernel,
        out_shape=outs,
        in_specs=in_specs,
        out_specs=[pl.BlockSpec(memory_space=out_kind)] * len(outs),
        scratch_shapes=scratch,
        compiler_params=pltpu.CompilerParams(vmem_limit_bytes=40 * 1024 * 1024),
        cost_estimate=pl.CostEstimate(flops=flops, bytes_accessed=moved, transcendentals=0),
    )(*scalars, *arrays)


def coupling_tables(coupling, slot_term, chaos):
    bf16 = jnp.bfloat16
    slots = slot_term.shape[0]
    by_source = slot_term.reshape(chaos, -1)
    slot_term = jnp.concatenate(
        [
            by_source[c, slot : slot + number]
            for c, slot, number, _ in slot_parts(slots // chaos, chaos)
        ]
    )
    raising = (slot_term[None, None, :] == coupling[:, :, 0:1]).astype(bf16)
    lowering = (slot_term[None, None, :] == coupling[:, :, 1:2]).astype(bf16)
    weighted = raising * coupling[:, :, 2:3].astype(bf16)
    matrices = jnp.einsum(
        "kps,kpr->ksr", weighted, lowering, preferred_element_type=jnp.float32
    ) + jnp.einsum("kps,kpr->ksr", lowering, raising, preferred_element_type=jnp.float32)
    spare = -slots % 16
    matrices = jnp.pad(matrices.astype(bf16), ((0, 0), (0, 0), (0, spare)))
    matrices = matrices.reshape(-1, slots // 8, 8, slots + spare).transpose(1, 0, 2, 3)
    matrices = matrices.reshape(-1, slots + spare)
    degree = jnp.sum(weighted.astype(jnp.float32), axis=1)
    factorial = jnp.where(degree > 2.5, 6.0, jnp.where(degree > 1.5, 2.0, 1.0))
    scale = jnp.sqrt(jnp.prod(factorial, axis=0))
    occupied = (slot_term >= 0).astype(jnp.float32)
    spread = jnp.ones((1, LANES), jnp.float32)
    return (
        jnp.concatenate([matrices, matrices], axis=1),
        (occupied * scale)[:, None] * spread,
        (occupied / scale)[:, None] * spread,
    )


def local_by_cells(source_chaos_terms, mean_conductivity, mode_shapes, coupling, slot_term, bounds):
    own, thick, cells = source_chaos_terms.shape
    chaos, spaces = lax.axis_size("chaos"), lax.axis_size("space")
    devices = chaos * spaces
    slots = own * chaos
    layers = thick * spaces
    columns = cells // LANES
    pieces = OWN_TILES * thick
    blocks = [block_of(device, spaces) for device in range(devices)]
    f32 = jnp.float32

    def shape(*sizes):
        return jax.ShapeDtypeStruct(sizes, f32)

    mix, weight, unweight = coupling_tables(coupling, slot_term, chaos)
    midpoint = 0.5 * (bounds[1] + bounds[0])
    half_span = 0.5 * (bounds[1] - bounds[0])
    sigma_one = midpoint / half_span
    rho_now = 1.0 / sigma_one
    scales = [1.0 / midpoint]
    for _ in range(ITERS - 1):
        rho_next = 1.0 / (2.0 * sigma_one - rho_now)
        scales += [rho_next * rho_now, 2.0 * rho_next / half_span]
        rho_now = rho_next
    scales = jnp.stack(scales)

    def by_columns(field):
        tiled = field.reshape(*field.shape[:-2], thick, columns, LANES)
        return jnp.swapaxes(tiled, -3, -2)

    scattered = call(
        functools.partial(scatter_kernel, blocks),
        [shape(devices, own, pieces, LANES)],
        [],
        [by_columns(source_chaos_terms).reshape(own, devices, pieces, LANES)],
        [pltpu.VMEM((own, devices, pieces, LANES), f32), pltpu.SemaphoreType.DMA((4,))],
        in_kinds=[pltpu.HBM],
    )[0]
    gathered = lax.all_to_all(scattered, BOTH, 0, 0, tiled=True).reshape(-1, LANES)

    row, column = lax.axis_index("chaos"), lax.axis_index("space")

    def block_at(space):
        return row * spaces + jnp.where(row % 2 == 0, space, spaces - 1 - space)

    block = block_at(column)
    inside = jnp.stack([block > 0, block < devices - 1]).astype(f32)
    odd = (block % 2)[None]
    modes = mode_shapes.shape[0] + 1
    steps = jnp.arange(spaces)
    picked = call(
        pick_kernel,
        [shape(modes * 3 * pieces, LANES)] * spaces,
        [block_at((column + steps) % spaces), scales],
        [
            mix,
            by_columns(mean_conductivity).reshape(-1, LANES),
            by_columns(mode_shapes).reshape(-1, LANES),
        ],
    )
    picked = [picked[0]] + [
        lax.ppermute(picked[n], "space", [(i, (i + n) % spaces) for i in range(spaces)])
        for n in range(1, spaces)
    ]
    a, b, own_b, face = call(
        functools.partial(coefficient_kernel, thick),
        [shape(modes, layers, tiles * LANES) for tiles in (FOLDED, FOLDED - 1, OWN_TILES, 2)],
        [(column - steps) % spaces],
        picked,
        [pltpu.VMEM((modes, 3 * OWN_TILES, layers, LANES), f32)],
    )

    message = shape((layers + layers // 2) * slots, LANES)
    start, to_chip, to_core = call(
        functools.partial(start_kernel, chaos, spaces),
        [shape(layers, OWN_TILES, slots, LANES), message, message],
        [odd],
        [a, weight, gathered],
    )
    place = {n: device for device, n in enumerate(blocks)}

    def swap(field, lowest):
        pairs = [(place[n], place[n + 1]) for n in range(lowest, devices - 1, 2)]
        return lax.ppermute(field, BOTH, pairs + [(b, a) for a, b in pairs])

    from_chip = swap(to_chip, 1)
    from_core = swap(to_core, 0)
    own_field = shape(layers, OWN_TILES, slots, LANES)
    own_total, own_edge = call(
        own_kernel,
        [own_field, own_field],
        [scales],
        [mix, a, own_b, start],
        flops=3000000000,
    )

    def held(tiles):
        return pltpu.VMEM((layers, tiles, slots, LANES), f32)

    sent = call(
        functools.partial(iterate_kernel, chaos, spaces),
        [shape(devices * 2 * own * pieces, LANES)],
        [scales, inside, odd],
        [mix, a, b, face, unweight, start, own_total, own_edge, from_chip, from_core],
        [
            held(FOLDED - 1),
            held(FOLDED),
            held(FOLDED - 1),
            held(FOLDED),
            held(OWN_TILES),
        ],
        flops=10000000000,
    )[0]
    sent = sent.reshape(devices, 2, own, pieces, LANES)
    received = lax.all_to_all(sent, BOTH, 0, 0, tiled=True)
    outs = call(
        functools.partial(collect_kernel, blocks),
        [shape(own, devices, pieces, LANES)] * 2,
        [],
        [received],
        [pltpu.SemaphoreType.DMA((2, devices))],
        in_kinds=[pl.ANY],
        out_kind=pltpu.HBM,
    )
    return tuple(
        jnp.transpose(out.reshape(own, columns, thick, LANES), (0, 2, 1, 3)).reshape(
            own, thick, cells
        )
        for out in outs
    )


def local(source_chaos_terms, mean_conductivity, mode_shapes, coupling, slot_term, bounds):
    own, thick, cells = source_chaos_terms.shape
    chaos, spaces = lax.axis_size("chaos"), lax.axis_size("space")
    fits = (
        thick * spaces == 8
        and cells == chaos * spaces * OWN_TILES * LANES
        and (own * chaos) % 8 == 0
        and spaces % 2 == 0
    )
    plan = local_by_cells if fits else local_by_slots
    return plan(
        source_chaos_terms, mean_conductivity, mode_shapes, coupling, slot_term, bounds
    )


def solution(mesh):
    in_specs = (
        P(("groups", "chaos"), "space", None),
        P("space", None),
        P(None, "space", None),
        P(),
        P(),
        P("groups"),
    )
    out_specs = (P(("groups", "chaos"), "space", None), P(("groups", "chaos"), "space", None))
    return jax.shard_map(local, mesh=mesh, in_specs=in_specs, out_specs=out_specs, check_vma=False)
```

```python
import functools

import jax
import jax.numpy as jnp
from jax import lax
from jax.experimental import pallas as pl
from jax.experimental.pallas import tpu as pltpu
from jax.sharding import PartitionSpec as P

NY = 64
ITERS = 3
LANES = 128
BOTH = ("chaos", "space")


full_precision = lax.Precision.HIGHEST


def with_halo(cells, sides, width):
    for axis, dim in sides:
        count = lax.axis_size(axis)
        ends = count - 1
        head = lax.slice_in_dim(cells, 0, width, axis=dim)
        tail = lax.slice_in_dim(cells, cells.shape[dim] - width, cells.shape[dim], axis=dim)
        cells = jnp.concatenate(
            [
                lax.ppermute(tail, axis, [(i, (i + 1) % count) for i in range(ends)]),
                cells,
                lax.ppermute(head, axis, [((i + 1) % count, i) for i in range(ends)]),
            ],
            axis=dim,
        )
    return cells


def mixing_matrices(coupling, slot_term):
    occupied = (slot_term >= 0).astype(jnp.float32)
    raising = (slot_term[None, None, :] == coupling[:, :, 0:1]).astype(jnp.float32)
    lowering = (slot_term[None, None, :] == coupling[:, :, 1:2]).astype(jnp.float32)
    weight = jnp.sqrt(coupling[:, :, 2].astype(jnp.float32))
    raised = jnp.einsum("kps,kp,kpr->ksr", raising, weight, lowering, precision=full_precision)
    mode_mats = raised + jnp.transpose(raised, (0, 2, 1))
    return jnp.concatenate([jnp.diag(occupied)[None], mode_mats], axis=0)


def shift_cells(values, offset, edge_mask):
    fill = jnp.zeros(values.shape[:-1] + (abs(offset),), values.dtype)
    if offset > 0:
        shifted = jnp.concatenate([values[..., offset:], fill], axis=-1)
    else:
        shifted = jnp.concatenate([fill, values[..., :offset]], axis=-1)
    return shifted * edge_mask


def diffuse(field_padded, conduct_padded):
    centre = field_padded[..., 1:-1, :]
    conduct = conduct_padded[..., 1:-1, :]
    accumulated = (
        0.5 * (conduct + conduct_padded[..., :-2, :]) * (centre - field_padded[..., :-2, :])
    )
    accumulated = accumulated + 0.5 * (conduct + conduct_padded[..., 2:, :]) * (
        centre - field_padded[..., 2:, :]
    )
    cells = centre.shape[-1]
    column_in_row = lax.iota(jnp.int32, cells) % NY
    upper_mask = (column_in_row < NY - 1).astype(centre.dtype)
    lower_mask = (column_in_row > 0).astype(centre.dtype)
    all_mask = jnp.ones((cells,), centre.dtype)
    for offset, edge_mask in ((1, upper_mask), (-1, lower_mask), (NY, all_mask), (-NY, all_mask)):
        neighbour = shift_cells(centre, offset, edge_mask)
        neighbour_conduct = shift_cells(conduct, offset, edge_mask)
        accumulated = accumulated + 0.5 * (conduct + neighbour_conduct) * (centre - neighbour)
    return accumulated


def local_by_slots(source_chaos_terms, mean_conductivity, mode_shapes, coupling, slot_term, bounds):
    slot_count = source_chaos_terms.shape[0]
    conductivity = jnp.concatenate(
        [mean_conductivity[None], mean_conductivity[None] * mode_shapes], axis=0
    )
    conduct_padded = with_halo(conductivity, (("space", 1),), 1)
    matrices = mixing_matrices(coupling, slot_term)
    first_own = lax.axis_index("chaos") * slot_count
    own_rows = lax.dynamic_slice_in_dim(matrices, first_own, slot_count, 1)
    own_terms = lax.dynamic_slice_in_dim(slot_term, first_own, slot_count, 0)
    occupied = (own_terms >= 0).astype(jnp.float32)[:, None, None]
    lower_bound = bounds[0]
    upper_bound = bounds[1]
    midpoint = 0.5 * (upper_bound + lower_bound)
    half_span = 0.5 * (upper_bound - lower_bound)
    sigma_one = midpoint / half_span
    rho_now = 1.0 / sigma_one
    residual = source_chaos_terms * occupied
    solution_field = jnp.zeros_like(residual)
    direction = residual / midpoint
    for iteration in range(ITERS):
        solution_field = solution_field + direction
        fields = jnp.einsum(
            "ksr,rzc->kszc",
            own_rows,
            lax.all_gather(direction, "chaos", axis=0, tiled=True),
            precision=full_precision,
        )
        field_padded = with_halo(fields, (("space", 2),), 1)
        diffused = diffuse(field_padded, conduct_padded[:, None])
        residual = residual - jnp.sum(diffused, axis=0)
        if iteration + 1 < ITERS:
            rho_next = 1.0 / (2.0 * sigma_one - rho_now)
            direction = rho_next * rho_now * direction + 2.0 * rho_next / half_span * residual
            rho_now = rho_next
    return (solution_field, residual)


OWN_TILES = 2
FOLDED = OWN_TILES + ITERS


def block_of(device, spaces):
    chaos, space = divmod(device, spaces)
    return chaos * spaces + (space if chaos % 2 == 0 else spaces - 1 - space)


def lane_masks(rows):
    lane = lax.broadcasted_iota(jnp.int32, (rows, LANES), 1)
    return lane < NY, lane % NY > 0, lane % NY < NY - 1


def plane_sums(tiles, masks, first=0):
    low_half, has_left, has_right = masks
    zero = jnp.zeros(tiles[0].shape, jnp.float32)
    swapped = [pltpu.roll(tile, NY, 1) for tile in tiles]
    sums = []
    for t in range(first, len(tiles) - 1):
        if t == 0:
            across = swapped[0] + jnp.where(low_half, swapped[2], swapped[1])
        elif t == 1:
            across = swapped[1] + jnp.where(low_half, swapped[0], swapped[2])
        elif t == 2:
            across = swapped[3] + jnp.where(low_half, swapped[1], swapped[0])
        else:
            across = swapped[t - 1] + swapped[t + 1]
        left = jnp.where(has_left, pltpu.roll(tiles[t], 1, 1), zero)
        right = jnp.where(has_right, pltpu.roll(tiles[t], LANES - 1, 1), zero)
        sums.append(across + (left + right))
    return sums


def neighbour_sums(read, layer, layers, count, masks, first=0):
    sums = plane_sums([read(layer, t) for t in range(count)], masks, first)
    for other in (layer - 1, layer + 1):
        if 0 <= other < layers:
            sums = [total + read(other, first + n) for n, total in enumerate(sums)]
    return sums


def split_stack(tiles, depth):
    wide = jnp.concatenate(tiles, axis=1)
    spare = depth // 2 - wide.shape[0]
    if spare:
        wide = jnp.concatenate([wide, jnp.zeros((spare, wide.shape[1]), wide.dtype)], axis=0)
    high = wide.astype(jnp.bfloat16)
    low = (wide - high.astype(jnp.float32)).astype(jnp.bfloat16)
    return jnp.concatenate([high, low], axis=0)


def lanes(t):
    return pl.ds(t * LANES, LANES)


def run_copies(copies):
    for copy in copies:
        copy.start()
    for copy in copies:
        copy.wait()


def scatter_kernel(blocks, in_ref, out_ref, held_ref, sems):
    own = in_ref.shape[0]
    parts = sems.shape[0]
    bounds = [own * n // parts for n in range(parts + 1)]
    spans = [pl.ds(a, b - a) for a, b in zip(bounds[:-1], bounds[1:])]
    copies = [
        pltpu.make_async_copy(in_ref.at[span], held_ref.at[span], sems.at[n])
        for n, span in enumerate(spans)
    ]
    for copy in copies:
        copy.start()
    for copy, span in zip(copies, spans):
        copy.wait()
        for device, block in enumerate(blocks):
            out_ref[device, span] = held_ref[span, block]


def pick_kernel(targets, scales, mix_ref, mean_ref, modes_ref, *outs):
    count, per_mode = mean_ref.shape[0], outs[0].shape[0] // (1 + modes_ref.shape[0] // mean_ref.shape[0])
    side = per_mode // 3
    last = count // side - 1
    for n, out_ref in enumerate(outs):
        block = targets[n]
        lower = jnp.where(block > 0, 1.0, 0.0)
        upper = jnp.where(block < last, 1.0, 0.0)
        before = jnp.maximum(block - 1, 0) * side
        after = jnp.minimum(block + 1, last) * side
        for k in range(out_ref.shape[0] // per_mode):
            ref, base = (mean_ref, 0) if k == 0 else (modes_ref, (k - 1) * count)
            first = k * per_mode
            out_ref[pl.ds(first, side), :] = ref[pl.ds(base + before, side), :] * lower
            out_ref[pl.ds(first + side, side), :] = ref[pl.ds(base + block * side, side), :]
            out_ref[pl.ds(first + 2 * side, side), :] = ref[pl.ds(base + after, side), :] * upper


def layer_sum(values, layer):
    layers = values.shape[0]
    zero = jnp.zeros(values.shape, jnp.float32)
    under = jnp.where(layer > 0, pltpu.roll(values, 1, 0), zero)
    over = jnp.where(layer < layers - 1, pltpu.roll(values, layers - 1, 0), zero)
    return under + over


def coefficient_kernel(thick, sources, *refs):
    *ins, a_ref, b_ref, own_b_ref, face_ref, held_ref = refs
    modes, layers, _ = a_ref.shape
    tiles = held_ref.shape[1]
    layer = lax.broadcasted_iota(jnp.int32, (layers, LANES), 0)
    masks = lane_masks(layers)
    low_half = masks[0]
    for n, in_ref in enumerate(ins):
        for k in range(modes):
            for u in range(tiles):
                held_ref[k, u, pl.ds(sources[n] * thick, thick), :] = in_ref[
                    pl.ds((k * tiles + u) * thick, thick), :
                ]
    mean = None
    for k in range(modes):
        runs = [held_ref[k, u] for u in range(tiles)]
        values = [
            runs[2],
            runs[3],
            jnp.where(low_half, runs[4], runs[1]),
            jnp.where(low_half, runs[1], runs[4]),
            jnp.where(low_half, runs[5], runs[0]),
        ]
        if k == 0:
            values = mean = [0.5 * value for value in values]
        else:
            values = [m * value for m, value in zip(mean, values)]
        sums = plane_sums(values, masks)
        for t in range(FOLDED):
            a_ref[k, :, lanes(t)] = values[t]
        for t in range(FOLDED - 1):
            b_ref[k, :, lanes(t)] = 6.0 * values[t] + (sums[t] + layer_sum(values[t], layer))
        outside = jnp.zeros((layers, LANES), jnp.float32)
        sums = plane_sums(values[:OWN_TILES] + [outside], masks)
        for t in range(OWN_TILES):
            own_b_ref[k, :, lanes(t)] = 6.0 * values[t] + (sums[t] + layer_sum(values[t], layer))
        face_ref[k, :, lanes(0)] = jnp.where(low_half, values[0], values[1])
        face_ref[k, :, lanes(1)] = pltpu.roll(values[2], NY, 1)


def collect_kernel(blocks, in_ref, *rest):
    *outs, sems = rest
    run_copies(
        [
            pltpu.make_async_copy(
                in_ref.at[device, n], out_ref.at[:, block], sems.at[n, device]
            )
            for n, out_ref in enumerate(outs)
            for device, block in enumerate(blocks)
        ]
    )


def slot_parts(own, chaos):
    whole = own // 8 * 8
    parts = [(c, 0, whole, c * whole) for c in range(chaos)]
    return parts + [
        (c, whole, own - whole, chaos * whole + c * (own - whole)) for c in range(chaos)
    ]


def start_kernel(chaos, spaces, odd, a_ref, weight_ref, in_ref, residual_ref, chip_ref, core_ref):
    upward = odd[0] > 0
    layers, tiles, slots, _ = residual_ref.shape
    own = slots // chaos
    thick = layers // spaces
    pieces = tiles * thick
    half = layers // 2
    low_half = lane_masks(slots)[0]
    weight = weight_ref[...]

    def put(place, up, down):
        rows = pl.ds(place * slots, slots)
        chip_ref[rows, :] = jnp.where(upward, up, down)
        core_ref[rows, :] = jnp.where(upward, down, up)

    for l in range(layers):
        i, z = divmod(l, thick)
        for t in range(tiles):
            rows = [
                in_ref[
                    pl.ds(
                        ((c * spaces + i) * own + slot) * pieces + t * thick + z,
                        number,
                        stride=pieces,
                    ),
                    :,
                ]
                for c, slot, number, _ in slot_parts(own, chaos)
            ]
            residual_ref[l, t] = weight * jnp.concatenate(rows, axis=0)
        put(l, residual_ref[l, 1], residual_ref[l, 0])
    for l in range(half):
        later = l + half
        put(
            layers + l,
            jnp.where(low_half, pltpu.roll(residual_ref[later, 0], NY, 1), residual_ref[l, 0]),
            jnp.where(low_half, residual_ref[l, 1], pltpu.roll(residual_ref[later, 1], NY, 1)),
        )


def mode_part(mixed, modes, k, n):
    group = 8 * (modes - 1)
    return jnp.concatenate(
        [
            mixed[row : row + 8, n * LANES : (n + 1) * LANES]
            for row in range((k - 1) * 8, mixed.shape[0], group)
        ],
        axis=0,
    )


def weighted_tiles(mixed, modes, place, beside, direct, around, a_of, b_of):
    results = []
    for t, tile in enumerate(direct):
        full = t < len(around)
        a = a_of(0, t)
        edge = a * tile
        total = b_of(0, t) * tile - a * around[t] if full else None
        for k in range(1, modes):
            a = a_of(k, t)
            part = mode_part(mixed, modes, k, place + t)
            edge = edge + a * part
            if full:
                total = total + (b_of(k, t) * part - a * mode_part(mixed, modes, k, beside + t))
        results.append((total, edge))
    return results


def own_kernel(scales, mix_ref, a_ref, b_ref, start_ref, total_ref, edge_ref):
    layers, tiles, slots, _ = start_ref.shape
    modes = a_ref.shape[0]
    masks = lane_masks(slots)
    mix = mix_ref[...]
    nothing = jnp.zeros((slots, LANES), jnp.float32)

    def read(l, t):
        return start_ref[l, t] * scales[0] if t < tiles else nothing

    def prepare(l):
        direct = [read(l, t) for t in range(tiles)]
        around = neighbour_sums(read, l, layers, tiles + 1, masks)
        mixed = jnp.dot(
            mix, split_stack(direct + around, mix.shape[1]), preferred_element_type=jnp.float32
        )
        return mixed, direct, around

    ahead = prepare(0)
    for l in range(layers):
        mixed, direct, around = ahead
        if l + 1 < layers:
            ahead = prepare(l + 1)
        results = weighted_tiles(
            mixed,
            modes,
            0,
            tiles,
            direct,
            around,
            lambda k, t: a_ref[k, l : l + 1, lanes(t)],
            lambda k, t: b_ref[k, l : l + 1, lanes(t)],
        )
        for t, (total, edge) in enumerate(results):
            total_ref[l, t] = total
            edge_ref[l, t] = edge


def iterate_kernel(
    chaos,
    spaces,
    scales,
    inside,
    odd,
    mix_ref,
    a_ref,
    b_ref,
    face_ref,
    unweight_ref,
    start_ref,
    own_total_ref,
    own_edge_ref,
    chip_ref,
    core_ref,
    sent_ref,
    r_ref,
    d_ref,
    total_ref,
    edge_ref,
    x_ref,
):
    layers, _, slots, _ = start_ref.shape
    modes = a_ref.shape[0]
    own = slots // chaos
    thick = layers // spaces
    pieces = OWN_TILES * thick
    half = layers // 2
    masks = lane_masks(slots)
    low_half = masks[0]
    mix = mix_ref[...]
    depth = mix.shape[1]
    upward = odd[0] > 0

    def message(start, size):
        chip, core = chip_ref[pl.ds(start, size), :], core_ref[pl.ds(start, size), :]
        return jnp.where(upward, core, chip), jnp.where(upward, chip, core)

    def send(field, l, t, value):
        i, z = divmod(l, thick)
        value = value * unweight_ref[...]
        for c, slot, number, row in slot_parts(own, chaos):
            first = (((c * spaces + i) * 2 + field) * own + slot) * pieces + t * thick + z
            sent_ref[pl.ds(first, number, stride=pieces), :] = value[row : row + number]

    def fold(l):
        below, above = message(l * slots, slots)
        far_below, far_above = message((layers + l % half) * slots, slots)
        if l < half:
            far = jnp.where(low_half, far_above, far_below)
        else:
            far = pltpu.roll(jnp.where(low_half, far_below, far_above), NY, 1)
        tiles = [
            start_ref[l, 0],
            start_ref[l, 1],
            jnp.where(low_half, above, below),
            jnp.where(low_half, below, above),
            far,
        ]
        for t, tile in enumerate(tiles):
            if t < FOLDED - 1:
                r_ref[l, t] = tile
            d_ref[l, t] = tile * scales[0]

    def read(l, t):
        return d_ref[l, t]

    zero = jnp.zeros((slots, LANES), jnp.float32)
    prepared = {}

    def prepare(step, l):
        count = FOLDED - step
        first = OWN_TILES if step == 0 else 0
        direct = [d_ref[l, t] for t in range(first, count)]
        around = neighbour_sums(read, l, layers, count, masks, first)
        extra = [jnp.where(low_half, d_ref[l, 0], d_ref[l, 1])] if step == 0 else []
        mixed = jnp.dot(
            mix, split_stack(direct + extra + around, depth), preferred_element_type=jnp.float32
        )
        prepared[step, l] = (mixed, direct, extra, around)

    def combine(step, l):
        first = OWN_TILES if step == 0 else 0
        mixed, direct, extra, around = prepared.pop((step, l))
        results = weighted_tiles(
            mixed,
            modes,
            0,
            len(direct) + len(extra),
            direct,
            around,
            lambda k, t: a_ref[k, l : l + 1, lanes(first + t)],
            lambda k, t: b_ref[k, l : l + 1, lanes(first + t)],
        )
        for t, (total, edge) in enumerate(results):
            edge_ref[l, first + t] = edge
            if total is not None:
                total_ref[l, first + t] = total
        if step > 0:
            return
        own_face = face_ref[0, l : l + 1, lanes(0)]
        other_face = face_ref[0, l : l + 1, lanes(1)]
        part = other_face * extra[0] - own_face * pltpu.roll(direct[0], NY, 1)
        for k in range(1, modes):
            own_face = face_ref[k, l : l + 1, lanes(0)]
            other_face = face_ref[k, l : l + 1, lanes(1)]
            own_mixed = mode_part(mixed, modes, k, len(direct))
            other_mixed = pltpu.roll(mode_part(mixed, modes, k, 0), NY, 1)
            part = part + (other_face * own_mixed - own_face * other_mixed)
        total_ref[l, 0] = own_total_ref[l, 0] + jnp.where(low_half, part, zero)
        total_ref[l, 1] = own_total_ref[l, 1] + jnp.where(low_half, zero, part)

    def update(step, l):
        count = FOLDED - step

        def read_edge(l, t):
            return own_edge_ref[l, t] if step == 0 and t < OWN_TILES else edge_ref[l, t]

        spread = neighbour_sums(read_edge, l, layers, count, masks)
        for t in range(count - 1):
            diffused = total_ref[l, t] - spread[t]
            if t >= OWN_TILES:
                lower, upper = inside[(t + 1) % 2], inside[t % 2]
                diffused = diffused * jnp.where(low_half, lower, upper)
            residual = r_ref[l, t] - diffused
            if step == ITERS - 1:
                send(1, l, t, residual)
                continue
            r_ref[l, t] = residual
            old = d_ref[l, t]
            direction = scales[1 + 2 * step] * old + scales[2 + 2 * step] * residual
            d_ref[l, t] = direction
            if t < OWN_TILES:
                value = (old if step == 0 else x_ref[l, t]) + direction
                if step == ITERS - 2:
                    send(0, l, t, value)
                else:
                    x_ref[l, t] = value

    tasks = []
    for l in range(layers):
        tasks.append((l - 1.5, lambda l=l: fold(l)))
        for step in range(ITERS):
            for wait, task in ((0, prepare), (1.25, combine), (2.5, update)):
                tasks.append((l + 4 * step + wait, functools.partial(task, step, l)))
    for _, task in sorted(tasks, key=lambda task: task[0]):
        task()


def call(
    kernel, outs, scalars, arrays, scratch=(), flops=0, in_kinds=None, out_kind=pltpu.VMEM, mebi=8
):
    kinds = in_kinds or [pltpu.VMEM] * len(arrays)
    in_specs = [pl.BlockSpec(memory_space=pltpu.SMEM)] * len(scalars) + [
        pl.BlockSpec(memory_space=kind) for kind in kinds
    ]
    arrays = [
        pltpu.with_memory_space_constraint(x, kind) if kind == pltpu.HBM else x
        for x, kind in zip(arrays, kinds)
    ]
    moved = sum(4 * x.size for x in arrays) + sum(4 * x.size for x in outs)
    return pl.pallas_call(
        kernel,
        out_shape=outs,
        in_specs=in_specs,
        out_specs=[pl.BlockSpec(memory_space=out_kind)] * len(outs),
        scratch_shapes=scratch,
        compiler_params=pltpu.CompilerParams(vmem_limit_bytes=mebi * 1024 * 1024),
        cost_estimate=pl.CostEstimate(flops=flops, bytes_accessed=moved, transcendentals=0),
    )(*scalars, *arrays)


def coupling_tables(coupling, slot_term, chaos):
    bf16 = jnp.bfloat16
    slots = slot_term.shape[0]
    by_source = slot_term.reshape(chaos, -1)
    slot_term = jnp.concatenate(
        [
            by_source[c, slot : slot + number]
            for c, slot, number, _ in slot_parts(slots // chaos, chaos)
        ]
    )
    raising = (slot_term[None, None, :] == coupling[:, :, 0:1]).astype(bf16)
    lowering = (slot_term[None, None, :] == coupling[:, :, 1:2]).astype(bf16)
    weighted = raising * coupling[:, :, 2:3].astype(bf16)
    matrices = jnp.einsum(
        "kps,kpr->ksr", weighted, lowering, preferred_element_type=jnp.float32
    ) + jnp.einsum("kps,kpr->ksr", lowering, raising, preferred_element_type=jnp.float32)
    spare = -slots % 16
    matrices = jnp.pad(matrices.astype(bf16), ((0, 0), (0, 0), (0, spare)))
    matrices = matrices.reshape(-1, slots // 8, 8, slots + spare).transpose(1, 0, 2, 3)
    matrices = matrices.reshape(-1, slots + spare)
    degree = jnp.sum(weighted.astype(jnp.float32), axis=1)
    factorial = jnp.where(degree > 2.5, 6.0, jnp.where(degree > 1.5, 2.0, 1.0))
    scale = jnp.sqrt(jnp.prod(factorial, axis=0))
    occupied = (slot_term >= 0).astype(jnp.float32)
    spread = jnp.ones((1, LANES), jnp.float32)
    return (
        jnp.concatenate([matrices, matrices], axis=1),
        (occupied * scale)[:, None] * spread,
        (occupied / scale)[:, None] * spread,
    )


def local_by_cells(source_chaos_terms, mean_conductivity, mode_shapes, coupling, slot_term, bounds):
    own, thick, cells = source_chaos_terms.shape
    chaos, spaces = lax.axis_size("chaos"), lax.axis_size("space")
    devices = chaos * spaces
    slots = own * chaos
    layers = thick * spaces
    columns = cells // LANES
    pieces = OWN_TILES * thick
    blocks = [block_of(device, spaces) for device in range(devices)]
    f32 = jnp.float32

    def shape(*sizes):
        return jax.ShapeDtypeStruct(sizes, f32)

    mix, weight, unweight = coupling_tables(coupling, slot_term, chaos)
    midpoint = 0.5 * (bounds[1] + bounds[0])
    half_span = 0.5 * (bounds[1] - bounds[0])
    sigma_one = midpoint / half_span
    rho_now = 1.0 / sigma_one
    scales = [1.0 / midpoint]
    for _ in range(ITERS - 1):
        rho_next = 1.0 / (2.0 * sigma_one - rho_now)
        scales += [rho_next * rho_now, 2.0 * rho_next / half_span]
        rho_now = rho_next
    scales = jnp.stack(scales)

    def by_columns(field):
        tiled = field.reshape(*field.shape[:-2], thick, columns, LANES)
        return jnp.swapaxes(tiled, -3, -2)

    scattered = call(
        functools.partial(scatter_kernel, blocks),
        [shape(devices, own, pieces, LANES)],
        [],
        [by_columns(source_chaos_terms).reshape(own, devices, pieces, LANES)],
        [pltpu.VMEM((own, devices, pieces, LANES), f32), pltpu.SemaphoreType.DMA((4,))],
        in_kinds=[pltpu.HBM],
    )[0]
    gathered = lax.all_to_all(scattered, BOTH, 0, 0, tiled=True).reshape(-1, LANES)

    row, column = lax.axis_index("chaos"), lax.axis_index("space")

    def block_at(space):
        return row * spaces + jnp.where(row % 2 == 0, space, spaces - 1 - space)

    block = block_at(column)
    inside = jnp.stack([block > 0, block < devices - 1]).astype(f32)
    odd = (block % 2)[None]
    modes = mode_shapes.shape[0] + 1
    steps = jnp.arange(spaces)
    picked = call(
        pick_kernel,
        [shape(modes * 3 * pieces, LANES)] * spaces,
        [block_at((column + steps) % spaces), scales],
        [
            mix,
            by_columns(mean_conductivity).reshape(-1, LANES),
            by_columns(mode_shapes).reshape(-1, LANES),
        ],
    )
    picked = [picked[0]] + [
        lax.ppermute(picked[n], "space", [(i, (i + n) % spaces) for i in range(spaces)])
        for n in range(1, spaces)
    ]
    a, b, own_b, face = call(
        functools.partial(coefficient_kernel, thick),
        [shape(modes, layers, tiles * LANES) for tiles in (FOLDED, FOLDED - 1, OWN_TILES, 2)],
        [(column - steps) % spaces],
        picked,
        [pltpu.VMEM((modes, 3 * OWN_TILES, layers, LANES), f32)],
    )

    message = shape((layers + layers // 2) * slots, LANES)
    start, to_chip, to_core = call(
        functools.partial(start_kernel, chaos, spaces),
        [shape(layers, OWN_TILES, slots, LANES), message, message],
        [odd],
        [a, weight, gathered],
    )
    place = {n: device for device, n in enumerate(blocks)}

    def swap(field, lowest):
        pairs = [(place[n], place[n + 1]) for n in range(lowest, devices - 1, 2)]
        return lax.ppermute(field, BOTH, pairs + [(b, a) for a, b in pairs])

    from_chip = swap(to_chip, 1)
    from_core = swap(to_core, 0)
    own_field = shape(layers, OWN_TILES, slots, LANES)
    own_total, own_edge = call(
        own_kernel,
        [own_field, own_field],
        [scales],
        [mix, a, own_b, start],
        flops=3000000000,
        mebi=16,
    )

    def held(tiles):
        return pltpu.VMEM((layers, tiles, slots, LANES), f32)

    sent = call(
        functools.partial(iterate_kernel, chaos, spaces),
        [shape(devices * 2 * own * pieces, LANES)],
        [scales, inside, odd],
        [mix, a, b, face, unweight, start, own_total, own_edge, from_chip, from_core],
        [
            held(FOLDED - 1),
            held(FOLDED),
            held(FOLDED - 1),
            held(FOLDED),
            held(OWN_TILES),
        ],
        flops=10000000000,
        mebi=24,
    )[0]
    sent = sent.reshape(devices, 2, own, pieces, LANES)
    received = lax.all_to_all(sent, BOTH, 0, 0, tiled=True)
    outs = call(
        functools.partial(collect_kernel, blocks),
        [shape(own, devices, pieces, LANES)] * 2,
        [],
        [received],
        [pltpu.SemaphoreType.DMA((2, devices))],
        in_kinds=[pl.ANY],
        out_kind=pltpu.HBM,
    )
    return tuple(
        jnp.transpose(out.reshape(own, columns, thick, LANES), (0, 2, 1, 3)).reshape(
            own, thick, cells
        )
        for out in outs
    )


def local(source_chaos_terms, mean_conductivity, mode_shapes, coupling, slot_term, bounds):
    own, thick, cells = source_chaos_terms.shape
    chaos, spaces = lax.axis_size("chaos"), lax.axis_size("space")
    fits = (
        thick * spaces == 8
        and cells == chaos * spaces * OWN_TILES * LANES
        and (own * chaos) % 8 == 0
        and spaces % 2 == 0
    )
    plan = local_by_cells if fits else local_by_slots
    return plan(
        source_chaos_terms, mean_conductivity, mode_shapes, coupling, slot_term, bounds
    )


def solution(mesh):
    in_specs = (
        P(("groups", "chaos"), "space", None),
        P("space", None),
        P(None, "space", None),
        P(),
        P(),
        P("groups"),
    )
    out_specs = (P(("groups", "chaos"), "space", None), P(("groups", "chaos"), "space", None))
    return jax.shard_map(local, mesh=mesh, in_specs=in_specs, out_specs=out_specs, check_vma=False)
```

```python
import functools

import jax
import jax.numpy as jnp
from jax import lax
from jax.experimental import pallas as pl
from jax.experimental.pallas import tpu as pltpu
from jax.sharding import PartitionSpec as P

NY = 64
ITERS = 3
LANES = 128
BOTH = ("chaos", "space")


full_precision = lax.Precision.HIGHEST


def with_halo(cells, sides, width):
    for axis, dim in sides:
        count = lax.axis_size(axis)
        ends = count - 1
        head = lax.slice_in_dim(cells, 0, width, axis=dim)
        tail = lax.slice_in_dim(cells, cells.shape[dim] - width, cells.shape[dim], axis=dim)
        cells = jnp.concatenate(
            [
                lax.ppermute(tail, axis, [(i, (i + 1) % count) for i in range(ends)]),
                cells,
                lax.ppermute(head, axis, [((i + 1) % count, i) for i in range(ends)]),
            ],
            axis=dim,
        )
    return cells


def mixing_matrices(coupling, slot_term):
    occupied = (slot_term >= 0).astype(jnp.float32)
    raising = (slot_term[None, None, :] == coupling[:, :, 0:1]).astype(jnp.float32)
    lowering = (slot_term[None, None, :] == coupling[:, :, 1:2]).astype(jnp.float32)
    weight = jnp.sqrt(coupling[:, :, 2].astype(jnp.float32))
    raised = jnp.einsum("kps,kp,kpr->ksr", raising, weight, lowering, precision=full_precision)
    mode_mats = raised + jnp.transpose(raised, (0, 2, 1))
    return jnp.concatenate([jnp.diag(occupied)[None], mode_mats], axis=0)


def shift_cells(values, offset, edge_mask):
    fill = jnp.zeros(values.shape[:-1] + (abs(offset),), values.dtype)
    if offset > 0:
        shifted = jnp.concatenate([values[..., offset:], fill], axis=-1)
    else:
        shifted = jnp.concatenate([fill, values[..., :offset]], axis=-1)
    return shifted * edge_mask


def diffuse(field_padded, conduct_padded):
    centre = field_padded[..., 1:-1, :]
    conduct = conduct_padded[..., 1:-1, :]
    accumulated = (
        0.5 * (conduct + conduct_padded[..., :-2, :]) * (centre - field_padded[..., :-2, :])
    )
    accumulated = accumulated + 0.5 * (conduct + conduct_padded[..., 2:, :]) * (
        centre - field_padded[..., 2:, :]
    )
    cells = centre.shape[-1]
    column_in_row = lax.iota(jnp.int32, cells) % NY
    upper_mask = (column_in_row < NY - 1).astype(centre.dtype)
    lower_mask = (column_in_row > 0).astype(centre.dtype)
    all_mask = jnp.ones((cells,), centre.dtype)
    for offset, edge_mask in ((1, upper_mask), (-1, lower_mask), (NY, all_mask), (-NY, all_mask)):
        neighbour = shift_cells(centre, offset, edge_mask)
        neighbour_conduct = shift_cells(conduct, offset, edge_mask)
        accumulated = accumulated + 0.5 * (conduct + neighbour_conduct) * (centre - neighbour)
    return accumulated


def local_by_slots(source_chaos_terms, mean_conductivity, mode_shapes, coupling, slot_term, bounds):
    slot_count = source_chaos_terms.shape[0]
    conductivity = jnp.concatenate(
        [mean_conductivity[None], mean_conductivity[None] * mode_shapes], axis=0
    )
    conduct_padded = with_halo(conductivity, (("space", 1),), 1)
    matrices = mixing_matrices(coupling, slot_term)
    first_own = lax.axis_index("chaos") * slot_count
    own_rows = lax.dynamic_slice_in_dim(matrices, first_own, slot_count, 1)
    own_terms = lax.dynamic_slice_in_dim(slot_term, first_own, slot_count, 0)
    occupied = (own_terms >= 0).astype(jnp.float32)[:, None, None]
    lower_bound = bounds[0]
    upper_bound = bounds[1]
    midpoint = 0.5 * (upper_bound + lower_bound)
    half_span = 0.5 * (upper_bound - lower_bound)
    sigma_one = midpoint / half_span
    rho_now = 1.0 / sigma_one
    residual = source_chaos_terms * occupied
    solution_field = jnp.zeros_like(residual)
    direction = residual / midpoint
    for iteration in range(ITERS):
        solution_field = solution_field + direction
        fields = jnp.einsum(
            "ksr,rzc->kszc",
            own_rows,
            lax.all_gather(direction, "chaos", axis=0, tiled=True),
            precision=full_precision,
        )
        field_padded = with_halo(fields, (("space", 2),), 1)
        diffused = diffuse(field_padded, conduct_padded[:, None])
        residual = residual - jnp.sum(diffused, axis=0)
        if iteration + 1 < ITERS:
            rho_next = 1.0 / (2.0 * sigma_one - rho_now)
            direction = rho_next * rho_now * direction + 2.0 * rho_next / half_span * residual
            rho_now = rho_next
    return (solution_field, residual)


OWN_TILES = 2
FOLDED = OWN_TILES + ITERS


def block_of(device, spaces):
    chaos, space = divmod(device, spaces)
    return chaos * spaces + (space if chaos % 2 == 0 else spaces - 1 - space)


def lane_masks(rows):
    lane = lax.broadcasted_iota(jnp.int32, (rows, LANES), 1)
    return lane < NY, lane % NY > 0, lane % NY < NY - 1


def plane_sums(tiles, masks, first=0):
    low_half, has_left, has_right = masks
    zero = jnp.zeros(tiles[0].shape, jnp.float32)
    swapped = [pltpu.roll(tile, NY, 1) for tile in tiles]
    sums = []
    for t in range(first, len(tiles) - 1):
        if t == 0:
            across = swapped[0] + jnp.where(low_half, swapped[2], swapped[1])
        elif t == 1:
            across = swapped[1] + jnp.where(low_half, swapped[0], swapped[2])
        elif t == 2:
            across = swapped[3] + jnp.where(low_half, swapped[1], swapped[0])
        else:
            across = swapped[t - 1] + swapped[t + 1]
        left = jnp.where(has_left, pltpu.roll(tiles[t], 1, 1), zero)
        right = jnp.where(has_right, pltpu.roll(tiles[t], LANES - 1, 1), zero)
        sums.append(across + (left + right))
    return sums


def neighbour_sums(read, layer, layers, count, masks, first=0):
    sums = plane_sums([read(layer, t) for t in range(count)], masks, first)
    for other in (layer - 1, layer + 1):
        if 0 <= other < layers:
            sums = [total + read(other, first + n) for n, total in enumerate(sums)]
    return sums


def split_stack(tiles, depth):
    wide = jnp.concatenate(tiles, axis=1)
    spare = depth // 2 - wide.shape[0]
    if spare:
        wide = jnp.concatenate([wide, jnp.zeros((spare, wide.shape[1]), wide.dtype)], axis=0)
    high = wide.astype(jnp.bfloat16)
    low = (wide - high.astype(jnp.float32)).astype(jnp.bfloat16)
    return jnp.concatenate([high, low], axis=0)


def lanes(t):
    return pl.ds(t * LANES, LANES)


def run_copies(copies):
    for copy in copies:
        copy.start()
    for copy in copies:
        copy.wait()


def scatter_kernel(blocks, in_ref, out_ref, sems):
    copies = [
        pltpu.make_async_copy(in_ref.at[:, block], out_ref.at[device], sems.at[device])
        for device, block in enumerate(blocks)
    ]
    for copy in copies:
        copy.start()
    for copy in copies:
        copy.wait()


def pick_kernel(targets, scales, mix_ref, mean_ref, modes_ref, *outs):
    count, per_mode = mean_ref.shape[0], outs[0].shape[0] // (1 + modes_ref.shape[0] // mean_ref.shape[0])
    side = per_mode // 3
    last = count // side - 1
    for n, out_ref in enumerate(outs):
        block = targets[n]
        lower = jnp.where(block > 0, 1.0, 0.0)
        upper = jnp.where(block < last, 1.0, 0.0)
        before = jnp.maximum(block - 1, 0) * side
        after = jnp.minimum(block + 1, last) * side
        for k in range(out_ref.shape[0] // per_mode):
            ref, base = (mean_ref, 0) if k == 0 else (modes_ref, (k - 1) * count)
            first = k * per_mode
            out_ref[pl.ds(first, side), :] = ref[pl.ds(base + before, side), :] * lower
            out_ref[pl.ds(first + side, side), :] = ref[pl.ds(base + block * side, side), :]
            out_ref[pl.ds(first + 2 * side, side), :] = ref[pl.ds(base + after, side), :] * upper


def layer_sum(values, layer):
    layers = values.shape[0]
    zero = jnp.zeros(values.shape, jnp.float32)
    under = jnp.where(layer > 0, pltpu.roll(values, 1, 0), zero)
    over = jnp.where(layer < layers - 1, pltpu.roll(values, layers - 1, 0), zero)
    return under + over


def coefficient_kernel(thick, sources, *refs):
    *ins, a_ref, b_ref, face_ref, held_ref = refs
    modes, layers, _ = a_ref.shape
    tiles = held_ref.shape[1]
    layer = lax.broadcasted_iota(jnp.int32, (layers, LANES), 0)
    masks = lane_masks(layers)
    low_half = masks[0]
    for n, in_ref in enumerate(ins):
        for k in range(modes):
            for u in range(tiles):
                held_ref[k, u, pl.ds(sources[n] * thick, thick), :] = in_ref[
                    pl.ds((k * tiles + u) * thick, thick), :
                ]
    mean = None
    for k in range(modes):
        runs = [held_ref[k, u] for u in range(tiles)]
        values = [
            runs[2],
            runs[3],
            jnp.where(low_half, runs[4], runs[1]),
            jnp.where(low_half, runs[1], runs[4]),
            jnp.where(low_half, runs[5], runs[0]),
        ]
        if k == 0:
            values = mean = [0.5 * value for value in values]
        else:
            values = [m * value for m, value in zip(mean, values)]
        sums = plane_sums(values, masks)
        for t in range(FOLDED):
            a_ref[k, :, lanes(t)] = values[t]
        for t in range(FOLDED - 1):
            b_ref[k, :, lanes(t)] = 6.0 * values[t] + (sums[t] + layer_sum(values[t], layer))
        face_ref[k] = pltpu.roll(jnp.where(low_half, values[0], values[1]), NY, 1)


def collect_kernel(blocks, in_ref, *rest):
    *outs, sems = rest
    run_copies(
        [
            pltpu.make_async_copy(
                in_ref.at[device, n], out_ref.at[:, block], sems.at[n, device]
            )
            for n, out_ref in enumerate(outs)
            for device, block in enumerate(blocks)
        ]
    )


def slot_parts(own, chaos):
    whole = own // 8 * 8
    parts = [(c, 0, whole, c * whole) for c in range(chaos)]
    return parts + [
        (c, whole, own - whole, chaos * whole + c * (own - whole)) for c in range(chaos)
    ]


def start_kernel(chaos, spaces, odd, a_ref, weight_ref, in_ref, residual_ref, chip_ref, core_ref):
    upward = odd[0] > 0
    layers, tiles, slots, _ = residual_ref.shape
    own = slots // chaos
    thick = layers // spaces
    pieces = tiles * thick
    half = layers // 2
    low_half = lane_masks(slots)[0]
    weight = weight_ref[...]

    def put(place, up, down):
        rows = pl.ds(place * slots, slots)
        chip_ref[rows, :] = jnp.where(upward, up, down)
        core_ref[rows, :] = jnp.where(upward, down, up)

    for l in range(layers):
        i, z = divmod(l, thick)
        for t in range(tiles):
            rows = [
                in_ref[
                    pl.ds(
                        ((c * spaces + i) * own + slot) * pieces + t * thick + z,
                        number,
                        stride=pieces,
                    ),
                    :,
                ]
                for c, slot, number, _ in slot_parts(own, chaos)
            ]
            residual_ref[l, t] = weight * jnp.concatenate(rows, axis=0)
        put(l, residual_ref[l, 1], residual_ref[l, 0])
    for l in range(half):
        later = l + half
        put(
            layers + l,
            jnp.where(low_half, pltpu.roll(residual_ref[later, 0], NY, 1), residual_ref[l, 0]),
            jnp.where(low_half, residual_ref[l, 1], pltpu.roll(residual_ref[later, 1], NY, 1)),
        )


def mode_part(mixed, modes, k, n):
    group = 8 * (modes - 1)
    return jnp.concatenate(
        [
            mixed[row : row + 8, n * LANES : (n + 1) * LANES]
            for row in range((k - 1) * 8, mixed.shape[0], group)
        ],
        axis=0,
    )


def weighted_tiles(mixed, modes, place, beside, direct, around, a_of, b_of):
    results = []
    for t, tile in enumerate(direct):
        full = t < len(around)
        a = a_of(0, t)
        edge = a * tile
        total = b_of(0, t) * tile - a * around[t] if full else None
        for k in range(1, modes):
            a = a_of(k, t)
            part = mode_part(mixed, modes, k, place + t)
            edge = edge + a * part
            if full:
                total = total + (b_of(k, t) * part - a * mode_part(mixed, modes, k, beside + t))
        results.append((total, edge))
    return results


def own_kernel(scales, mix_ref, a_ref, b_ref, start_ref, total_ref, edge_ref):
    layers, tiles, slots, _ = start_ref.shape
    modes = a_ref.shape[0]
    masks = lane_masks(slots)
    mix = mix_ref[...]
    nothing = jnp.zeros((slots, LANES), jnp.float32)

    def read(l, t):
        return start_ref[l, t] * scales[0] if t < tiles else nothing

    def prepare(l):
        direct = [read(l, t) for t in range(tiles)]
        around = neighbour_sums(read, l, layers, tiles + 1, masks)
        mixed = jnp.dot(
            mix, split_stack(direct + around, mix.shape[1]), preferred_element_type=jnp.float32
        )
        return mixed, direct, around

    ahead = prepare(0)
    for l in range(layers):
        mixed, direct, around = ahead
        if l + 1 < layers:
            ahead = prepare(l + 1)
        results = weighted_tiles(
            mixed,
            modes,
            0,
            tiles,
            direct,
            around,
            lambda k, t: a_ref[k, l : l + 1, lanes(t)],
            lambda k, t: b_ref[k, l : l + 1, lanes(t)],
        )
        for t, (total, edge) in enumerate(results):
            total_ref[l, t] = total
            edge_ref[l, t] = edge


def iterate_kernel(
    chaos,
    spaces,
    scales,
    inside,
    odd,
    mix_ref,
    a_ref,
    b_ref,
    face_ref,
    unweight_ref,
    start_ref,
    own_total_ref,
    own_edge_ref,
    chip_ref,
    core_ref,
    sent_ref,
    r_ref,
    d_ref,
    total_ref,
    edge_ref,
    x_ref,
):
    layers, _, slots, _ = start_ref.shape
    modes = a_ref.shape[0]
    own = slots // chaos
    thick = layers // spaces
    pieces = OWN_TILES * thick
    half = layers // 2
    masks = lane_masks(slots)
    low_half = masks[0]
    mix = mix_ref[...]
    depth = mix.shape[1]
    upward = odd[0] > 0

    def message(start, size):
        chip, core = chip_ref[pl.ds(start, size), :], core_ref[pl.ds(start, size), :]
        return jnp.where(upward, core, chip), jnp.where(upward, chip, core)

    def send(field, l, t, value):
        i, z = divmod(l, thick)
        value = value * unweight_ref[...]
        for c, slot, number, row in slot_parts(own, chaos):
            first = (((c * spaces + i) * 2 + field) * own + slot) * pieces + t * thick + z
            sent_ref[pl.ds(first, number, stride=pieces), :] = value[row : row + number]

    def fold(l):
        below, above = message(l * slots, slots)
        far_below, far_above = message((layers + l % half) * slots, slots)
        if l < half:
            far = jnp.where(low_half, far_above, far_below)
        else:
            far = pltpu.roll(jnp.where(low_half, far_below, far_above), NY, 1)
        tiles = [
            start_ref[l, 0],
            start_ref[l, 1],
            jnp.where(low_half, above, below),
            jnp.where(low_half, below, above),
            far,
        ]
        for t, tile in enumerate(tiles):
            if t < FOLDED - 1:
                r_ref[l, t] = tile
            d_ref[l, t] = tile * scales[0]

    def read(l, t):
        return d_ref[l, t]

    zero = jnp.zeros((slots, LANES), jnp.float32)
    prepared = {}

    def prepare(step, l):
        count = FOLDED - step
        first = OWN_TILES if step == 0 else 0
        direct = [d_ref[l, t] for t in range(first, count)]
        around = neighbour_sums(read, l, layers, count, masks, first)
        mixed = jnp.dot(
            mix, split_stack(direct + around, depth), preferred_element_type=jnp.float32
        )
        prepared[step, l] = (mixed, direct, around)

    def combine(step, l):
        first = OWN_TILES if step == 0 else 0
        mixed, direct, around = prepared.pop((step, l))
        results = weighted_tiles(
            mixed,
            modes,
            0,
            len(direct),
            direct,
            around,
            lambda k, t: a_ref[k, l : l + 1, lanes(first + t)],
            lambda k, t: b_ref[k, l : l + 1, lanes(first + t)],
        )
        for t, (total, edge) in enumerate(results):
            edge_ref[l, first + t] = edge
            if total is not None:
                total_ref[l, first + t] = total
        if step > 0:
            return
        part = face_ref[0, l : l + 1, :] * direct[0]
        for k in range(1, modes):
            part = part + face_ref[k, l : l + 1, :] * mode_part(mixed, modes, k, 0)
        part = pltpu.roll(part, NY, 1)
        total_ref[l, 0] = own_total_ref[l, 0] - jnp.where(low_half, part, zero)
        total_ref[l, 1] = own_total_ref[l, 1] - jnp.where(low_half, zero, part)

    def update(step, l):
        count = FOLDED - step

        def read_edge(l, t):
            return own_edge_ref[l, t] if step == 0 and t < OWN_TILES else edge_ref[l, t]

        spread = neighbour_sums(read_edge, l, layers, count, masks)
        for t in range(count - 1):
            diffused = total_ref[l, t] - spread[t]
            if t >= OWN_TILES:
                lower, upper = inside[(t + 1) % 2], inside[t % 2]
                diffused = diffused * jnp.where(low_half, lower, upper)
            residual = r_ref[l, t] - diffused
            if step == ITERS - 1:
                send(1, l, t, residual)
                continue
            r_ref[l, t] = residual
            old = d_ref[l, t]
            direction = scales[1 + 2 * step] * old + scales[2 + 2 * step] * residual
            d_ref[l, t] = direction
            if t < OWN_TILES:
                value = (old if step == 0 else x_ref[l, t]) + direction
                if step == ITERS - 2:
                    send(0, l, t, value)
                else:
                    x_ref[l, t] = value

    tasks = []
    for l in range(layers):
        tasks.append((l - 1.5, lambda l=l: fold(l)))
        for step in range(ITERS):
            for wait, task in ((0, prepare), (1.25, combine), (2.5, update)):
                tasks.append((l + 4 * step + wait, functools.partial(task, step, l)))
    for _, task in sorted(tasks, key=lambda task: task[0]):
        task()


def call(
    kernel, outs, scalars, arrays, scratch=(), flops=0, in_kinds=None, out_kind=pltpu.VMEM, mebi=8
):
    kinds = in_kinds or [pltpu.VMEM] * len(arrays)
    in_specs = [pl.BlockSpec(memory_space=pltpu.SMEM)] * len(scalars) + [
        pl.BlockSpec(memory_space=kind) for kind in kinds
    ]
    arrays = [
        pltpu.with_memory_space_constraint(x, kind) if kind == pltpu.HBM else x
        for x, kind in zip(arrays, kinds)
    ]
    moved = sum(4 * x.size for x in arrays) + sum(4 * x.size for x in outs)
    return pl.pallas_call(
        kernel,
        out_shape=outs,
        in_specs=in_specs,
        out_specs=[pl.BlockSpec(memory_space=out_kind)] * len(outs),
        scratch_shapes=scratch,
        compiler_params=pltpu.CompilerParams(vmem_limit_bytes=mebi * 1024 * 1024),
        cost_estimate=pl.CostEstimate(flops=flops, bytes_accessed=moved, transcendentals=0),
    )(*scalars, *arrays)


def coupling_tables(coupling, slot_term, chaos):
    bf16 = jnp.bfloat16
    slots = slot_term.shape[0]
    by_source = slot_term.reshape(chaos, -1)
    slot_term = jnp.concatenate(
        [
            by_source[c, slot : slot + number]
            for c, slot, number, _ in slot_parts(slots // chaos, chaos)
        ]
    )
    raising = (slot_term[None, None, :] == coupling[:, :, 0:1]).astype(bf16)
    lowering = (slot_term[None, None, :] == coupling[:, :, 1:2]).astype(bf16)
    weighted = raising * coupling[:, :, 2:3].astype(bf16)
    matrices = jnp.einsum(
        "kps,kpr->ksr", weighted, lowering, preferred_element_type=jnp.float32
    ) + jnp.einsum("kps,kpr->ksr", lowering, raising, preferred_element_type=jnp.float32)
    spare = -slots % 16
    matrices = jnp.pad(matrices.astype(bf16), ((0, 0), (0, 0), (0, spare)))
    matrices = matrices.reshape(-1, slots // 8, 8, slots + spare).transpose(1, 0, 2, 3)
    matrices = matrices.reshape(-1, slots + spare)
    degree = jnp.sum(weighted.astype(jnp.float32), axis=1)
    factorial = jnp.where(degree > 2.5, 6.0, jnp.where(degree > 1.5, 2.0, 1.0))
    scale = jnp.sqrt(jnp.prod(factorial, axis=0))
    occupied = (slot_term >= 0).astype(jnp.float32)
    spread = jnp.ones((1, LANES), jnp.float32)
    return (
        jnp.concatenate([matrices, matrices], axis=1),
        (occupied * scale)[:, None] * spread,
        (occupied / scale)[:, None] * spread,
    )


def local_by_cells(source_chaos_terms, mean_conductivity, mode_shapes, coupling, slot_term, bounds):
    own, thick, cells = source_chaos_terms.shape
    chaos, spaces = lax.axis_size("chaos"), lax.axis_size("space")
    devices = chaos * spaces
    slots = own * chaos
    layers = thick * spaces
    columns = cells // LANES
    pieces = OWN_TILES * thick
    blocks = [block_of(device, spaces) for device in range(devices)]
    f32 = jnp.float32

    def shape(*sizes):
        return jax.ShapeDtypeStruct(sizes, f32)

    mix, weight, unweight = coupling_tables(coupling, slot_term, chaos)
    midpoint = 0.5 * (bounds[1] + bounds[0])
    half_span = 0.5 * (bounds[1] - bounds[0])
    sigma_one = midpoint / half_span
    rho_now = 1.0 / sigma_one
    scales = [1.0 / midpoint]
    for _ in range(ITERS - 1):
        rho_next = 1.0 / (2.0 * sigma_one - rho_now)
        scales += [rho_next * rho_now, 2.0 * rho_next / half_span]
        rho_now = rho_next
    scales = jnp.stack(scales)

    def by_columns(field):
        tiled = field.reshape(*field.shape[:-2], thick, columns, LANES)
        return jnp.swapaxes(tiled, -3, -2)

    scattered = call(
        functools.partial(scatter_kernel, blocks),
        [shape(devices, own, pieces, LANES)],
        [],
        [by_columns(source_chaos_terms).reshape(own, devices, pieces, LANES)],
        [pltpu.SemaphoreType.DMA((devices,))],
        in_kinds=[pltpu.HBM],
        out_kind=pltpu.HBM,
    )[0]
    gathered = lax.all_to_all(scattered, BOTH, 0, 0, tiled=True).reshape(-1, LANES)

    row, column = lax.axis_index("chaos"), lax.axis_index("space")

    def block_at(space):
        return row * spaces + jnp.where(row % 2 == 0, space, spaces - 1 - space)

    block = block_at(column)
    inside = jnp.stack([block > 0, block < devices - 1]).astype(f32)
    odd = (block % 2)[None]
    modes = mode_shapes.shape[0] + 1
    steps = jnp.arange(spaces)
    picked = call(
        pick_kernel,
        [shape(modes * 3 * pieces, LANES)] * spaces,
        [block_at((column + steps) % spaces), scales],
        [
            mix,
            by_columns(mean_conductivity).reshape(-1, LANES),
            by_columns(mode_shapes).reshape(-1, LANES),
        ],
    )
    picked = [picked[0]] + [
        lax.ppermute(picked[n], "space", [(i, (i + n) % spaces) for i in range(spaces)])
        for n in range(1, spaces)
    ]
    a, b, face = call(
        functools.partial(coefficient_kernel, thick),
        [shape(modes, layers, tiles * LANES) for tiles in (FOLDED, FOLDED - 1, 1)],
        [(column - steps) % spaces],
        picked,
        [pltpu.VMEM((modes, 3 * OWN_TILES, layers, LANES), f32)],
    )

    message = shape((layers + layers // 2) * slots, LANES)
    start, to_chip, to_core = call(
        functools.partial(start_kernel, chaos, spaces),
        [shape(layers, OWN_TILES, slots, LANES), message, message],
        [odd],
        [a, weight, gathered],
    )
    place = {n: device for device, n in enumerate(blocks)}

    def swap(field, lowest):
        pairs = [(place[n], place[n + 1]) for n in range(lowest, devices - 1, 2)]
        return lax.ppermute(field, BOTH, pairs + [(b, a) for a, b in pairs])

    from_chip = swap(to_chip, 1)
    from_core = swap(to_core, 0)
    own_field = shape(layers, OWN_TILES, slots, LANES)
    own_total, own_edge = call(
        own_kernel,
        [own_field, own_field],
        [scales],
        [mix, a, b, start],
        flops=3000000000,
        mebi=16,
    )

    def held(tiles):
        return pltpu.VMEM((layers, tiles, slots, LANES), f32)

    sent = call(
        functools.partial(iterate_kernel, chaos, spaces),
        [shape(devices * 2 * own * pieces, LANES)],
        [scales, inside, odd],
        [mix, a, b, face, unweight, start, own_total, own_edge, from_chip, from_core],
        [
            held(FOLDED - 1),
            held(FOLDED),
            held(FOLDED - 1),
            held(FOLDED),
            held(OWN_TILES),
        ],
        flops=10000000000,
        mebi=24,
    )[0]
    sent = sent.reshape(devices, 2, own, pieces, LANES)
    received = lax.all_to_all(sent, BOTH, 0, 0, tiled=True)
    outs = call(
        functools.partial(collect_kernel, blocks),
        [shape(own, devices, pieces, LANES)] * 2,
        [],
        [received],
        [pltpu.SemaphoreType.DMA((2, devices))],
        in_kinds=[pl.ANY],
        out_kind=pltpu.HBM,
    )
    return tuple(
        jnp.transpose(out.reshape(own, columns, thick, LANES), (0, 2, 1, 3)).reshape(
            own, thick, cells
        )
        for out in outs
    )


def local(source_chaos_terms, mean_conductivity, mode_shapes, coupling, slot_term, bounds):
    own, thick, cells = source_chaos_terms.shape
    chaos, spaces = lax.axis_size("chaos"), lax.axis_size("space")
    fits = (
        thick * spaces == 8
        and cells == chaos * spaces * OWN_TILES * LANES
        and (own * chaos) % 8 == 0
        and spaces % 2 == 0
    )
    plan = local_by_cells if fits else local_by_slots
    return plan(
        source_chaos_terms, mean_conductivity, mode_shapes, coupling, slot_term, bounds
    )


def solution(mesh):
    in_specs = (
        P(("groups", "chaos"), "space", None),
        P("space", None),
        P(None, "space", None),
        P(),
        P(),
        P("groups"),
    )
    out_specs = (P(("groups", "chaos"), "space", None), P(("groups", "chaos"), "space", None))
    return jax.shard_map(local, mesh=mesh, in_specs=in_specs, out_specs=out_specs, check_vma=False)
```

```python
import functools

import jax
import jax.numpy as jnp
from jax import lax
from jax.experimental import pallas as pl
from jax.experimental.pallas import tpu as pltpu
from jax.sharding import PartitionSpec as P

NY = 64
ITERS = 3
LANES = 128
BOTH = ("chaos", "space")


full_precision = lax.Precision.HIGHEST


def with_halo(cells, sides, width):
    for axis, dim in sides:
        count = lax.axis_size(axis)
        ends = count - 1
        head = lax.slice_in_dim(cells, 0, width, axis=dim)
        tail = lax.slice_in_dim(cells, cells.shape[dim] - width, cells.shape[dim], axis=dim)
        cells = jnp.concatenate(
            [
                lax.ppermute(tail, axis, [(i, (i + 1) % count) for i in range(ends)]),
                cells,
                lax.ppermute(head, axis, [((i + 1) % count, i) for i in range(ends)]),
            ],
            axis=dim,
        )
    return cells


def mixing_matrices(coupling, slot_term):
    occupied = (slot_term >= 0).astype(jnp.float32)
    raising = (slot_term[None, None, :] == coupling[:, :, 0:1]).astype(jnp.float32)
    lowering = (slot_term[None, None, :] == coupling[:, :, 1:2]).astype(jnp.float32)
    weight = jnp.sqrt(coupling[:, :, 2].astype(jnp.float32))
    raised = jnp.einsum("kps,kp,kpr->ksr", raising, weight, lowering, precision=full_precision)
    mode_mats = raised + jnp.transpose(raised, (0, 2, 1))
    return jnp.concatenate([jnp.diag(occupied)[None], mode_mats], axis=0)


def shift_cells(values, offset, edge_mask):
    fill = jnp.zeros(values.shape[:-1] + (abs(offset),), values.dtype)
    if offset > 0:
        shifted = jnp.concatenate([values[..., offset:], fill], axis=-1)
    else:
        shifted = jnp.concatenate([fill, values[..., :offset]], axis=-1)
    return shifted * edge_mask


def diffuse(field_padded, conduct_padded):
    centre = field_padded[..., 1:-1, :]
    conduct = conduct_padded[..., 1:-1, :]
    accumulated = (
        0.5 * (conduct + conduct_padded[..., :-2, :]) * (centre - field_padded[..., :-2, :])
    )
    accumulated = accumulated + 0.5 * (conduct + conduct_padded[..., 2:, :]) * (
        centre - field_padded[..., 2:, :]
    )
    cells = centre.shape[-1]
    column_in_row = lax.iota(jnp.int32, cells) % NY
    upper_mask = (column_in_row < NY - 1).astype(centre.dtype)
    lower_mask = (column_in_row > 0).astype(centre.dtype)
    all_mask = jnp.ones((cells,), centre.dtype)
    for offset, edge_mask in ((1, upper_mask), (-1, lower_mask), (NY, all_mask), (-NY, all_mask)):
        neighbour = shift_cells(centre, offset, edge_mask)
        neighbour_conduct = shift_cells(conduct, offset, edge_mask)
        accumulated = accumulated + 0.5 * (conduct + neighbour_conduct) * (centre - neighbour)
    return accumulated


def local_by_slots(source_chaos_terms, mean_conductivity, mode_shapes, coupling, slot_term, bounds):
    slot_count = source_chaos_terms.shape[0]
    conductivity = jnp.concatenate(
        [mean_conductivity[None], mean_conductivity[None] * mode_shapes], axis=0
    )
    conduct_padded = with_halo(conductivity, (("space", 1),), 1)
    matrices = mixing_matrices(coupling, slot_term)
    first_own = lax.axis_index("chaos") * slot_count
    own_rows = lax.dynamic_slice_in_dim(matrices, first_own, slot_count, 1)
    own_terms = lax.dynamic_slice_in_dim(slot_term, first_own, slot_count, 0)
    occupied = (own_terms >= 0).astype(jnp.float32)[:, None, None]
    lower_bound = bounds[0]
    upper_bound = bounds[1]
    midpoint = 0.5 * (upper_bound + lower_bound)
    half_span = 0.5 * (upper_bound - lower_bound)
    sigma_one = midpoint / half_span
    rho_now = 1.0 / sigma_one
    residual = source_chaos_terms * occupied
    solution_field = jnp.zeros_like(residual)
    direction = residual / midpoint
    for iteration in range(ITERS):
        solution_field = solution_field + direction
        fields = jnp.einsum(
            "ksr,rzc->kszc",
            own_rows,
            lax.all_gather(direction, "chaos", axis=0, tiled=True),
            precision=full_precision,
        )
        field_padded = with_halo(fields, (("space", 2),), 1)
        diffused = diffuse(field_padded, conduct_padded[:, None])
        residual = residual - jnp.sum(diffused, axis=0)
        if iteration + 1 < ITERS:
            rho_next = 1.0 / (2.0 * sigma_one - rho_now)
            direction = rho_next * rho_now * direction + 2.0 * rho_next / half_span * residual
            rho_now = rho_next
    return (solution_field, residual)


OWN_TILES = 2
FOLDED = OWN_TILES + ITERS


def block_of(device, spaces):
    chaos, space = divmod(device, spaces)
    return chaos * spaces + (space if chaos % 2 == 0 else spaces - 1 - space)


def lane_masks(rows):
    lane = lax.broadcasted_iota(jnp.int32, (rows, LANES), 1)
    return lane < NY, lane % NY > 0, lane % NY < NY - 1


def plane_sums(tiles, masks, first=0):
    low_half, has_left, has_right = masks
    zero = jnp.zeros(tiles[0].shape, jnp.float32)
    swapped = [pltpu.roll(tile, NY, 1) for tile in tiles]
    sums = []
    for t in range(first, len(tiles) - 1):
        if t == 0:
            across = swapped[0] + jnp.where(low_half, swapped[2], swapped[1])
        elif t == 1:
            across = swapped[1] + jnp.where(low_half, swapped[0], swapped[2])
        elif t == 2:
            across = swapped[3] + jnp.where(low_half, swapped[1], swapped[0])
        else:
            across = swapped[t - 1] + swapped[t + 1]
        left = jnp.where(has_left, pltpu.roll(tiles[t], 1, 1), zero)
        right = jnp.where(has_right, pltpu.roll(tiles[t], LANES - 1, 1), zero)
        sums.append(across + (left + right))
    return sums


def neighbour_sums(read, layer, layers, count, masks, first=0):
    sums = plane_sums([read(layer, t) for t in range(count)], masks, first)
    for other in (layer - 1, layer + 1):
        if 0 <= other < layers:
            sums = [total + read(other, first + n) for n, total in enumerate(sums)]
    return sums


def split_stack(tiles, depth):
    wide = jnp.concatenate(tiles, axis=1)
    spare = depth // 2 - wide.shape[0]
    if spare:
        wide = jnp.concatenate([wide, jnp.zeros((spare, wide.shape[1]), wide.dtype)], axis=0)
    high = wide.astype(jnp.bfloat16)
    low = (wide - high.astype(jnp.float32)).astype(jnp.bfloat16)
    return jnp.concatenate([high, low], axis=0)


def lanes(t):
    return pl.ds(t * LANES, LANES)


def run_copies(copies):
    for copy in copies:
        copy.start()
    for copy in copies:
        copy.wait()


def scatter_kernel(blocks, in_ref, out_ref, held_ref, sems):
    own = in_ref.shape[0]
    parts = sems.shape[0]
    bounds = [own * n // parts for n in range(parts + 1)]
    spans = [pl.ds(a, b - a) for a, b in zip(bounds[:-1], bounds[1:])]
    copies = [
        pltpu.make_async_copy(in_ref.at[span], held_ref.at[span], sems.at[n])
        for n, span in enumerate(spans)
    ]
    for copy in copies:
        copy.start()
    for copy, span in zip(copies, spans):
        copy.wait()
        for device, block in enumerate(blocks):
            out_ref[device, span] = held_ref[span, block]


def pick_kernel(targets, scales, mix_ref, mean_ref, modes_ref, *outs):
    count, per_mode = mean_ref.shape[0], outs[0].shape[0] // (1 + modes_ref.shape[0] // mean_ref.shape[0])
    side = per_mode // 3
    last = count // side - 1
    for n, out_ref in enumerate(outs):
        block = targets[n]
        lower = jnp.where(block > 0, 1.0, 0.0)
        upper = jnp.where(block < last, 1.0, 0.0)
        before = jnp.maximum(block - 1, 0) * side
        after = jnp.minimum(block + 1, last) * side
        for k in range(out_ref.shape[0] // per_mode):
            ref, base = (mean_ref, 0) if k == 0 else (modes_ref, (k - 1) * count)
            first = k * per_mode
            out_ref[pl.ds(first, side), :] = ref[pl.ds(base + before, side), :] * lower
            out_ref[pl.ds(first + side, side), :] = ref[pl.ds(base + block * side, side), :]
            out_ref[pl.ds(first + 2 * side, side), :] = ref[pl.ds(base + after, side), :] * upper


def layer_sum(values, layer):
    layers = values.shape[0]
    zero = jnp.zeros(values.shape, jnp.float32)
    under = jnp.where(layer > 0, pltpu.roll(values, 1, 0), zero)
    over = jnp.where(layer < layers - 1, pltpu.roll(values, layers - 1, 0), zero)
    return under + over


def coefficient_kernel(thick, sources, *refs):
    *ins, a_ref, b_ref, face_ref, held_ref = refs
    modes, layers, _ = a_ref.shape
    tiles = held_ref.shape[1]
    layer = lax.broadcasted_iota(jnp.int32, (layers, LANES), 0)
    masks = lane_masks(layers)
    low_half = masks[0]
    for n, in_ref in enumerate(ins):
        for k in range(modes):
            for u in range(tiles):
                held_ref[k, u, pl.ds(sources[n] * thick, thick), :] = in_ref[
                    pl.ds((k * tiles + u) * thick, thick), :
                ]
    mean = None
    for k in range(modes):
        runs = [held_ref[k, u] for u in range(tiles)]
        values = [
            runs[2],
            runs[3],
            jnp.where(low_half, runs[4], runs[1]),
            jnp.where(low_half, runs[1], runs[4]),
            jnp.where(low_half, runs[5], runs[0]),
        ]
        if k == 0:
            values = mean = [0.5 * value for value in values]
        else:
            values = [m * value for m, value in zip(mean, values)]
        sums = plane_sums(values, masks)
        for t in range(FOLDED):
            a_ref[k, :, lanes(t)] = values[t]
        for t in range(FOLDED - 1):
            b_ref[k, :, lanes(t)] = 6.0 * values[t] + (sums[t] + layer_sum(values[t], layer))
        face_ref[k] = pltpu.roll(jnp.where(low_half, values[0], values[1]), NY, 1)


def collect_kernel(blocks, in_ref, *rest):
    *outs, sems = rest
    run_copies(
        [
            pltpu.make_async_copy(
                in_ref.at[device, n], out_ref.at[:, block], sems.at[n, device]
            )
            for n, out_ref in enumerate(outs)
            for device, block in enumerate(blocks)
        ]
    )


def slot_parts(own, chaos):
    whole = own // 8 * 8
    parts = [(c, 0, whole, c * whole) for c in range(chaos)]
    return parts + [
        (c, whole, own - whole, chaos * whole + c * (own - whole)) for c in range(chaos)
    ]


def start_kernel(chaos, spaces, odd, a_ref, weight_ref, in_ref, residual_ref, chip_ref, core_ref):
    upward = odd[0] > 0
    layers, tiles, slots, _ = residual_ref.shape
    own = slots // chaos
    thick = layers // spaces
    pieces = tiles * thick
    half = layers // 2
    low_half = lane_masks(slots)[0]
    weight = weight_ref[...]

    def put(place, up, down):
        rows = pl.ds(place * slots, slots)
        chip_ref[rows, :] = jnp.where(upward, up, down)
        core_ref[rows, :] = jnp.where(upward, down, up)

    for l in range(layers):
        i, z = divmod(l, thick)
        for t in range(tiles):
            rows = [
                in_ref[
                    pl.ds(
                        ((c * spaces + i) * own + slot) * pieces + t * thick + z,
                        number,
                        stride=pieces,
                    ),
                    :,
                ]
                for c, slot, number, _ in slot_parts(own, chaos)
            ]
            residual_ref[l, t] = weight * jnp.concatenate(rows, axis=0)
        put(l, residual_ref[l, 1], residual_ref[l, 0])
    for l in range(half):
        later = l + half
        put(
            layers + l,
            jnp.where(low_half, pltpu.roll(residual_ref[later, 0], NY, 1), residual_ref[l, 0]),
            jnp.where(low_half, residual_ref[l, 1], pltpu.roll(residual_ref[later, 1], NY, 1)),
        )


def mode_part(mixed, modes, k, n):
    group = 8 * (modes - 1)
    return jnp.concatenate(
        [
            mixed[row : row + 8, n * LANES : (n + 1) * LANES]
            for row in range((k - 1) * 8, mixed.shape[0], group)
        ],
        axis=0,
    )


def weighted_tiles(mixed, modes, place, beside, direct, around, a_of, b_of):
    results = []
    for t, tile in enumerate(direct):
        full = t < len(around)
        a = a_of(0, t)
        edge = a * tile
        total = b_of(0, t) * tile - a * around[t] if full else None
        for k in range(1, modes):
            a = a_of(k, t)
            part = mode_part(mixed, modes, k, place + t)
            edge = edge + a * part
            if full:
                total = total + (b_of(k, t) * part - a * mode_part(mixed, modes, k, beside + t))
        results.append((total, edge))
    return results


def own_kernel(scales, mix_ref, a_ref, b_ref, start_ref, total_ref, edge_ref):
    layers, tiles, slots, _ = start_ref.shape
    modes = a_ref.shape[0]
    masks = lane_masks(slots)
    mix = mix_ref[...]
    nothing = jnp.zeros((slots, LANES), jnp.float32)

    def read(l, t):
        return start_ref[l, t] * scales[0] if t < tiles else nothing

    def prepare(l):
        direct = [read(l, t) for t in range(tiles)]
        around = neighbour_sums(read, l, layers, tiles + 1, masks)
        mixed = jnp.dot(
            mix, split_stack(direct + around, mix.shape[1]), preferred_element_type=jnp.float32
        )
        return mixed, direct, around

    ahead = prepare(0)
    for l in range(layers):
        mixed, direct, around = ahead
        if l + 1 < layers:
            ahead = prepare(l + 1)
        results = weighted_tiles(
            mixed,
            modes,
            0,
            tiles,
            direct,
            around,
            lambda k, t: a_ref[k, l : l + 1, lanes(t)],
            lambda k, t: b_ref[k, l : l + 1, lanes(t)],
        )
        for t, (total, edge) in enumerate(results):
            total_ref[l, t] = total
            edge_ref[l, t] = edge


def iterate_kernel(
    chaos,
    spaces,
    scales,
    inside,
    odd,
    mix_ref,
    a_ref,
    b_ref,
    face_ref,
    unweight_ref,
    start_ref,
    own_total_ref,
    own_edge_ref,
    chip_ref,
    core_ref,
    sent_ref,
    r_ref,
    d_ref,
    total_ref,
    edge_ref,
    x_ref,
):
    layers, _, slots, _ = start_ref.shape
    modes = a_ref.shape[0]
    own = slots // chaos
    thick = layers // spaces
    pieces = OWN_TILES * thick
    half = layers // 2
    masks = lane_masks(slots)
    low_half = masks[0]
    mix = mix_ref[...]
    depth = mix.shape[1]
    upward = odd[0] > 0

    def message(start, size):
        chip, core = chip_ref[pl.ds(start, size), :], core_ref[pl.ds(start, size), :]
        return jnp.where(upward, core, chip), jnp.where(upward, chip, core)

    def send(field, l, t, value):
        i, z = divmod(l, thick)
        value = value * unweight_ref[...]
        for c, slot, number, row in slot_parts(own, chaos):
            first = (((c * spaces + i) * 2 + field) * own + slot) * pieces + t * thick + z
            sent_ref[pl.ds(first, number, stride=pieces), :] = value[row : row + number]

    def fold(l):
        below, above = message(l * slots, slots)
        far_below, far_above = message((layers + l % half) * slots, slots)
        if l < half:
            far = jnp.where(low_half, far_above, far_below)
        else:
            far = pltpu.roll(jnp.where(low_half, far_below, far_above), NY, 1)
        tiles = [
            start_ref[l, 0],
            start_ref[l, 1],
            jnp.where(low_half, above, below),
            jnp.where(low_half, below, above),
            far,
        ]
        for t, tile in enumerate(tiles):
            if t < FOLDED - 1:
                r_ref[l, t] = tile
            d_ref[l, t] = tile * scales[0]

    def read(l, t):
        return d_ref[l, t]

    zero = jnp.zeros((slots, LANES), jnp.float32)
    prepared = {}

    def prepare(step, l):
        count = FOLDED - step
        first = OWN_TILES if step == 0 else 0
        direct = [d_ref[l, t] for t in range(first, count)]
        around = neighbour_sums(read, l, layers, count, masks, first)
        mixed = jnp.dot(
            mix, split_stack(direct + around, depth), preferred_element_type=jnp.float32
        )
        prepared[step, l] = (mixed, direct, around)

    def combine(step, l):
        first = OWN_TILES if step == 0 else 0
        mixed, direct, around = prepared.pop((step, l))
        results = weighted_tiles(
            mixed,
            modes,
            0,
            len(direct),
            direct,
            around,
            lambda k, t: a_ref[k, l : l + 1, lanes(first + t)],
            lambda k, t: b_ref[k, l : l + 1, lanes(first + t)],
        )
        for t, (total, edge) in enumerate(results):
            edge_ref[l, first + t] = edge
            if total is not None:
                total_ref[l, first + t] = total
        if step > 0:
            return
        part = face_ref[0, l : l + 1, :] * direct[0]
        for k in range(1, modes):
            part = part + face_ref[k, l : l + 1, :] * mode_part(mixed, modes, k, 0)
        part = pltpu.roll(part, NY, 1)
        total_ref[l, 0] = own_total_ref[l, 0] - jnp.where(low_half, part, zero)
        total_ref[l, 1] = own_total_ref[l, 1] - jnp.where(low_half, zero, part)

    def update(step, l):
        count = FOLDED - step

        def read_edge(l, t):
            return own_edge_ref[l, t] if step == 0 and t < OWN_TILES else edge_ref[l, t]

        spread = neighbour_sums(read_edge, l, layers, count, masks)
        for t in range(count - 1):
            diffused = total_ref[l, t] - spread[t]
            if t >= OWN_TILES:
                lower, upper = inside[(t + 1) % 2], inside[t % 2]
                diffused = diffused * jnp.where(low_half, lower, upper)
            residual = r_ref[l, t] - diffused
            if step == ITERS - 1:
                send(1, l, t, residual)
                continue
            r_ref[l, t] = residual
            old = d_ref[l, t]
            direction = scales[1 + 2 * step] * old + scales[2 + 2 * step] * residual
            d_ref[l, t] = direction
            if t < OWN_TILES:
                value = (old if step == 0 else x_ref[l, t]) + direction
                if step == ITERS - 2:
                    send(0, l, t, value)
                else:
                    x_ref[l, t] = value

    tasks = []
    for l in range(layers):
        tasks.append((l - 1.5, lambda l=l: fold(l)))
        for step in range(ITERS):
            for wait, task in ((0, prepare), (1.25, combine), (2.5, update)):
                tasks.append((l + 4 * step + wait, functools.partial(task, step, l)))
    for _, task in sorted(tasks, key=lambda task: task[0]):
        task()


def call(
    kernel, outs, scalars, arrays, scratch=(), flops=0, in_kinds=None, out_kind=pltpu.VMEM, mebi=8
):
    kinds = in_kinds or [pltpu.VMEM] * len(arrays)
    in_specs = [pl.BlockSpec(memory_space=pltpu.SMEM)] * len(scalars) + [
        pl.BlockSpec(memory_space=kind) for kind in kinds
    ]
    arrays = [
        pltpu.with_memory_space_constraint(x, kind) if kind == pltpu.HBM else x
        for x, kind in zip(arrays, kinds)
    ]
    moved = sum(4 * x.size for x in arrays) + sum(4 * x.size for x in outs)
    return pl.pallas_call(
        kernel,
        out_shape=outs,
        in_specs=in_specs,
        out_specs=[pl.BlockSpec(memory_space=out_kind)] * len(outs),
        scratch_shapes=scratch,
        compiler_params=pltpu.CompilerParams(vmem_limit_bytes=mebi * 1024 * 1024),
        cost_estimate=pl.CostEstimate(flops=flops, bytes_accessed=moved, transcendentals=0),
    )(*scalars, *arrays)


def coupling_tables(coupling, slot_term, chaos):
    bf16 = jnp.bfloat16
    slots = slot_term.shape[0]
    by_source = slot_term.reshape(chaos, -1)
    slot_term = jnp.concatenate(
        [
            by_source[c, slot : slot + number]
            for c, slot, number, _ in slot_parts(slots // chaos, chaos)
        ]
    )
    raising = (slot_term[None, None, :] == coupling[:, :, 0:1]).astype(bf16)
    lowering = (slot_term[None, None, :] == coupling[:, :, 1:2]).astype(bf16)
    weighted = raising * coupling[:, :, 2:3].astype(bf16)
    matrices = jnp.einsum(
        "kps,kpr->ksr", weighted, lowering, preferred_element_type=jnp.float32
    ) + jnp.einsum("kps,kpr->ksr", lowering, raising, preferred_element_type=jnp.float32)
    spare = -slots % 16
    matrices = jnp.pad(matrices.astype(bf16), ((0, 0), (0, 0), (0, spare)))
    matrices = matrices.reshape(-1, slots // 8, 8, slots + spare).transpose(1, 0, 2, 3)
    matrices = matrices.reshape(-1, slots + spare)
    degree = jnp.sum(weighted.astype(jnp.float32), axis=1)
    factorial = jnp.where(degree > 2.5, 6.0, jnp.where(degree > 1.5, 2.0, 1.0))
    scale = jnp.sqrt(jnp.prod(factorial, axis=0))
    occupied = (slot_term >= 0).astype(jnp.float32)
    spread = jnp.ones((1, LANES), jnp.float32)
    return (
        jnp.concatenate([matrices, matrices], axis=1),
        (occupied * scale)[:, None] * spread,
        (occupied / scale)[:, None] * spread,
    )


def local_by_cells(source_chaos_terms, mean_conductivity, mode_shapes, coupling, slot_term, bounds):
    own, thick, cells = source_chaos_terms.shape
    chaos, spaces = lax.axis_size("chaos"), lax.axis_size("space")
    devices = chaos * spaces
    slots = own * chaos
    layers = thick * spaces
    columns = cells // LANES
    pieces = OWN_TILES * thick
    blocks = [block_of(device, spaces) for device in range(devices)]
    f32 = jnp.float32

    def shape(*sizes):
        return jax.ShapeDtypeStruct(sizes, f32)

    mix, weight, unweight = coupling_tables(coupling, slot_term, chaos)
    midpoint = 0.5 * (bounds[1] + bounds[0])
    half_span = 0.5 * (bounds[1] - bounds[0])
    sigma_one = midpoint / half_span
    rho_now = 1.0 / sigma_one
    scales = [1.0 / midpoint]
    for _ in range(ITERS - 1):
        rho_next = 1.0 / (2.0 * sigma_one - rho_now)
        scales += [rho_next * rho_now, 2.0 * rho_next / half_span]
        rho_now = rho_next
    scales = jnp.stack(scales)

    def by_columns(field):
        tiled = field.reshape(*field.shape[:-2], thick, columns, LANES)
        return jnp.swapaxes(tiled, -3, -2)

    scattered = call(
        functools.partial(scatter_kernel, blocks),
        [shape(devices, own, pieces, LANES)],
        [],
        [by_columns(source_chaos_terms).reshape(own, devices, pieces, LANES)],
        [pltpu.VMEM((own, devices, pieces, LANES), f32), pltpu.SemaphoreType.DMA((4,))],
        in_kinds=[pltpu.HBM],
    )[0]
    gathered = lax.all_to_all(scattered, BOTH, 0, 0, tiled=True).reshape(-1, LANES)

    row, column = lax.axis_index("chaos"), lax.axis_index("space")

    def block_at(space):
        return row * spaces + jnp.where(row % 2 == 0, space, spaces - 1 - space)

    block = block_at(column)
    inside = jnp.stack([block > 0, block < devices - 1]).astype(f32)
    odd = (block % 2)[None]
    modes = mode_shapes.shape[0] + 1
    steps = jnp.arange(spaces)
    picked = call(
        pick_kernel,
        [shape(modes * 3 * pieces, LANES)] * spaces,
        [block_at((column + steps) % spaces), scales],
        [
            mix,
            by_columns(mean_conductivity).reshape(-1, LANES),
            by_columns(mode_shapes).reshape(-1, LANES),
        ],
    )
    picked = [picked[0]] + [
        lax.ppermute(picked[n], "space", [(i, (i + n) % spaces) for i in range(spaces)])
        for n in range(1, spaces)
    ]
    a, b, face = call(
        functools.partial(coefficient_kernel, thick),
        [shape(modes, layers, tiles * LANES) for tiles in (FOLDED, FOLDED - 1, 1)],
        [(column - steps) % spaces],
        picked,
        [pltpu.VMEM((modes, 3 * OWN_TILES, layers, LANES), f32)],
    )

    message = shape((layers + layers // 2) * slots, LANES)
    start, to_chip, to_core = call(
        functools.partial(start_kernel, chaos, spaces),
        [shape(layers, OWN_TILES, slots, LANES), message, message],
        [odd],
        [a, weight, gathered],
    )
    place = {n: device for device, n in enumerate(blocks)}

    def swap(field, lowest):
        pairs = [(place[n], place[n + 1]) for n in range(lowest, devices - 1, 2)]
        return lax.ppermute(field, BOTH, pairs + [(b, a) for a, b in pairs])

    from_chip = swap(to_chip, 1)
    from_core = swap(to_core, 0)
    own_field = shape(layers, OWN_TILES, slots, LANES)
    own_total, own_edge = call(
        own_kernel,
        [own_field, own_field],
        [scales],
        [mix, a, b, start],
        flops=3000000000,
        mebi=16,
    )

    def held(tiles):
        return pltpu.VMEM((layers, tiles, slots, LANES), f32)

    sent = call(
        functools.partial(iterate_kernel, chaos, spaces),
        [shape(devices * 2 * own * pieces, LANES)],
        [scales, inside, odd],
        [mix, a, b, face, unweight, start, own_total, own_edge, from_chip, from_core],
        [
            held(FOLDED - 1),
            held(FOLDED),
            held(FOLDED - 1),
            held(FOLDED),
            held(OWN_TILES),
        ],
        flops=10000000000,
        mebi=24,
    )[0]
    sent = sent.reshape(devices, 2, own, pieces, LANES)
    received = lax.all_to_all(sent, BOTH, 0, 0, tiled=True)
    outs = call(
        functools.partial(collect_kernel, blocks),
        [shape(own, devices, pieces, LANES)] * 2,
        [],
        [received],
        [pltpu.SemaphoreType.DMA((2, devices))],
        in_kinds=[pl.ANY],
        out_kind=pltpu.HBM,
    )
    return tuple(
        jnp.transpose(out.reshape(own, columns, thick, LANES), (0, 2, 1, 3)).reshape(
            own, thick, cells
        )
        for out in outs
    )


def local(source_chaos_terms, mean_conductivity, mode_shapes, coupling, slot_term, bounds):
    own, thick, cells = source_chaos_terms.shape
    chaos, spaces = lax.axis_size("chaos"), lax.axis_size("space")
    fits = (
        thick * spaces == 8
        and cells == chaos * spaces * OWN_TILES * LANES
        and (own * chaos) % 8 == 0
        and spaces % 2 == 0
    )
    plan = local_by_cells if fits else local_by_slots
    return plan(
        source_chaos_terms, mean_conductivity, mode_shapes, coupling, slot_term, bounds
    )


def solution(mesh):
    in_specs = (
        P(("groups", "chaos"), "space", None),
        P("space", None),
        P(None, "space", None),
        P(),
        P(),
        P("groups"),
    )
    out_specs = (P(("groups", "chaos"), "space", None), P(("groups", "chaos"), "space", None))
    return jax.shard_map(local, mesh=mesh, in_specs=in_specs, out_specs=out_specs, check_vma=False)
```

```python
import functools

import jax
import jax.numpy as jnp
from jax import lax
from jax.experimental import pallas as pl
from jax.experimental.pallas import tpu as pltpu
from jax.sharding import PartitionSpec as P

NY = 64
ITERS = 3
LANES = 128
BOTH = ("chaos", "space")


full_precision = lax.Precision.HIGHEST


def with_halo(cells, sides, width):
    for axis, dim in sides:
        count = lax.axis_size(axis)
        ends = count - 1
        head = lax.slice_in_dim(cells, 0, width, axis=dim)
        tail = lax.slice_in_dim(cells, cells.shape[dim] - width, cells.shape[dim], axis=dim)
        cells = jnp.concatenate(
            [
                lax.ppermute(tail, axis, [(i, (i + 1) % count) for i in range(ends)]),
                cells,
                lax.ppermute(head, axis, [((i + 1) % count, i) for i in range(ends)]),
            ],
            axis=dim,
        )
    return cells


def mixing_matrices(coupling, slot_term):
    occupied = (slot_term >= 0).astype(jnp.float32)
    raising = (slot_term[None, None, :] == coupling[:, :, 0:1]).astype(jnp.float32)
    lowering = (slot_term[None, None, :] == coupling[:, :, 1:2]).astype(jnp.float32)
    weight = jnp.sqrt(coupling[:, :, 2].astype(jnp.float32))
    raised = jnp.einsum("kps,kp,kpr->ksr", raising, weight, lowering, precision=full_precision)
    mode_mats = raised + jnp.transpose(raised, (0, 2, 1))
    return jnp.concatenate([jnp.diag(occupied)[None], mode_mats], axis=0)


def shift_cells(values, offset, edge_mask):
    fill = jnp.zeros(values.shape[:-1] + (abs(offset),), values.dtype)
    if offset > 0:
        shifted = jnp.concatenate([values[..., offset:], fill], axis=-1)
    else:
        shifted = jnp.concatenate([fill, values[..., :offset]], axis=-1)
    return shifted * edge_mask


def diffuse(field_padded, conduct_padded):
    centre = field_padded[..., 1:-1, :]
    conduct = conduct_padded[..., 1:-1, :]
    accumulated = (
        0.5 * (conduct + conduct_padded[..., :-2, :]) * (centre - field_padded[..., :-2, :])
    )
    accumulated = accumulated + 0.5 * (conduct + conduct_padded[..., 2:, :]) * (
        centre - field_padded[..., 2:, :]
    )
    cells = centre.shape[-1]
    column_in_row = lax.iota(jnp.int32, cells) % NY
    upper_mask = (column_in_row < NY - 1).astype(centre.dtype)
    lower_mask = (column_in_row > 0).astype(centre.dtype)
    all_mask = jnp.ones((cells,), centre.dtype)
    for offset, edge_mask in ((1, upper_mask), (-1, lower_mask), (NY, all_mask), (-NY, all_mask)):
        neighbour = shift_cells(centre, offset, edge_mask)
        neighbour_conduct = shift_cells(conduct, offset, edge_mask)
        accumulated = accumulated + 0.5 * (conduct + neighbour_conduct) * (centre - neighbour)
    return accumulated


def local_by_slots(source_chaos_terms, mean_conductivity, mode_shapes, coupling, slot_term, bounds):
    slot_count = source_chaos_terms.shape[0]
    conductivity = jnp.concatenate(
        [mean_conductivity[None], mean_conductivity[None] * mode_shapes], axis=0
    )
    conduct_padded = with_halo(conductivity, (("space", 1),), 1)
    matrices = mixing_matrices(coupling, slot_term)
    first_own = lax.axis_index("chaos") * slot_count
    own_rows = lax.dynamic_slice_in_dim(matrices, first_own, slot_count, 1)
    own_terms = lax.dynamic_slice_in_dim(slot_term, first_own, slot_count, 0)
    occupied = (own_terms >= 0).astype(jnp.float32)[:, None, None]
    lower_bound = bounds[0]
    upper_bound = bounds[1]
    midpoint = 0.5 * (upper_bound + lower_bound)
    half_span = 0.5 * (upper_bound - lower_bound)
    sigma_one = midpoint / half_span
    rho_now = 1.0 / sigma_one
    residual = source_chaos_terms * occupied
    solution_field = jnp.zeros_like(residual)
    direction = residual / midpoint
    for iteration in range(ITERS):
        solution_field = solution_field + direction
        fields = jnp.einsum(
            "ksr,rzc->kszc",
            own_rows,
            lax.all_gather(direction, "chaos", axis=0, tiled=True),
            precision=full_precision,
        )
        field_padded = with_halo(fields, (("space", 2),), 1)
        diffused = diffuse(field_padded, conduct_padded[:, None])
        residual = residual - jnp.sum(diffused, axis=0)
        if iteration + 1 < ITERS:
            rho_next = 1.0 / (2.0 * sigma_one - rho_now)
            direction = rho_next * rho_now * direction + 2.0 * rho_next / half_span * residual
            rho_now = rho_next
    return (solution_field, residual)


OWN_TILES = 2
FOLDED = OWN_TILES + ITERS


def block_of(device, spaces):
    chaos, space = divmod(device, spaces)
    return chaos * spaces + (space if chaos % 2 == 0 else spaces - 1 - space)


def lane_masks(rows):
    lane = lax.broadcasted_iota(jnp.int32, (rows, LANES), 1)
    return lane < NY, lane % NY > 0, lane % NY < NY - 1


def plane_sums(tiles, masks, first=0):
    low_half, has_left, has_right = masks
    zero = jnp.zeros(tiles[0].shape, jnp.float32)
    swapped = [pltpu.roll(tile, NY, 1) for tile in tiles]
    sums = []
    for t in range(first, len(tiles) - 1):
        if t == 0:
            across = swapped[0] + jnp.where(low_half, swapped[2], swapped[1])
        elif t == 1:
            across = swapped[1] + jnp.where(low_half, swapped[0], swapped[2])
        elif t == 2:
            across = swapped[3] + jnp.where(low_half, swapped[1], swapped[0])
        else:
            across = swapped[t - 1] + swapped[t + 1]
        left = jnp.where(has_left, pltpu.roll(tiles[t], 1, 1), zero)
        right = jnp.where(has_right, pltpu.roll(tiles[t], LANES - 1, 1), zero)
        sums.append(across + (left + right))
    return sums


def neighbour_sums(read, layer, layers, count, masks, first=0):
    sums = plane_sums([read(layer, t) for t in range(count)], masks, first)
    for other in (layer - 1, layer + 1):
        if 0 <= other < layers:
            sums = [total + read(other, first + n) for n, total in enumerate(sums)]
    return sums


def split_stack(tiles, depth):
    wide = jnp.concatenate(tiles, axis=1)
    spare = depth // 2 - wide.shape[0]
    if spare:
        wide = jnp.concatenate([wide, jnp.zeros((spare, wide.shape[1]), wide.dtype)], axis=0)
    high = wide.astype(jnp.bfloat16)
    low = (wide - high.astype(jnp.float32)).astype(jnp.bfloat16)
    return jnp.concatenate([high, low], axis=0)


def lanes(t):
    return pl.ds(t * LANES, LANES)


def run_copies(copies):
    for copy in copies:
        copy.start()
    for copy in copies:
        copy.wait()


def scatter_kernel(blocks, in_ref, out_ref, held_ref, in_sems, out_sems):
    own = in_ref.shape[0]
    parts = in_sems.shape[0]
    bounds = [own * n // parts for n in range(parts + 1)]
    spans = [pl.ds(a, b - a) for a, b in zip(bounds[:-1], bounds[1:])]
    copies = [
        pltpu.make_async_copy(in_ref.at[span], held_ref.at[span], in_sems.at[n])
        for n, span in enumerate(spans)
    ]
    for copy in copies:
        copy.start()
    leaving = []
    for n, (copy, span) in enumerate(zip(copies, spans)):
        copy.wait()
        for device, block in enumerate(blocks):
            leaving.append(
                pltpu.make_async_copy(
                    held_ref.at[span, block], out_ref.at[device, span], out_sems.at[n, device]
                )
            )
            leaving[-1].start()
    for copy in leaving:
        copy.wait()


def pick_kernel(targets, scales, mix_ref, mean_ref, modes_ref, *outs):
    count, per_mode = mean_ref.shape[0], outs[0].shape[0] // (1 + modes_ref.shape[0] // mean_ref.shape[0])
    side = per_mode // 3
    last = count // side - 1
    for n, out_ref in enumerate(outs):
        block = targets[n]
        lower = jnp.where(block > 0, 1.0, 0.0)
        upper = jnp.where(block < last, 1.0, 0.0)
        before = jnp.maximum(block - 1, 0) * side
        after = jnp.minimum(block + 1, last) * side
        for k in range(out_ref.shape[0] // per_mode):
            ref, base = (mean_ref, 0) if k == 0 else (modes_ref, (k - 1) * count)
            first = k * per_mode
            out_ref[pl.ds(first, side), :] = ref[pl.ds(base + before, side), :] * lower
            out_ref[pl.ds(first + side, side), :] = ref[pl.ds(base + block * side, side), :]
            out_ref[pl.ds(first + 2 * side, side), :] = ref[pl.ds(base + after, side), :] * upper


def layer_sum(values, layer):
    layers = values.shape[0]
    zero = jnp.zeros(values.shape, jnp.float32)
    under = jnp.where(layer > 0, pltpu.roll(values, 1, 0), zero)
    over = jnp.where(layer < layers - 1, pltpu.roll(values, layers - 1, 0), zero)
    return under + over


def coefficient_kernel(thick, sources, *refs):
    *ins, a_ref, b_ref, face_ref, held_ref = refs
    modes, layers, _ = a_ref.shape
    tiles = held_ref.shape[1]
    layer = lax.broadcasted_iota(jnp.int32, (layers, LANES), 0)
    masks = lane_masks(layers)
    low_half = masks[0]
    for n, in_ref in enumerate(ins):
        for k in range(modes):
            for u in range(tiles):
                held_ref[k, u, pl.ds(sources[n] * thick, thick), :] = in_ref[
                    pl.ds((k * tiles + u) * thick, thick), :
                ]
    mean = None
    for k in range(modes):
        runs = [held_ref[k, u] for u in range(tiles)]
        values = [
            runs[2],
            runs[3],
            jnp.where(low_half, runs[4], runs[1]),
            jnp.where(low_half, runs[1], runs[4]),
            jnp.where(low_half, runs[5], runs[0]),
        ]
        if k == 0:
            values = mean = [0.5 * value for value in values]
        else:
            values = [m * value for m, value in zip(mean, values)]
        sums = plane_sums(values, masks)
        for t in range(FOLDED):
            a_ref[k, :, lanes(t)] = values[t]
        for t in range(FOLDED - 1):
            b_ref[k, :, lanes(t)] = 6.0 * values[t] + (sums[t] + layer_sum(values[t], layer))
        face_ref[k] = pltpu.roll(jnp.where(low_half, values[0], values[1]), NY, 1)


def collect_kernel(blocks, in_ref, *rest):
    *outs, sems = rest
    run_copies(
        [
            pltpu.make_async_copy(
                in_ref.at[device, n], out_ref.at[:, block], sems.at[n, device]
            )
            for n, out_ref in enumerate(outs)
            for device, block in enumerate(blocks)
        ]
    )


def slot_parts(own, chaos):
    whole = own // 8 * 8
    parts = [(c, 0, whole, c * whole) for c in range(chaos)]
    return parts + [
        (c, whole, own - whole, chaos * whole + c * (own - whole)) for c in range(chaos)
    ]


def start_kernel(chaos, spaces, odd, a_ref, weight_ref, in_ref, residual_ref, chip_ref, core_ref):
    upward = odd[0] > 0
    layers, tiles, slots, _ = residual_ref.shape
    own = slots // chaos
    thick = layers // spaces
    pieces = tiles * thick
    half = layers // 2
    low_half = lane_masks(slots)[0]
    weight = weight_ref[...]

    def put(place, up, down):
        rows = pl.ds(place * slots, slots)
        chip_ref[rows, :] = jnp.where(upward, up, down)
        core_ref[rows, :] = jnp.where(upward, down, up)

    for l in range(layers):
        i, z = divmod(l, thick)
        for t in range(tiles):
            rows = [
                in_ref[
                    pl.ds(
                        ((c * spaces + i) * own + slot) * pieces + t * thick + z,
                        number,
                        stride=pieces,
                    ),
                    :,
                ]
                for c, slot, number, _ in slot_parts(own, chaos)
            ]
            residual_ref[l, t] = weight * jnp.concatenate(rows, axis=0)
        put(l, residual_ref[l, 1], residual_ref[l, 0])
    for l in range(half):
        later = l + half
        put(
            layers + l,
            jnp.where(low_half, pltpu.roll(residual_ref[later, 0], NY, 1), residual_ref[l, 0]),
            jnp.where(low_half, residual_ref[l, 1], pltpu.roll(residual_ref[later, 1], NY, 1)),
        )


def mode_part(mixed, modes, k, n):
    group = 8 * (modes - 1)
    return jnp.concatenate(
        [
            mixed[row : row + 8, n * LANES : (n + 1) * LANES]
            for row in range((k - 1) * 8, mixed.shape[0], group)
        ],
        axis=0,
    )


def weighted_tiles(mixed, modes, place, beside, direct, around, a_of, b_of):
    results = []
    for t, tile in enumerate(direct):
        full = t < len(around)
        a = a_of(0, t)
        edge = a * tile
        total = b_of(0, t) * tile - a * around[t] if full else None
        for k in range(1, modes):
            a = a_of(k, t)
            part = mode_part(mixed, modes, k, place + t)
            edge = edge + a * part
            if full:
                total = total + (b_of(k, t) * part - a * mode_part(mixed, modes, k, beside + t))
        results.append((total, edge))
    return results


def own_kernel(scales, mix_ref, a_ref, b_ref, start_ref, total_ref, edge_ref):
    layers, tiles, slots, _ = start_ref.shape
    modes = a_ref.shape[0]
    masks = lane_masks(slots)
    mix = mix_ref[...]
    nothing = jnp.zeros((slots, LANES), jnp.float32)

    def read(l, t):
        return start_ref[l, t] * scales[0] if t < tiles else nothing

    def prepare(l):
        direct = [read(l, t) for t in range(tiles)]
        around = neighbour_sums(read, l, layers, tiles + 1, masks)
        mixed = jnp.dot(
            mix, split_stack(direct + around, mix.shape[1]), preferred_element_type=jnp.float32
        )
        return mixed, direct, around

    ahead = prepare(0)
    for l in range(layers):
        mixed, direct, around = ahead
        if l + 1 < layers:
            ahead = prepare(l + 1)
        results = weighted_tiles(
            mixed,
            modes,
            0,
            tiles,
            direct,
            around,
            lambda k, t: a_ref[k, l : l + 1, lanes(t)],
            lambda k, t: b_ref[k, l : l + 1, lanes(t)],
        )
        for t, (total, edge) in enumerate(results):
            total_ref[l, t] = total
            edge_ref[l, t] = edge


def iterate_kernel(
    chaos,
    spaces,
    scales,
    inside,
    odd,
    mix_ref,
    a_ref,
    b_ref,
    face_ref,
    unweight_ref,
    start_ref,
    own_total_ref,
    own_edge_ref,
    chip_ref,
    core_ref,
    sent_ref,
    r_ref,
    d_ref,
    total_ref,
    edge_ref,
    x_ref,
):
    layers, _, slots, _ = start_ref.shape
    modes = a_ref.shape[0]
    own = slots // chaos
    thick = layers // spaces
    pieces = OWN_TILES * thick
    half = layers // 2
    masks = lane_masks(slots)
    low_half = masks[0]
    mix = mix_ref[...]
    depth = mix.shape[1]
    upward = odd[0] > 0

    def message(start, size):
        chip, core = chip_ref[pl.ds(start, size), :], core_ref[pl.ds(start, size), :]
        return jnp.where(upward, core, chip), jnp.where(upward, chip, core)

    def send(field, l, t, value):
        i, z = divmod(l, thick)
        value = value * unweight_ref[...]
        for c, slot, number, row in slot_parts(own, chaos):
            first = (((c * spaces + i) * 2 + field) * own + slot) * pieces + t * thick + z
            sent_ref[pl.ds(first, number, stride=pieces), :] = value[row : row + number]

    def fold(l):
        below, above = message(l * slots, slots)
        far_below, far_above = message((layers + l % half) * slots, slots)
        if l < half:
            far = jnp.where(low_half, far_above, far_below)
        else:
            far = pltpu.roll(jnp.where(low_half, far_below, far_above), NY, 1)
        tiles = [
            start_ref[l, 0],
            start_ref[l, 1],
            jnp.where(low_half, above, below),
            jnp.where(low_half, below, above),
            far,
        ]
        for t, tile in enumerate(tiles):
            if t < FOLDED - 1:
                r_ref[l, t] = tile
            d_ref[l, t] = tile * scales[0]

    def read(l, t):
        return d_ref[l, t]

    zero = jnp.zeros((slots, LANES), jnp.float32)
    prepared = {}

    def prepare(step, l):
        count = FOLDED - step
        first = OWN_TILES if step == 0 else 0
        direct = [d_ref[l, t] for t in range(first, count)]
        around = neighbour_sums(read, l, layers, count, masks, first)
        mixed = jnp.dot(
            mix, split_stack(direct + around, depth), preferred_element_type=jnp.float32
        )
        prepared[step, l] = (mixed, direct, around)

    def combine(step, l):
        first = OWN_TILES if step == 0 else 0
        mixed, direct, around = prepared.pop((step, l))
        results = weighted_tiles(
            mixed,
            modes,
            0,
            len(direct),
            direct,
            around,
            lambda k, t: a_ref[k, l : l + 1, lanes(first + t)],
            lambda k, t: b_ref[k, l : l + 1, lanes(first + t)],
        )
        for t, (total, edge) in enumerate(results):
            edge_ref[l, first + t] = edge
            if total is not None:
                total_ref[l, first + t] = total
        if step > 0:
            return
        part = face_ref[0, l : l + 1, :] * direct[0]
        for k in range(1, modes):
            part = part + face_ref[k, l : l + 1, :] * mode_part(mixed, modes, k, 0)
        part = pltpu.roll(part, NY, 1)
        total_ref[l, 0] = own_total_ref[l, 0] - jnp.where(low_half, part, zero)
        total_ref[l, 1] = own_total_ref[l, 1] - jnp.where(low_half, zero, part)

    def update(step, l):
        count = FOLDED - step

        def read_edge(l, t):
            return own_edge_ref[l, t] if step == 0 and t < OWN_TILES else edge_ref[l, t]

        spread = neighbour_sums(read_edge, l, layers, count, masks)
        for t in range(count - 1):
            diffused = total_ref[l, t] - spread[t]
            if t >= OWN_TILES:
                lower, upper = inside[(t + 1) % 2], inside[t % 2]
                diffused = diffused * jnp.where(low_half, lower, upper)
            residual = r_ref[l, t] - diffused
            if step == ITERS - 1:
                send(1, l, t, residual)
                continue
            r_ref[l, t] = residual
            old = d_ref[l, t]
            direction = scales[1 + 2 * step] * old + scales[2 + 2 * step] * residual
            d_ref[l, t] = direction
            if t < OWN_TILES:
                value = (old if step == 0 else x_ref[l, t]) + direction
                if step == ITERS - 2:
                    send(0, l, t, value)
                else:
                    x_ref[l, t] = value

    tasks = []
    for l in range(layers):
        tasks.append((l - 1.5, lambda l=l: fold(l)))
        for step in range(ITERS):
            for wait, task in ((0, prepare), (1.25, combine), (2.5, update)):
                tasks.append((l + 4 * step + wait, functools.partial(task, step, l)))
    for _, task in sorted(tasks, key=lambda task: task[0]):
        task()


def call(
    kernel, outs, scalars, arrays, scratch=(), flops=0, in_kinds=None, out_kind=pltpu.VMEM, mebi=8
):
    kinds = in_kinds or [pltpu.VMEM] * len(arrays)
    in_specs = [pl.BlockSpec(memory_space=pltpu.SMEM)] * len(scalars) + [
        pl.BlockSpec(memory_space=kind) for kind in kinds
    ]
    arrays = [
        pltpu.with_memory_space_constraint(x, kind) if kind == pltpu.HBM else x
        for x, kind in zip(arrays, kinds)
    ]
    moved = sum(4 * x.size for x in arrays) + sum(4 * x.size for x in outs)
    return pl.pallas_call(
        kernel,
        out_shape=outs,
        in_specs=in_specs,
        out_specs=[pl.BlockSpec(memory_space=out_kind)] * len(outs),
        scratch_shapes=scratch,
        compiler_params=pltpu.CompilerParams(vmem_limit_bytes=mebi * 1024 * 1024),
        cost_estimate=pl.CostEstimate(flops=flops, bytes_accessed=moved, transcendentals=0),
    )(*scalars, *arrays)


def coupling_tables(coupling, slot_term, chaos):
    bf16 = jnp.bfloat16
    slots = slot_term.shape[0]
    by_source = slot_term.reshape(chaos, -1)
    slot_term = jnp.concatenate(
        [
            by_source[c, slot : slot + number]
            for c, slot, number, _ in slot_parts(slots // chaos, chaos)
        ]
    )
    raising = (slot_term[None, None, :] == coupling[:, :, 0:1]).astype(bf16)
    lowering = (slot_term[None, None, :] == coupling[:, :, 1:2]).astype(bf16)
    weighted = raising * coupling[:, :, 2:3].astype(bf16)
    matrices = jnp.einsum(
        "kps,kpr->ksr", weighted, lowering, preferred_element_type=jnp.float32
    ) + jnp.einsum("kps,kpr->ksr", lowering, raising, preferred_element_type=jnp.float32)
    spare = -slots % 16
    matrices = jnp.pad(matrices.astype(bf16), ((0, 0), (0, 0), (0, spare)))
    matrices = matrices.reshape(-1, slots // 8, 8, slots + spare).transpose(1, 0, 2, 3)
    matrices = matrices.reshape(-1, slots + spare)
    degree = jnp.sum(weighted.astype(jnp.float32), axis=1)
    factorial = jnp.where(degree > 2.5, 6.0, jnp.where(degree > 1.5, 2.0, 1.0))
    scale = jnp.sqrt(jnp.prod(factorial, axis=0))
    occupied = (slot_term >= 0).astype(jnp.float32)
    spread = jnp.ones((1, LANES), jnp.float32)
    return (
        jnp.concatenate([matrices, matrices], axis=1),
        (occupied * scale)[:, None] * spread,
        (occupied / scale)[:, None] * spread,
    )


def local_by_cells(source_chaos_terms, mean_conductivity, mode_shapes, coupling, slot_term, bounds):
    own, thick, cells = source_chaos_terms.shape
    chaos, spaces = lax.axis_size("chaos"), lax.axis_size("space")
    devices = chaos * spaces
    slots = own * chaos
    layers = thick * spaces
    columns = cells // LANES
    pieces = OWN_TILES * thick
    blocks = [block_of(device, spaces) for device in range(devices)]
    f32 = jnp.float32

    def shape(*sizes):
        return jax.ShapeDtypeStruct(sizes, f32)

    mix, weight, unweight = coupling_tables(coupling, slot_term, chaos)
    midpoint = 0.5 * (bounds[1] + bounds[0])
    half_span = 0.5 * (bounds[1] - bounds[0])
    sigma_one = midpoint / half_span
    rho_now = 1.0 / sigma_one
    scales = [1.0 / midpoint]
    for _ in range(ITERS - 1):
        rho_next = 1.0 / (2.0 * sigma_one - rho_now)
        scales += [rho_next * rho_now, 2.0 * rho_next / half_span]
        rho_now = rho_next
    scales = jnp.stack(scales)

    def by_columns(field):
        tiled = field.reshape(*field.shape[:-2], thick, columns, LANES)
        return jnp.swapaxes(tiled, -3, -2)

    scattered = call(
        functools.partial(scatter_kernel, blocks),
        [shape(devices, own, pieces, LANES)],
        [],
        [by_columns(source_chaos_terms).reshape(own, devices, pieces, LANES)],
        [
            pltpu.VMEM((own, devices, pieces, LANES), f32),
            pltpu.SemaphoreType.DMA((2,)),
            pltpu.SemaphoreType.DMA((2, devices)),
        ],
        in_kinds=[pltpu.HBM],
        out_kind=pltpu.HBM,
    )[0]
    gathered = lax.all_to_all(scattered, BOTH, 0, 0, tiled=True).reshape(-1, LANES)

    row, column = lax.axis_index("chaos"), lax.axis_index("space")

    def block_at(space):
        return row * spaces + jnp.where(row % 2 == 0, space, spaces - 1 - space)

    block = block_at(column)
    inside = jnp.stack([block > 0, block < devices - 1]).astype(f32)
    odd = (block % 2)[None]
    modes = mode_shapes.shape[0] + 1
    steps = jnp.arange(spaces)
    picked = call(
        pick_kernel,
        [shape(modes * 3 * pieces, LANES)] * spaces,
        [block_at((column + steps) % spaces), scales],
        [
            mix,
            by_columns(mean_conductivity).reshape(-1, LANES),
            by_columns(mode_shapes).reshape(-1, LANES),
        ],
    )
    picked = [picked[0]] + [
        lax.ppermute(picked[n], "space", [(i, (i + n) % spaces) for i in range(spaces)])
        for n in range(1, spaces)
    ]
    a, b, face = call(
        functools.partial(coefficient_kernel, thick),
        [shape(modes, layers, tiles * LANES) for tiles in (FOLDED, FOLDED - 1, 1)],
        [(column - steps) % spaces],
        picked,
        [pltpu.VMEM((modes, 3 * OWN_TILES, layers, LANES), f32)],
    )

    message = shape((layers + layers // 2) * slots, LANES)
    start, to_chip, to_core = call(
        functools.partial(start_kernel, chaos, spaces),
        [shape(layers, OWN_TILES, slots, LANES), message, message],
        [odd],
        [a, weight, gathered],
    )
    place = {n: device for device, n in enumerate(blocks)}

    def swap(field, lowest):
        pairs = [(place[n], place[n + 1]) for n in range(lowest, devices - 1, 2)]
        return lax.ppermute(field, BOTH, pairs + [(b, a) for a, b in pairs])

    from_chip = swap(to_chip, 1)
    from_core = swap(to_core, 0)
    own_field = shape(layers, OWN_TILES, slots, LANES)
    own_total, own_edge = call(
        own_kernel,
        [own_field, own_field],
        [scales],
        [mix, a, b, start],
        flops=3000000000,
        mebi=16,
    )

    def held(tiles):
        return pltpu.VMEM((layers, tiles, slots, LANES), f32)

    sent = call(
        functools.partial(iterate_kernel, chaos, spaces),
        [shape(devices * 2 * own * pieces, LANES)],
        [scales, inside, odd],
        [mix, a, b, face, unweight, start, own_total, own_edge, from_chip, from_core],
        [
            held(FOLDED - 1),
            held(FOLDED),
            held(FOLDED - 1),
            held(FOLDED),
            held(OWN_TILES),
        ],
        flops=10000000000,
        mebi=24,
    )[0]
    sent = sent.reshape(devices, 2, own, pieces, LANES)
    received = lax.all_to_all(sent, BOTH, 0, 0, tiled=True)
    outs = call(
        functools.partial(collect_kernel, blocks),
        [shape(own, devices, pieces, LANES)] * 2,
        [],
        [received],
        [pltpu.SemaphoreType.DMA((2, devices))],
        in_kinds=[pl.ANY],
        out_kind=pltpu.HBM,
    )
    return tuple(
        jnp.transpose(out.reshape(own, columns, thick, LANES), (0, 2, 1, 3)).reshape(
            own, thick, cells
        )
        for out in outs
    )


def local(source_chaos_terms, mean_conductivity, mode_shapes, coupling, slot_term, bounds):
    own, thick, cells = source_chaos_terms.shape
    chaos, spaces = lax.axis_size("chaos"), lax.axis_size("space")
    fits = (
        thick * spaces == 8
        and cells == chaos * spaces * OWN_TILES * LANES
        and (own * chaos) % 8 == 0
        and spaces % 2 == 0
    )
    plan = local_by_cells if fits else local_by_slots
    return plan(
        source_chaos_terms, mean_conductivity, mode_shapes, coupling, slot_term, bounds
    )


def solution(mesh):
    in_specs = (
        P(("groups", "chaos"), "space", None),
        P("space", None),
        P(None, "space", None),
        P(),
        P(),
        P("groups"),
    )
    out_specs = (P(("groups", "chaos"), "space", None), P(("groups", "chaos"), "space", None))
    return jax.shard_map(local, mesh=mesh, in_specs=in_specs, out_specs=out_specs, check_vma=False)
```
